32 devices in a mesh: sec: 8 (over z, y), girth: 4 (over x, core).
Axes of the slice: x: 2, y: 2, z: 4, core: 2. Of those that a mesh axis runs over, the one named last changes fastest.
Arguments:
- displacement: float32 [5, 512, 2048], P(None, 'sec', 'girth'), may hold values from -6 to 6
- velocity: float32 [5, 512, 2048], P(None, 'sec', 'girth'), may hold values from -6 to 6
- stress: float32 [8, 512, 2048], P(None, 'sec', 'girth'), may hold values from -3 to 3
- thickness: int32 [512, 2048], P('sec', 'girth'), may hold values from 8 to 32
- pressure: float32 [512, 2048], P('sec', 'girth'), may hold values from 0.2 to 1
- weld_from: int32 [32, 32, 16], P(('sec', 'girth')), may hold values from -1 to 32767, as said below
- weld_to: int32 [32, 32, 16], P(('sec', 'girth')), may hold values from -1 to 32767, as said below
- weld_stiff: float32 [32, 32, 16], P(('sec', 'girth')), may hold values from 0.5 to 4
Outputs:
- displacement_out: float32 [5, 512, 2048], P(None, 'sec', 'girth')
- velocity_out: float32 [5, 512, 2048], P(None, 'sec', 'girth')
- stress_out: float32 [8, 512, 2048], P(None, 'sec', 'girth')
- section_moment: float32 [512], P('sec')
The draws below stay inside these ranges and needn't reach their ends.
Inputs may be any that keep to these rules, and one draw needn't show every extreme that they name: weld_from[s, p, c] and weld_to[p, s, c] are the two nodes (numbered row by row within a device's 64 x 512 block) of one joint between devices s and p, or both -1 for an unused slot; in each pair (s, p) the used slots come first; each device s uses all 16 slots towards the next device along sec+girth (the last towards the first). `weld_to`: see weld_from.
All inputs are finite; a program needn't handle non-finite values.
Results may differ from the reference program's by a relative error of at most 0.00021.
Values sent between devices are 32-bit elements; how exact they have to be, the bound alone decides.
No kernel may reach another device: no remote copies, remote signals or barrier semaphores. Data moves between devices by JAX's collectives and lax.ppermute only.
A program may use at most 64 MiB of HBM per device.

```python
import math
import jax
import jax.numpy as jnp
from jax import lax

CL = 64
CG = 512
CAP = 16
STEPS = 3
NL = 512
NG = 2048
N_SEC = 8
N_GIRTH = 4
DEVICES = 32


def weld_plan(key):
    key = jax.random.fold_in(key, 5)
    devices = N_SEC * N_GIRTH
    busy_key, count_key = jax.random.split(key, 2)
    busy_level = jax.random.randint(busy_key, (devices, 1), 1, 5)
    ceiling = CAP * busy_level // 4
    counts = jax.random.randint(count_key, (devices, devices), ceiling // 2, ceiling + 1)
    source = lax.broadcasted_iota(jnp.int32, (devices, devices), 0)
    target = lax.broadcasted_iota(jnp.int32, (devices, devices), 1)
    counts = jnp.where(target == (source + 1) % devices, CAP, counts)
    slot_index = lax.broadcasted_iota(jnp.int32, (devices, devices, CAP), 2)
    return slot_index < counts[:, :, None]


def draw_weld_from(key, part):
    in_use = weld_plan(key)
    key = jax.random.fold_in(key, 11)
    node_ids = jax.random.randint(key, in_use.shape, 0, CL * CG)
    return jnp.where(in_use, node_ids, -1)


def draw_weld_to(key, part):
    in_use = weld_plan(key)
    key = jax.random.fold_in(key, 13)
    node_ids = jax.random.randint(key, in_use.shape, 0, CL * CG)
    return jnp.where(jnp.transpose(in_use, (1, 0, 2)), node_ids, -1)


def draw_stress(key, part):
    key = jax.random.fold_in(key, 7)
    column = jnp.arange(NG, dtype=jnp.int32).astype(jnp.float32)
    height = jnp.sin(2.0 * jnp.pi / NG * (column + 0.5))
    random_part = 0.5 * jax.random.truncated_normal(key, -4.0, 4.0, (8, NL, NG), jnp.float32)
    profile = jnp.zeros((8, 1, 1), jnp.float32).at[0].set(0.6)
    return random_part + profile * height[None, None, :]


def touch_ends(values, stream_key, smallest, high):
    place = [jax.random.randint(jax.random.fold_in(stream_key, axis), (), 0, length) for axis, length in enumerate(values.shape)]
    longest = values.shape.index(max(values.shape))
    neighbour = place[:longest] + [(place[longest] + 1) % values.shape[longest]] + place[longest + 1:]
    return values.at[tuple(place)].set(smallest).at[tuple(neighbour)].set(high)


def block_scale(key, extent, cuts, low, high):
    def one(dim, blocks):
        steps = jax.random.uniform(jax.random.fold_in(jax.random.fold_in(key, 6), dim), (blocks,), jnp.float32, low / len(cuts), high / len(cuts))
        return jnp.repeat(jnp.exp(steps), extent[dim] // blocks).reshape((-1,) + (1,) * (len(extent) - dim - 1))

    level = one(*cuts[0])
    for cut in cuts[1:]:
        level = level * one(*cut)
    return level


def scatter_about(own_key, shape, deviation, most, cuts=(), kind=jnp.bfloat16):
    loudness = block_scale(own_key, shape, cuts, -0.22, 0.18) if cuts else 1.0
    entries = jax.random.normal(own_key, shape, jnp.float32) * deviation * loudness
    return jnp.minimum(jnp.maximum(entries, -most), most).astype(kind)


def setup_inputs(seed: int = 0) -> dict:
    keys = jax.random.split(jax.random.key(seed), 9)
    return {
        "displacement": scatter_about(keys[0], (5, NL, NG), 1.0, 6.0, ((1, 8), (2, 4)), jnp.float32),
        "velocity": scatter_about(keys[1], (5, NL, NG), 1.0, 6.0, ((1, 8), (2, 4)), jnp.float32),
        "stress": draw_stress(jax.random.fold_in(keys[8], 71), 0),
        "thickness": touch_ends(jax.random.randint(keys[3], (NL, NG), 8, 33), jax.random.fold_in(keys[3], 1), 8, 32).astype(jnp.int32),
        "pressure": jnp.clip(0.2 + 0.8 * jax.random.uniform(keys[4], (NL, NG), jnp.float32) ** block_scale(keys[4], (NL, NG), ((0, 8), (1, 4)), -0.2, 0.2), 0.2, 1.0),
        "weld_from": draw_weld_from(jax.random.fold_in(keys[8], 71), 0),
        "weld_to": draw_weld_to(jax.random.fold_in(keys[8], 71), 0),
        "weld_stiff": jnp.clip(jnp.exp(math.log(4.0) - 2.0794415 * jax.random.uniform(keys[7], (DEVICES, DEVICES, CAP), jnp.float32) ** block_scale(keys[7], (DEVICES, DEVICES, CAP), ((0, 32),), -0.2, 0.2)), 0.5, 4.0),
    }


young_modulus = 4.0
poisson_ratio = 0.3
plate_modulus = young_modulus / (1.0 - poisson_ratio * poisson_ratio)
shear_modulus = young_modulus / (2.0 * (1.0 + poisson_ratio))
shear_factor = 5.0 / 6.0
time_step = 0.2
spacing_mm = 50.0
rotary_share = 1.0 / 12.0

def along_length(values):
    padded = jnp.pad(values, ((0, 0), (1, 1), (0, 0)))
    return 0.5 * (padded[:, 2:, :] - padded[:, :-2, :])

def along_girth(values):
    return 0.5 * (jnp.roll(values, -1, axis=2) - jnp.roll(values, 1, axis=2))

def resultants(stress, plate_ratio):
    bending_arm = plate_ratio * plate_ratio / 6.0
    return jnp.concatenate([plate_ratio * stress[0:3], bending_arm * stress[3:6], shear_factor * plate_ratio * stress[6:8]])

def lengthwise_set(result):
    return jnp.stack([result[0], result[2], result[6], result[3], result[5]])

def girthwise_set(result):
    return jnp.stack([result[2], result[1], result[7], result[5], result[4]])

def nodal_force(along_x, along_y, result):
    return jnp.stack([along_x[0] + along_y[0], along_x[1] + along_y[1], along_x[2] + along_y[2], along_x[3] + along_y[3] - result[6], along_x[4] + along_y[4] - result[7]])

def radial_return(trial_state):
    normal_xx = trial_state[0]
    normal_yy = trial_state[1]
    shear_xy = trial_state[2]
    offset = normal_xx - 0.5 * normal_yy
    equivalent = jnp.sqrt(offset * offset + 0.75 * normal_yy * normal_yy + 3.0 * shear_xy * shear_xy)
    return trial_state / jnp.maximum(equivalent, 1.0)

def stress_update(stress, along_x, along_y, velocity, plate_ratio):
    strain_xx = along_x[0]
    strain_yy = along_y[1]
    strain_xy = along_y[0] + along_x[1]
    curve_xx = along_x[3]
    curve_yy = along_y[4]
    curve_xy = along_y[3] + along_x[4]
    membrane = stress[0:3] + time_step * jnp.stack([plate_modulus * (strain_xx + poisson_ratio * strain_yy), plate_modulus * (strain_yy + poisson_ratio * strain_xx), shear_modulus * strain_xy])
    fiber_half = 0.5 * plate_ratio
    bending = stress[3:6] + time_step * fiber_half * jnp.stack([plate_modulus * (curve_xx + poisson_ratio * curve_yy), plate_modulus * (curve_yy + poisson_ratio * curve_xx), shear_modulus * curve_xy])
    shear_part = stress[6:8] + time_step * shear_modulus * jnp.stack([along_x[2] + velocity[3], along_y[2] + velocity[4]])
    return jnp.concatenate([radial_return(membrane), radial_return(bending), shear_part])

def global_node(device, local_node):
    section = device // N_GIRTH
    sector = device % N_GIRTH
    node_row = section * CL + local_node // CG
    node_col = sector * CG + local_node % CG
    return node_row * NG + node_col

def reference(displacement, velocity, stress, thickness, pressure, weld_from, weld_to, weld_stiff):
    plate_ratio = thickness.astype(jnp.float32) / spacing_mm
    rotary = plate_ratio * (1.0 + plate_ratio * plate_ratio) / 12.0
    inertia = jnp.stack([plate_ratio, plate_ratio, plate_ratio, rotary, rotary])
    shape_all = weld_from.shape
    source = lax.broadcasted_iota(jnp.int32, shape_all, 0)
    target = lax.broadcasted_iota(jnp.int32, shape_all, 1)
    far_local = jnp.transpose(weld_to, (1, 0, 2))
    near_node = global_node(source, jnp.maximum(weld_from, 0)).reshape(-1)
    far_node = global_node(target, jnp.maximum(far_local, 0)).reshape(-1)
    spring = jnp.where(weld_from >= 0, weld_stiff, 0.0).reshape(-1)
    field_scale = jnp.array([1.0, 1.0, 1.0, rotary_share, rotary_share], jnp.float32).reshape(5, 1)
    for step_index in range(STEPS):
        flattened = displacement.reshape(5, -1)
        pull = field_scale * spring[None, :] * (flattened[:, far_node] - flattened[:, near_node])
        welds = jnp.zeros_like(flattened).at[:, near_node].add(pull).at[:, far_node].add(-pull)
        result = resultants(stress, plate_ratio)
        summed = nodal_force(along_length(lengthwise_set(result)), along_girth(girthwise_set(result)), result)
        summed = summed + welds.reshape(displacement.shape)
        summed = summed.at[2].add(pressure)
        velocity = velocity + time_step * summed / inertia
        displacement = displacement + time_step * velocity
        stress = stress_update(stress, along_length(velocity), along_girth(velocity), velocity, plate_ratio)
    column = jnp.arange(NG, dtype=jnp.int32).astype(jnp.float32)
    height = jnp.sin(2.0 * jnp.pi / NG * (column + 0.5))
    moment = lax.optimization_barrier(jnp.sum(plate_ratio * stress[0] * height[None, :], axis=1)) / NG
    return (displacement, velocity, stress, moment)
```

```python
import functools

import jax
import jax.numpy as jnp
from jax import lax
from jax.experimental import pallas as pl
from jax.experimental.pallas import tpu as pltpu
from jax.sharding import PartitionSpec as P

STEPS = 3
FIELDS = 5
RESULTS = 8
PAD_ROWS = 8
LANES = 128
VMEM_BYTES = 40 * 1024 * 1024

young_modulus = 4.0
poisson_ratio = 0.3
plate_modulus = young_modulus / (1.0 - poisson_ratio * poisson_ratio)
shear_modulus = young_modulus / (2.0 * (1.0 + poisson_ratio))
shear_factor = 5.0 / 6.0
time_step = 0.2
spacing_mm = 50.0
rotary_share = 1.0 / 12.0

F32 = jnp.float32
BF16 = jnp.bfloat16


def split(values):
    high = values.astype(BF16)
    low = (values - high.astype(F32)).astype(BF16)
    return high, low


def dot(a, b, contract):
    return lax.dot_general(a, b, (contract, ((), ())), preferred_element_type=F32)


def slot_marks(devices, slots):
    total = devices * slots
    lane = lax.broadcasted_iota(jnp.int32, (devices, total), 1)
    device = lax.broadcasted_iota(jnp.int32, (devices, total), 0)
    by_device = (lane // slots == device).astype(F32).astype(BF16)
    lane = lax.broadcasted_iota(jnp.int32, (slots, total), 1)
    place = lax.broadcasted_iota(jnp.int32, (slots, total), 0)
    by_place = (lane % slots == place).astype(F32)
    return by_device, by_place


def expand(blocks, by_device, by_place):
    slots, total = by_place.shape
    wide = dot(blocks, by_device, ((0,), (0,)))
    wide = wide.reshape(wide.shape[0] // slots, slots, total) * by_place[None]
    return jnp.sum(wide, axis=1)


def collapse(rows, by_device, by_place):
    slots, _ = by_place.shape
    marks = by_place.astype(BF16)
    pieces = []
    for part in (0, 1):
        blocks = [split(row)[part] * marks for row in rows]
        blocks += [jnp.zeros_like(marks)] * (LANES // slots - len(rows))
        pieces.append(jnp.concatenate(blocks, axis=0))
    return dot(by_device, pieces[0], ((1,), (1,))) + dot(by_device, pieces[1], ((1,), (1,)))


def pick(fields, column_marks, row_marks):
    rows = fields[0].shape[0]
    parts = [split(field) for field in fields]
    high = jnp.concatenate([part[0] for part in parts], axis=0)
    low = jnp.concatenate([part[1] for part in parts], axis=0)
    by_column = dot(high, column_marks, ((1,), (0,))) + dot(low, column_marks, ((1,), (0,)))
    marks = row_marks.astype(F32)
    return [
        jnp.sum(by_column[rows * f : rows * (f + 1)] * marks, axis=0, keepdims=True)
        for f in range(len(fields))
    ]


def spread(pulls, column_marks, row_marks):
    high, low = split(pulls)
    total = None
    for part in (high, low):
        marked = jnp.concatenate(
            [part[f : f + 1] * row_marks for f in range(FIELDS)], axis=0
        )
        summed = dot(marked, column_marks, ((1,), (1,)))
        total = summed if total is None else total + summed
    return total


def place():
    sec, girth = lax.axis_index("sec"), lax.axis_index("girth")
    return sec, girth, lax.axis_size("sec"), lax.axis_size("girth")


def tile_of(ref, device):
    return ref[pl.ds(pl.multiple_of(device * 8, 8), 8), :]


def set_tile(ref, device, value):
    ref[pl.ds(pl.multiple_of(device * 8, 8), 8), :] = value


def girth_neighbours():
    sec, girth, _, girths = place()
    left = sec * girths + lax.rem(girth + girths - 1, girths)
    right = sec * girths + lax.rem(girth + 1, girths)
    return left, right


def corner_neighbours():
    sec, girth, secs, girths = place()
    me = sec * girths + girth
    out = []
    for step in (-1, 1):
        row = sec + step
        inside = jnp.logical_and(row >= 0, row < secs)
        for turn in (girths - 1, 1):
            device = row * girths + lax.rem(girth + turn, girths)
            out.append((jnp.where(inside, device, me), inside))
    return out


def edge_rows(columns):
    rows = columns[0][0].shape[0]
    lane = lax.broadcasted_iota(jnp.int32, (rows, LANES), 1)
    halves = [jnp.zeros((rows, LANES), F32), jnp.zeros((rows, LANES), F32)]
    for value, source, half, row in columns:
        moved = pltpu.roll(value, (row - source) % LANES, 1)
        halves[half] = jnp.where(lane == row, moved, halves[half])
    return jnp.concatenate(halves, axis=0).T


def edge_columns(left_tile, right_tile):
    stacked = jnp.concatenate(
        [left_tile, right_tile, jnp.zeros((LANES - 16, LANES), F32)], axis=0
    )
    turned = stacked.T
    return turned[: LANES // 2], turned[LANES // 2 :]


def edge_block(pieces):
    rows = pieces[0][0].shape[0]
    lane = lax.broadcasted_iota(jnp.int32, (rows, LANES), 1)
    block = jnp.zeros((rows, LANES), F32)
    for value, source, target in pieces:
        block = jnp.where(lane == target, pltpu.roll(value, (target - source) % LANES, 1), block)
    return block


def row_chunk(ref, f, start):
    count = ref.shape[1]
    if start < 0:
        return jnp.concatenate([ref[f, count + start : count, :], ref[f, 0 : 8 + start, :]], axis=0)
    if start + 8 > count:
        return jnp.concatenate([ref[f, start:count, :], ref[f, 0 : start + 8 - count, :]], axis=0)
    return ref[f, start : start + 8, :]


def difference_x(ref, f, start):
    return row_chunk(ref, f, start + 1) - row_chunk(ref, f, start - 1)


def difference_y(value):
    lanes = value.shape[1]
    return pltpu.roll(value, lanes - 1, 1) - pltpu.roll(value, 1, 1)


def radial_return(xx, yy, xy):
    offset = xx - 0.5 * yy
    square = offset * offset + 0.75 * yy * yy + 3.0 * xy * xy
    scale = lax.rsqrt(jnp.maximum(square, 1.0))
    return xx * scale, yy * scale, xy * scale


def stress_chunk(vel_ref, stress, plate, start):
    current = [vel_ref[f, start : start + 8, :] for f in range(FIELDS)]
    along_x = [difference_x(vel_ref, f, start) for f in range(FIELDS)]
    along_y = [difference_y(value) for value in current]
    normal = 0.5 * time_step * plate_modulus
    skew = 0.5 * time_step * shear_modulus
    arm = 0.5 * plate
    membrane = radial_return(
        stress[0] + normal * (along_x[0] + poisson_ratio * along_y[1]),
        stress[1] + normal * (along_y[1] + poisson_ratio * along_x[0]),
        stress[2] + skew * (along_y[0] + along_x[1]),
    )
    bending = radial_return(
        stress[3] + (normal * arm) * (along_x[3] + poisson_ratio * along_y[4]),
        stress[4] + (normal * arm) * (along_y[4] + poisson_ratio * along_x[3]),
        stress[5] + (skew * arm) * (along_y[3] + along_x[4]),
    )
    shear = (
        stress[6] + skew * (along_x[2] + 2.0 * current[3]),
        stress[7] + skew * (along_y[2] + 2.0 * current[4]),
    )
    return membrane + bending + shear


def resultants(stress, plate):
    arm = plate * plate * (1.0 / 6.0)
    shear = shear_factor * plate
    return (
        [plate * value for value in stress[0:3]]
        + [arm * value for value in stress[3:6]]
        + [shear * value for value in stress[6:8]]
    )


def force_chunk(res_ref, start, cols):
    def both(x, y):
        along_x = difference_x(res_ref, x, start)[:, :cols]
        along_y = difference_y(res_ref[y, start : start + 8, :])[:, :cols]
        return 0.5 * (along_x + along_y)

    return [
        both(0, 2),
        both(2, 1),
        both(6, 7),
        both(3, 5) - res_ref[6, start : start + 8, :cols],
        both(5, 4) - res_ref[7, start : start + 8, :cols],
    ]


def send_edges(payload, near, far, halo_rows, corners):
    devices = payload.shape[0] // 8
    payload[...] = jnp.zeros(payload.shape, F32)
    payload[pl.ds(0, devices, stride=8), :] = near
    payload[pl.ds(1, devices, stride=8), :] = far
    row = lax.broadcasted_iota(jnp.int32, (8, LANES), 0)
    for device, tile in zip(girth_neighbours(), (halo_rows[0:8], halo_rows[8:16])):
        set_tile(payload, device, jnp.where(row < 2, tile_of(payload, device), tile))
    for (device, _), corner in zip(corner_neighbours(), corners):
        set_tile(payload, device, jnp.where(row == 7, corner, tile_of(payload, device)))


def start_kernel(
    disp, stress, thickness, weld_from, weld_to, weld_stiff,
    payload, to_next, to_last, column_marks, row_marks, picked, spring,
):
    rows, cols = thickness.shape
    _, devices, slots = weld_from.shape
    shift = cols.bit_length() - 1
    by_device, by_place = slot_marks(devices, slots)
    near, far = weld_from[0], weld_to[0]
    stiff = jnp.where(near >= 0, weld_stiff[0], 0.0)
    index_parts = []
    for index in (near, far):
        index = jnp.maximum(index, 0)
        column = index & (cols - 1)
        index_parts += [index >> shift, column >> 1, column & 1]
    index_parts = [part.astype(F32).astype(BF16) for part in index_parts]
    index_parts += list(split(stiff))
    wide = [expand(part, by_device, by_place) for part in index_parts]
    row_index = jnp.concatenate([wide[0], wide[3]], axis=1)
    column_index = jnp.concatenate([2.0 * wide[1] + wide[2], 2.0 * wide[4] + wide[5]], axis=1)
    stiff_row = wide[6] + wide[7]
    total = row_index.shape[1]
    spring[...] = jnp.broadcast_to(stiff_row, spring.shape)
    row_iota = lax.broadcasted_iota(jnp.int32, (rows, total), 0).astype(F32)
    row_hits = (row_iota == row_index).astype(F32).astype(BF16)
    row_marks[...] = row_hits
    for start in range(0, cols, 64):
        iota = (lax.broadcasted_iota(jnp.int32, (64, total), 0) + start).astype(F32)
        column_marks[start : start + 64, :] = (iota == column_index).astype(F32).astype(BF16)
    values = pick([disp[f] for f in range(FIELDS)], column_marks[...], row_hits)
    picked[...] = jnp.concatenate(values + [values[0]] * 3, axis=0)
    half = total // 2
    near_out = collapse([value[:, :half] for value in values] + [stiff_row], by_device, by_place)
    far_out = collapse([value[:, half:] for value in values], by_device, by_place)

    plate = thickness[...].astype(F32) * (1.0 / spacing_mm)
    columns = []
    for f in range(RESULTS + 1):
        left = stress[f, :, 0:LANES] if f < RESULTS else plate[:, 0:LANES]
        right = stress[f, :, cols - LANES :] if f < RESULTS else plate[:, cols - LANES :]
        columns.append((left, 0, f // 5, 2 + f % 5))
        columns.append((right, LANES - 1, f // 5, 10 + f % 5))
    halo_rows = edge_rows(columns)
    send_edges(payload, near_out, far_out, halo_rows, [])
    for ref, row in ((to_next, rows - 1), (to_last, 0)):
        ref[...] = jnp.zeros(ref.shape, F32)
        for f in range(RESULTS):
            ref[f : f + 1, :] = stress[f, row : row + 1, :]
        ref[RESULTS : RESULTS + 1, :] = plate[row : row + 1, :]


def fill_halo(ref, f, above, below, sides, corner):
    rows, cols = ref.shape[1] - PAD_ROWS, ref.shape[2] - LANES
    depth = above.shape[0]
    ref[f, rows:, :cols] = jnp.concatenate(
        [below, jnp.zeros((PAD_ROWS - 2 * depth, cols), F32), above], axis=0
    )
    ref[f, :rows, cols:] = sides
    ref[f, rows:, cols:] = corner


def load_velocity(vel_ext, velocity, incoming, above, below):
    rows = velocity.shape[1]
    cols = velocity.shape[2]
    left, right = girth_neighbours()
    first, second = edge_columns(tile_of(incoming, left), tile_of(incoming, right))
    row = lax.broadcasted_iota(jnp.int32, (8, LANES), 0)
    corner_tiles = [
        jnp.broadcast_to(jnp.where(inside, tile_of(incoming, device)[7:8], 0.0), (8, LANES))
        for device, inside in corner_neighbours()
    ]
    for f in range(FIELDS):
        vel_ext[f, :rows, :cols] = velocity[f]
        sides = edge_block(
            [
                (first, 2 + f, LANES - 2),
                (second, 2 + f, LANES - 1),
                (first, 10 + f, 0),
                (second, 10 + f, 1),
            ]
        )
        upper = edge_block([(corner_tiles[0], f, LANES - 1), (corner_tiles[1], f, 0)])
        lower = edge_block([(corner_tiles[2], f, LANES - 1), (corner_tiles[3], f, 0)])
        corner = jnp.where(row == 0, lower, jnp.where(row == 7, upper, 0.0))
        fill_halo(
            vel_ext, f, above[2 * f : 2 * f + 2, :], below[2 * f : 2 * f + 2, :], sides, corner
        )


def load_stress(stress_ext, plate_ext, stress, thickness, incoming, above, below):
    rows, cols = thickness.shape
    left, right = girth_neighbours()
    halves = edge_columns(tile_of(incoming, left), tile_of(incoming, right))
    plate_ext[0, :rows, :cols] = thickness[...].astype(F32) * (1.0 / spacing_mm)
    empty = jnp.zeros((PAD_ROWS, LANES), F32)
    for f in range(RESULTS + 1):
        lane = 2 + f % 5
        half = halves[f // 5]
        sides = edge_block([(half, lane, LANES - 1), (half, 8 + lane, 0)])
        ref, k = (stress_ext, f) if f < RESULTS else (plate_ext, 0)
        if f < RESULTS:
            ref[k, :rows, :cols] = stress[f]
        fill_halo(ref, k, above[f : f + 1, :], below[f : f + 1, :], sides, empty)


def step_kernel(first, last, *refs):
    if first:
        (incoming, above, below, stress, thickness, velocity, disp, pressure,
         column_marks, row_marks, picked, spring) = refs[:12]
        out = refs[12:]
        plate_ext, spring_out = out[:2]
        out = out[2:]
    else:
        (incoming, above, below, stress, plate_ext, velocity, disp, pressure,
         column_marks, row_marks, picked, spring) = refs[:12]
        out = refs[12:]
    stress_ext, velocity_out, disp_out = out[:3]
    out = out[3:]
    if last:
        to_left, to_right, to_next, to_last, res_ext, vel_ext, weld = out
    else:
        picked_out, payload, to_next, to_last, res_ext, vel_ext, weld = out

    _, rows, cols = velocity.shape
    devices = incoming.shape[0] // 8
    total = picked.shape[1]
    half = total // 2
    by_device, by_place = slot_marks(devices, half // devices)

    other = []
    for row in (1, 0):
        high, low = split(incoming[pl.ds(row, devices, stride=8), :])
        other.append(expand(high, by_device, by_place) + expand(low, by_device, by_place))
    if first:
        stiffness = jnp.concatenate([spring[0:1, :], other[1][5:6]], axis=1)
        spring_out[...] = jnp.broadcast_to(stiffness, spring_out.shape)
    else:
        stiffness = spring[0:1, :]
    field = lax.broadcasted_iota(jnp.int32, (8, total), 0)
    scale = jnp.where(field < 3, 1.0, rotary_share) * stiffness
    pulls = scale * (jnp.concatenate(other, axis=1) - picked[...])
    weld[...] = spread(pulls, column_marks[...], row_marks[...])

    if first:
        load_stress(stress_ext, plate_ext, stress, thickness, incoming, above, below)
        for start in range(0, rows + PAD_ROWS, 8):
            chunk = [stress_ext[k, start : start + 8, :] for k in range(RESULTS)]
            for k, value in enumerate(resultants(chunk, plate_ext[0, start : start + 8, :])):
                res_ext[k, start : start + 8, :] = value
    else:
        load_velocity(vel_ext, velocity, incoming, above, below)
        for start in range(0, rows + PAD_ROWS, 8):
            plate = plate_ext[0, start : start + 8, :]
            chunk = [stress[k, start : start + 8, :] for k in range(RESULTS)]
            chunk = stress_chunk(vel_ext, chunk, plate, start)
            for k, value in enumerate(chunk):
                stress_ext[k, start : start + 8, :] = value
            for k, value in enumerate(resultants(chunk, plate)):
                res_ext[k, start : start + 8, :] = value

    for start in range(0, rows, 8):
        part = slice(start, start + 8)
        plate = plate_ext[0, part, :cols]
        linear = time_step / plate
        angular = (12.0 * linear) / (1.0 + plate * plate)
        force = force_chunk(res_ext, start, cols)
        force[2] = force[2] + pressure[part, :]
        for f in range(FIELDS):
            joined = force[f] + weld[f * rows + start : f * rows + start + 8, :]
            speed = velocity[f, part, :] + (linear if f < 3 else angular) * joined
            velocity_out[f, part, :] = speed
            disp_out[f, part, :] = disp[f, part, :] + time_step * speed

    ends = (cols - LANES, cols)
    if last:
        columns = []
        for f in range(FIELDS):
            columns.append((velocity_out[f, :, 0:LANES], 0, 0, f))
            columns.append((velocity_out[f, :, ends[0] : ends[1]], LANES - 1, 0, 8 + f))
        halo_rows = edge_rows(columns)
        to_left[...] = halo_rows[0:8]
        to_right[...] = halo_rows[8:16]
        for ref, row in ((to_next, rows - 1), (to_last, 0)):
            ref[...] = jnp.zeros(ref.shape, F32)
            for f in range(FIELDS):
                ref[f : f + 1, :] = velocity_out[f, row : row + 1, :]
        return
    values = pick([disp_out[f] for f in range(FIELDS)], column_marks[...], row_marks[...])
    picked_out[...] = jnp.concatenate(values + [values[0]] * 3, axis=0)
    near_out = collapse([value[:, :half] for value in values], by_device, by_place)
    far_out = collapse([value[:, half:] for value in values], by_device, by_place)
    columns = []
    for f in range(FIELDS):
        left_lanes = velocity_out[f, :, 0:LANES]
        right_lanes = velocity_out[f, :, ends[0] : ends[1]]
        for depth in (0, 1):
            columns.append((left_lanes, depth, depth, 2 + f))
            columns.append((right_lanes, LANES - 2 + depth, depth, 10 + f))
    corners = []
    lane = lax.broadcasted_iota(jnp.int32, (8, LANES), 1)
    for row in (0, rows - 1):
        tile = slice(row // 8 * 8, row // 8 * 8 + 8)
        for side in (0, 1):
            value = jnp.zeros((8, LANES), F32)
            for f in range(FIELDS):
                part = velocity_out[f, tile, ends[0] : ends[1]] if side else velocity_out[f, tile, 0:LANES]
                source = LANES - 1 if side else 0
                value = jnp.where(lane == f, pltpu.roll(part, (f - source) % LANES, 1), value)
            corners.append(jnp.broadcast_to(value[row % 8 : row % 8 + 1], (8, LANES)))
    send_edges(payload, near_out, far_out, edge_rows(columns), corners)
    for ref, start in ((to_next, rows - 2), (to_last, 0)):
        ref[...] = jnp.zeros(ref.shape, F32)
        for f in range(FIELDS):
            ref[2 * f : 2 * f + 2, :] = velocity_out[f, start : start + 2, :]


def final_kernel(
    from_left, from_right, above, below, stress, plate_ext, velocity, height,
    stress_out, moment, vel_ext,
):
    _, rows, cols = velocity.shape
    first, _ = edge_columns(from_left[...], from_right[...])
    empty = jnp.zeros((PAD_ROWS, LANES), F32)
    for f in range(FIELDS):
        vel_ext[f, :rows, :cols] = velocity[f]
        sides = edge_block([(first, f, LANES - 1), (first, 8 + f, 0)])
        fill_halo(vel_ext, f, above[f : f + 1, :], below[f : f + 1, :], sides, empty)
    weight = height[0:1, :]
    parts = []
    for start in range(0, rows, 8):
        part = slice(start, start + 8)
        chunk = [stress[k, part, :] for k in range(RESULTS)]
        plate = plate_ext[0, part, :]
        chunk = stress_chunk(vel_ext, chunk, plate, start)
        for k, value in enumerate(chunk):
            stress_out[k, part, :] = value[:, :cols]
        weighted = plate[:, :cols] * chunk[0][:, :cols] * weight
        parts.append(jnp.sum(weighted, axis=1, keepdims=True))
    column = jnp.broadcast_to(jnp.concatenate(parts, axis=0), (rows, LANES))
    if rows < LANES:
        column = jnp.concatenate([column, jnp.zeros((LANES - rows, LANES), F32)], axis=0)
    moment[...] = column.T[0:8, :rows]


def call(kernel, outs, scratch, *operands):
    whole = pl.BlockSpec(memory_space=pltpu.VMEM)
    return pl.pallas_call(
        kernel,
        out_shape=[jax.ShapeDtypeStruct(shape, dtype) for shape, dtype in outs],
        in_specs=[whole] * len(operands),
        out_specs=[whole] * len(outs),
        scratch_shapes=[pltpu.VMEM(shape, dtype) for shape, dtype in scratch],
        compiler_params=pltpu.CompilerParams(vmem_limit_bytes=VMEM_BYTES),
    )(*operands)


def to_next_section(values):
    count = lax.axis_size("sec")
    return lax.ppermute(values, "sec", [(i, i + 1) for i in range(count - 1)])


def to_last_section(values):
    count = lax.axis_size("sec")
    return lax.ppermute(values, "sec", [(i + 1, i) for i in range(count - 1)])


def turn(values, step):
    count = lax.axis_size("girth")
    return lax.ppermute(values, "girth", [(i, (i + step) % count) for i in range(count)])


def local(displacement, velocity, stress, thickness, pressure, weld_from, weld_to, weld_stiff):
    rows, cols = thickness.shape
    _, devices, slots = weld_from.shape
    total = 2 * devices * slots
    girth_total = cols * lax.axis_size("girth")
    column = (lax.axis_index("girth") * cols + lax.iota(jnp.int32, cols)).astype(F32)
    height = jnp.sin(2.0 * jnp.pi / girth_total * (column + 0.5)) / girth_total
    height = jnp.broadcast_to(height[None, :], (8, cols))

    message = (devices * 8, LANES)
    strip = (16, cols)
    block = (FIELDS, rows, cols)
    stress_shape = (RESULTS, rows + PAD_ROWS, cols + LANES)
    plate_shape = (1, rows + PAD_ROWS, cols + LANES)
    slot_rows = (8, total)
    scratch = [
        (stress_shape, F32),
        ((FIELDS, rows + PAD_ROWS, cols + LANES), F32),
        ((FIELDS * rows, cols), F32),
    ]

    payload, to_next, to_last, column_marks, row_marks, picked, spring = call(
        start_kernel,
        [
            (message, F32), (strip, F32), (strip, F32), ((cols, total), BF16),
            ((rows, total), BF16), (slot_rows, F32), ((8, total // 2), F32),
        ],
        [],
        displacement, stress, thickness, weld_from, weld_to, weld_stiff,
    )
    plate = None
    for step in range(STEPS):
        first, last = step == 0, step == STEPS - 1
        incoming = lax.all_to_all(payload, ("sec", "girth"), 0, 0, tiled=True)
        above, below = to_next_section(to_next), to_last_section(to_last)
        outs = [(stress_shape, F32), (block, F32), (block, F32)]
        if first:
            outs = [(plate_shape, F32), (slot_rows, F32)] + outs
        if last:
            edge = (8, LANES)
            outs += [(edge, F32), (edge, F32), ((8, cols), F32), ((8, cols), F32)]
        else:
            outs += [(slot_rows, F32), (message, F32), (strip, F32), (strip, F32)]
        results = call(
            functools.partial(step_kernel, first, last),
            outs,
            scratch,
            incoming, above, below, stress, thickness if first else plate, velocity,
            displacement, pressure, column_marks, row_marks, picked, spring,
        )
        if first:
            plate, spring = results[:2]
            results = results[2:]
        stress, velocity, displacement = results[:3]
        if last:
            to_left, to_right, to_next, to_last = results[3:]
        else:
            picked, payload, to_next, to_last = results[3:]

    from_left, from_right = turn(to_right, 1), turn(to_left, -1)
    above, below = to_next_section(to_next), to_last_section(to_last)
    stress, partial_moment = call(
        final_kernel,
        [((RESULTS, rows, cols), F32), ((8, rows), F32)],
        [((FIELDS, rows + PAD_ROWS, cols + LANES), F32)],
        from_left, from_right, above, below, stress, plate, velocity, height,
    )
    moment = lax.psum(partial_moment[0], "girth")
    return (displacement, velocity, stress, moment)


def solution(mesh):
    in_specs = (
        P(None, "sec", "girth"),
        P(None, "sec", "girth"),
        P(None, "sec", "girth"),
        P("sec", "girth"),
        P("sec", "girth"),
        P(("sec", "girth"), None, None),
        P(("sec", "girth"), None, None),
        P(("sec", "girth"), None, None),
    )
    out_specs = (
        P(None, "sec", "girth"),
        P(None, "sec", "girth"),
        P(None, "sec", "girth"),
        P("sec"),
    )
    return jax.shard_map(local, mesh=mesh, in_specs=in_specs, out_specs=out_specs, check_vma=False)
```

```python
import functools

import jax
import jax.numpy as jnp
from jax import lax
from jax.experimental import pallas as pl
from jax.experimental.pallas import tpu as pltpu
from jax.sharding import PartitionSpec as P

STEPS = 3
FIELDS = 5
RESULTS = 8
PAD_ROWS = 8
LANES = 128
VMEM_PER_SLOT = 5 * 1024

young_modulus = 4.0
poisson_ratio = 0.3
plate_modulus = young_modulus / (1.0 - poisson_ratio * poisson_ratio)
shear_modulus = young_modulus / (2.0 * (1.0 + poisson_ratio))
shear_factor = 5.0 / 6.0
time_step = 0.2
spacing_mm = 50.0
rotary_share = 1.0 / 12.0

F32 = jnp.float32
BF16 = jnp.bfloat16


def split(values):
    high = values.astype(BF16)
    low = (values - high.astype(F32)).astype(BF16)
    return high, low


def dot(a, b, contract):
    return lax.dot_general(a, b, (contract, ((), ())), preferred_element_type=F32)


def slot_marks(devices, slots):
    total = devices * slots
    lane = lax.broadcasted_iota(jnp.int32, (devices, total), 1)
    device = lax.broadcasted_iota(jnp.int32, (devices, total), 0)
    by_device = (lane // slots == device).astype(F32).astype(BF16)
    lane = lax.broadcasted_iota(jnp.int32, (slots, total), 1)
    place = lax.broadcasted_iota(jnp.int32, (slots, total), 0)
    by_place = (lane % slots == place).astype(F32)
    return by_device, by_place


def expand(blocks, by_device, by_place, turned=False):
    slots, total = by_place.shape
    wide = dot(blocks, by_device, ((1 if turned else 0,), (0,)))
    wide = wide.reshape(wide.shape[0] // slots, slots, total) * by_place[None]
    return jnp.sum(wide, axis=1)


def collapse(rows, by_device, by_place):
    slots, _ = by_place.shape
    marks = by_place.astype(BF16)
    pieces = []
    for part in (0, 1):
        blocks = [split(row)[part] * marks for row in rows]
        blocks += [jnp.zeros_like(marks)] * (LANES // slots - len(rows))
        pieces.append(jnp.concatenate(blocks, axis=0))
    return dot(by_device, pieces[0], ((1,), (1,))) + dot(by_device, pieces[1], ((1,), (1,)))


def pick(fields, column_marks, row_marks):
    rows = fields[0].shape[0]
    parts = [split(field) for field in fields]
    high = jnp.concatenate([part[0] for part in parts], axis=0)
    low = jnp.concatenate([part[1] for part in parts], axis=0)
    by_column = dot(high, column_marks, ((1,), (0,))) + dot(low, column_marks, ((1,), (0,)))
    marks = row_marks.astype(F32)
    return [
        jnp.sum(by_column[rows * f : rows * (f + 1)] * marks, axis=0, keepdims=True)
        for f in range(len(fields))
    ]


def spread(pulls, column_marks, row_marks):
    high, low = split(pulls)
    total = None
    for part in (high, low):
        marked = jnp.concatenate(
            [part[f : f + 1] * row_marks for f in range(FIELDS)], axis=0
        )
        summed = dot(marked, column_marks, ((1,), (1,)))
        total = summed if total is None else total + summed
    return total


def place():
    sec, girth = lax.axis_index("sec"), lax.axis_index("girth")
    return sec, girth, lax.axis_size("sec"), lax.axis_size("girth")


def tile_of(ref, device):
    return ref[pl.ds(pl.multiple_of(device * 8, 8), 8), :]


def set_tile(ref, device, value):
    ref[pl.ds(pl.multiple_of(device * 8, 8), 8), :] = value


def girth_neighbours():
    sec, girth, _, girths = place()
    left = sec * girths + lax.rem(girth + girths - 1, girths)
    right = sec * girths + lax.rem(girth + 1, girths)
    return left, right


def corner_neighbours():
    sec, girth, secs, girths = place()
    me = sec * girths + girth
    out = []
    for step in (-1, 1):
        row = sec + step
        inside = jnp.logical_and(row >= 0, row < secs)
        for turn in (girths - 1, 1):
            device = row * girths + lax.rem(girth + turn, girths)
            out.append((jnp.where(inside, device, me), inside))
    return out


def edge_rows(columns):
    rows = columns[0][0].shape[0]
    lane = lax.broadcasted_iota(jnp.int32, (rows, LANES), 1)
    halves = [jnp.zeros((rows, LANES), F32), jnp.zeros((rows, LANES), F32)]
    for value, source, half, row in columns:
        moved = pltpu.roll(value, (row - source) % LANES, 1)
        halves[half] = jnp.where(lane == row, moved, halves[half])
    return jnp.concatenate(halves, axis=0).T


def edge_columns(left_tile, right_tile):
    stacked = jnp.concatenate(
        [left_tile, right_tile, jnp.zeros((LANES - 16, LANES), F32)], axis=0
    )
    turned = stacked.T
    return turned[: LANES // 2], turned[LANES // 2 :]


def edge_block(pieces):
    rows = pieces[0][0].shape[0]
    lane = lax.broadcasted_iota(jnp.int32, (rows, LANES), 1)
    block = jnp.zeros((rows, LANES), F32)
    for value, source, target in pieces:
        block = jnp.where(lane == target, pltpu.roll(value, (target - source) % LANES, 1), block)
    return block


def row_chunk(ref, f, start):
    count = ref.shape[1]
    if start < 0:
        return jnp.concatenate([ref[f, count + start : count, :], ref[f, 0 : 8 + start, :]], axis=0)
    if start + 8 > count:
        return jnp.concatenate([ref[f, start:count, :], ref[f, 0 : start + 8 - count, :]], axis=0)
    return ref[f, start : start + 8, :]


def difference_x(ref, f, start):
    return row_chunk(ref, f, start + 1) - row_chunk(ref, f, start - 1)


def difference_y(value):
    lanes = value.shape[1]
    return pltpu.roll(value, lanes - 1, 1) - pltpu.roll(value, 1, 1)


def radial_return(xx, yy, xy):
    offset = xx - 0.5 * yy
    square = offset * offset + 0.75 * yy * yy + 3.0 * xy * xy
    scale = lax.rsqrt(jnp.maximum(square, 1.0))
    return xx * scale, yy * scale, xy * scale


def stress_chunk(vel_ref, stress, plate, start):
    current = [vel_ref[f, start : start + 8, :] for f in range(FIELDS)]
    along_x = [difference_x(vel_ref, f, start) for f in range(FIELDS)]
    along_y = [difference_y(value) for value in current]
    normal = 0.5 * time_step * plate_modulus
    skew = 0.5 * time_step * shear_modulus
    arm = 0.5 * plate
    membrane = radial_return(
        stress[0] + normal * (along_x[0] + poisson_ratio * along_y[1]),
        stress[1] + normal * (along_y[1] + poisson_ratio * along_x[0]),
        stress[2] + skew * (along_y[0] + along_x[1]),
    )
    bending = radial_return(
        stress[3] + (normal * arm) * (along_x[3] + poisson_ratio * along_y[4]),
        stress[4] + (normal * arm) * (along_y[4] + poisson_ratio * along_x[3]),
        stress[5] + (skew * arm) * (along_y[3] + along_x[4]),
    )
    shear = (
        stress[6] + skew * (along_x[2] + 2.0 * current[3]),
        stress[7] + skew * (along_y[2] + 2.0 * current[4]),
    )
    return membrane + bending + shear


def resultants(stress, plate):
    arm = plate * plate * (1.0 / 6.0)
    shear = shear_factor * plate
    return (
        [plate * value for value in stress[0:3]]
        + [arm * value for value in stress[3:6]]
        + [shear * value for value in stress[6:8]]
    )


def force_chunk(res_ref, start, cols):
    def both(x, y):
        along_x = difference_x(res_ref, x, start)[:, :cols]
        along_y = difference_y(res_ref[y, start : start + 8, :])[:, :cols]
        return 0.5 * (along_x + along_y)

    return [
        both(0, 2),
        both(2, 1),
        both(6, 7),
        both(3, 5) - res_ref[6, start : start + 8, :cols],
        both(5, 4) - res_ref[7, start : start + 8, :cols],
    ]


def send_edges(payload, near, far, halo_rows, corners):
    devices = payload.shape[0] // 8
    payload[...] = jnp.zeros(payload.shape, F32)
    payload[pl.ds(0, devices, stride=8), :] = near
    payload[pl.ds(1, devices, stride=8), :] = far
    row = lax.broadcasted_iota(jnp.int32, (8, LANES), 0)
    for device, tile in zip(girth_neighbours(), (halo_rows[0:8], halo_rows[8:16])):
        set_tile(payload, device, jnp.where(row < 2, tile_of(payload, device), tile))
    for (device, _), corner in zip(corner_neighbours(), corners):
        set_tile(payload, device, jnp.where(row == 7, corner, tile_of(payload, device)))


def fetch(done, pairs):
    copies = [
        pltpu.make_async_copy(source, target, done.at[k])
        for k, (source, target) in enumerate(pairs)
    ]
    for copy in copies:
        copy.start()
    return copies


def start_kernel(
    disp_in, stress_in, thickness_in, from_in, to_in, stiff_in,
    payload, to_next, to_last, column_marks, row_marks, picked, spring,
    disp, stress_left, stress_right, stress_top, stress_bottom, thickness,
    weld_from, weld_to, weld_stiff, done,
):
    rows, cols = thickness.shape
    _, slots, devices = weld_from.shape
    copies = fetch(
        done,
        [
            (from_in, weld_from),
            (to_in, weld_to),
            (stiff_in, weld_stiff),
            (disp_in, disp),
            (thickness_in, thickness),
            (stress_in.at[:, :, 0:LANES], stress_left),
            (stress_in.at[:, :, cols - LANES : cols], stress_right),
            (stress_in.at[:, 0:8, :], stress_top),
            (stress_in.at[:, rows - 8 : rows, :], stress_bottom),
        ],
    )
    shift = cols.bit_length() - 1
    by_device, by_place = slot_marks(devices, slots)
    for copy in copies[:3]:
        copy.wait()
    near, far = weld_from[0], weld_to[0]
    stiff = jnp.where(near >= 0, weld_stiff[0], 0.0)
    index_parts = []
    for index in (near, far):
        index = jnp.maximum(index, 0)
        column = index & (cols - 1)
        index_parts += [index >> shift, column >> 1, column & 1]
    index_parts = [part.astype(F32).astype(BF16) for part in index_parts]
    index_parts += list(split(stiff))
    wide = [expand(part, by_device, by_place, turned=True) for part in index_parts]
    row_index = jnp.concatenate([wide[0], wide[3]], axis=1)
    column_index = jnp.concatenate([2.0 * wide[1] + wide[2], 2.0 * wide[4] + wide[5]], axis=1)
    stiff_row = wide[6] + wide[7]
    total = row_index.shape[1]
    spring[...] = jnp.broadcast_to(stiff_row, spring.shape)
    row_iota = lax.broadcasted_iota(jnp.int32, (rows, total), 0).astype(F32)
    row_hits = (row_iota == row_index).astype(F32).astype(BF16)
    row_marks[...] = row_hits
    for start in range(0, cols, 64):
        iota = (lax.broadcasted_iota(jnp.int32, (64, total), 0) + start).astype(F32)
        column_marks[start : start + 64, :] = (iota == column_index).astype(F32).astype(BF16)
    copies[3].wait()
    values = pick([disp[f] for f in range(FIELDS)], column_marks[...], row_hits)
    picked[...] = jnp.concatenate(values + [values[0]] * 3, axis=0)
    half = total // 2
    near_out = collapse([value[:, :half] for value in values] + [stiff_row], by_device, by_place)
    far_out = collapse([value[:, half:] for value in values], by_device, by_place)

    for copy in copies[4:]:
        copy.wait()
    plate = thickness[...].astype(F32) * (1.0 / spacing_mm)
    columns = []
    for f in range(RESULTS + 1):
        left = stress_left[f] if f < RESULTS else plate[:, 0:LANES]
        right = stress_right[f] if f < RESULTS else plate[:, cols - LANES :]
        columns.append((left, 0, f // 5, 2 + f % 5))
        columns.append((right, LANES - 1, f // 5, 10 + f % 5))
    halo_rows = edge_rows(columns)
    send_edges(payload, near_out, far_out, halo_rows, [])
    for ref, stress, row in ((to_next, stress_bottom, rows - 1), (to_last, stress_top, 0)):
        ref[...] = jnp.zeros(ref.shape, F32)
        for f in range(RESULTS):
            ref[f : f + 1, :] = stress[f, row % 8 : row % 8 + 1, :]
        ref[RESULTS : RESULTS + 1, :] = plate[row : row + 1, :]


def fill_halo(ref, f, above, below, sides, corner):
    rows, cols = ref.shape[1] - PAD_ROWS, ref.shape[2] - LANES
    depth = above.shape[0]
    ref[f, rows:, :cols] = jnp.concatenate(
        [below, jnp.zeros((PAD_ROWS - 2 * depth, cols), F32), above], axis=0
    )
    ref[f, :rows, cols:] = sides
    ref[f, rows:, cols:] = corner


def load_velocity(vel_ext, velocity, incoming, above, below):
    rows = velocity.shape[1]
    cols = velocity.shape[2]
    left, right = girth_neighbours()
    first, second = edge_columns(tile_of(incoming, left), tile_of(incoming, right))
    row = lax.broadcasted_iota(jnp.int32, (8, LANES), 0)
    corner_tiles = [
        jnp.broadcast_to(jnp.where(inside, tile_of(incoming, device)[7:8], 0.0), (8, LANES))
        for device, inside in corner_neighbours()
    ]
    for f in range(FIELDS):
        vel_ext[f, :rows, :cols] = velocity[f]
        sides = edge_block(
            [
                (first, 2 + f, LANES - 2),
                (second, 2 + f, LANES - 1),
                (first, 10 + f, 0),
                (second, 10 + f, 1),
            ]
        )
        upper = edge_block([(corner_tiles[0], f, LANES - 1), (corner_tiles[1], f, 0)])
        lower = edge_block([(corner_tiles[2], f, LANES - 1), (corner_tiles[3], f, 0)])
        corner = jnp.where(row == 0, lower, jnp.where(row == 7, upper, 0.0))
        fill_halo(
            vel_ext, f, above[2 * f : 2 * f + 2, :], below[2 * f : 2 * f + 2, :], sides, corner
        )


def load_stress(stress_ext, plate_ext, thickness, incoming, above, below):
    rows, cols = thickness.shape
    left, right = girth_neighbours()
    halves = edge_columns(tile_of(incoming, left), tile_of(incoming, right))
    plate_ext[0, :rows, :cols] = thickness[...].astype(F32) * (1.0 / spacing_mm)
    empty = jnp.zeros((PAD_ROWS, LANES), F32)
    for f in range(RESULTS + 1):
        lane = 2 + f % 5
        half = halves[f // 5]
        sides = edge_block([(half, lane, LANES - 1), (half, 8 + lane, 0)])
        ref, k = (stress_ext, f) if f < RESULTS else (plate_ext, 0)
        fill_halo(ref, k, above[f : f + 1, :], below[f : f + 1, :], sides, empty)


def step_kernel(first, last, *refs):
    (stress, plate_ext, velocity, disp, pressure,
     incoming, above, below, column_marks, row_marks, picked, spring) = refs[:12]
    out = refs[12:]
    if first:
        plate_ext, spring_out = out[:2]
        out = out[2:]
    stress_ext, velocity_out, disp_out = out[:3]
    out = out[3:]
    if last:
        to_left, to_right, to_next, to_last, res_ext, vel_ext, weld = out
    else:
        picked_out, payload, to_next, to_last, res_ext, vel_ext, weld = out[:7]
    if first:
        velocity_in, disp_in, pressure_in, thickness_in = velocity, disp, pressure, refs[1]
        velocity, disp, pressure, thickness, done = out[7:]
        copies = fetch(
            done,
            [
                (stress, stress_ext.at[:, : velocity.shape[1], : velocity.shape[2]]),
                (thickness_in, thickness),
                (velocity_in, velocity),
                (disp_in, disp),
                (pressure_in, pressure),
            ],
        )

    _, rows, cols = velocity.shape
    devices = incoming.shape[0] // 8
    total = picked.shape[1]
    half = total // 2
    by_device, by_place = slot_marks(devices, half // devices)

    other = []
    for row in (1, 0):
        high, low = split(incoming[pl.ds(row, devices, stride=8), :])
        other.append(expand(high, by_device, by_place) + expand(low, by_device, by_place))
    if first:
        stiffness = jnp.concatenate([spring[0:1, :], other[1][5:6]], axis=1)
        spring_out[...] = jnp.broadcast_to(stiffness, spring_out.shape)
    else:
        stiffness = spring[0:1, :]
    field = lax.broadcasted_iota(jnp.int32, (8, total), 0)
    scale = jnp.where(field < 3, 1.0, rotary_share) * stiffness
    pulls = scale * (jnp.concatenate(other, axis=1) - picked[...])
    weld[...] = spread(pulls, column_marks[...], row_marks[...])

    if first:
        for copy in copies:
            copy.wait()
        load_stress(stress_ext, plate_ext, thickness, incoming, above, below)
        for start in range(0, rows + PAD_ROWS, 8):
            chunk = [stress_ext[k, start : start + 8, :] for k in range(RESULTS)]
            for k, value in enumerate(resultants(chunk, plate_ext[0, start : start + 8, :])):
                res_ext[k, start : start + 8, :] = value
    else:
        load_velocity(vel_ext, velocity, incoming, above, below)
        for start in range(0, rows + PAD_ROWS, 8):
            plate = plate_ext[0, start : start + 8, :]
            chunk = [stress[k, start : start + 8, :] for k in range(RESULTS)]
            chunk = stress_chunk(vel_ext, chunk, plate, start)
            for k, value in enumerate(chunk):
                stress_ext[k, start : start + 8, :] = value
            for k, value in enumerate(resultants(chunk, plate)):
                res_ext[k, start : start + 8, :] = value

    for start in range(0, rows, 8):
        part = slice(start, start + 8)
        plate = plate_ext[0, part, :cols]
        linear = time_step / plate
        angular = (12.0 * linear) / (1.0 + plate * plate)
        force = force_chunk(res_ext, start, cols)
        force[2] = force[2] + pressure[part, :]
        for f in range(FIELDS):
            joined = force[f] + weld[f * rows + start : f * rows + start + 8, :]
            speed = velocity[f, part, :] + (linear if f < 3 else angular) * joined
            velocity_out[f, part, :] = speed
            disp_out[f, part, :] = disp[f, part, :] + time_step * speed

    ends = (cols - LANES, cols)
    if last:
        columns = []
        for f in range(FIELDS):
            columns.append((velocity_out[f, :, 0:LANES], 0, 0, f))
            columns.append((velocity_out[f, :, ends[0] : ends[1]], LANES - 1, 0, 8 + f))
        halo_rows = edge_rows(columns)
        to_left[...] = halo_rows[0:8]
        to_right[...] = halo_rows[8:16]
        for ref, row in ((to_next, rows - 1), (to_last, 0)):
            ref[...] = jnp.zeros(ref.shape, F32)
            for f in range(FIELDS):
                ref[f : f + 1, :] = velocity_out[f, row : row + 1, :]
        return
    values = pick([disp_out[f] for f in range(FIELDS)], column_marks[...], row_marks[...])
    picked_out[...] = jnp.concatenate(values + [values[0]] * 3, axis=0)
    near_out = collapse([value[:, :half] for value in values], by_device, by_place)
    far_out = collapse([value[:, half:] for value in values], by_device, by_place)
    columns = []
    for f in range(FIELDS):
        left_lanes = velocity_out[f, :, 0:LANES]
        right_lanes = velocity_out[f, :, ends[0] : ends[1]]
        for depth in (0, 1):
            columns.append((left_lanes, depth, depth, 2 + f))
            columns.append((right_lanes, LANES - 2 + depth, depth, 10 + f))
    corners = []
    lane = lax.broadcasted_iota(jnp.int32, (8, LANES), 1)
    for row in (0, rows - 1):
        tile = slice(row // 8 * 8, row // 8 * 8 + 8)
        for side in (0, 1):
            value = jnp.zeros((8, LANES), F32)
            for f in range(FIELDS):
                part = velocity_out[f, tile, ends[0] : ends[1]] if side else velocity_out[f, tile, 0:LANES]
                source = LANES - 1 if side else 0
                value = jnp.where(lane == f, pltpu.roll(part, (f - source) % LANES, 1), value)
            corners.append(jnp.broadcast_to(value[row % 8 : row % 8 + 1], (8, LANES)))
    send_edges(payload, near_out, far_out, edge_rows(columns), corners)
    for ref, start in ((to_next, rows - 2), (to_last, 0)):
        ref[...] = jnp.zeros(ref.shape, F32)
        for f in range(FIELDS):
            ref[2 * f : 2 * f + 2, :] = velocity_out[f, start : start + 2, :]


def final_kernel(
    from_left, from_right, above, below, stress, plate_ext, velocity, height,
    stress_out, moment, vel_ext,
):
    _, rows, cols = velocity.shape
    first, _ = edge_columns(from_left[...], from_right[...])
    empty = jnp.zeros((PAD_ROWS, LANES), F32)
    for f in range(FIELDS):
        vel_ext[f, :rows, :cols] = velocity[f]
        sides = edge_block([(first, f, LANES - 1), (first, 8 + f, 0)])
        fill_halo(vel_ext, f, above[f : f + 1, :], below[f : f + 1, :], sides, empty)
    weight = height[0:1, :]
    parts = []
    for start in range(0, rows, 8):
        part = slice(start, start + 8)
        chunk = [stress[k, part, :] for k in range(RESULTS)]
        plate = plate_ext[0, part, :]
        chunk = stress_chunk(vel_ext, chunk, plate, start)
        for k, value in enumerate(chunk):
            stress_out[k, part, :] = value[:, :cols]
        weighted = plate[:, :cols] * chunk[0][:, :cols] * weight
        parts.append(jnp.sum(weighted, axis=1, keepdims=True))
    column = jnp.broadcast_to(jnp.concatenate(parts, axis=0), (rows, LANES))
    if rows < LANES:
        column = jnp.concatenate([column, jnp.zeros((LANES - rows, LANES), F32)], axis=0)
    moment[...] = column.T[0:8, :rows]


def call(kernel, vmem_bytes, outs, scratch, *operands, far=0):
    operands = [
        pltpu.with_memory_space_constraint(value, pltpu.HBM) if k < far else value
        for k, value in enumerate(operands)
    ]
    whole = pl.BlockSpec(memory_space=pltpu.VMEM)
    scratch = [pltpu.VMEM(shape, dtype) for shape, dtype in scratch]
    if far:
        scratch.append(pltpu.SemaphoreType.DMA((9,)))
    return pl.pallas_call(
        kernel,
        out_shape=[jax.ShapeDtypeStruct(shape, dtype) for shape, dtype in outs],
        in_specs=[pl.BlockSpec(memory_space=pltpu.HBM)] * far + [whole] * (len(operands) - far),
        out_specs=[whole] * len(outs),
        scratch_shapes=scratch,
        compiler_params=pltpu.CompilerParams(vmem_limit_bytes=vmem_bytes),
    )(*operands)


def to_next_section(values):
    count = lax.axis_size("sec")
    return lax.ppermute(values, "sec", [(i, i + 1) for i in range(count - 1)])


def to_last_section(values):
    count = lax.axis_size("sec")
    return lax.ppermute(values, "sec", [(i + 1, i) for i in range(count - 1)])


def turn(values, step):
    count = lax.axis_size("girth")
    return lax.ppermute(values, "girth", [(i, (i + step) % count) for i in range(count)])


def local(displacement, velocity, stress, thickness, pressure, weld_from, weld_to, weld_stiff):
    rows, cols = thickness.shape
    _, devices, slots = weld_from.shape
    total = 2 * devices * slots
    girth_total = cols * lax.axis_size("girth")
    column = (lax.axis_index("girth") * cols + lax.iota(jnp.int32, cols)).astype(F32)
    height = jnp.sin(2.0 * jnp.pi / girth_total * (column + 0.5)) / girth_total
    height = jnp.broadcast_to(height[None, :], (8, cols))

    vmem_bytes = 8 * 1024 * 1024 + total * VMEM_PER_SLOT
    message = (devices * 8, LANES)
    strip = (16, cols)
    block = (FIELDS, rows, cols)
    stress_shape = (RESULTS, rows + PAD_ROWS, cols + LANES)
    plate_shape = (1, rows + PAD_ROWS, cols + LANES)
    slot_rows = (8, total)
    scratch = [
        (stress_shape, F32),
        ((FIELDS, rows + PAD_ROWS, cols + LANES), F32),
        ((FIELDS * rows, cols), F32),
    ]

    first_scratch = [
        (block, F32), (block, F32), ((rows, cols), F32), ((rows, cols), jnp.int32),
    ]

    payload, to_next, to_last, column_marks, row_marks, picked, spring = call(
        start_kernel,
        vmem_bytes,
        [
            (message, F32), (strip, F32), (strip, F32), ((cols, total), BF16),
            ((rows, total), BF16), (slot_rows, F32), ((8, total // 2), F32),
        ],
        [
            (block, F32), ((RESULTS, rows, LANES), F32), ((RESULTS, rows, LANES), F32),
            ((RESULTS, 8, cols), F32), ((RESULTS, 8, cols), F32), ((rows, cols), jnp.int32),
            ((1, slots, devices), jnp.int32), ((1, slots, devices), jnp.int32),
            ((1, slots, devices), F32),
        ],
        displacement, stress, thickness,
        *[jnp.swapaxes(array, 1, 2) for array in (weld_from, weld_to, weld_stiff)],
        far=6,
    )
    plate = None
    for step in range(STEPS):
        first, last = step == 0, step == STEPS - 1
        incoming = lax.all_to_all(payload, ("sec", "girth"), 0, 0, tiled=True)
        above, below = to_next_section(to_next), to_last_section(to_last)
        outs = [(stress_shape, F32), (block, F32), (block, F32)]
        if first:
            outs = [(plate_shape, F32), (slot_rows, F32)] + outs
        if last:
            edge = (8, LANES)
            outs += [(edge, F32), (edge, F32), ((8, cols), F32), ((8, cols), F32)]
        else:
            outs += [(slot_rows, F32), (message, F32), (strip, F32), (strip, F32)]
        results = call(
            functools.partial(step_kernel, first, last),
            vmem_bytes,
            outs,
            scratch + (first_scratch if first else []),
            stress, thickness if first else plate, velocity, displacement, pressure,
            incoming, above, below, column_marks, row_marks, picked, spring,
            far=5 if first else 0,
        )
        if first:
            plate, spring = results[:2]
            results = results[2:]
        stress, velocity, displacement = results[:3]
        if last:
            to_left, to_right, to_next, to_last = results[3:]
        else:
            picked, payload, to_next, to_last = results[3:]

    from_left, from_right = turn(to_right, 1), turn(to_left, -1)
    above, below = to_next_section(to_next), to_last_section(to_last)
    stress, partial_moment = call(
        final_kernel,
        vmem_bytes,
        [((RESULTS, rows, cols), F32), ((8, rows), F32)],
        [((FIELDS, rows + PAD_ROWS, cols + LANES), F32)],
        from_left, from_right, above, below, stress, plate, velocity, height,
    )
    moment = lax.psum(partial_moment[0], "girth")
    return (displacement, velocity, stress, moment)


def solution(mesh):
    in_specs = (
        P(None, "sec", "girth"),
        P(None, "sec", "girth"),
        P(None, "sec", "girth"),
        P("sec", "girth"),
        P("sec", "girth"),
        P(("sec", "girth"), None, None),
        P(("sec", "girth"), None, None),
        P(("sec", "girth"), None, None),
    )
    out_specs = (
        P(None, "sec", "girth"),
        P(None, "sec", "girth"),
        P(None, "sec", "girth"),
        P("sec"),
    )
    return jax.shard_map(local, mesh=mesh, in_specs=in_specs, out_specs=out_specs, check_vma=False)
```

```python
import functools

import jax
import jax.numpy as jnp
from jax import lax
from jax.experimental import pallas as pl
from jax.experimental.pallas import tpu as pltpu
from jax.sharding import PartitionSpec as P

STEPS = 3
FIELDS = 5
RESULTS = 8
PAD_ROWS = 8
LANES = 128
VMEM_PER_SLOT = 5 * 1024

young_modulus = 4.0
poisson_ratio = 0.3
plate_modulus = young_modulus / (1.0 - poisson_ratio * poisson_ratio)
shear_modulus = young_modulus / (2.0 * (1.0 + poisson_ratio))
shear_factor = 5.0 / 6.0
time_step = 0.2
spacing_mm = 50.0
rotary_share = 1.0 / 12.0

F32 = jnp.float32
BF16 = jnp.bfloat16


def split(values):
    high = values.astype(BF16)
    low = (values - high.astype(F32)).astype(BF16)
    return high, low


def dot(a, b, contract):
    return lax.dot_general(a, b, (contract, ((), ())), preferred_element_type=F32)


def slot_marks(devices, slots):
    total = devices * slots
    lane = lax.broadcasted_iota(jnp.int32, (devices, total), 1)
    device = lax.broadcasted_iota(jnp.int32, (devices, total), 0)
    by_device = (lane // slots == device).astype(F32).astype(BF16)
    lane = lax.broadcasted_iota(jnp.int32, (slots, total), 1)
    place = lax.broadcasted_iota(jnp.int32, (slots, total), 0)
    by_place = (lane % slots == place).astype(F32)
    return by_device, by_place


def expand(blocks, by_device, by_place, turned=False):
    slots, total = by_place.shape
    wide = dot(blocks, by_device, ((1 if turned else 0,), (0,)))
    wide = wide.reshape(wide.shape[0] // slots, slots, total) * by_place[None]
    return jnp.sum(wide, axis=1)


def collapse(rows, by_device, by_place):
    slots, _ = by_place.shape
    marks = by_place.astype(BF16)
    pieces = []
    for part in (0, 1):
        blocks = [split(row)[part] * marks for row in rows]
        blocks += [jnp.zeros_like(marks)] * (LANES // slots - len(rows))
        pieces.append(jnp.concatenate(blocks, axis=0))
    return dot(by_device, pieces[0], ((1,), (1,))) + dot(by_device, pieces[1], ((1,), (1,)))


def pick(fields, column_marks, row_marks):
    rows = fields[0].shape[0]
    parts = [split(field) for field in fields]
    high = jnp.concatenate([part[0] for part in parts], axis=0)
    low = jnp.concatenate([part[1] for part in parts], axis=0)
    by_column = dot(high, column_marks, ((1,), (0,))) + dot(low, column_marks, ((1,), (0,)))
    marks = row_marks.astype(F32)
    return [
        jnp.sum(by_column[rows * f : rows * (f + 1)] * marks, axis=0, keepdims=True)
        for f in range(len(fields))
    ]


def spread(pulls, column_marks, row_marks):
    high, low = split(pulls)
    total = None
    for part in (high, low):
        marked = jnp.concatenate(
            [part[f : f + 1] * row_marks for f in range(FIELDS)], axis=0
        )
        summed = dot(marked, column_marks, ((1,), (1,)))
        total = summed if total is None else total + summed
    return total


def place():
    sec, girth = lax.axis_index("sec"), lax.axis_index("girth")
    return sec, girth, lax.axis_size("sec"), lax.axis_size("girth")


def tile_of(ref, device):
    return ref[pl.ds(pl.multiple_of(device * 8, 8), 8), :]


def set_tile(ref, device, value):
    ref[pl.ds(pl.multiple_of(device * 8, 8), 8), :] = value


def girth_neighbours():
    sec, girth, _, girths = place()
    left = sec * girths + lax.rem(girth + girths - 1, girths)
    right = sec * girths + lax.rem(girth + 1, girths)
    return left, right


def corner_neighbours():
    sec, girth, secs, girths = place()
    me = sec * girths + girth
    out = []
    for step in (-1, 1):
        row = sec + step
        inside = jnp.logical_and(row >= 0, row < secs)
        for turn in (girths - 1, 1):
            device = row * girths + lax.rem(girth + turn, girths)
            out.append((jnp.where(inside, device, me), inside))
    return out


def edge_rows(columns):
    rows = columns[0][0].shape[0]
    lane = lax.broadcasted_iota(jnp.int32, (rows, LANES), 1)
    halves = [jnp.zeros((rows, LANES), F32), jnp.zeros((rows, LANES), F32)]
    for value, source, half, row in columns:
        moved = pltpu.roll(value, (row - source) % LANES, 1)
        halves[half] = jnp.where(lane == row, moved, halves[half])
    return jnp.concatenate(halves, axis=0).T


def edge_columns(left_tile, right_tile):
    stacked = jnp.concatenate(
        [left_tile, right_tile, jnp.zeros((LANES - 16, LANES), F32)], axis=0
    )
    turned = stacked.T
    return turned[: LANES // 2], turned[LANES // 2 :]


def edge_block(pieces):
    rows = pieces[0][0].shape[0]
    lane = lax.broadcasted_iota(jnp.int32, (rows, LANES), 1)
    block = jnp.zeros((rows, LANES), F32)
    for value, source, target in pieces:
        block = jnp.where(lane == target, pltpu.roll(value, (target - source) % LANES, 1), block)
    return block


def row_chunk(ref, f, start):
    count = ref.shape[1]
    if start < 0:
        return jnp.concatenate([ref[f, count + start : count, :], ref[f, 0 : 8 + start, :]], axis=0)
    if start + 8 > count:
        return jnp.concatenate([ref[f, start:count, :], ref[f, 0 : start + 8 - count, :]], axis=0)
    return ref[f, start : start + 8, :]


def difference_x(ref, f, start):
    return row_chunk(ref, f, start + 1) - row_chunk(ref, f, start - 1)


def difference_y(value):
    lanes = value.shape[1]
    return pltpu.roll(value, lanes - 1, 1) - pltpu.roll(value, 1, 1)


def radial_return(xx, yy, xy):
    offset = xx - 0.5 * yy
    square = offset * offset + 0.75 * yy * yy + 3.0 * xy * xy
    scale = lax.rsqrt(jnp.maximum(square, 1.0))
    return xx * scale, yy * scale, xy * scale


def stress_chunk(vel_ref, stress, plate, start):
    current = [vel_ref[f, start : start + 8, :] for f in range(FIELDS)]
    along_x = [difference_x(vel_ref, f, start) for f in range(FIELDS)]
    along_y = [difference_y(value) for value in current]
    normal = 0.5 * time_step * plate_modulus
    skew = 0.5 * time_step * shear_modulus
    arm = 0.5 * plate
    membrane = radial_return(
        stress[0] + normal * (along_x[0] + poisson_ratio * along_y[1]),
        stress[1] + normal * (along_y[1] + poisson_ratio * along_x[0]),
        stress[2] + skew * (along_y[0] + along_x[1]),
    )
    bending = radial_return(
        stress[3] + (normal * arm) * (along_x[3] + poisson_ratio * along_y[4]),
        stress[4] + (normal * arm) * (along_y[4] + poisson_ratio * along_x[3]),
        stress[5] + (skew * arm) * (along_y[3] + along_x[4]),
    )
    shear = (
        stress[6] + skew * (along_x[2] + 2.0 * current[3]),
        stress[7] + skew * (along_y[2] + 2.0 * current[4]),
    )
    return membrane + bending + shear


def resultants(stress, plate):
    arm = plate * plate * (1.0 / 6.0)
    shear = shear_factor * plate
    return (
        [plate * value for value in stress[0:3]]
        + [arm * value for value in stress[3:6]]
        + [shear * value for value in stress[6:8]]
    )


def force_chunk(res_ref, start, cols):
    def both(x, y):
        along_x = difference_x(res_ref, x, start)[:, :cols]
        along_y = difference_y(res_ref[y, start : start + 8, :])[:, :cols]
        return 0.5 * (along_x + along_y)

    return [
        both(0, 2),
        both(2, 1),
        both(6, 7),
        both(3, 5) - res_ref[6, start : start + 8, :cols],
        both(5, 4) - res_ref[7, start : start + 8, :cols],
    ]


def send_edges(payload, near, far, halo_rows, corners):
    devices = payload.shape[0] // 8
    payload[...] = jnp.zeros(payload.shape, F32)
    payload[pl.ds(0, devices, stride=8), :] = near
    payload[pl.ds(1, devices, stride=8), :] = far
    row = lax.broadcasted_iota(jnp.int32, (8, LANES), 0)
    for device, tile in zip(girth_neighbours(), (halo_rows[0:8], halo_rows[8:16])):
        set_tile(payload, device, jnp.where(row < 2, tile_of(payload, device), tile))
    for (device, _), corner in zip(corner_neighbours(), corners):
        set_tile(payload, device, jnp.where(row == 7, corner, tile_of(payload, device)))


def fetch(done, pairs):
    copies = [
        pltpu.make_async_copy(source, target, done.at[k])
        for k, (source, target) in enumerate(pairs)
    ]
    for copy in copies:
        copy.start()
    return copies


def start_kernel(
    disp_in, stress_in, thickness_in, from_in, to_in, stiff_in,
    payload, to_next, to_last, column_marks, row_marks, picked, spring,
    disp, stress_left, stress_right, stress_top, stress_bottom, thickness,
    weld_from, weld_to, weld_stiff, done,
):
    rows, cols = thickness.shape
    _, slots, devices = weld_from.shape
    copies = fetch(
        done,
        [
            (from_in, weld_from),
            (to_in, weld_to),
            (stiff_in, weld_stiff),
            (disp_in, disp),
            (thickness_in, thickness),
            (stress_in.at[:, :, 0:LANES], stress_left),
            (stress_in.at[:, :, cols - LANES : cols], stress_right),
            (stress_in.at[:, 0:8, :], stress_top),
            (stress_in.at[:, rows - 8 : rows, :], stress_bottom),
        ],
    )
    shift = cols.bit_length() - 1
    by_device, by_place = slot_marks(devices, slots)
    for copy in copies[:3]:
        copy.wait()
    near, far = weld_from[0], weld_to[0]
    stiff = jnp.where(near >= 0, weld_stiff[0], 0.0)
    index_parts = []
    for index in (near, far):
        index = jnp.maximum(index, 0)
        column = index & (cols - 1)
        index_parts += [index >> shift, column >> 1, column & 1]
    index_parts = [part.astype(F32).astype(BF16) for part in index_parts]
    index_parts += list(split(stiff))
    wide = [expand(part, by_device, by_place, turned=True) for part in index_parts]
    row_index = jnp.concatenate([wide[0], wide[3]], axis=1)
    column_index = jnp.concatenate([2.0 * wide[1] + wide[2], 2.0 * wide[4] + wide[5]], axis=1)
    stiff_row = wide[6] + wide[7]
    total = row_index.shape[1]
    spring[...] = jnp.broadcast_to(stiff_row, spring.shape)
    row_iota = lax.broadcasted_iota(jnp.int32, (rows, total), 0).astype(F32)
    row_hits = (row_iota == row_index).astype(F32).astype(BF16)
    row_marks[...] = row_hits
    for start in range(0, cols, 64):
        iota = (lax.broadcasted_iota(jnp.int32, (64, total), 0) + start).astype(F32)
        column_marks[start : start + 64, :] = (iota == column_index).astype(F32).astype(BF16)
    copies[3].wait()
    values = pick([disp[f] for f in range(FIELDS)], column_marks[...], row_hits)
    picked[...] = jnp.concatenate(values + [values[0]] * 3, axis=0)
    half = total // 2
    near_out = collapse([value[:, :half] for value in values] + [stiff_row], by_device, by_place)
    far_out = collapse([value[:, half:] for value in values], by_device, by_place)

    for copy in copies[4:]:
        copy.wait()
    plate = thickness[...].astype(F32) * (1.0 / spacing_mm)
    columns = []
    for f in range(RESULTS + 1):
        left = stress_left[f] if f < RESULTS else plate[:, 0:LANES]
        right = stress_right[f] if f < RESULTS else plate[:, cols - LANES :]
        columns.append((left, 0, f // 5, 2 + f % 5))
        columns.append((right, LANES - 1, f // 5, 10 + f % 5))
    halo_rows = edge_rows(columns)
    send_edges(payload, near_out, far_out, halo_rows, [])
    for ref, stress, row in ((to_next, stress_bottom, rows - 1), (to_last, stress_top, 0)):
        ref[...] = jnp.zeros(ref.shape, F32)
        for f in range(RESULTS):
            ref[f : f + 1, :] = stress[f, row % 8 : row % 8 + 1, :]
        ref[RESULTS : RESULTS + 1, :] = plate[row : row + 1, :]


def fill_halo(ref, f, above, below, sides, corner):
    rows, cols = ref.shape[1] - PAD_ROWS, ref.shape[2] - LANES
    depth = above.shape[0]
    ref[f, rows:, :cols] = jnp.concatenate(
        [below, jnp.zeros((PAD_ROWS - 2 * depth, cols), F32), above], axis=0
    )
    ref[f, :rows, cols:] = sides
    ref[f, rows:, cols:] = corner


def load_velocity(vel_ext, incoming, above, below):
    left, right = girth_neighbours()
    first, second = edge_columns(tile_of(incoming, left), tile_of(incoming, right))
    row = lax.broadcasted_iota(jnp.int32, (8, LANES), 0)
    corner_tiles = [
        jnp.broadcast_to(jnp.where(inside, tile_of(incoming, device)[7:8], 0.0), (8, LANES))
        for device, inside in corner_neighbours()
    ]
    for f in range(FIELDS):
        sides = edge_block(
            [
                (first, 2 + f, LANES - 2),
                (second, 2 + f, LANES - 1),
                (first, 10 + f, 0),
                (second, 10 + f, 1),
            ]
        )
        upper = edge_block([(corner_tiles[0], f, LANES - 1), (corner_tiles[1], f, 0)])
        lower = edge_block([(corner_tiles[2], f, LANES - 1), (corner_tiles[3], f, 0)])
        corner = jnp.where(row == 0, lower, jnp.where(row == 7, upper, 0.0))
        fill_halo(
            vel_ext, f, above[2 * f : 2 * f + 2, :], below[2 * f : 2 * f + 2, :], sides, corner
        )


def load_stress(stress_ext, plate_ext, thickness, incoming, above, below):
    rows, cols = thickness.shape
    left, right = girth_neighbours()
    halves = edge_columns(tile_of(incoming, left), tile_of(incoming, right))
    plate_ext[0, :rows, :cols] = thickness[...].astype(F32) * (1.0 / spacing_mm)
    empty = jnp.zeros((PAD_ROWS, LANES), F32)
    for f in range(RESULTS + 1):
        lane = 2 + f % 5
        half = halves[f // 5]
        sides = edge_block([(half, lane, LANES - 1), (half, 8 + lane, 0)])
        ref, k = (stress_ext, f) if f < RESULTS else (plate_ext, 0)
        fill_halo(ref, k, above[f : f + 1, :], below[f : f + 1, :], sides, empty)


def step_kernel(first, last, *refs):
    (stress_in, velocity_in, disp_in, thickness_in, pressure_in) = refs[:5]
    if first:
        incoming, above, below, column_marks, row_marks, picked, spring = refs[5:12]
        out = refs[12:]
    else:
        incoming, above, below, column_marks, row_marks, picked, spring, plate_ext = refs[5:13]
        out = refs[13:]
    stress_out, velocity_out, disp_out = out[:3]
    out = out[3:]
    if first:
        plate_ext, spring_out = out[:2]
        out = out[2:]
    if last:
        to_left, to_right, to_next, to_last = out[:4]
    else:
        picked_out, payload, to_next, to_last = out[:4]
    (stress_ext, res_ext, vel_ext, weld, velocity, disp, thickness, pressure,
     got, sent) = out[4:]

    _, rows, cols = velocity.shape
    devices = incoming.shape[0] // 8
    total = picked.shape[1]
    half = total // 2
    by_device, by_place = slot_marks(devices, half // devices)
    inner = (slice(None), slice(0, rows), slice(0, cols))
    copies = fetch(
        got,
        [
            (velocity_in, vel_ext.at[inner] if not first else velocity),
            (stress_in, stress_ext.at[inner] if first else stress_ext),
            (disp_in, disp),
            (pressure_in, pressure),
        ]
        + ([(thickness_in, thickness)] if first else []),
    )
    sends = []

    def send(source, target):
        copy = pltpu.make_async_copy(source, target, sent.at[len(sends)])
        copy.start()
        sends.append(copy)

    other = []
    for row in (1, 0):
        high, low = split(incoming[pl.ds(row, devices, stride=8), :])
        other.append(expand(high, by_device, by_place) + expand(low, by_device, by_place))
    if first:
        stiffness = jnp.concatenate([spring[0:1, :], other[1][5:6]], axis=1)
        spring_out[...] = jnp.broadcast_to(stiffness, spring_out.shape)
    else:
        stiffness = spring[0:1, :]
    field = lax.broadcasted_iota(jnp.int32, (8, total), 0)
    scale = jnp.where(field < 3, 1.0, rotary_share) * stiffness
    pulls = scale * (jnp.concatenate(other, axis=1) - picked[...])
    weld[...] = spread(pulls, column_marks[...], row_marks[...])

    for copy in copies:
        copy.wait()
    if first:
        load_stress(stress_ext, plate_ext, thickness, incoming, above, below)
    else:
        load_velocity(vel_ext, incoming, above, below)
    for start in range(0, rows + PAD_ROWS, 8):
        plate = plate_ext[0, start : start + 8, :]
        chunk = [stress_ext[k, start : start + 8, :] for k in range(RESULTS)]
        if not first:
            chunk = stress_chunk(vel_ext, chunk, plate, start)
            for k, value in enumerate(chunk):
                stress_ext[k, start : start + 8, :] = value
        for k, value in enumerate(resultants(chunk, plate)):
            res_ext[k, start : start + 8, :] = value
    send(stress_ext, stress_out)

    for start in range(0, rows, 8):
        part = slice(start, start + 8)
        plate = plate_ext[0, part, :cols]
        linear = time_step / plate
        angular = (12.0 * linear) / (1.0 + plate * plate)
        force = force_chunk(res_ext, start, cols)
        force[2] = force[2] + pressure[part, :]
        for f in range(FIELDS):
            joined = force[f] + weld[f * rows + start : f * rows + start + 8, :]
            before = velocity[f, part, :] if first else vel_ext[f, part, :cols]
            speed = before + (linear if f < 3 else angular) * joined
            velocity[f, part, :] = speed
            disp[f, part, :] = disp[f, part, :] + time_step * speed
        if start % 32 == 24:
            done = slice(start - 24, start + 8)
            for source, target in ((velocity, velocity_out), (disp, disp_out)):
                send(source.at[:, done, :], target.at[:, done, :])

    ends = (cols - LANES, cols)
    if last:
        columns = []
        for f in range(FIELDS):
            columns.append((velocity[f, :, 0:LANES], 0, 0, f))
            columns.append((velocity[f, :, ends[0] : ends[1]], LANES - 1, 0, 8 + f))
        halo_rows = edge_rows(columns)
        to_left[...] = halo_rows[0:8]
        to_right[...] = halo_rows[8:16]
        for ref, row in ((to_next, rows - 1), (to_last, 0)):
            ref[...] = jnp.zeros(ref.shape, F32)
            for f in range(FIELDS):
                ref[f : f + 1, :] = velocity[f, row : row + 1, :]
        for copy in sends:
            copy.wait()
        return
    values = pick([disp[f] for f in range(FIELDS)], column_marks[...], row_marks[...])
    picked_out[...] = jnp.concatenate(values + [values[0]] * 3, axis=0)
    near_out = collapse([value[:, :half] for value in values], by_device, by_place)
    far_out = collapse([value[:, half:] for value in values], by_device, by_place)
    columns = []
    for f in range(FIELDS):
        left_lanes = velocity[f, :, 0:LANES]
        right_lanes = velocity[f, :, ends[0] : ends[1]]
        for depth in (0, 1):
            columns.append((left_lanes, depth, depth, 2 + f))
            columns.append((right_lanes, LANES - 2 + depth, depth, 10 + f))
    corners = []
    lane = lax.broadcasted_iota(jnp.int32, (8, LANES), 1)
    for row in (0, rows - 1):
        tile = slice(row // 8 * 8, row // 8 * 8 + 8)
        for side in (0, 1):
            value = jnp.zeros((8, LANES), F32)
            for f in range(FIELDS):
                part = velocity[f, tile, ends[0] : ends[1]] if side else velocity[f, tile, 0:LANES]
                source = LANES - 1 if side else 0
                value = jnp.where(lane == f, pltpu.roll(part, (f - source) % LANES, 1), value)
            corners.append(jnp.broadcast_to(value[row % 8 : row % 8 + 1], (8, LANES)))
    send_edges(payload, near_out, far_out, edge_rows(columns), corners)
    for ref, start in ((to_next, rows - 2), (to_last, 0)):
        ref[...] = jnp.zeros(ref.shape, F32)
        for f in range(FIELDS):
            ref[2 * f : 2 * f + 2, :] = velocity[f, start : start + 2, :]
    for copy in sends:
        copy.wait()


def final_kernel(
    stress_in, velocity_in, from_left, from_right, above, below, plate_ext, height,
    stress_out, moment, stress, vel_ext, got, sent,
):
    rows, cols = vel_ext.shape[1] - PAD_ROWS, vel_ext.shape[2] - LANES
    inner = (slice(None), slice(0, rows), slice(0, cols))
    copies = fetch(got, [(velocity_in, vel_ext.at[inner]), (stress_in, stress)])
    first, _ = edge_columns(from_left[...], from_right[...])
    empty = jnp.zeros((PAD_ROWS, LANES), F32)
    for f in range(FIELDS):
        sides = edge_block([(first, f, LANES - 1), (first, 8 + f, 0)])
        fill_halo(vel_ext, f, above[f : f + 1, :], below[f : f + 1, :], sides, empty)
    for copy in copies:
        copy.wait()
    weight = height[0:1, :]
    parts = []
    sends = []
    for start in range(0, rows, 8):
        part = slice(start, start + 8)
        chunk = [stress[k, part, :] for k in range(RESULTS)]
        plate = plate_ext[0, part, :]
        chunk = stress_chunk(vel_ext, chunk, plate, start)
        for k, value in enumerate(chunk):
            stress[k, part, :] = value
        if start % 16 == 8:
            done = slice(start - 8, start + 8)
            copy = pltpu.make_async_copy(
                stress.at[:, done, :cols], stress_out.at[:, done, :], sent.at[len(sends)]
            )
            copy.start()
            sends.append(copy)
        weighted = plate[:, :cols] * chunk[0][:, :cols] * weight
        parts.append(jnp.sum(weighted, axis=1, keepdims=True))
    column = jnp.broadcast_to(jnp.concatenate(parts, axis=0), (rows, LANES))
    if rows < LANES:
        column = jnp.concatenate([column, jnp.zeros((LANES - rows, LANES), F32)], axis=0)
    moment[...] = column.T[0:8, :rows]
    for copy in sends:
        copy.wait()


def call(kernel, vmem_bytes, outs, scratch, *operands, far=0, far_out=0, copies=(1,)):
    operands = [
        pltpu.with_memory_space_constraint(value, pltpu.HBM) if k < far else value
        for k, value in enumerate(operands)
    ]
    whole = pl.BlockSpec(memory_space=pltpu.VMEM)
    away = pl.BlockSpec(memory_space=pltpu.HBM)
    scratch = [pltpu.VMEM(shape, dtype) for shape, dtype in scratch]
    scratch += [pltpu.SemaphoreType.DMA((count,)) for count in copies]
    return pl.pallas_call(
        kernel,
        out_shape=[
            pltpu.HBM(shape, dtype) if k < far_out else jax.ShapeDtypeStruct(shape, dtype)
            for k, (shape, dtype) in enumerate(outs)
        ],
        in_specs=[away] * far + [whole] * (len(operands) - far),
        out_specs=[away] * far_out + [whole] * (len(outs) - far_out),
        scratch_shapes=scratch,
        compiler_params=pltpu.CompilerParams(vmem_limit_bytes=vmem_bytes),
    )(*operands)


def to_next_section(values):
    count = lax.axis_size("sec")
    return lax.ppermute(values, "sec", [(i, i + 1) for i in range(count - 1)])


def to_last_section(values):
    count = lax.axis_size("sec")
    return lax.ppermute(values, "sec", [(i + 1, i) for i in range(count - 1)])


def turn(values, step):
    count = lax.axis_size("girth")
    return lax.ppermute(values, "girth", [(i, (i + step) % count) for i in range(count)])


def local(displacement, velocity, stress, thickness, pressure, weld_from, weld_to, weld_stiff):
    rows, cols = thickness.shape
    _, devices, slots = weld_from.shape
    total = 2 * devices * slots
    girth_total = cols * lax.axis_size("girth")
    column = (lax.axis_index("girth") * cols + lax.iota(jnp.int32, cols)).astype(F32)
    height = jnp.sin(2.0 * jnp.pi / girth_total * (column + 0.5)) / girth_total
    height = jnp.broadcast_to(height[None, :], (8, cols))

    vmem_bytes = 8 * 1024 * 1024 + total * VMEM_PER_SLOT
    message = (devices * 8, LANES)
    strip = (16, cols)
    block = (FIELDS, rows, cols)
    stress_shape = (RESULTS, rows + PAD_ROWS, cols + LANES)
    plate_shape = (1, rows + PAD_ROWS, cols + LANES)
    slot_rows = (8, total)
    scratch = [
        (stress_shape, F32),
        (stress_shape, F32),
        ((FIELDS, rows + PAD_ROWS, cols + LANES), F32),
        ((FIELDS * rows, cols), F32),
        (block, F32),
        (block, F32),
        ((rows, cols), jnp.int32),
        ((rows, cols), F32),
    ]

    payload, to_next, to_last, column_marks, row_marks, picked, spring = call(
        start_kernel,
        vmem_bytes,
        [
            (message, F32), (strip, F32), (strip, F32), ((cols, total), BF16),
            ((rows, total), BF16), (slot_rows, F32), ((8, total // 2), F32),
        ],
        [
            (block, F32), ((RESULTS, rows, LANES), F32), ((RESULTS, rows, LANES), F32),
            ((RESULTS, 8, cols), F32), ((RESULTS, 8, cols), F32), ((rows, cols), jnp.int32),
            ((1, slots, devices), jnp.int32), ((1, slots, devices), jnp.int32),
            ((1, slots, devices), F32),
        ],
        displacement, stress, thickness,
        *[jnp.swapaxes(array, 1, 2) for array in (weld_from, weld_to, weld_stiff)],
        far=6,
        copies=(9,),
    )
    plate = None
    for step in range(STEPS):
        first, last = step == 0, step == STEPS - 1
        incoming = lax.all_to_all(payload, ("sec", "girth"), 0, 0, tiled=True)
        above, below = to_next_section(to_next), to_last_section(to_last)
        outs = [(stress_shape, F32), (block, F32), (block, F32)]
        if first:
            outs += [(plate_shape, F32), (slot_rows, F32)]
        if last:
            edge = (8, LANES)
            outs += [(edge, F32), (edge, F32), ((8, cols), F32), ((8, cols), F32)]
        else:
            outs += [(slot_rows, F32), (message, F32), (strip, F32), (strip, F32)]
        results = call(
            functools.partial(step_kernel, first, last),
            vmem_bytes,
            outs,
            scratch,
            stress, velocity, displacement, thickness, pressure,
            incoming, above, below, column_marks, row_marks, picked, spring,
            *([] if first else [plate]),
            far=5,
            far_out=3,
            copies=(5, 1 + 2 * (rows // 32)),
        )
        stress, velocity, displacement = results[:3]
        results = results[3:]
        if first:
            plate, spring = results[:2]
            results = results[2:]
        if last:
            to_left, to_right, to_next, to_last = results
        else:
            picked, payload, to_next, to_last = results

    from_left, from_right = turn(to_right, 1), turn(to_left, -1)
    above, below = to_next_section(to_next), to_last_section(to_last)
    stress, partial_moment = call(
        final_kernel,
        vmem_bytes,
        [((RESULTS, rows, cols), F32), ((8, rows), F32)],
        [(stress_shape, F32), ((FIELDS, rows + PAD_ROWS, cols + LANES), F32)],
        stress, velocity, from_left, from_right, above, below, plate, height,
        far=2,
        far_out=1,
        copies=(2, rows // 16),
    )
    moment = lax.psum(partial_moment[0], "girth")
    return (displacement, velocity, stress, moment)


def solution(mesh):
    in_specs = (
        P(None, "sec", "girth"),
        P(None, "sec", "girth"),
        P(None, "sec", "girth"),
        P("sec", "girth"),
        P("sec", "girth"),
        P(("sec", "girth"), None, None),
        P(("sec", "girth"), None, None),
        P(("sec", "girth"), None, None),
    )
    out_specs = (
        P(None, "sec", "girth"),
        P(None, "sec", "girth"),
        P(None, "sec", "girth"),
        P("sec"),
    )
    return jax.shard_map(local, mesh=mesh, in_specs=in_specs, out_specs=out_specs, check_vma=False)
```

```python
import functools

import jax
import jax.numpy as jnp
from jax import lax
from jax.experimental import pallas as pl
from jax.experimental.pallas import tpu as pltpu
from jax.sharding import PartitionSpec as P

STEPS = 3
FIELDS = 5
RESULTS = 8
PAD_ROWS = 8
LANES = 128
VMEM_PER_SLOT = 5 * 1024

young_modulus = 4.0
poisson_ratio = 0.3
plate_modulus = young_modulus / (1.0 - poisson_ratio * poisson_ratio)
shear_modulus = young_modulus / (2.0 * (1.0 + poisson_ratio))
shear_factor = 5.0 / 6.0
time_step = 0.2
spacing_mm = 50.0
rotary_share = 1.0 / 12.0

F32 = jnp.float32
BF16 = jnp.bfloat16


def split(values):
    high = values.astype(BF16)
    low = (values - high.astype(F32)).astype(BF16)
    return high, low


def dot(a, b, contract):
    return lax.dot_general(a, b, (contract, ((), ())), preferred_element_type=F32)


def device_marks(devices, slots, outgoing=False):
    total = devices * slots
    lane = lax.broadcasted_iota(jnp.int32, (devices, total), 1)
    device = lax.broadcasted_iota(jnp.int32, (devices, total), 0)
    if outgoing:
        girths = lax.axis_size("girth")
        secs = devices // girths
        device = device % secs * girths + device // secs
    return (lane // slots == device).astype(F32).astype(BF16)


def slot_marks(devices, slots):
    total = devices * slots
    by_device = device_marks(devices, slots)
    lane = lax.broadcasted_iota(jnp.int32, (slots, total), 1)
    place = lax.broadcasted_iota(jnp.int32, (slots, total), 0)
    by_place = (lane % slots == place).astype(F32)
    return by_device, by_place


def expand(blocks, by_device, by_place, turned=False):
    slots, total = by_place.shape
    wide = dot(blocks, by_device, ((1 if turned else 0,), (0,)))
    wide = wide.reshape(wide.shape[0] // slots, slots, total) * by_place[None]
    return jnp.sum(wide, axis=1)


def collapse(rows, by_device, by_place):
    slots, _ = by_place.shape
    marks = by_place.astype(BF16)
    pieces = []
    for part in (0, 1):
        blocks = [split(row)[part] * marks for row in rows]
        blocks += [jnp.zeros_like(marks)] * (LANES // slots - len(rows))
        pieces.append(jnp.concatenate(blocks, axis=0))
    return dot(by_device, pieces[0], ((1,), (1,))) + dot(by_device, pieces[1], ((1,), (1,)))


def pick(fields, column_marks, row_marks):
    rows = fields[0].shape[0]
    parts = [split(field) for field in fields]
    high = jnp.concatenate([part[0] for part in parts], axis=0)
    low = jnp.concatenate([part[1] for part in parts], axis=0)
    by_column = dot(high, column_marks, ((1,), (0,))) + dot(low, column_marks, ((1,), (0,)))
    marks = row_marks.astype(F32)
    return [
        jnp.sum(by_column[rows * f : rows * (f + 1)] * marks, axis=0, keepdims=True)
        for f in range(len(fields))
    ]


def spread(pulls, column_marks, row_marks):
    high, low = split(pulls)
    total = None
    for part in (high, low):
        marked = jnp.concatenate(
            [part[f : f + 1] * row_marks for f in range(FIELDS)], axis=0
        )
        summed = dot(marked, column_marks, ((1,), (1,)))
        total = summed if total is None else total + summed
    return total


def place():
    sec, girth = lax.axis_index("sec"), lax.axis_index("girth")
    return sec, girth, lax.axis_size("sec"), lax.axis_size("girth")


def tile_of(ref, device):
    return ref[pl.ds(pl.multiple_of(device * 8, 8), 8), :]


def set_tile(ref, device, value):
    ref[pl.ds(pl.multiple_of(device * 8, 8), 8), :] = value


def girth_neighbours():
    sec, girth, _, girths = place()
    left = sec * girths + lax.rem(girth + girths - 1, girths)
    right = sec * girths + lax.rem(girth + 1, girths)
    return left, right


def corner_neighbours():
    sec, girth, secs, girths = place()
    me = sec * girths + girth
    out = []
    for step in (-1, 1):
        row = sec + step
        inside = jnp.logical_and(row >= 0, row < secs)
        for turn in (girths - 1, 1):
            device = row * girths + lax.rem(girth + turn, girths)
            out.append((jnp.where(inside, device, me), inside))
    return out


def edge_rows(columns):
    rows = columns[0][0].shape[0]
    lane = lax.broadcasted_iota(jnp.int32, (rows, LANES), 1)
    halves = [jnp.zeros((rows, LANES), F32), jnp.zeros((rows, LANES), F32)]
    for value, source, half, row in columns:
        moved = pltpu.roll(value, (row - source) % LANES, 1)
        halves[half] = jnp.where(lane == row, moved, halves[half])
    return jnp.concatenate(halves, axis=0).T


def edge_columns(left_tile, right_tile):
    stacked = jnp.concatenate(
        [left_tile, right_tile, jnp.zeros((LANES - 16, LANES), F32)], axis=0
    )
    turned = stacked.T
    return turned[: LANES // 2], turned[LANES // 2 :]


def edge_block(pieces):
    rows = pieces[0][0].shape[0]
    lane = lax.broadcasted_iota(jnp.int32, (rows, LANES), 1)
    block = jnp.zeros((rows, LANES), F32)
    for value, source, target in pieces:
        block = jnp.where(lane == target, pltpu.roll(value, (target - source) % LANES, 1), block)
    return block


def row_chunk(ref, f, start):
    count = ref.shape[1]
    if start < 0:
        return jnp.concatenate([ref[f, count + start : count, :], ref[f, 0 : 8 + start, :]], axis=0)
    if start + 8 > count:
        return jnp.concatenate([ref[f, start:count, :], ref[f, 0 : start + 8 - count, :]], axis=0)
    return ref[f, start : start + 8, :]


def difference_x(ref, f, start):
    return row_chunk(ref, f, start + 1) - row_chunk(ref, f, start - 1)


def difference_y(value):
    lanes = value.shape[1]
    return pltpu.roll(value, lanes - 1, 1) - pltpu.roll(value, 1, 1)


def radial_return(xx, yy, xy):
    offset = xx - 0.5 * yy
    square = offset * offset + 0.75 * yy * yy + 3.0 * xy * xy
    scale = lax.rsqrt(jnp.maximum(square, 1.0))
    return xx * scale, yy * scale, xy * scale


def stress_chunk(vel_ref, stress, plate, start):
    current = [vel_ref[f, start : start + 8, :] for f in range(FIELDS)]
    along_x = [difference_x(vel_ref, f, start) for f in range(FIELDS)]
    along_y = [difference_y(value) for value in current]
    normal = 0.5 * time_step * plate_modulus
    skew = 0.5 * time_step * shear_modulus
    arm = 0.5 * plate
    membrane = radial_return(
        stress[0] + normal * (along_x[0] + poisson_ratio * along_y[1]),
        stress[1] + normal * (along_y[1] + poisson_ratio * along_x[0]),
        stress[2] + skew * (along_y[0] + along_x[1]),
    )
    bending = radial_return(
        stress[3] + (normal * arm) * (along_x[3] + poisson_ratio * along_y[4]),
        stress[4] + (normal * arm) * (along_y[4] + poisson_ratio * along_x[3]),
        stress[5] + (skew * arm) * (along_y[3] + along_x[4]),
    )
    shear = (
        stress[6] + skew * (along_x[2] + 2.0 * current[3]),
        stress[7] + skew * (along_y[2] + 2.0 * current[4]),
    )
    return membrane + bending + shear


def resultants(stress, plate):
    arm = plate * plate * (1.0 / 6.0)
    shear = shear_factor * plate
    return (
        [plate * value for value in stress[0:3]]
        + [arm * value for value in stress[3:6]]
        + [shear * value for value in stress[6:8]]
    )


def force_chunk(res_ref, start, cols):
    def both(x, y):
        along_x = difference_x(res_ref, x, start)[:, :cols]
        along_y = difference_y(res_ref[y, start : start + 8, :])[:, :cols]
        return 0.5 * (along_x + along_y)

    return [
        both(0, 2),
        both(2, 1),
        both(6, 7),
        both(3, 5) - res_ref[6, start : start + 8, :cols],
        both(5, 4) - res_ref[7, start : start + 8, :cols],
    ]


def send_edges(payload, near, far, halo_rows, corners):
    devices = payload.shape[0] // 8
    payload[...] = jnp.zeros(payload.shape, F32)
    payload[pl.ds(0, devices, stride=8), :] = near
    payload[pl.ds(1, devices, stride=8), :] = far
    _, _, secs, girths = place()
    row = lax.broadcasted_iota(jnp.int32, (8, LANES), 0)

    def slot_of(device):
        return lax.rem(device, girths) * secs + lax.div(device, girths)

    for device, tile in zip(girth_neighbours(), (halo_rows[0:8], halo_rows[8:16])):
        slot = slot_of(device)
        set_tile(payload, slot, jnp.where(row < 2, tile_of(payload, slot), tile))
    for (device, _), corner in zip(corner_neighbours(), corners):
        slot = slot_of(device)
        set_tile(payload, slot, jnp.where(row == 7, corner, tile_of(payload, slot)))


def fetch(done, pairs):
    copies = [
        pltpu.make_async_copy(source, target, done.at[k])
        for k, (source, target) in enumerate(pairs)
    ]
    for copy in copies:
        copy.start()
    return copies


def start_kernel(
    disp_in, stress_in, thickness_in, from_in, to_in, stiff_in,
    payload, to_next, to_last, column_marks, row_marks, picked, spring,
    disp, stress_left, stress_right, stress_top, stress_bottom, thickness,
    weld_from, weld_to, weld_stiff, done,
):
    rows, cols = thickness.shape
    _, slots, devices = weld_from.shape
    copies = fetch(
        done,
        [
            (from_in, weld_from),
            (to_in, weld_to),
            (stiff_in, weld_stiff),
            (disp_in, disp),
            (thickness_in, thickness),
            (stress_in.at[:, :, 0:LANES], stress_left),
            (stress_in.at[:, :, cols - LANES : cols], stress_right),
            (stress_in.at[:, 0:8, :], stress_top),
            (stress_in.at[:, rows - 8 : rows, :], stress_bottom),
        ],
    )
    shift = cols.bit_length() - 1
    by_device, by_place = slot_marks(devices, slots)
    for copy in copies[:3]:
        copy.wait()
    near, far = weld_from[0], weld_to[0]
    stiff = jnp.where(near >= 0, weld_stiff[0], 0.0)
    index_parts = []
    for index in (near, far):
        index = jnp.maximum(index, 0)
        column = index & (cols - 1)
        index_parts += [index >> shift, column >> 1, column & 1]
    index_parts = [part.astype(F32).astype(BF16) for part in index_parts]
    index_parts += list(split(stiff))
    wide = [expand(part, by_device, by_place, turned=True) for part in index_parts]
    row_index = jnp.concatenate([wide[0], wide[3]], axis=1)
    column_index = jnp.concatenate([2.0 * wide[1] + wide[2], 2.0 * wide[4] + wide[5]], axis=1)
    stiff_row = wide[6] + wide[7]
    total = row_index.shape[1]
    spring[...] = jnp.broadcast_to(stiff_row, spring.shape)
    row_iota = lax.broadcasted_iota(jnp.int32, (rows, total), 0).astype(F32)
    row_hits = (row_iota == row_index).astype(F32).astype(BF16)
    row_marks[...] = row_hits
    for start in range(0, cols, 64):
        iota = (lax.broadcasted_iota(jnp.int32, (64, total), 0) + start).astype(F32)
        column_marks[start : start + 64, :] = (iota == column_index).astype(F32).astype(BF16)
    copies[3].wait()
    values = pick([disp[f] for f in range(FIELDS)], column_marks[...], row_hits)
    picked[...] = jnp.concatenate(values + [values[0]] * 3, axis=0)
    half = total // 2
    outgoing = device_marks(devices, slots, outgoing=True)
    near_out = collapse([value[:, :half] for value in values] + [stiff_row], outgoing, by_place)
    far_out = collapse([value[:, half:] for value in values], outgoing, by_place)

    for copy in copies[4:]:
        copy.wait()
    plate = thickness[...].astype(F32) * (1.0 / spacing_mm)
    columns = []
    for f in range(RESULTS + 1):
        left = stress_left[f] if f < RESULTS else plate[:, 0:LANES]
        right = stress_right[f] if f < RESULTS else plate[:, cols - LANES :]
        columns.append((left, 0, f // 5, 2 + f % 5))
        columns.append((right, LANES - 1, f // 5, 10 + f % 5))
    halo_rows = edge_rows(columns)
    send_edges(payload, near_out, far_out, halo_rows, [])
    for ref, stress, row in ((to_next, stress_bottom, rows - 1), (to_last, stress_top, 0)):
        ref[...] = jnp.zeros(ref.shape, F32)
        for f in range(RESULTS):
            ref[f : f + 1, :] = stress[f, row % 8 : row % 8 + 1, :]
        ref[RESULTS : RESULTS + 1, :] = plate[row : row + 1, :]


def fill_halo(ref, f, above, below, sides, corner):
    rows, cols = ref.shape[1] - PAD_ROWS, ref.shape[2] - LANES
    depth = above.shape[0]
    ref[f, rows:, :cols] = jnp.concatenate(
        [below, jnp.zeros((PAD_ROWS - 2 * depth, cols), F32), above], axis=0
    )
    ref[f, :rows, cols:] = sides
    ref[f, rows:, cols:] = corner


def load_velocity(vel_ext, incoming, above, below):
    left, right = girth_neighbours()
    first, second = edge_columns(tile_of(incoming, left), tile_of(incoming, right))
    row = lax.broadcasted_iota(jnp.int32, (8, LANES), 0)
    corner_tiles = [
        jnp.broadcast_to(jnp.where(inside, tile_of(incoming, device)[7:8], 0.0), (8, LANES))
        for device, inside in corner_neighbours()
    ]
    for f in range(FIELDS):
        sides = edge_block(
            [
                (first, 2 + f, LANES - 2),
                (second, 2 + f, LANES - 1),
                (first, 10 + f, 0),
                (second, 10 + f, 1),
            ]
        )
        upper = edge_block([(corner_tiles[0], f, LANES - 1), (corner_tiles[1], f, 0)])
        lower = edge_block([(corner_tiles[2], f, LANES - 1), (corner_tiles[3], f, 0)])
        corner = jnp.where(row == 0, lower, jnp.where(row == 7, upper, 0.0))
        fill_halo(
            vel_ext, f, above[2 * f : 2 * f + 2, :], below[2 * f : 2 * f + 2, :], sides, corner
        )


def load_stress(stress_ext, plate_ext, thickness, incoming, above, below):
    rows, cols = thickness.shape
    left, right = girth_neighbours()
    halves = edge_columns(tile_of(incoming, left), tile_of(incoming, right))
    plate_ext[0, :rows, :cols] = thickness[...].astype(F32) * (1.0 / spacing_mm)
    empty = jnp.zeros((PAD_ROWS, LANES), F32)
    for f in range(RESULTS + 1):
        lane = 2 + f % 5
        half = halves[f // 5]
        sides = edge_block([(half, lane, LANES - 1), (half, 8 + lane, 0)])
        ref, k = (stress_ext, f) if f < RESULTS else (plate_ext, 0)
        fill_halo(ref, k, above[f : f + 1, :], below[f : f + 1, :], sides, empty)


def step_kernel(first, last, *refs):
    (stress_in, velocity_in, disp_in, thickness_in, pressure_in) = refs[:5]
    if first:
        incoming, above, below, column_marks, row_marks, picked, spring = refs[5:12]
        out = refs[12:]
    else:
        incoming, above, below, column_marks, row_marks, picked, spring, plate_ext = refs[5:13]
        out = refs[13:]
    stress_out, velocity_out, disp_out = out[:3]
    out = out[3:]
    if first:
        plate_ext, spring_out = out[:2]
        out = out[2:]
    if last:
        to_left, to_right, to_next, to_last = out[:4]
    else:
        picked_out, payload, to_next, to_last = out[:4]
    (stress_ext, res_ext, vel_ext, weld, velocity, disp, thickness, pressure,
     got, sent) = out[4:]

    _, rows, cols = velocity.shape
    devices = incoming.shape[0] // 8
    total = picked.shape[1]
    half = total // 2
    by_device, by_place = slot_marks(devices, half // devices)
    inner = (slice(None), slice(0, rows), slice(0, cols))
    copies = fetch(
        got,
        [
            (velocity_in, vel_ext.at[inner] if not first else velocity),
            (stress_in, stress_ext.at[inner] if first else stress_ext),
            (disp_in, disp),
            (pressure_in, pressure),
        ]
        + ([(thickness_in, thickness)] if first else []),
    )
    sends = []

    def send(source, target):
        copy = pltpu.make_async_copy(source, target, sent.at[len(sends)])
        copy.start()
        sends.append(copy)

    other = []
    for row in (1, 0):
        high, low = split(incoming[pl.ds(row, devices, stride=8), :])
        other.append(expand(high, by_device, by_place) + expand(low, by_device, by_place))
    if first:
        stiffness = jnp.concatenate([spring[0:1, :], other[1][5:6]], axis=1)
        spring_out[...] = jnp.broadcast_to(stiffness, spring_out.shape)
    else:
        stiffness = spring[0:1, :]
    field = lax.broadcasted_iota(jnp.int32, (8, total), 0)
    scale = jnp.where(field < 3, 1.0, rotary_share) * stiffness
    pulls = scale * (jnp.concatenate(other, axis=1) - picked[...])
    weld[...] = spread(pulls, column_marks[...], row_marks[...])

    for copy in copies:
        copy.wait()
    if first:
        load_stress(stress_ext, plate_ext, thickness, incoming, above, below)
    else:
        load_velocity(vel_ext, incoming, above, below)
    for start in range(0, rows + PAD_ROWS, 8):
        plate = plate_ext[0, start : start + 8, :]
        chunk = [stress_ext[k, start : start + 8, :] for k in range(RESULTS)]
        if not first:
            chunk = stress_chunk(vel_ext, chunk, plate, start)
            for k, value in enumerate(chunk):
                stress_ext[k, start : start + 8, :] = value
        for k, value in enumerate(resultants(chunk, plate)):
            res_ext[k, start : start + 8, :] = value
    send(stress_ext, stress_out)

    for start in range(0, rows, 8):
        part = slice(start, start + 8)
        plate = plate_ext[0, part, :cols]
        linear = time_step / plate
        angular = (12.0 * linear) / (1.0 + plate * plate)
        force = force_chunk(res_ext, start, cols)
        force[2] = force[2] + pressure[part, :]
        for f in range(FIELDS):
            joined = force[f] + weld[f * rows + start : f * rows + start + 8, :]
            before = velocity[f, part, :] if first else vel_ext[f, part, :cols]
            speed = before + (linear if f < 3 else angular) * joined
            velocity[f, part, :] = speed
            disp[f, part, :] = disp[f, part, :] + time_step * speed
        if start % 32 == 24:
            done = slice(start - 24, start + 8)
            for source, target in ((velocity, velocity_out), (disp, disp_out)):
                send(source.at[:, done, :], target.at[:, done, :])

    ends = (cols - LANES, cols)
    if last:
        columns = []
        for f in range(FIELDS):
            columns.append((velocity[f, :, 0:LANES], 0, 0, f))
            columns.append((velocity[f, :, ends[0] : ends[1]], LANES - 1, 0, 8 + f))
        halo_rows = edge_rows(columns)
        to_left[...] = halo_rows[0:8]
        to_right[...] = halo_rows[8:16]
        for ref, row in ((to_next, rows - 1), (to_last, 0)):
            ref[...] = jnp.zeros(ref.shape, F32)
            for f in range(FIELDS):
                ref[f : f + 1, :] = velocity[f, row : row + 1, :]
        for copy in sends:
            copy.wait()
        return
    values = pick([disp[f] for f in range(FIELDS)], column_marks[...], row_marks[...])
    picked_out[...] = jnp.concatenate(values + [values[0]] * 3, axis=0)
    outgoing = device_marks(devices, half // devices, outgoing=True)
    near_out = collapse([value[:, :half] for value in values], outgoing, by_place)
    far_out = collapse([value[:, half:] for value in values], outgoing, by_place)
    columns = []
    for f in range(FIELDS):
        left_lanes = velocity[f, :, 0:LANES]
        right_lanes = velocity[f, :, ends[0] : ends[1]]
        for depth in (0, 1):
            columns.append((left_lanes, depth, depth, 2 + f))
            columns.append((right_lanes, LANES - 2 + depth, depth, 10 + f))
    corners = []
    lane = lax.broadcasted_iota(jnp.int32, (8, LANES), 1)
    for row in (0, rows - 1):
        tile = slice(row // 8 * 8, row // 8 * 8 + 8)
        for side in (0, 1):
            value = jnp.zeros((8, LANES), F32)
            for f in range(FIELDS):
                part = velocity[f, tile, ends[0] : ends[1]] if side else velocity[f, tile, 0:LANES]
                source = LANES - 1 if side else 0
                value = jnp.where(lane == f, pltpu.roll(part, (f - source) % LANES, 1), value)
            corners.append(jnp.broadcast_to(value[row % 8 : row % 8 + 1], (8, LANES)))
    send_edges(payload, near_out, far_out, edge_rows(columns), corners)
    for ref, start in ((to_next, rows - 2), (to_last, 0)):
        ref[...] = jnp.zeros(ref.shape, F32)
        for f in range(FIELDS):
            ref[2 * f : 2 * f + 2, :] = velocity[f, start : start + 2, :]
    for copy in sends:
        copy.wait()


def final_kernel(
    stress_in, velocity_in, from_left, from_right, above, below, plate_ext, height,
    stress_out, moment, stress, vel_ext, got, sent,
):
    rows, cols = vel_ext.shape[1] - PAD_ROWS, vel_ext.shape[2] - LANES
    inner = (slice(None), slice(0, rows), slice(0, cols))
    copies = fetch(got, [(velocity_in, vel_ext.at[inner]), (stress_in, stress)])
    first, _ = edge_columns(from_left[...], from_right[...])
    empty = jnp.zeros((PAD_ROWS, LANES), F32)
    for f in range(FIELDS):
        sides = edge_block([(first, f, LANES - 1), (first, 8 + f, 0)])
        fill_halo(vel_ext, f, above[f : f + 1, :], below[f : f + 1, :], sides, empty)
    for copy in copies:
        copy.wait()
    weight = height[0:1, :]
    parts = []
    sends = []
    for start in range(0, rows, 8):
        part = slice(start, start + 8)
        chunk = [stress[k, part, :] for k in range(RESULTS)]
        plate = plate_ext[0, part, :]
        chunk = stress_chunk(vel_ext, chunk, plate, start)
        for k, value in enumerate(chunk):
            stress[k, part, :] = value
        if start % 16 == 8:
            done = slice(start - 8, start + 8)
            copy = pltpu.make_async_copy(
                stress.at[:, done, :cols], stress_out.at[:, done, :], sent.at[len(sends)]
            )
            copy.start()
            sends.append(copy)
        weighted = plate[:, :cols] * chunk[0][:, :cols] * weight
        parts.append(jnp.sum(weighted, axis=1, keepdims=True))
    column = jnp.broadcast_to(jnp.concatenate(parts, axis=0), (rows, LANES))
    if rows < LANES:
        column = jnp.concatenate([column, jnp.zeros((LANES - rows, LANES), F32)], axis=0)
    moment[...] = column.T[0:8, :rows]
    for copy in sends:
        copy.wait()


def call(kernel, vmem_bytes, outs, scratch, *operands, far=0, far_out=0, copies=(1,)):
    operands = [
        pltpu.with_memory_space_constraint(value, pltpu.HBM) if k < far else value
        for k, value in enumerate(operands)
    ]
    whole = pl.BlockSpec(memory_space=pltpu.VMEM)
    away = pl.BlockSpec(memory_space=pltpu.HBM)
    scratch = [pltpu.VMEM(shape, dtype) for shape, dtype in scratch]
    scratch += [pltpu.SemaphoreType.DMA((count,)) for count in copies]
    return pl.pallas_call(
        kernel,
        out_shape=[
            pltpu.HBM(shape, dtype) if k < far_out else jax.ShapeDtypeStruct(shape, dtype)
            for k, (shape, dtype) in enumerate(outs)
        ],
        in_specs=[away] * far + [whole] * (len(operands) - far),
        out_specs=[away] * far_out + [whole] * (len(outs) - far_out),
        scratch_shapes=scratch,
        compiler_params=pltpu.CompilerParams(vmem_limit_bytes=vmem_bytes),
    )(*operands)


def to_next_section(values):
    count = lax.axis_size("sec")
    return lax.ppermute(values, "sec", [(i, i + 1) for i in range(count - 1)])


def to_last_section(values):
    count = lax.axis_size("sec")
    return lax.ppermute(values, "sec", [(i + 1, i) for i in range(count - 1)])


def exchange(tiles):
    secs, girths = lax.axis_size("sec"), lax.axis_size("girth")
    shape = (8, LANES)
    near = lax.all_to_all(tiles.reshape((girths, secs) + shape), "girth", 0, 0, tiled=True)
    near = jnp.swapaxes(near, 0, 1)
    far = lax.all_to_all(near, "sec", 0, 0, tiled=True)
    return far.reshape(tiles.shape)


def turn(values, step):
    count = lax.axis_size("girth")
    return lax.ppermute(values, "girth", [(i, (i + step) % count) for i in range(count)])


def local(displacement, velocity, stress, thickness, pressure, weld_from, weld_to, weld_stiff):
    rows, cols = thickness.shape
    _, devices, slots = weld_from.shape
    total = 2 * devices * slots
    girth_total = cols * lax.axis_size("girth")
    column = (lax.axis_index("girth") * cols + lax.iota(jnp.int32, cols)).astype(F32)
    height = jnp.sin(2.0 * jnp.pi / girth_total * (column + 0.5)) / girth_total
    height = jnp.broadcast_to(height[None, :], (8, cols))

    vmem_bytes = 8 * 1024 * 1024 + total * VMEM_PER_SLOT
    message = (devices * 8, LANES)
    strip = (16, cols)
    block = (FIELDS, rows, cols)
    stress_shape = (RESULTS, rows + PAD_ROWS, cols + LANES)
    plate_shape = (1, rows + PAD_ROWS, cols + LANES)
    slot_rows = (8, total)
    scratch = [
        (stress_shape, F32),
        (stress_shape, F32),
        ((FIELDS, rows + PAD_ROWS, cols + LANES), F32),
        ((FIELDS * rows, cols), F32),
        (block, F32),
        (block, F32),
        ((rows, cols), jnp.int32),
        ((rows, cols), F32),
    ]

    payload, to_next, to_last, column_marks, row_marks, picked, spring = call(
        start_kernel,
        vmem_bytes,
        [
            (message, F32), (strip, F32), (strip, F32), ((cols, total), BF16),
            ((rows, total), BF16), (slot_rows, F32), ((8, total // 2), F32),
        ],
        [
            (block, F32), ((RESULTS, rows, LANES), F32), ((RESULTS, rows, LANES), F32),
            ((RESULTS, 8, cols), F32), ((RESULTS, 8, cols), F32), ((rows, cols), jnp.int32),
            ((1, slots, devices), jnp.int32), ((1, slots, devices), jnp.int32),
            ((1, slots, devices), F32),
        ],
        displacement, stress, thickness,
        *[jnp.swapaxes(array, 1, 2) for array in (weld_from, weld_to, weld_stiff)],
        far=6,
        copies=(9,),
    )
    plate = None
    for step in range(STEPS):
        first, last = step == 0, step == STEPS - 1
        incoming = exchange(payload)
        above, below = to_next_section(to_next), to_last_section(to_last)
        outs = [(stress_shape, F32), (block, F32), (block, F32)]
        if first:
            outs += [(plate_shape, F32), (slot_rows, F32)]
        if last:
            edge = (8, LANES)
            outs += [(edge, F32), (edge, F32), ((8, cols), F32), ((8, cols), F32)]
        else:
            outs += [(slot_rows, F32), (message, F32), (strip, F32), (strip, F32)]
        results = call(
            functools.partial(step_kernel, first, last),
            vmem_bytes,
            outs,
            scratch,
            stress, velocity, displacement, thickness, pressure,
            incoming, above, below, column_marks, row_marks, picked, spring,
            *([] if first else [plate]),
            far=5,
            far_out=3,
            copies=(5, 1 + 2 * (rows // 32)),
        )
        stress, velocity, displacement = results[:3]
        results = results[3:]
        if first:
            plate, spring = results[:2]
            results = results[2:]
        if last:
            to_left, to_right, to_next, to_last = results
        else:
            picked, payload, to_next, to_last = results

    from_left, from_right = turn(to_right, 1), turn(to_left, -1)
    above, below = to_next_section(to_next), to_last_section(to_last)
    stress, partial_moment = call(
        final_kernel,
        vmem_bytes,
        [((RESULTS, rows, cols), F32), ((8, rows), F32)],
        [(stress_shape, F32), ((FIELDS, rows + PAD_ROWS, cols + LANES), F32)],
        stress, velocity, from_left, from_right, above, below, plate, height,
        far=2,
        far_out=1,
        copies=(2, rows // 16),
    )
    moment = lax.psum(partial_moment[0], "girth")
    return (displacement, velocity, stress, moment)


def solution(mesh):
    in_specs = (
        P(None, "sec", "girth"),
        P(None, "sec", "girth"),
        P(None, "sec", "girth"),
        P("sec", "girth"),
        P("sec", "girth"),
        P(("sec", "girth"), None, None),
        P(("sec", "girth"), None, None),
        P(("sec", "girth"), None, None),
    )
    out_specs = (
        P(None, "sec", "girth"),
        P(None, "sec", "girth"),
        P(None, "sec", "girth"),
        P("sec"),
    )
    return jax.shard_map(local, mesh=mesh, in_specs=in_specs, out_specs=out_specs, check_vma=False)
```

```python
import functools

import jax
import jax.numpy as jnp
from jax import lax
from jax.experimental import pallas as pl
from jax.experimental.pallas import tpu as pltpu
from jax.sharding import PartitionSpec as P

STEPS = 3
CORNER_LANE = 112
FIELDS = 5
RESULTS = 8
PAD_ROWS = 8
LANES = 128
VMEM_PER_SLOT = 5 * 1024

young_modulus = 4.0
poisson_ratio = 0.3
plate_modulus = young_modulus / (1.0 - poisson_ratio * poisson_ratio)
shear_modulus = young_modulus / (2.0 * (1.0 + poisson_ratio))
shear_factor = 5.0 / 6.0
time_step = 0.2
spacing_mm = 50.0
rotary_share = 1.0 / 12.0

F32 = jnp.float32
BF16 = jnp.bfloat16


def split(values):
    high = values.astype(BF16)
    low = (values - high.astype(F32)).astype(BF16)
    return high, low


def dot(a, b, contract):
    return lax.dot_general(a, b, (contract, ((), ())), preferred_element_type=F32)


def slot_marks(devices, slots):
    total = devices * slots
    lane = lax.broadcasted_iota(jnp.int32, (devices, total), 1)
    device = lax.broadcasted_iota(jnp.int32, (devices, total), 0)
    by_device = (lane // slots == device).astype(F32).astype(BF16)
    lane = lax.broadcasted_iota(jnp.int32, (slots, total), 1)
    place = lax.broadcasted_iota(jnp.int32, (slots, total), 0)
    by_place = (lane % slots == place).astype(F32)
    return by_device, by_place


def expand(blocks, by_device, by_place, turned=False):
    slots, total = by_place.shape
    wide = dot(blocks, by_device, ((1 if turned else 0,), (0,)))
    wide = wide.reshape(wide.shape[0] // slots, slots, total) * by_place[None]
    return jnp.sum(wide, axis=1)


def collapse(rows, by_device, by_place):
    slots, _ = by_place.shape
    marks = by_place.astype(BF16)
    pieces = []
    for part in (0, 1):
        blocks = [split(row)[part] * marks for row in rows]
        blocks += [jnp.zeros_like(marks)] * (LANES // slots - len(rows))
        pieces.append(jnp.concatenate(blocks, axis=0))
    return dot(by_device, pieces[0], ((1,), (1,))) + dot(by_device, pieces[1], ((1,), (1,)))


def pick(fields, column_marks, row_marks):
    rows = fields[0].shape[0]
    parts = [split(field) for field in fields]
    high = jnp.concatenate([part[0] for part in parts], axis=0)
    low = jnp.concatenate([part[1] for part in parts], axis=0)
    by_column = dot(high, column_marks, ((1,), (0,))) + dot(low, column_marks, ((1,), (0,)))
    marks = row_marks.astype(F32)
    return [
        jnp.sum(by_column[rows * f : rows * (f + 1)] * marks, axis=0, keepdims=True)
        for f in range(len(fields))
    ]


def spread(pulls, column_marks, row_marks):
    high, low = split(pulls)
    total = None
    for part in (high, low):
        marked = jnp.concatenate(
            [part[f : f + 1] * row_marks for f in range(FIELDS)], axis=0
        )
        summed = dot(marked, column_marks, ((1,), (1,)))
        total = summed if total is None else total + summed
    return total


def place():
    sec, girth = lax.axis_index("sec"), lax.axis_index("girth")
    return sec, girth, lax.axis_size("sec"), lax.axis_size("girth")


def tile_of(ref, device):
    return ref[pl.ds(pl.multiple_of(device * 8, 8), 8), :]


def set_tile(ref, device, value):
    ref[pl.ds(pl.multiple_of(device * 8, 8), 8), :] = value


def corner_neighbours():
    sec, girth, secs, girths = place()
    me = sec * girths + girth
    out = []
    for step in (-1, 1):
        row = sec + step
        inside = jnp.logical_and(row >= 0, row < secs)
        for turn in (girths - 1, 1):
            device = row * girths + lax.rem(girth + turn, girths)
            out.append((jnp.where(inside, device, me), inside))
    return out


def edge_rows(columns):
    rows = columns[0][0].shape[0]
    lane = lax.broadcasted_iota(jnp.int32, (rows, LANES), 1)
    halves = [jnp.zeros((rows, LANES), F32), jnp.zeros((rows, LANES), F32)]
    for value, source, half, row in columns:
        moved = pltpu.roll(value, (row - source) % LANES, 1)
        halves[half] = jnp.where(lane == row, moved, halves[half])
    return jnp.concatenate(halves, axis=0).T


def edge_columns(left_tile, right_tile):
    stacked = jnp.concatenate(
        [left_tile, right_tile, jnp.zeros((LANES - 16, LANES), F32)], axis=0
    )
    turned = stacked.T
    return turned[: LANES // 2], turned[LANES // 2 :]


def edge_block(pieces):
    rows = pieces[0][0].shape[0]
    lane = lax.broadcasted_iota(jnp.int32, (rows, LANES), 1)
    block = jnp.zeros((rows, LANES), F32)
    for value, source, target in pieces:
        block = jnp.where(lane == target, pltpu.roll(value, (target - source) % LANES, 1), block)
    return block


def row_chunk(ref, f, start):
    count = ref.shape[1]
    if start < 0:
        return jnp.concatenate([ref[f, count + start : count, :], ref[f, 0 : 8 + start, :]], axis=0)
    if start + 8 > count:
        return jnp.concatenate([ref[f, start:count, :], ref[f, 0 : start + 8 - count, :]], axis=0)
    return ref[f, start : start + 8, :]


def difference_x(ref, f, start):
    return row_chunk(ref, f, start + 1) - row_chunk(ref, f, start - 1)


def difference_y(value):
    lanes = value.shape[1]
    return pltpu.roll(value, lanes - 1, 1) - pltpu.roll(value, 1, 1)


def radial_return(xx, yy, xy):
    offset = xx - 0.5 * yy
    square = offset * offset + 0.75 * yy * yy + 3.0 * xy * xy
    scale = lax.rsqrt(jnp.maximum(square, 1.0))
    return xx * scale, yy * scale, xy * scale


def stress_chunk(vel_ref, stress, plate, start):
    current = [vel_ref[f, start : start + 8, :] for f in range(FIELDS)]
    along_x = [difference_x(vel_ref, f, start) for f in range(FIELDS)]
    along_y = [difference_y(value) for value in current]
    normal = 0.5 * time_step * plate_modulus
    skew = 0.5 * time_step * shear_modulus
    arm = 0.5 * plate
    membrane = radial_return(
        stress[0] + normal * (along_x[0] + poisson_ratio * along_y[1]),
        stress[1] + normal * (along_y[1] + poisson_ratio * along_x[0]),
        stress[2] + skew * (along_y[0] + along_x[1]),
    )
    bending = radial_return(
        stress[3] + (normal * arm) * (along_x[3] + poisson_ratio * along_y[4]),
        stress[4] + (normal * arm) * (along_y[4] + poisson_ratio * along_x[3]),
        stress[5] + (skew * arm) * (along_y[3] + along_x[4]),
    )
    shear = (
        stress[6] + skew * (along_x[2] + 2.0 * current[3]),
        stress[7] + skew * (along_y[2] + 2.0 * current[4]),
    )
    return membrane + bending + shear


def resultants(stress, plate):
    arm = plate * plate * (1.0 / 6.0)
    shear = shear_factor * plate
    return (
        [plate * value for value in stress[0:3]]
        + [arm * value for value in stress[3:6]]
        + [shear * value for value in stress[6:8]]
    )


def force_chunk(res_ref, start, cols):
    def both(x, y):
        along_x = difference_x(res_ref, x, start)[:, :cols]
        along_y = difference_y(res_ref[y, start : start + 8, :])[:, :cols]
        return 0.5 * (along_x + along_y)

    return [
        both(0, 2),
        both(2, 1),
        both(6, 7),
        both(3, 5) - res_ref[6, start : start + 8, :cols],
        both(5, 4) - res_ref[7, start : start + 8, :cols],
    ]


def send_joints(payload, near, far, corners):
    devices = payload.shape[0] // 2
    payload[pl.ds(0, devices, stride=2), :] = near
    payload[pl.ds(1, devices, stride=2), :] = far
    row = lax.broadcasted_iota(jnp.int32, (8, LANES), 0)
    lane = lax.broadcasted_iota(jnp.int32, (8, LANES), 1)
    free = jnp.logical_and(lane >= CORNER_LANE, lane < CORNER_LANE + FIELDS)
    for (device, _), corner in zip(corner_neighbours(), corners):
        tile = lax.div(device, 4)
        here = jnp.logical_and(free, row == 2 * lax.rem(device, 4))
        set_tile(payload, tile, jnp.where(here, corner, tile_of(payload, tile)))


def corner_of(incoming, device):
    row = lax.broadcasted_iota(jnp.int32, (8, LANES), 0)
    tile = tile_of(incoming, lax.div(device, 4))
    return jnp.sum(jnp.where(row == 2 * lax.rem(device, 4), tile, 0.0), axis=0, keepdims=True)


def fetch(done, pairs):
    copies = [
        pltpu.make_async_copy(source, target, done.at[k])
        for k, (source, target) in enumerate(pairs)
    ]
    for copy in copies:
        copy.start()
    return copies


def start_kernel(
    disp_in, stress_in, thickness_in, from_in, to_in, stiff_in,
    payload, to_next, to_last, to_left, to_right,
    column_marks, row_marks, picked, spring,
    disp, stress_left, stress_right, stress_top, stress_bottom, thickness,
    weld_from, weld_to, weld_stiff, done,
):
    rows, cols = thickness.shape
    _, slots, devices = weld_from.shape
    copies = fetch(
        done,
        [
            (from_in, weld_from),
            (to_in, weld_to),
            (stiff_in, weld_stiff),
            (disp_in, disp),
            (thickness_in, thickness),
            (stress_in.at[:, :, 0:LANES], stress_left),
            (stress_in.at[:, :, cols - LANES : cols], stress_right),
            (stress_in.at[:, 0:8, :], stress_top),
            (stress_in.at[:, rows - 8 : rows, :], stress_bottom),
        ],
    )
    shift = cols.bit_length() - 1
    by_device, by_place = slot_marks(devices, slots)
    for copy in copies[:3]:
        copy.wait()
    near, far = weld_from[0], weld_to[0]
    stiff = jnp.where(near >= 0, weld_stiff[0], 0.0)
    index_parts = []
    for index in (near, far):
        index = jnp.maximum(index, 0)
        column = index & (cols - 1)
        index_parts += [index >> shift, column >> 1, column & 1]
    index_parts = [part.astype(F32).astype(BF16) for part in index_parts]
    index_parts += list(split(stiff))
    wide = [expand(part, by_device, by_place, turned=True) for part in index_parts]
    row_index = jnp.concatenate([wide[0], wide[3]], axis=1)
    column_index = jnp.concatenate([2.0 * wide[1] + wide[2], 2.0 * wide[4] + wide[5]], axis=1)
    stiff_row = wide[6] + wide[7]
    total = row_index.shape[1]
    spring[...] = jnp.broadcast_to(stiff_row, spring.shape)
    row_iota = lax.broadcasted_iota(jnp.int32, (rows, total), 0).astype(F32)
    row_hits = (row_iota == row_index).astype(F32).astype(BF16)
    row_marks[...] = row_hits
    for start in range(0, cols, 64):
        iota = (lax.broadcasted_iota(jnp.int32, (64, total), 0) + start).astype(F32)
        column_marks[start : start + 64, :] = (iota == column_index).astype(F32).astype(BF16)
    copies[3].wait()
    values = pick([disp[f] for f in range(FIELDS)], column_marks[...], row_hits)
    picked[...] = jnp.concatenate(values + [values[0]] * 3, axis=0)
    half = total // 2
    near_out = collapse([value[:, :half] for value in values] + [stiff_row], by_device, by_place)
    far_out = collapse([value[:, half:] for value in values], by_device, by_place)

    for copy in copies[4:]:
        copy.wait()
    plate = thickness[...].astype(F32) * (1.0 / spacing_mm)
    columns = []
    for f in range(RESULTS + 1):
        left = stress_left[f] if f < RESULTS else plate[:, 0:LANES]
        right = stress_right[f] if f < RESULTS else plate[:, cols - LANES :]
        columns.append((left, 0, f // 5, 2 + f % 5))
        columns.append((right, LANES - 1, f // 5, 10 + f % 5))
    halo_rows = edge_rows(columns)
    to_left[...] = halo_rows[0:8]
    to_right[...] = halo_rows[8:16]
    send_joints(payload, near_out, far_out, [])
    for ref, stress, row in ((to_next, stress_bottom, rows - 1), (to_last, stress_top, 0)):
        ref[...] = jnp.zeros(ref.shape, F32)
        for f in range(RESULTS):
            ref[f : f + 1, :] = stress[f, row % 8 : row % 8 + 1, :]
        ref[RESULTS : RESULTS + 1, :] = plate[row : row + 1, :]


def fill_halo(ref, f, above, below, sides, corner):
    rows, cols = ref.shape[1] - PAD_ROWS, ref.shape[2] - LANES
    depth = above.shape[0]
    ref[f, rows:, :cols] = jnp.concatenate(
        [below, jnp.zeros((PAD_ROWS - 2 * depth, cols), F32), above], axis=0
    )
    ref[f, :rows, cols:] = sides
    ref[f, rows:, cols:] = corner


def load_velocity(vel_ext, incoming, above, below, from_left, from_right):
    first, second = edge_columns(from_left[...], from_right[...])
    row = lax.broadcasted_iota(jnp.int32, (8, LANES), 0)
    corner_tiles = [
        jnp.broadcast_to(jnp.where(inside, corner_of(incoming, device), 0.0), (8, LANES))
        for device, inside in corner_neighbours()
    ]
    for f in range(FIELDS):
        sides = edge_block(
            [
                (first, 2 + f, LANES - 2),
                (second, 2 + f, LANES - 1),
                (first, 10 + f, 0),
                (second, 10 + f, 1),
            ]
        )
        upper = edge_block([(corner_tiles[0], CORNER_LANE + f, LANES - 1), (corner_tiles[1], CORNER_LANE + f, 0)])
        lower = edge_block([(corner_tiles[2], CORNER_LANE + f, LANES - 1), (corner_tiles[3], CORNER_LANE + f, 0)])
        corner = jnp.where(row == 0, lower, jnp.where(row == 7, upper, 0.0))
        fill_halo(
            vel_ext, f, above[2 * f : 2 * f + 2, :], below[2 * f : 2 * f + 2, :], sides, corner
        )


def load_stress(stress_ext, plate_ext, thickness, above, below, from_left, from_right):
    rows, cols = thickness.shape
    halves = edge_columns(from_left[...], from_right[...])
    plate_ext[0, :rows, :cols] = thickness[...].astype(F32) * (1.0 / spacing_mm)
    empty = jnp.zeros((PAD_ROWS, LANES), F32)
    for f in range(RESULTS + 1):
        lane = 2 + f % 5
        half = halves[f // 5]
        sides = edge_block([(half, lane, LANES - 1), (half, 8 + lane, 0)])
        ref, k = (stress_ext, f) if f < RESULTS else (plate_ext, 0)
        fill_halo(ref, k, above[f : f + 1, :], below[f : f + 1, :], sides, empty)


def step_kernel(first, last, *refs):
    (stress_in, velocity_in, disp_in, thickness_in, pressure_in) = refs[:5]
    if first:
        out = refs[14:]
    else:
        plate_ext = refs[14]
        out = refs[15:]
    (incoming, above, below, from_left, from_right,
     column_marks, row_marks, picked, spring) = refs[5:14]
    stress_out, velocity_out, disp_out = out[:3]
    out = out[3:]
    if first:
        plate_ext, spring_out = out[:2]
        out = out[2:]
    to_left, to_right, to_next, to_last = out[:4]
    out = out[4:]
    if not last:
        picked_out, payload = out[:2]
        out = out[2:]
    (stress_ext, res_ext, vel_ext, weld, velocity, disp, thickness, pressure,
     got, sent) = out

    _, rows, cols = velocity.shape
    devices = incoming.shape[0] // 2
    total = picked.shape[1]
    half = total // 2
    by_device, by_place = slot_marks(devices, half // devices)
    inner = (slice(None), slice(0, rows), slice(0, cols))
    copies = fetch(
        got,
        [
            (velocity_in, vel_ext.at[inner] if not first else velocity),
            (stress_in, stress_ext.at[inner] if first else stress_ext),
            (disp_in, disp),
            (pressure_in, pressure),
        ]
        + ([(thickness_in, thickness)] if first else []),
    )
    sends = []

    def send(source, target):
        copy = pltpu.make_async_copy(source, target, sent.at[len(sends)])
        copy.start()
        sends.append(copy)

    other = []
    for row in (1, 0):
        high, low = split(incoming[pl.ds(row, devices, stride=2), :])
        other.append(expand(high, by_device, by_place) + expand(low, by_device, by_place))
    if first:
        stiffness = jnp.concatenate([spring[0:1, :], other[1][5:6]], axis=1)
        spring_out[...] = jnp.broadcast_to(stiffness, spring_out.shape)
    else:
        stiffness = spring[0:1, :]
    field = lax.broadcasted_iota(jnp.int32, (8, total), 0)
    scale = jnp.where(field < 3, 1.0, rotary_share) * stiffness
    pulls = scale * (jnp.concatenate(other, axis=1) - picked[...])
    weld[...] = spread(pulls, column_marks[...], row_marks[...])

    for copy in copies:
        copy.wait()
    if first:
        load_stress(stress_ext, plate_ext, thickness, above, below, from_left, from_right)
    else:
        load_velocity(vel_ext, incoming, above, below, from_left, from_right)
    for start in range(0, rows + PAD_ROWS, 8):
        plate = plate_ext[0, start : start + 8, :]
        chunk = [stress_ext[k, start : start + 8, :] for k in range(RESULTS)]
        if not first:
            chunk = stress_chunk(vel_ext, chunk, plate, start)
            for k, value in enumerate(chunk):
                stress_ext[k, start : start + 8, :] = value
        for k, value in enumerate(resultants(chunk, plate)):
            res_ext[k, start : start + 8, :] = value
    send(stress_ext, stress_out)

    for start in range(0, rows, 8):
        part = slice(start, start + 8)
        plate = plate_ext[0, part, :cols]
        linear = time_step / plate
        angular = (12.0 * linear) / (1.0 + plate * plate)
        force = force_chunk(res_ext, start, cols)
        force[2] = force[2] + pressure[part, :]
        for f in range(FIELDS):
            joined = force[f] + weld[f * rows + start : f * rows + start + 8, :]
            before = velocity[f, part, :] if first else vel_ext[f, part, :cols]
            speed = before + (linear if f < 3 else angular) * joined
            velocity[f, part, :] = speed
            disp[f, part, :] = disp[f, part, :] + time_step * speed
        if start % 32 == 24:
            done = slice(start - 24, start + 8)
            for source, target in ((velocity, velocity_out), (disp, disp_out)):
                send(source.at[:, done, :], target.at[:, done, :])

    ends = (cols - LANES, cols)
    if last:
        columns = []
        for f in range(FIELDS):
            columns.append((velocity[f, :, 0:LANES], 0, 0, f))
            columns.append((velocity[f, :, ends[0] : ends[1]], LANES - 1, 0, 8 + f))
        halo_rows = edge_rows(columns)
        to_left[...] = halo_rows[0:8]
        to_right[...] = halo_rows[8:16]
        for ref, row in ((to_next, rows - 1), (to_last, 0)):
            ref[...] = jnp.zeros(ref.shape, F32)
            for f in range(FIELDS):
                ref[f : f + 1, :] = velocity[f, row : row + 1, :]
        for copy in sends:
            copy.wait()
        return
    values = pick([disp[f] for f in range(FIELDS)], column_marks[...], row_marks[...])
    picked_out[...] = jnp.concatenate(values + [values[0]] * 3, axis=0)
    near_out = collapse([value[:, :half] for value in values], by_device, by_place)
    far_out = collapse([value[:, half:] for value in values], by_device, by_place)
    columns = []
    for f in range(FIELDS):
        left_lanes = velocity[f, :, 0:LANES]
        right_lanes = velocity[f, :, ends[0] : ends[1]]
        for depth in (0, 1):
            columns.append((left_lanes, depth, depth, 2 + f))
            columns.append((right_lanes, LANES - 2 + depth, depth, 10 + f))
    corners = []
    lane = lax.broadcasted_iota(jnp.int32, (8, LANES), 1)
    for row in (0, rows - 1):
        tile = slice(row // 8 * 8, row // 8 * 8 + 8)
        for side in (0, 1):
            value = jnp.zeros((8, LANES), F32)
            for f in range(FIELDS):
                part = velocity[f, tile, ends[0] : ends[1]] if side else velocity[f, tile, 0:LANES]
                source = LANES - 1 if side else 0
                target = CORNER_LANE + f
                value = jnp.where(lane == target, pltpu.roll(part, (target - source) % LANES, 1), value)
            corners.append(jnp.broadcast_to(value[row % 8 : row % 8 + 1], (8, LANES)))
    halo_rows = edge_rows(columns)
    to_left[...] = halo_rows[0:8]
    to_right[...] = halo_rows[8:16]
    send_joints(payload, near_out, far_out, corners)
    for ref, start in ((to_next, rows - 2), (to_last, 0)):
        ref[...] = jnp.zeros(ref.shape, F32)
        for f in range(FIELDS):
            ref[2 * f : 2 * f + 2, :] = velocity[f, start : start + 2, :]
    for copy in sends:
        copy.wait()


def final_kernel(
    stress_in, velocity_in, from_left, from_right, above, below, plate_ext, height,
    stress_out, moment, stress, vel_ext, got, sent,
):
    rows, cols = vel_ext.shape[1] - PAD_ROWS, vel_ext.shape[2] - LANES
    inner = (slice(None), slice(0, rows), slice(0, cols))
    copies = fetch(got, [(velocity_in, vel_ext.at[inner]), (stress_in, stress)])
    first, _ = edge_columns(from_left[...], from_right[...])
    empty = jnp.zeros((PAD_ROWS, LANES), F32)
    for f in range(FIELDS):
        sides = edge_block([(first, f, LANES - 1), (first, 8 + f, 0)])
        fill_halo(vel_ext, f, above[f : f + 1, :], below[f : f + 1, :], sides, empty)
    for copy in copies:
        copy.wait()
    weight = height[0:1, :]
    parts = []
    sends = []
    for start in range(0, rows, 8):
        part = slice(start, start + 8)
        chunk = [stress[k, part, :] for k in range(RESULTS)]
        plate = plate_ext[0, part, :]
        chunk = stress_chunk(vel_ext, chunk, plate, start)
        for k, value in enumerate(chunk):
            stress[k, part, :] = value
        if start % 16 == 8:
            done = slice(start - 8, start + 8)
            copy = pltpu.make_async_copy(
                stress.at[:, done, :cols], stress_out.at[:, done, :], sent.at[len(sends)]
            )
            copy.start()
            sends.append(copy)
        weighted = plate[:, :cols] * chunk[0][:, :cols] * weight
        parts.append(jnp.sum(weighted, axis=1, keepdims=True))
    column = jnp.broadcast_to(jnp.concatenate(parts, axis=0), (rows, LANES))
    if rows < LANES:
        column = jnp.concatenate([column, jnp.zeros((LANES - rows, LANES), F32)], axis=0)
    moment[...] = column.T[0:8, :rows]
    for copy in sends:
        copy.wait()


def call(kernel, vmem_bytes, outs, scratch, *operands, far=0, far_out=0, copies=(1,)):
    operands = [
        pltpu.with_memory_space_constraint(value, pltpu.HBM) if k < far else value
        for k, value in enumerate(operands)
    ]
    whole = pl.BlockSpec(memory_space=pltpu.VMEM)
    away = pl.BlockSpec(memory_space=pltpu.HBM)
    scratch = [pltpu.VMEM(shape, dtype) for shape, dtype in scratch]
    scratch += [pltpu.SemaphoreType.DMA((count,)) for count in copies]
    return pl.pallas_call(
        kernel,
        out_shape=[
            pltpu.HBM(shape, dtype) if k < far_out else jax.ShapeDtypeStruct(shape, dtype)
            for k, (shape, dtype) in enumerate(outs)
        ],
        in_specs=[away] * far + [whole] * (len(operands) - far),
        out_specs=[away] * far_out + [whole] * (len(outs) - far_out),
        scratch_shapes=scratch,
        compiler_params=pltpu.CompilerParams(vmem_limit_bytes=vmem_bytes),
    )(*operands)


def to_next_section(values):
    count = lax.axis_size("sec")
    return lax.ppermute(values, "sec", [(i, i + 1) for i in range(count - 1)])


def to_last_section(values):
    count = lax.axis_size("sec")
    return lax.ppermute(values, "sec", [(i + 1, i) for i in range(count - 1)])


def exchange(joints):
    blocks = joints.reshape(joints.shape[0] // 2, 2, LANES)
    blocks = lax.all_to_all(blocks, ("sec", "girth"), 0, 0, tiled=True)
    return blocks.reshape(joints.shape)


def turn(values, step):
    count = lax.axis_size("girth")
    return lax.ppermute(values, "girth", [(i, (i + step) % count) for i in range(count)])


def local(displacement, velocity, stress, thickness, pressure, weld_from, weld_to, weld_stiff):
    rows, cols = thickness.shape
    _, devices, slots = weld_from.shape
    total = 2 * devices * slots
    girth_total = cols * lax.axis_size("girth")
    column = (lax.axis_index("girth") * cols + lax.iota(jnp.int32, cols)).astype(F32)
    height = jnp.sin(2.0 * jnp.pi / girth_total * (column + 0.5)) / girth_total
    height = jnp.broadcast_to(height[None, :], (8, cols))

    vmem_bytes = 8 * 1024 * 1024 + total * VMEM_PER_SLOT
    message = (devices * 2, LANES)
    edge = (8, LANES)
    strip = (16, cols)
    block = (FIELDS, rows, cols)
    stress_shape = (RESULTS, rows + PAD_ROWS, cols + LANES)
    plate_shape = (1, rows + PAD_ROWS, cols + LANES)
    slot_rows = (8, total)
    scratch = [
        (stress_shape, F32),
        (stress_shape, F32),
        ((FIELDS, rows + PAD_ROWS, cols + LANES), F32),
        ((FIELDS * rows, cols), F32),
        (block, F32),
        (block, F32),
        ((rows, cols), jnp.int32),
        ((rows, cols), F32),
    ]

    payload, to_next, to_last, to_left, to_right, column_marks, row_marks, picked, spring = call(
        start_kernel,
        vmem_bytes,
        [
            (message, F32), (strip, F32), (strip, F32), (edge, F32), (edge, F32),
            ((cols, total), BF16), ((rows, total), BF16), (slot_rows, F32), ((8, total // 2), F32),
        ],
        [
            (block, F32), ((RESULTS, rows, LANES), F32), ((RESULTS, rows, LANES), F32),
            ((RESULTS, 8, cols), F32), ((RESULTS, 8, cols), F32), ((rows, cols), jnp.int32),
            ((1, slots, devices), jnp.int32), ((1, slots, devices), jnp.int32),
            ((1, slots, devices), F32),
        ],
        displacement, stress, thickness,
        *[jnp.swapaxes(array, 1, 2) for array in (weld_from, weld_to, weld_stiff)],
        far=6,
        copies=(9,),
    )
    plate = None
    for step in range(STEPS):
        first, last = step == 0, step == STEPS - 1
        incoming = exchange(payload)
        from_left, from_right = turn(to_right, 1), turn(to_left, -1)
        above, below = to_next_section(to_next), to_last_section(to_last)
        outs = [(stress_shape, F32), (block, F32), (block, F32)]
        if first:
            outs += [(plate_shape, F32), (slot_rows, F32)]
        halo = (8, cols) if last else strip
        outs += [(edge, F32), (edge, F32), (halo, F32), (halo, F32)]
        if not last:
            outs += [(slot_rows, F32), (message, F32)]
        results = call(
            functools.partial(step_kernel, first, last),
            vmem_bytes,
            outs,
            scratch,
            stress, velocity, displacement, thickness, pressure,
            incoming, above, below, from_left, from_right,
            column_marks, row_marks, picked, spring,
            *([] if first else [plate]),
            far=5,
            far_out=3,
            copies=(5, 1 + 2 * (rows // 32)),
        )
        stress, velocity, displacement = results[:3]
        results = results[3:]
        if first:
            plate, spring = results[:2]
            results = results[2:]
        to_left, to_right, to_next, to_last = results[:4]
        if not last:
            picked, payload = results[4:]

    from_left, from_right = turn(to_right, 1), turn(to_left, -1)
    above, below = to_next_section(to_next), to_last_section(to_last)
    stress, partial_moment = call(
        final_kernel,
        vmem_bytes,
        [((RESULTS, rows, cols), F32), ((8, rows), F32)],
        [(stress_shape, F32), ((FIELDS, rows + PAD_ROWS, cols + LANES), F32)],
        stress, velocity, from_left, from_right, above, below, plate, height,
        far=2,
        far_out=1,
        copies=(2, rows // 16),
    )
    moment = lax.psum(partial_moment[0], "girth")
    return (displacement, velocity, stress, moment)


def solution(mesh):
    in_specs = (
        P(None, "sec", "girth"),
        P(None, "sec", "girth"),
        P(None, "sec", "girth"),
        P("sec", "girth"),
        P("sec", "girth"),
        P(("sec", "girth"), None, None),
        P(("sec", "girth"), None, None),
        P(("sec", "girth"), None, None),
    )
    out_specs = (
        P(None, "sec", "girth"),
        P(None, "sec", "girth"),
        P(None, "sec", "girth"),
        P("sec"),
    )
    return jax.shard_map(local, mesh=mesh, in_specs=in_specs, out_specs=out_specs, check_vma=False)
```

```python
import functools

import jax
import jax.numpy as jnp
from jax import lax
from jax.experimental import pallas as pl
from jax.experimental.pallas import tpu as pltpu
from jax.sharding import PartitionSpec as P

STEPS = 3
CORNER_LANE = 112
FIELDS = 5
RESULTS = 8
PAD_ROWS = 8
LANES = 128
VMEM_PER_SLOT = 5 * 1024

young_modulus = 4.0
poisson_ratio = 0.3
plate_modulus = young_modulus / (1.0 - poisson_ratio * poisson_ratio)
shear_modulus = young_modulus / (2.0 * (1.0 + poisson_ratio))
shear_factor = 5.0 / 6.0
time_step = 0.2
spacing_mm = 50.0
rotary_share = 1.0 / 12.0

F32 = jnp.float32
BF16 = jnp.bfloat16


def split(values):
    high = values.astype(BF16)
    low = (values - high.astype(F32)).astype(BF16)
    return high, low


def dot(a, b, contract):
    return lax.dot_general(a, b, (contract, ((), ())), preferred_element_type=F32)


def slot_marks(devices, slots):
    total = devices * slots
    lane = lax.broadcasted_iota(jnp.int32, (devices, total), 1)
    device = lax.broadcasted_iota(jnp.int32, (devices, total), 0)
    by_device = (lane // slots == device).astype(F32).astype(BF16)
    lane = lax.broadcasted_iota(jnp.int32, (slots, total), 1)
    place = lax.broadcasted_iota(jnp.int32, (slots, total), 0)
    by_place = (lane % slots == place).astype(F32)
    return by_device, by_place


def expand(blocks, by_device, by_place, turned=False):
    slots, total = by_place.shape
    wide = dot(blocks, by_device, ((1 if turned else 0,), (0,)))
    wide = wide.reshape(wide.shape[0] // slots, slots, total) * by_place[None]
    return jnp.sum(wide, axis=1)


def collapse(rows, by_device, by_place):
    slots, _ = by_place.shape
    marks = by_place.astype(BF16)
    pieces = []
    for part in (0, 1):
        blocks = [split(row)[part] * marks for row in rows]
        blocks += [jnp.zeros_like(marks)] * (LANES // slots - len(rows))
        pieces.append(jnp.concatenate(blocks, axis=0))
    return dot(by_device, pieces[0], ((1,), (1,))) + dot(by_device, pieces[1], ((1,), (1,)))


def pick(fields, column_marks, row_marks):
    rows = fields[0].shape[0]
    parts = [split(field) for field in fields]
    high = jnp.concatenate([part[0] for part in parts], axis=0)
    low = jnp.concatenate([part[1] for part in parts], axis=0)
    by_column = dot(high, column_marks, ((1,), (0,))) + dot(low, column_marks, ((1,), (0,)))
    marks = row_marks.astype(F32)
    return [
        jnp.sum(by_column[rows * f : rows * (f + 1)] * marks, axis=0, keepdims=True)
        for f in range(len(fields))
    ]


def spread(pulls, column_marks, row_marks):
    high, low = split(pulls)
    total = None
    for part in (high, low):
        marked = jnp.concatenate(
            [part[f : f + 1] * row_marks for f in range(FIELDS)], axis=0
        )
        summed = dot(marked, column_marks, ((1,), (1,)))
        total = summed if total is None else total + summed
    return total


def place():
    sec, girth = lax.axis_index("sec"), lax.axis_index("girth")
    return sec, girth, lax.axis_size("sec"), lax.axis_size("girth")


def tile_of(ref, device):
    return ref[pl.ds(pl.multiple_of(device * 8, 8), 8), :]


def set_tile(ref, device, value):
    ref[pl.ds(pl.multiple_of(device * 8, 8), 8), :] = value


def corner_neighbours():
    sec, girth, secs, girths = place()
    me = sec * girths + girth
    out = []
    for step in (-1, 1):
        row = sec + step
        inside = jnp.logical_and(row >= 0, row < secs)
        for turn in (girths - 1, 1):
            device = row * girths + lax.rem(girth + turn, girths)
            out.append((jnp.where(inside, device, me), inside))
    return out


def edge_rows(columns):
    rows = columns[0][0].shape[0]
    lane = lax.broadcasted_iota(jnp.int32, (rows, LANES), 1)
    halves = [jnp.zeros((rows, LANES), F32), jnp.zeros((rows, LANES), F32)]
    for value, source, half, row in columns:
        moved = pltpu.roll(value, (row - source) % LANES, 1)
        halves[half] = jnp.where(lane == row, moved, halves[half])
    return jnp.concatenate(halves, axis=0).T


def edge_columns(left_tile, right_tile):
    stacked = jnp.concatenate(
        [left_tile, right_tile, jnp.zeros((LANES - 16, LANES), F32)], axis=0
    )
    turned = stacked.T
    return turned[: LANES // 2], turned[LANES // 2 :]


def edge_block(pieces):
    rows = pieces[0][0].shape[0]
    lane = lax.broadcasted_iota(jnp.int32, (rows, LANES), 1)
    block = jnp.zeros((rows, LANES), F32)
    for value, source, target in pieces:
        block = jnp.where(lane == target, pltpu.roll(value, (target - source) % LANES, 1), block)
    return block


def row_chunk(ref, f, start):
    count = ref.shape[1]
    if start < 0:
        return jnp.concatenate([ref[f, count + start : count, :], ref[f, 0 : 8 + start, :]], axis=0)
    if start + 8 > count:
        return jnp.concatenate([ref[f, start:count, :], ref[f, 0 : start + 8 - count, :]], axis=0)
    return ref[f, start : start + 8, :]


def difference_x(ref, f, start):
    return row_chunk(ref, f, start + 1) - row_chunk(ref, f, start - 1)


def difference_y(value):
    lanes = value.shape[1]
    return pltpu.roll(value, lanes - 1, 1) - pltpu.roll(value, 1, 1)


def radial_return(xx, yy, xy):
    offset = xx - 0.5 * yy
    square = offset * offset + 0.75 * yy * yy + 3.0 * xy * xy
    scale = lax.rsqrt(jnp.maximum(square, 1.0))
    return xx * scale, yy * scale, xy * scale


def stress_chunk(vel_ref, stress, plate, start):
    current = [vel_ref[f, start : start + 8, :] for f in range(FIELDS)]
    along_x = [difference_x(vel_ref, f, start) for f in range(FIELDS)]
    along_y = [difference_y(value) for value in current]
    normal = 0.5 * time_step * plate_modulus
    skew = 0.5 * time_step * shear_modulus
    arm = 0.5 * plate
    membrane = radial_return(
        stress[0] + normal * (along_x[0] + poisson_ratio * along_y[1]),
        stress[1] + normal * (along_y[1] + poisson_ratio * along_x[0]),
        stress[2] + skew * (along_y[0] + along_x[1]),
    )
    bending = radial_return(
        stress[3] + (normal * arm) * (along_x[3] + poisson_ratio * along_y[4]),
        stress[4] + (normal * arm) * (along_y[4] + poisson_ratio * along_x[3]),
        stress[5] + (skew * arm) * (along_y[3] + along_x[4]),
    )
    shear = (
        stress[6] + skew * (along_x[2] + 2.0 * current[3]),
        stress[7] + skew * (along_y[2] + 2.0 * current[4]),
    )
    return membrane + bending + shear


def resultants(stress, plate):
    arm = plate * plate * (1.0 / 6.0)
    shear = shear_factor * plate
    return (
        [plate * value for value in stress[0:3]]
        + [arm * value for value in stress[3:6]]
        + [shear * value for value in stress[6:8]]
    )


def force_chunk(res_ref, start, cols):
    def both(x, y):
        along_x = difference_x(res_ref, x, start)[:, :cols]
        along_y = difference_y(res_ref[y, start : start + 8, :])[:, :cols]
        return 0.5 * (along_x + along_y)

    return [
        both(0, 2),
        both(2, 1),
        both(6, 7),
        both(3, 5) - res_ref[6, start : start + 8, :cols],
        both(5, 4) - res_ref[7, start : start + 8, :cols],
    ]


def send_joints(payload, near, far, corners):
    devices = payload.shape[0] // 2
    payload[pl.ds(0, devices, stride=2), :] = near
    payload[pl.ds(1, devices, stride=2), :] = far
    row = lax.broadcasted_iota(jnp.int32, (8, LANES), 0)
    lane = lax.broadcasted_iota(jnp.int32, (8, LANES), 1)
    free = jnp.logical_and(lane >= CORNER_LANE, lane < CORNER_LANE + FIELDS)
    for (device, _), corner in zip(corner_neighbours(), corners):
        tile = lax.div(device, 4)
        here = jnp.logical_and(free, row == 2 * lax.rem(device, 4))
        set_tile(payload, tile, jnp.where(here, corner, tile_of(payload, tile)))


def in_order(axis, low, high):
    even = lax.rem(lax.axis_index(axis), 2) == 0
    return jnp.where(even, high, low), jnp.where(even, low, high)


def send_sides(pair, halo_rows):
    for ref, value in zip(pair, in_order("girth", halo_rows[0:8], halo_rows[8:16])):
        ref[...] = value


def send_ends(pair, low, high):
    for ref in pair:
        ref[...] = jnp.zeros(ref.shape, F32)
    start = 0
    for top, bottom in zip(low, high):
        count = top.shape[0]
        for ref, value in zip(pair, in_order("sec", top, bottom)):
            ref[start : start + count, :] = value
        start += count


def corner_of(incoming, device):
    row = lax.broadcasted_iota(jnp.int32, (8, LANES), 0)
    tile = tile_of(incoming, lax.div(device, 4))
    return jnp.sum(jnp.where(row == 2 * lax.rem(device, 4), tile, 0.0), axis=0, keepdims=True)


def fetch(done, pairs):
    copies = [
        pltpu.make_async_copy(source, target, done.at[k])
        for k, (source, target) in enumerate(pairs)
    ]
    for copy in copies:
        copy.start()
    return copies


def start_kernel(
    disp_in, stress_in, thickness_in, from_in, to_in, stiff_in,
    payload, sec_first, sec_second, girth_first, girth_second,
    column_marks, row_marks, picked, spring,
    disp, stress_left, stress_right, stress_top, stress_bottom, thickness,
    weld_from, weld_to, weld_stiff, done,
):
    rows, cols = thickness.shape
    _, slots, devices = weld_from.shape
    sec_pair, girth_pair = (sec_first, sec_second), (girth_first, girth_second)
    copies = fetch(
        done,
        [
            (from_in, weld_from),
            (to_in, weld_to),
            (stiff_in, weld_stiff),
            (disp_in, disp),
            (thickness_in, thickness),
            (stress_in.at[:, :, 0:LANES], stress_left),
            (stress_in.at[:, :, cols - LANES : cols], stress_right),
            (stress_in.at[:, 0:8, :], stress_top),
            (stress_in.at[:, rows - 8 : rows, :], stress_bottom),
        ],
    )
    shift = cols.bit_length() - 1
    by_device, by_place = slot_marks(devices, slots)
    for copy in copies[:3]:
        copy.wait()
    near, far = weld_from[0], weld_to[0]
    stiff = jnp.where(near >= 0, weld_stiff[0], 0.0)
    index_parts = []
    for index in (near, far):
        index = jnp.maximum(index, 0)
        column = index & (cols - 1)
        index_parts += [index >> shift, column >> 1, column & 1]
    index_parts = [part.astype(F32).astype(BF16) for part in index_parts]
    index_parts += list(split(stiff))
    wide = [expand(part, by_device, by_place, turned=True) for part in index_parts]
    row_index = jnp.concatenate([wide[0], wide[3]], axis=1)
    column_index = jnp.concatenate([2.0 * wide[1] + wide[2], 2.0 * wide[4] + wide[5]], axis=1)
    stiff_row = wide[6] + wide[7]
    total = row_index.shape[1]
    spring[...] = jnp.broadcast_to(stiff_row, spring.shape)
    row_iota = lax.broadcasted_iota(jnp.int32, (rows, total), 0).astype(F32)
    row_hits = (row_iota == row_index).astype(F32).astype(BF16)
    row_marks[...] = row_hits
    for start in range(0, cols, 64):
        iota = (lax.broadcasted_iota(jnp.int32, (64, total), 0) + start).astype(F32)
        column_marks[start : start + 64, :] = (iota == column_index).astype(F32).astype(BF16)
    copies[3].wait()
    values = pick([disp[f] for f in range(FIELDS)], column_marks[...], row_hits)
    picked[...] = jnp.concatenate(values + [values[0]] * 3, axis=0)
    half = total // 2
    near_out = collapse([value[:, :half] for value in values] + [stiff_row], by_device, by_place)
    far_out = collapse([value[:, half:] for value in values], by_device, by_place)

    for copy in copies[4:]:
        copy.wait()
    plate = thickness[...].astype(F32) * (1.0 / spacing_mm)
    columns = []
    for f in range(RESULTS + 1):
        left = stress_left[f] if f < RESULTS else plate[:, 0:LANES]
        right = stress_right[f] if f < RESULTS else plate[:, cols - LANES :]
        columns.append((left, 0, f // 5, 2 + f % 5))
        columns.append((right, LANES - 1, f // 5, 10 + f % 5))
    send_sides(girth_pair, edge_rows(columns))
    send_joints(payload, near_out, far_out, [])
    send_ends(
        sec_pair,
        [stress_top[f, 0:1, :] for f in range(RESULTS)] + [plate[0:1, :]],
        [stress_bottom[f, 7:8, :] for f in range(RESULTS)] + [plate[rows - 1 : rows, :]],
    )


def fill_halo(ref, f, above, below, sides, corner):
    rows, cols = ref.shape[1] - PAD_ROWS, ref.shape[2] - LANES
    depth = above.shape[0]
    ref[f, rows:, :cols] = jnp.concatenate(
        [below, jnp.zeros((PAD_ROWS - 2 * depth, cols), F32), above], axis=0
    )
    ref[f, :rows, cols:] = sides
    ref[f, rows:, cols:] = corner


def load_velocity(vel_ext, incoming, above, below, left, right):
    first, second = edge_columns(left, right)
    row = lax.broadcasted_iota(jnp.int32, (8, LANES), 0)
    corner_tiles = [
        jnp.broadcast_to(jnp.where(inside, corner_of(incoming, device), 0.0), (8, LANES))
        for device, inside in corner_neighbours()
    ]
    for f in range(FIELDS):
        sides = edge_block(
            [
                (first, 2 + f, LANES - 2),
                (second, 2 + f, LANES - 1),
                (first, 10 + f, 0),
                (second, 10 + f, 1),
            ]
        )
        upper = edge_block([(corner_tiles[0], CORNER_LANE + f, LANES - 1), (corner_tiles[1], CORNER_LANE + f, 0)])
        lower = edge_block([(corner_tiles[2], CORNER_LANE + f, LANES - 1), (corner_tiles[3], CORNER_LANE + f, 0)])
        corner = jnp.where(row == 0, lower, jnp.where(row == 7, upper, 0.0))
        fill_halo(
            vel_ext, f, above[2 * f : 2 * f + 2, :], below[2 * f : 2 * f + 2, :], sides, corner
        )


def load_stress(stress_ext, plate_ext, thickness, above, below, left, right):
    rows, cols = thickness.shape
    halves = edge_columns(left, right)
    plate_ext[0, :rows, :cols] = thickness[...].astype(F32) * (1.0 / spacing_mm)
    empty = jnp.zeros((PAD_ROWS, LANES), F32)
    for f in range(RESULTS + 1):
        lane = 2 + f % 5
        half = halves[f // 5]
        sides = edge_block([(half, lane, LANES - 1), (half, 8 + lane, 0)])
        ref, k = (stress_ext, f) if f < RESULTS else (plate_ext, 0)
        fill_halo(ref, k, above[f : f + 1, :], below[f : f + 1, :], sides, empty)


def step_kernel(first, last, *refs):
    (stress_in, velocity_in, disp_in, thickness_in, pressure_in) = refs[:5]
    if first:
        out = refs[14:]
    else:
        plate_ext = refs[14]
        out = refs[15:]
    (incoming, sec_first, sec_second, girth_first, girth_second,
     column_marks, row_marks, picked, spring) = refs[5:14]
    stress_out, velocity_out, disp_out = out[:3]
    out = out[3:]
    if first:
        plate_ext, spring_out = out[:2]
        out = out[2:]
    girth_pair, sec_pair = out[0:2], out[2:4]
    out = out[4:]
    if not last:
        picked_out, payload = out[:2]
        out = out[2:]
    (stress_ext, res_ext, vel_ext, weld, velocity, disp, thickness, pressure,
     got, sent) = out

    _, rows, cols = velocity.shape
    devices = incoming.shape[0] // 2
    total = picked.shape[1]
    half = total // 2
    by_device, by_place = slot_marks(devices, half // devices)
    inner = (slice(None), slice(0, rows), slice(0, cols))
    copies = fetch(
        got,
        [
            (velocity_in, vel_ext.at[inner] if not first else velocity),
            (stress_in, stress_ext.at[inner] if first else stress_ext),
            (disp_in, disp),
            (pressure_in, pressure),
        ]
        + ([(thickness_in, thickness)] if first else []),
    )
    sends = []

    def send(source, target):
        copy = pltpu.make_async_copy(source, target, sent.at[len(sends)])
        copy.start()
        sends.append(copy)

    other = []
    for row in (1, 0):
        high, low = split(incoming[pl.ds(row, devices, stride=2), :])
        other.append(expand(high, by_device, by_place) + expand(low, by_device, by_place))
    if first:
        stiffness = jnp.concatenate([spring[0:1, :], other[1][5:6]], axis=1)
        spring_out[...] = jnp.broadcast_to(stiffness, spring_out.shape)
    else:
        stiffness = spring[0:1, :]
    field = lax.broadcasted_iota(jnp.int32, (8, total), 0)
    scale = jnp.where(field < 3, 1.0, rotary_share) * stiffness
    pulls = scale * (jnp.concatenate(other, axis=1) - picked[...])
    weld[...] = spread(pulls, column_marks[...], row_marks[...])

    above, below = in_order("sec", sec_first[...], sec_second[...])
    left, right = in_order("girth", girth_first[...], girth_second[...])
    for copy in copies:
        copy.wait()
    if first:
        load_stress(stress_ext, plate_ext, thickness, above, below, left, right)
    else:
        load_velocity(vel_ext, incoming, above, below, left, right)
    for start in range(0, rows + PAD_ROWS, 8):
        plate = plate_ext[0, start : start + 8, :]
        chunk = [stress_ext[k, start : start + 8, :] for k in range(RESULTS)]
        if not first:
            chunk = stress_chunk(vel_ext, chunk, plate, start)
            for k, value in enumerate(chunk):
                stress_ext[k, start : start + 8, :] = value
        for k, value in enumerate(resultants(chunk, plate)):
            res_ext[k, start : start + 8, :] = value
    send(stress_ext, stress_out)

    for start in range(0, rows, 8):
        part = slice(start, start + 8)
        plate = plate_ext[0, part, :cols]
        linear = time_step / plate
        angular = (12.0 * linear) / (1.0 + plate * plate)
        force = force_chunk(res_ext, start, cols)
        force[2] = force[2] + pressure[part, :]
        for f in range(FIELDS):
            joined = force[f] + weld[f * rows + start : f * rows + start + 8, :]
            before = velocity[f, part, :] if first else vel_ext[f, part, :cols]
            speed = before + (linear if f < 3 else angular) * joined
            velocity[f, part, :] = speed
            disp[f, part, :] = disp[f, part, :] + time_step * speed
        if start % 32 == 24:
            done = slice(start - 24, start + 8)
            for source, target in ((velocity, velocity_out), (disp, disp_out)):
                send(source.at[:, done, :], target.at[:, done, :])

    ends = (cols - LANES, cols)
    if last:
        columns = []
        for f in range(FIELDS):
            columns.append((velocity[f, :, 0:LANES], 0, 0, f))
            columns.append((velocity[f, :, ends[0] : ends[1]], LANES - 1, 0, 8 + f))
        send_sides(girth_pair, edge_rows(columns))
        send_ends(
            sec_pair,
            [velocity[f, 0:1, :] for f in range(FIELDS)],
            [velocity[f, rows - 1 : rows, :] for f in range(FIELDS)],
        )
        for copy in sends:
            copy.wait()
        return
    values = pick([disp[f] for f in range(FIELDS)], column_marks[...], row_marks[...])
    picked_out[...] = jnp.concatenate(values + [values[0]] * 3, axis=0)
    near_out = collapse([value[:, :half] for value in values], by_device, by_place)
    far_out = collapse([value[:, half:] for value in values], by_device, by_place)
    columns = []
    for f in range(FIELDS):
        left_lanes = velocity[f, :, 0:LANES]
        right_lanes = velocity[f, :, ends[0] : ends[1]]
        for depth in (0, 1):
            columns.append((left_lanes, depth, depth, 2 + f))
            columns.append((right_lanes, LANES - 2 + depth, depth, 10 + f))
    corners = []
    lane = lax.broadcasted_iota(jnp.int32, (8, LANES), 1)
    for row in (0, rows - 1):
        tile = slice(row // 8 * 8, row // 8 * 8 + 8)
        for side in (0, 1):
            value = jnp.zeros((8, LANES), F32)
            for f in range(FIELDS):
                part = velocity[f, tile, ends[0] : ends[1]] if side else velocity[f, tile, 0:LANES]
                source = LANES - 1 if side else 0
                target = CORNER_LANE + f
                value = jnp.where(lane == target, pltpu.roll(part, (target - source) % LANES, 1), value)
            corners.append(jnp.broadcast_to(value[row % 8 : row % 8 + 1], (8, LANES)))
    send_sides(girth_pair, edge_rows(columns))
    send_joints(payload, near_out, far_out, corners)
    send_ends(
        sec_pair,
        [velocity[f, 0:2, :] for f in range(FIELDS)],
        [velocity[f, rows - 2 : rows, :] for f in range(FIELDS)],
    )
    for copy in sends:
        copy.wait()


def final_kernel(
    stress_in, velocity_in, sec_first, sec_second, girth_first, girth_second, plate_ext, height,
    stress_out, moment, stress, vel_ext, got, sent,
):
    rows, cols = vel_ext.shape[1] - PAD_ROWS, vel_ext.shape[2] - LANES
    inner = (slice(None), slice(0, rows), slice(0, cols))
    copies = fetch(got, [(velocity_in, vel_ext.at[inner]), (stress_in, stress)])
    above, below = in_order("sec", sec_first[...], sec_second[...])
    left, right = in_order("girth", girth_first[...], girth_second[...])
    first, _ = edge_columns(left, right)
    empty = jnp.zeros((PAD_ROWS, LANES), F32)
    for f in range(FIELDS):
        sides = edge_block([(first, f, LANES - 1), (first, 8 + f, 0)])
        fill_halo(vel_ext, f, above[f : f + 1, :], below[f : f + 1, :], sides, empty)
    for copy in copies:
        copy.wait()
    weight = height[0:1, :]
    parts = []
    sends = []
    for start in range(0, rows, 8):
        part = slice(start, start + 8)
        chunk = [stress[k, part, :] for k in range(RESULTS)]
        plate = plate_ext[0, part, :]
        chunk = stress_chunk(vel_ext, chunk, plate, start)
        for k, value in enumerate(chunk):
            stress[k, part, :] = value
        if start % 16 == 8:
            done = slice(start - 8, start + 8)
            copy = pltpu.make_async_copy(
                stress.at[:, done, :cols], stress_out.at[:, done, :], sent.at[len(sends)]
            )
            copy.start()
            sends.append(copy)
        weighted = plate[:, :cols] * chunk[0][:, :cols] * weight
        parts.append(jnp.sum(weighted, axis=1, keepdims=True))
    column = jnp.broadcast_to(jnp.concatenate(parts, axis=0), (rows, LANES))
    if rows < LANES:
        column = jnp.concatenate([column, jnp.zeros((LANES - rows, LANES), F32)], axis=0)
    moment[...] = column.T[0:8, :rows]
    for copy in sends:
        copy.wait()


def call(kernel, vmem_bytes, outs, scratch, *operands, far=0, far_out=0, copies=(1,)):
    operands = [
        pltpu.with_memory_space_constraint(value, pltpu.HBM) if k < far else value
        for k, value in enumerate(operands)
    ]
    whole = pl.BlockSpec(memory_space=pltpu.VMEM)
    away = pl.BlockSpec(memory_space=pltpu.HBM)
    scratch = [pltpu.VMEM(shape, dtype) for shape, dtype in scratch]
    scratch += [pltpu.SemaphoreType.DMA((count,)) for count in copies]
    return pl.pallas_call(
        kernel,
        out_shape=[
            pltpu.HBM(shape, dtype) if k < far_out else jax.ShapeDtypeStruct(shape, dtype)
            for k, (shape, dtype) in enumerate(outs)
        ],
        in_specs=[away] * far + [whole] * (len(operands) - far),
        out_specs=[away] * far_out + [whole] * (len(outs) - far_out),
        scratch_shapes=scratch,
        compiler_params=pltpu.CompilerParams(vmem_limit_bytes=vmem_bytes),
    )(*operands)


def swap(pair, axis, around):
    count = lax.axis_size(axis)
    out = []
    for start, value in enumerate(pair):
        couples = [(i, (i + 1) % count) for i in range(start, count, 2)]
        couples = [(i, j) for i, j in couples if j > i or around]
        out.append(lax.ppermute(value, axis, couples + [(j, i) for i, j in couples]))
    return out


def exchange(joints):
    blocks = joints.reshape(joints.shape[0] // 2, 2, LANES)
    blocks = lax.all_to_all(blocks, ("sec", "girth"), 0, 0, tiled=True)
    return blocks.reshape(joints.shape)


def local(displacement, velocity, stress, thickness, pressure, weld_from, weld_to, weld_stiff):
    rows, cols = thickness.shape
    _, devices, slots = weld_from.shape
    total = 2 * devices * slots
    girth_total = cols * lax.axis_size("girth")
    column = (lax.axis_index("girth") * cols + lax.iota(jnp.int32, cols)).astype(F32)
    height = jnp.sin(2.0 * jnp.pi / girth_total * (column + 0.5)) / girth_total
    height = jnp.broadcast_to(height[None, :], (8, cols))

    vmem_bytes = 8 * 1024 * 1024 + total * VMEM_PER_SLOT
    message = (devices * 2, LANES)
    edge = (8, LANES)
    strip = (16, cols)
    block = (FIELDS, rows, cols)
    stress_shape = (RESULTS, rows + PAD_ROWS, cols + LANES)
    plate_shape = (1, rows + PAD_ROWS, cols + LANES)
    slot_rows = (8, total)
    scratch = [
        (stress_shape, F32),
        (stress_shape, F32),
        ((FIELDS, rows + PAD_ROWS, cols + LANES), F32),
        ((FIELDS * rows, cols), F32),
        (block, F32),
        (block, F32),
        ((rows, cols), jnp.int32),
        ((rows, cols), F32),
    ]

    (payload, sec_first, sec_second, girth_first, girth_second,
     column_marks, row_marks, picked, spring) = call(
        start_kernel,
        vmem_bytes,
        [
            (message, F32), (strip, F32), (strip, F32), (edge, F32), (edge, F32),
            ((cols, total), BF16), ((rows, total), BF16), (slot_rows, F32), ((8, total // 2), F32),
        ],
        [
            (block, F32), ((RESULTS, rows, LANES), F32), ((RESULTS, rows, LANES), F32),
            ((RESULTS, 8, cols), F32), ((RESULTS, 8, cols), F32), ((rows, cols), jnp.int32),
            ((1, slots, devices), jnp.int32), ((1, slots, devices), jnp.int32),
            ((1, slots, devices), F32),
        ],
        displacement, stress, thickness,
        *[jnp.swapaxes(array, 1, 2) for array in (weld_from, weld_to, weld_stiff)],
        far=6,
        copies=(9,),
    )
    plate = None
    for step in range(STEPS):
        first, last = step == 0, step == STEPS - 1
        incoming = exchange(payload)
        ends = swap((sec_first, sec_second), "sec", False)
        sides = swap((girth_first, girth_second), "girth", True)
        outs = [(stress_shape, F32), (block, F32), (block, F32)]
        if first:
            outs += [(plate_shape, F32), (slot_rows, F32)]
        halo = (8, cols) if last else strip
        outs += [(edge, F32), (edge, F32), (halo, F32), (halo, F32)]
        if not last:
            outs += [(slot_rows, F32), (message, F32)]
        results = call(
            functools.partial(step_kernel, first, last),
            vmem_bytes,
            outs,
            scratch,
            stress, velocity, displacement, thickness, pressure,
            incoming, *ends, *sides,
            column_marks, row_marks, picked, spring,
            *([] if first else [plate]),
            far=5,
            far_out=3,
            copies=(5, 1 + 2 * (rows // 32)),
        )
        stress, velocity, displacement = results[:3]
        results = results[3:]
        if first:
            plate, spring = results[:2]
            results = results[2:]
        girth_first, girth_second, sec_first, sec_second = results[:4]
        if not last:
            picked, payload = results[4:]

    ends = swap((sec_first, sec_second), "sec", False)
    sides = swap((girth_first, girth_second), "girth", True)
    stress, partial_moment = call(
        final_kernel,
        vmem_bytes,
        [((RESULTS, rows, cols), F32), ((8, rows), F32)],
        [(stress_shape, F32), ((FIELDS, rows + PAD_ROWS, cols + LANES), F32)],
        stress, velocity, *ends, *sides, plate, height,
        far=2,
        far_out=1,
        copies=(2, rows // 16),
    )
    moment = lax.psum(partial_moment[0], "girth")
    return (displacement, velocity, stress, moment)


def solution(mesh):
    in_specs = (
        P(None, "sec", "girth"),
        P(None, "sec", "girth"),
        P(None, "sec", "girth"),
        P("sec", "girth"),
        P("sec", "girth"),
        P(("sec", "girth"), None, None),
        P(("sec", "girth"), None, None),
        P(("sec", "girth"), None, None),
    )
    out_specs = (
        P(None, "sec", "girth"),
        P(None, "sec", "girth"),
        P(None, "sec", "girth"),
        P("sec"),
    )
    return jax.shard_map(local, mesh=mesh, in_specs=in_specs, out_specs=out_specs, check_vma=False)
```

```python
import functools

import jax
import jax.numpy as jnp
from jax import lax
from jax.experimental import pallas as pl
from jax.experimental.pallas import tpu as pltpu
from jax.sharding import PartitionSpec as P

STEPS = 3
CORNER_LANE = 112
FIELDS = 5
RESULTS = 8
PAD_ROWS = 8
LANES = 128
VMEM_PER_SLOT = 5 * 1024

young_modulus = 4.0
poisson_ratio = 0.3
plate_modulus = young_modulus / (1.0 - poisson_ratio * poisson_ratio)
shear_modulus = young_modulus / (2.0 * (1.0 + poisson_ratio))
shear_factor = 5.0 / 6.0
time_step = 0.2
spacing_mm = 50.0
rotary_share = 1.0 / 12.0

F32 = jnp.float32
BF16 = jnp.bfloat16


def split(values):
    high = values.astype(BF16)
    low = (values - high.astype(F32)).astype(BF16)
    return high, low


def dot(a, b, contract):
    return lax.dot_general(a, b, (contract, ((), ())), preferred_element_type=F32)


def slot_marks(devices, slots):
    total = devices * slots
    lane = lax.broadcasted_iota(jnp.int32, (devices, total), 1)
    device = lax.broadcasted_iota(jnp.int32, (devices, total), 0)
    by_device = (lane // slots == device).astype(F32).astype(BF16)
    lane = lax.broadcasted_iota(jnp.int32, (slots, total), 1)
    place = lax.broadcasted_iota(jnp.int32, (slots, total), 0)
    by_place = (lane % slots == place).astype(F32)
    return by_device, by_place


def expand(blocks, by_device, by_place, turned=False):
    slots, total = by_place.shape
    wide = dot(blocks, by_device, ((1 if turned else 0,), (0,)))
    wide = wide.reshape(wide.shape[0] // slots, slots, total) * by_place[None]
    return jnp.sum(wide, axis=1)


def collapse(rows, by_device, by_place):
    slots, _ = by_place.shape
    marks = by_place.astype(BF16)
    pieces = []
    for part in (0, 1):
        blocks = [split(row)[part] * marks for row in rows]
        blocks += [jnp.zeros_like(marks)] * (LANES // slots - len(rows))
        pieces.append(jnp.concatenate(blocks, axis=0))
    return dot(by_device, pieces[0], ((1,), (1,))) + dot(by_device, pieces[1], ((1,), (1,)))


def pick(fields, column_marks, row_marks):
    rows = fields[0].shape[0]
    parts = [split(field) for field in fields]
    high = jnp.concatenate([part[0] for part in parts], axis=0)
    low = jnp.concatenate([part[1] for part in parts], axis=0)
    by_column = dot(high, column_marks, ((1,), (0,))) + dot(low, column_marks, ((1,), (0,)))
    marks = row_marks.astype(F32)
    return [
        jnp.sum(by_column[rows * f : rows * (f + 1)] * marks, axis=0, keepdims=True)
        for f in range(len(fields))
    ]


def spread(pulls, column_marks, row_marks):
    high, low = split(pulls)
    total = None
    for part in (high, low):
        marked = jnp.concatenate(
            [part[f : f + 1] * row_marks for f in range(FIELDS)], axis=0
        )
        summed = dot(marked, column_marks, ((1,), (1,)))
        total = summed if total is None else total + summed
    return total


def place():
    sec, girth = lax.axis_index("sec"), lax.axis_index("girth")
    return sec, girth, lax.axis_size("sec"), lax.axis_size("girth")


def tile_of(ref, device):
    return ref[pl.ds(pl.multiple_of(device * 8, 8), 8), :]


def set_tile(ref, device, value):
    ref[pl.ds(pl.multiple_of(device * 8, 8), 8), :] = value


def corner_neighbours():
    sec, girth, secs, girths = place()
    me = sec * girths + girth
    out = []
    for step in (-1, 1):
        row = sec + step
        inside = jnp.logical_and(row >= 0, row < secs)
        for turn in (girths - 1, 1):
            device = row * girths + lax.rem(girth + turn, girths)
            out.append((jnp.where(inside, device, me), inside))
    return out


def edge_rows(columns):
    rows = columns[0][0].shape[0]
    lane = lax.broadcasted_iota(jnp.int32, (rows, LANES), 1)
    halves = [jnp.zeros((rows, LANES), F32), jnp.zeros((rows, LANES), F32)]
    for value, source, half, row in columns:
        moved = pltpu.roll(value, (row - source) % LANES, 1)
        halves[half] = jnp.where(lane == row, moved, halves[half])
    return jnp.concatenate(halves, axis=0).T


def edge_columns(left_tile, right_tile):
    stacked = jnp.concatenate(
        [left_tile, right_tile, jnp.zeros((LANES - 16, LANES), F32)], axis=0
    )
    turned = stacked.T
    return turned[: LANES // 2], turned[LANES // 2 :]


def edge_block(pieces):
    rows = pieces[0][0].shape[0]
    lane = lax.broadcasted_iota(jnp.int32, (rows, LANES), 1)
    block = jnp.zeros((rows, LANES), F32)
    for value, source, target in pieces:
        block = jnp.where(lane == target, pltpu.roll(value, (target - source) % LANES, 1), block)
    return block


def row_chunk(ref, f, start):
    count = ref.shape[1]
    if start < 0:
        return jnp.concatenate([ref[f, count + start : count, :], ref[f, 0 : 8 + start, :]], axis=0)
    if start + 8 > count:
        return jnp.concatenate([ref[f, start:count, :], ref[f, 0 : start + 8 - count, :]], axis=0)
    return ref[f, start : start + 8, :]


def difference_x(ref, f, start):
    return row_chunk(ref, f, start + 1) - row_chunk(ref, f, start - 1)


def difference_y(value):
    lanes = value.shape[1]
    return pltpu.roll(value, lanes - 1, 1) - pltpu.roll(value, 1, 1)


def radial_return(xx, yy, xy):
    offset = xx - 0.5 * yy
    square = offset * offset + 0.75 * yy * yy + 3.0 * xy * xy
    scale = lax.rsqrt(jnp.maximum(square, 1.0))
    return xx * scale, yy * scale, xy * scale


def stress_chunk(vel_ref, stress, plate, start):
    current = [vel_ref[f, start : start + 8, :] for f in range(FIELDS)]
    along_x = [difference_x(vel_ref, f, start) for f in range(FIELDS)]
    along_y = [difference_y(value) for value in current]
    normal = 0.5 * time_step * plate_modulus
    skew = 0.5 * time_step * shear_modulus
    arm = 0.5 * plate
    membrane = radial_return(
        stress[0] + normal * (along_x[0] + poisson_ratio * along_y[1]),
        stress[1] + normal * (along_y[1] + poisson_ratio * along_x[0]),
        stress[2] + skew * (along_y[0] + along_x[1]),
    )
    bending = radial_return(
        stress[3] + (normal * arm) * (along_x[3] + poisson_ratio * along_y[4]),
        stress[4] + (normal * arm) * (along_y[4] + poisson_ratio * along_x[3]),
        stress[5] + (skew * arm) * (along_y[3] + along_x[4]),
    )
    shear = (
        stress[6] + skew * (along_x[2] + 2.0 * current[3]),
        stress[7] + skew * (along_y[2] + 2.0 * current[4]),
    )
    return membrane + bending + shear


def resultants(stress, plate):
    arm = plate * plate * (1.0 / 6.0)
    shear = shear_factor * plate
    return (
        [plate * value for value in stress[0:3]]
        + [arm * value for value in stress[3:6]]
        + [shear * value for value in stress[6:8]]
    )


def force_chunk(res_ref, start, cols):
    def both(x, y):
        along_x = difference_x(res_ref, x, start)[:, :cols]
        along_y = difference_y(res_ref[y, start : start + 8, :])[:, :cols]
        return 0.5 * (along_x + along_y)

    return [
        both(0, 2),
        both(2, 1),
        both(6, 7),
        both(3, 5) - res_ref[6, start : start + 8, :cols],
        both(5, 4) - res_ref[7, start : start + 8, :cols],
    ]


def send_joints(payload, near, far, corners):
    devices = payload.shape[0] // 2
    payload[pl.ds(0, devices, stride=2), :] = near
    payload[pl.ds(1, devices, stride=2), :] = far
    row = lax.broadcasted_iota(jnp.int32, (8, LANES), 0)
    lane = lax.broadcasted_iota(jnp.int32, (8, LANES), 1)
    free = jnp.logical_and(lane >= CORNER_LANE, lane < CORNER_LANE + FIELDS)
    for (device, _), corner in zip(corner_neighbours(), corners):
        tile = lax.div(device, 4)
        here = jnp.logical_and(free, row == 2 * lax.rem(device, 4))
        set_tile(payload, tile, jnp.where(here, corner, tile_of(payload, tile)))


def in_order(axis, low, high):
    even = lax.rem(lax.axis_index(axis), 2) == 0
    return jnp.where(even, high, low), jnp.where(even, low, high)


def send_sides(pair, halo_rows):
    for ref, value in zip(pair, in_order("girth", halo_rows[0:8], halo_rows[8:16])):
        ref[...] = value


def send_ends(pair, low, high):
    for ref in pair:
        ref[...] = jnp.zeros(ref.shape, F32)
    start = 0
    for top, bottom in zip(low, high):
        count = top.shape[0]
        for ref, value in zip(pair, in_order("sec", top, bottom)):
            ref[start : start + count, :] = value
        start += count


def corner_of(incoming, device):
    row = lax.broadcasted_iota(jnp.int32, (8, LANES), 0)
    tile = tile_of(incoming, lax.div(device, 4))
    return jnp.sum(jnp.where(row == 2 * lax.rem(device, 4), tile, 0.0), axis=0, keepdims=True)


def fetch(done, pairs):
    copies = [
        pltpu.make_async_copy(source, target, done.at[k])
        for k, (source, target) in enumerate(pairs)
    ]
    for copy in copies:
        copy.start()
    return copies


def start_kernel(
    disp_in, stress_in, thickness_in, from_in, to_in, stiff_in,
    payload, sec_first, sec_second, girth_first, girth_second,
    column_marks, row_marks, picked, spring,
    disp, stress_left, stress_right, stress_top, stress_bottom, thickness,
    weld_from, weld_to, weld_stiff, done,
):
    rows, cols = thickness.shape
    _, slots, devices = weld_from.shape
    sec_pair, girth_pair = (sec_first, sec_second), (girth_first, girth_second)
    copies = fetch(
        done,
        [
            (from_in, weld_from),
            (to_in, weld_to),
            (stiff_in, weld_stiff),
            (disp_in, disp),
            (thickness_in, thickness),
            (stress_in.at[:, :, 0:LANES], stress_left),
            (stress_in.at[:, :, cols - LANES : cols], stress_right),
            (stress_in.at[:, 0:8, :], stress_top),
            (stress_in.at[:, rows - 8 : rows, :], stress_bottom),
        ],
    )
    shift = cols.bit_length() - 1
    by_device, by_place = slot_marks(devices, slots)
    for copy in copies[:3]:
        copy.wait()
    near, far = weld_from[0], weld_to[0]
    stiff = jnp.where(near >= 0, weld_stiff[0], 0.0)
    index_parts = []
    for index in (near, far):
        index = jnp.maximum(index, 0)
        column = index & (cols - 1)
        index_parts += [index >> shift, column >> 1, column & 1]
    index_parts = [part.astype(F32).astype(BF16) for part in index_parts]
    index_parts += list(split(stiff))
    wide = [expand(part, by_device, by_place, turned=True) for part in index_parts]
    row_index = jnp.concatenate([wide[0], wide[3]], axis=1)
    column_index = jnp.concatenate([2.0 * wide[1] + wide[2], 2.0 * wide[4] + wide[5]], axis=1)
    stiff_row = wide[6] + wide[7]
    total = row_index.shape[1]
    spring[...] = jnp.broadcast_to(stiff_row, spring.shape)
    row_iota = lax.broadcasted_iota(jnp.int32, (rows, total), 0).astype(F32)
    row_hits = (row_iota == row_index).astype(F32).astype(BF16)
    row_marks[...] = row_hits
    for start in range(0, cols, 64):
        iota = (lax.broadcasted_iota(jnp.int32, (64, total), 0) + start).astype(F32)
        column_marks[start : start + 64, :] = (iota == column_index).astype(F32).astype(BF16)
    copies[3].wait()
    values = pick([disp[f] for f in range(FIELDS)], column_marks[...], row_hits)
    picked[...] = jnp.concatenate(values + [values[0]] * 3, axis=0)
    half = total // 2
    near_out = collapse([value[:, :half] for value in values] + [stiff_row], by_device, by_place)
    far_out = collapse([value[:, half:] for value in values], by_device, by_place)

    for copy in copies[4:]:
        copy.wait()
    plate = thickness[...].astype(F32) * (1.0 / spacing_mm)
    columns = []
    for f in range(RESULTS + 1):
        left = stress_left[f] if f < RESULTS else plate[:, 0:LANES]
        right = stress_right[f] if f < RESULTS else plate[:, cols - LANES :]
        columns.append((left, 0, f // 5, 2 + f % 5))
        columns.append((right, LANES - 1, f // 5, 10 + f % 5))
    send_sides(girth_pair, edge_rows(columns))
    send_joints(payload, near_out, far_out, [])
    send_ends(
        sec_pair,
        [stress_top[f, 0:1, :] for f in range(RESULTS)] + [plate[0:1, :]],
        [stress_bottom[f, 7:8, :] for f in range(RESULTS)] + [plate[rows - 1 : rows, :]],
    )


def fill_halo(ref, f, above, below, sides, corner):
    rows, cols = ref.shape[1] - PAD_ROWS, ref.shape[2] - LANES
    depth = above.shape[0]
    ref[f, rows:, :cols] = jnp.concatenate(
        [below, jnp.zeros((PAD_ROWS - 2 * depth, cols), F32), above], axis=0
    )
    ref[f, :rows, cols:] = sides
    ref[f, rows:, cols:] = corner


def load_velocity(vel_ext, velocity, incoming, above, below, left, right):
    first, second = edge_columns(left, right)
    row = lax.broadcasted_iota(jnp.int32, (8, LANES), 0)
    corner_tiles = [
        jnp.broadcast_to(jnp.where(inside, corner_of(incoming, device), 0.0), (8, LANES))
        for device, inside in corner_neighbours()
    ]
    for f in range(FIELDS):
        vel_ext[f, : velocity.shape[1], : velocity.shape[2]] = velocity[f]
        sides = edge_block(
            [
                (first, 2 + f, LANES - 2),
                (second, 2 + f, LANES - 1),
                (first, 10 + f, 0),
                (second, 10 + f, 1),
            ]
        )
        upper = edge_block([(corner_tiles[0], CORNER_LANE + f, LANES - 1), (corner_tiles[1], CORNER_LANE + f, 0)])
        lower = edge_block([(corner_tiles[2], CORNER_LANE + f, LANES - 1), (corner_tiles[3], CORNER_LANE + f, 0)])
        corner = jnp.where(row == 0, lower, jnp.where(row == 7, upper, 0.0))
        fill_halo(
            vel_ext, f, above[2 * f : 2 * f + 2, :], below[2 * f : 2 * f + 2, :], sides, corner
        )


def load_stress(stress_ext, plate_ext, thickness, above, below, left, right):
    rows, cols = thickness.shape
    halves = edge_columns(left, right)
    plate_ext[0, :rows, :cols] = thickness[...].astype(F32) * (1.0 / spacing_mm)
    empty = jnp.zeros((PAD_ROWS, LANES), F32)
    for f in range(RESULTS + 1):
        lane = 2 + f % 5
        half = halves[f // 5]
        sides = edge_block([(half, lane, LANES - 1), (half, 8 + lane, 0)])
        ref, k = (stress_ext, f) if f < RESULTS else (plate_ext, 0)
        fill_halo(ref, k, above[f : f + 1, :], below[f : f + 1, :], sides, empty)


def step_kernel(first, last, *refs):
    if first:
        stress_in, velocity_in, disp_in, thickness_in, pressure_in = refs[:5]
        refs = refs[5:]
    else:
        pressure_in, stress_in, velocity_in, disp_in = refs[:4]
        refs = refs[4:]
    (incoming, sec_first, sec_second, girth_first, girth_second,
     column_marks, row_marks, picked, spring) = refs[:9]
    refs = refs[9:]
    if not first:
        plate_ext, refs = refs[0], refs[1:]
    if last:
        velocity_out, disp_out, stress_ext, velocity = refs[:4]
        refs = refs[4:]
    else:
        stress_ext, velocity, disp = refs[:3]
        refs = refs[3:]
    if first:
        plate_ext, spring_out = refs[:2]
        refs = refs[2:]
    girth_pair, sec_pair = refs[0:2], refs[2:4]
    refs = refs[4:]
    if not last:
        picked_out, payload = refs[:2]
        refs = refs[2:]
    res_ext, vel_ext, weld, pressure = refs[:4]
    refs = refs[4:]
    if first:
        thickness, got = refs
    elif last:
        disp, got, sent = refs
    else:
        (got,) = refs

    _, rows, cols = velocity.shape
    devices = incoming.shape[0] // 2
    total = picked.shape[1]
    half = total // 2
    by_device, by_place = slot_marks(devices, half // devices)
    inner = (slice(None), slice(0, rows), slice(0, cols))
    pairs = [(pressure_in, pressure)]
    if first:
        pairs += [
            (stress_in, stress_ext.at[inner]),
            (velocity_in, velocity),
            (disp_in, disp),
            (thickness_in, thickness),
        ]
    copies = fetch(got, pairs)
    sends = []

    other = []
    for row in (1, 0):
        high, low = split(incoming[pl.ds(row, devices, stride=2), :])
        other.append(expand(high, by_device, by_place) + expand(low, by_device, by_place))
    if first:
        stiffness = jnp.concatenate([spring[0:1, :], other[1][5:6]], axis=1)
        spring_out[...] = jnp.broadcast_to(stiffness, spring_out.shape)
    else:
        stiffness = spring[0:1, :]
    field = lax.broadcasted_iota(jnp.int32, (8, total), 0)
    scale = jnp.where(field < 3, 1.0, rotary_share) * stiffness
    pulls = scale * (jnp.concatenate(other, axis=1) - picked[...])
    weld[...] = spread(pulls, column_marks[...], row_marks[...])

    above, below = in_order("sec", sec_first[...], sec_second[...])
    left, right = in_order("girth", girth_first[...], girth_second[...])
    for copy in copies:
        copy.wait()
    if first:
        load_stress(stress_ext, plate_ext, thickness, above, below, left, right)
    else:
        load_velocity(vel_ext, velocity_in, incoming, above, below, left, right)
    for start in range(0, rows + PAD_ROWS, 8):
        plate = plate_ext[0, start : start + 8, :]
        source = stress_ext if first else stress_in
        chunk = [source[k, start : start + 8, :] for k in range(RESULTS)]
        if not first:
            chunk = stress_chunk(vel_ext, chunk, plate, start)
            for k, value in enumerate(chunk):
                stress_ext[k, start : start + 8, :] = value
        for k, value in enumerate(resultants(chunk, plate)):
            res_ext[k, start : start + 8, :] = value

    for start in range(0, rows, 8):
        part = slice(start, start + 8)
        plate = plate_ext[0, part, :cols]
        linear = time_step / plate
        angular = (12.0 * linear) / (1.0 + plate * plate)
        force = force_chunk(res_ext, start, cols)
        force[2] = force[2] + pressure[part, :]
        for f in range(FIELDS):
            joined = force[f] + weld[f * rows + start : f * rows + start + 8, :]
            speed = (velocity if first else velocity_in)[f, part, :]
            speed = speed + (linear if f < 3 else angular) * joined
            velocity[f, part, :] = speed
            moved = (disp if first else disp_in)[f, part, :]
            disp[f, part, :] = moved + time_step * speed
        if last and start % 32 == 24:
            done = slice(start - 24, start + 8)
            for source, target in ((velocity, velocity_out), (disp, disp_out)):
                copy = pltpu.make_async_copy(
                    source.at[:, done, :], target.at[:, done, :], sent.at[len(sends)]
                )
                copy.start()
                sends.append(copy)

    ends = (cols - LANES, cols)
    if last:
        columns = []
        for f in range(FIELDS):
            columns.append((velocity[f, :, 0:LANES], 0, 0, f))
            columns.append((velocity[f, :, ends[0] : ends[1]], LANES - 1, 0, 8 + f))
        send_sides(girth_pair, edge_rows(columns))
        send_ends(
            sec_pair,
            [velocity[f, 0:1, :] for f in range(FIELDS)],
            [velocity[f, rows - 1 : rows, :] for f in range(FIELDS)],
        )
        for copy in sends:
            copy.wait()
        return
    values = pick([disp[f] for f in range(FIELDS)], column_marks[...], row_marks[...])
    picked_out[...] = jnp.concatenate(values + [values[0]] * 3, axis=0)
    near_out = collapse([value[:, :half] for value in values], by_device, by_place)
    far_out = collapse([value[:, half:] for value in values], by_device, by_place)
    columns = []
    for f in range(FIELDS):
        left_lanes = velocity[f, :, 0:LANES]
        right_lanes = velocity[f, :, ends[0] : ends[1]]
        for depth in (0, 1):
            columns.append((left_lanes, depth, depth, 2 + f))
            columns.append((right_lanes, LANES - 2 + depth, depth, 10 + f))
    corners = []
    lane = lax.broadcasted_iota(jnp.int32, (8, LANES), 1)
    for row in (0, rows - 1):
        tile = slice(row // 8 * 8, row // 8 * 8 + 8)
        for side in (0, 1):
            value = jnp.zeros((8, LANES), F32)
            for f in range(FIELDS):
                part = velocity[f, tile, ends[0] : ends[1]] if side else velocity[f, tile, 0:LANES]
                source = LANES - 1 if side else 0
                target = CORNER_LANE + f
                value = jnp.where(lane == target, pltpu.roll(part, (target - source) % LANES, 1), value)
            corners.append(jnp.broadcast_to(value[row % 8 : row % 8 + 1], (8, LANES)))
    send_sides(girth_pair, edge_rows(columns))
    send_joints(payload, near_out, far_out, corners)
    send_ends(
        sec_pair,
        [velocity[f, 0:2, :] for f in range(FIELDS)],
        [velocity[f, rows - 2 : rows, :] for f in range(FIELDS)],
    )


def final_kernel(
    stress, velocity, sec_first, sec_second, girth_first, girth_second, plate_ext, height,
    stress_out, moment, made, vel_ext, sent,
):
    rows, cols = vel_ext.shape[1] - PAD_ROWS, vel_ext.shape[2] - LANES
    above, below = in_order("sec", sec_first[...], sec_second[...])
    left, right = in_order("girth", girth_first[...], girth_second[...])
    first, _ = edge_columns(left, right)
    empty = jnp.zeros((PAD_ROWS, LANES), F32)
    for f in range(FIELDS):
        vel_ext[f, :rows, :cols] = velocity[f]
        sides = edge_block([(first, f, LANES - 1), (first, 8 + f, 0)])
        fill_halo(vel_ext, f, above[f : f + 1, :], below[f : f + 1, :], sides, empty)
    weight = height[0:1, :]
    parts = []
    sends = []
    for start in range(0, rows, 8):
        part = slice(start, start + 8)
        chunk = [stress[k, part, :] for k in range(RESULTS)]
        plate = plate_ext[0, part, :]
        chunk = stress_chunk(vel_ext, chunk, plate, start)
        for k, value in enumerate(chunk):
            made[k, part, :] = value[:, :cols]
        if start % 16 == 8:
            done = slice(start - 8, start + 8)
            copy = pltpu.make_async_copy(
                made.at[:, done, :], stress_out.at[:, done, :], sent.at[len(sends)]
            )
            copy.start()
            sends.append(copy)
        weighted = plate[:, :cols] * chunk[0][:, :cols] * weight
        parts.append(jnp.sum(weighted, axis=1, keepdims=True))
    column = jnp.broadcast_to(jnp.concatenate(parts, axis=0), (rows, LANES))
    if rows < LANES:
        column = jnp.concatenate([column, jnp.zeros((LANES - rows, LANES), F32)], axis=0)
    moment[...] = column.T[0:8, :rows]
    for copy in sends:
        copy.wait()


def call(kernel, vmem_bytes, outs, scratch, *operands, far=0, kept=0, far_out=0, kept_out=0, copies):
    def placed(k, away, here):
        return pltpu.HBM if k < away else pltpu.VMEM if k < away + here else None

    operands = [
        pltpu.with_memory_space_constraint(value, placed(k, far, kept))
        if placed(k, far, kept) is not None
        else value
        for k, value in enumerate(operands)
    ]
    results = [
        (placed(k, far_out, kept_out) or jax.ShapeDtypeStruct)(shape, dtype)
        for k, (shape, dtype) in enumerate(outs)
    ]
    whole = pl.BlockSpec(memory_space=pltpu.VMEM)
    away = pl.BlockSpec(memory_space=pltpu.HBM)
    scratch = [pltpu.VMEM(shape, dtype) for shape, dtype in scratch]
    scratch += [pltpu.SemaphoreType.DMA((count,)) for count in copies]
    return pl.pallas_call(
        kernel,
        out_shape=results,
        in_specs=[away] * far + [whole] * (len(operands) - far),
        out_specs=[away] * far_out + [whole] * (len(outs) - far_out),
        scratch_shapes=scratch,
        compiler_params=pltpu.CompilerParams(vmem_limit_bytes=vmem_bytes),
    )(*operands)


def swap(pair, axis, around):
    count = lax.axis_size(axis)
    out = []
    for start, value in enumerate(pair):
        couples = [(i, (i + 1) % count) for i in range(start, count, 2)]
        couples = [(i, j) for i, j in couples if j > i or around]
        out.append(lax.ppermute(value, axis, couples + [(j, i) for i, j in couples]))
    return out


def sum_over(value, axis):
    count = lax.axis_size(axis)
    if count & (count - 1):
        return lax.psum(value, axis)
    parts = [value] + [
        lax.ppermute(value, axis, [(i, i ^ step) for i in range(count)]) for step in range(1, count)
    ]
    while len(parts) > 1:
        parts = [a + b for a, b in zip(parts[0::2], parts[1::2])]
    return parts[0]


def exchange(joints):
    blocks = joints.reshape(joints.shape[0] // 2, 2, LANES)
    blocks = lax.all_to_all(blocks, ("sec", "girth"), 0, 0, tiled=True)
    return blocks.reshape(joints.shape)


def local(displacement, velocity, stress, thickness, pressure, weld_from, weld_to, weld_stiff):
    rows, cols = thickness.shape
    _, devices, slots = weld_from.shape
    total = 2 * devices * slots
    girth_total = cols * lax.axis_size("girth")
    column = (lax.axis_index("girth") * cols + lax.iota(jnp.int32, cols)).astype(F32)
    height = jnp.sin(2.0 * jnp.pi / girth_total * (column + 0.5)) / girth_total
    height = jnp.broadcast_to(height[None, :], (8, cols))

    vmem_bytes = 8 * 1024 * 1024 + total * VMEM_PER_SLOT
    message = (devices * 2, LANES)
    edge = (8, LANES)
    strip = (16, cols)
    block = (FIELDS, rows, cols)
    stress_shape = (RESULTS, rows + PAD_ROWS, cols + LANES)
    plate_shape = (1, rows + PAD_ROWS, cols + LANES)
    slot_rows = (8, total)
    scratch = [
        (stress_shape, F32),
        ((FIELDS, rows + PAD_ROWS, cols + LANES), F32),
        ((FIELDS * rows, cols), F32),
        ((rows, cols), F32),
    ]

    (payload, sec_first, sec_second, girth_first, girth_second,
     column_marks, row_marks, picked, spring) = call(
        start_kernel,
        vmem_bytes,
        [
            (message, F32), (strip, F32), (strip, F32), (edge, F32), (edge, F32),
            ((cols, total), BF16), ((rows, total), BF16), (slot_rows, F32), ((8, total // 2), F32),
        ],
        [
            (block, F32), ((RESULTS, rows, LANES), F32), ((RESULTS, rows, LANES), F32),
            ((RESULTS, 8, cols), F32), ((RESULTS, 8, cols), F32), ((rows, cols), jnp.int32),
            ((1, slots, devices), jnp.int32), ((1, slots, devices), jnp.int32),
            ((1, slots, devices), F32),
        ],
        displacement, stress, thickness,
        *[jnp.swapaxes(array, 1, 2) for array in (weld_from, weld_to, weld_stiff)],
        far=6,
        copies=(9,),
    )
    plate = None
    for step in range(STEPS):
        first, last = step == 0, step == STEPS - 1
        incoming = exchange(payload)
        ends = swap((sec_first, sec_second), "sec", False)
        sides = swap((girth_first, girth_second), "girth", True)
        outs = [(stress_shape, F32), (block, F32)] + [(block, F32)] * (not last)
        if first:
            outs += [(plate_shape, F32), (slot_rows, F32)]
        if last:
            outs = [(block, F32), (block, F32)] + outs
        halo = (8, cols) if last else strip
        outs += [(edge, F32), (edge, F32), (halo, F32), (halo, F32)]
        if not last:
            outs += [(slot_rows, F32), (message, F32)]
        state = [stress, velocity, displacement]
        own = [((rows, cols), jnp.int32)] if first else [(block, F32)] if last else []
        results = call(
            functools.partial(step_kernel, first, last),
            vmem_bytes,
            outs,
            scratch + own,
            *(state + [thickness, pressure] if first else [pressure] + state),
            incoming, *ends, *sides,
            column_marks, row_marks, picked, spring,
            *([] if first else [plate]),
            far=5 if first else 1,
            kept=0 if first else 3,
            far_out=2 if last else 0,
            kept_out=2 if last else 3,
            copies=(5, 2 * (rows // 32)) if last else (5,),
        )
        if last:
            velocity_out, displacement, stress, velocity = results[:4]
            results = results[4:]
        else:
            stress, velocity, displacement = results[:3]
            results = results[3:]
        if first:
            plate, spring = results[:2]
            results = results[2:]
        girth_first, girth_second, sec_first, sec_second = results[:4]
        if not last:
            picked, payload = results[4:]

    ends = swap((sec_first, sec_second), "sec", False)
    sides = swap((girth_first, girth_second), "girth", True)
    stress, partial_moment = call(
        final_kernel,
        vmem_bytes,
        [((RESULTS, rows, cols), F32), ((8, rows), F32)],
        [((RESULTS, rows, cols), F32), ((FIELDS, rows + PAD_ROWS, cols + LANES), F32)],
        stress, velocity, *ends, *sides, plate, height,
        kept=2,
        far_out=1,
        copies=(rows // 16,),
    )
    moment = sum_over(partial_moment, "girth")[0]
    return (displacement, velocity_out, stress, moment)


def solution(mesh):
    in_specs = (
        P(None, "sec", "girth"),
        P(None, "sec", "girth"),
        P(None, "sec", "girth"),
        P("sec", "girth"),
        P("sec", "girth"),
        P(("sec", "girth"), None, None),
        P(("sec", "girth"), None, None),
        P(("sec", "girth"), None, None),
    )
    out_specs = (
        P(None, "sec", "girth"),
        P(None, "sec", "girth"),
        P(None, "sec", "girth"),
        P("sec"),
    )
    return jax.shard_map(local, mesh=mesh, in_specs=in_specs, out_specs=out_specs, check_vma=False)
```

```python
import functools

import jax
import jax.numpy as jnp
from jax import lax
from jax.experimental import pallas as pl
from jax.experimental.pallas import tpu as pltpu
from jax.sharding import PartitionSpec as P

STEPS = 3
CORNER_LANE = 112
PIECE = 24
FIELDS = 5
RESULTS = 8
PAD_ROWS = 8
LANES = 128
VMEM_PER_SLOT = 5 * 1024

young_modulus = 4.0
poisson_ratio = 0.3
plate_modulus = young_modulus / (1.0 - poisson_ratio * poisson_ratio)
shear_modulus = young_modulus / (2.0 * (1.0 + poisson_ratio))
shear_factor = 5.0 / 6.0
time_step = 0.2
spacing_mm = 50.0
rotary_share = 1.0 / 12.0

F32 = jnp.float32
BF16 = jnp.bfloat16


def split(values):
    high = values.astype(BF16)
    low = (values - high.astype(F32)).astype(BF16)
    return high, low


def dot(a, b, contract):
    return lax.dot_general(a, b, (contract, ((), ())), preferred_element_type=F32)


def slot_marks(devices, slots):
    total = devices * slots
    lane = lax.broadcasted_iota(jnp.int32, (devices, total), 1)
    device = lax.broadcasted_iota(jnp.int32, (devices, total), 0)
    by_device = (lane // slots == device).astype(F32).astype(BF16)
    lane = lax.broadcasted_iota(jnp.int32, (slots, total), 1)
    place = lax.broadcasted_iota(jnp.int32, (slots, total), 0)
    by_place = (lane % slots == place).astype(F32)
    return by_device, by_place


def expand(blocks, by_device, by_place, turned=False):
    slots, total = by_place.shape
    wide = dot(blocks, by_device, ((1 if turned else 0,), (0,)))
    wide = wide.reshape(wide.shape[0] // slots, slots, total) * by_place[None]
    return jnp.sum(wide, axis=1)


def collapse(rows, by_device, by_place):
    slots, _ = by_place.shape
    marks = by_place.astype(BF16)
    pieces = []
    for part in (0, 1):
        blocks = [split(row)[part] * marks for row in rows]
        blocks += [jnp.zeros_like(marks)] * (LANES // slots - len(rows))
        pieces.append(jnp.concatenate(blocks, axis=0))
    return dot(by_device, pieces[0], ((1,), (1,))) + dot(by_device, pieces[1], ((1,), (1,)))


def pick(fields, column_marks, row_marks):
    rows = fields[0].shape[0]
    parts = [split(field) for field in fields]
    high = jnp.concatenate([part[0] for part in parts], axis=0)
    low = jnp.concatenate([part[1] for part in parts], axis=0)
    by_column = dot(high, column_marks, ((1,), (0,))) + dot(low, column_marks, ((1,), (0,)))
    marks = row_marks.astype(F32)
    return [
        jnp.sum(by_column[rows * f : rows * (f + 1)] * marks, axis=0, keepdims=True)
        for f in range(len(fields))
    ]


def spread(pulls, column_marks, row_marks):
    high, low = split(pulls)
    total = None
    for part in (high, low):
        marked = jnp.concatenate(
            [part[f : f + 1] * row_marks for f in range(FIELDS)], axis=0
        )
        summed = dot(marked, column_marks, ((1,), (1,)))
        total = summed if total is None else total + summed
    return total


def place():
    sec, girth = lax.axis_index("sec"), lax.axis_index("girth")
    return sec, girth, lax.axis_size("sec"), lax.axis_size("girth")


def tile_of(ref, device):
    return ref[pl.ds(pl.multiple_of(device * 8, 8), 8), :]


def set_tile(ref, device, value):
    ref[pl.ds(pl.multiple_of(device * 8, 8), 8), :] = value


def corner_neighbours():
    sec, girth, secs, girths = place()
    me = sec * girths + girth
    out = []
    for step in (-1, 1):
        row = sec + step
        inside = jnp.logical_and(row >= 0, row < secs)
        for turn in (girths - 1, 1):
            device = row * girths + lax.rem(girth + turn, girths)
            out.append((jnp.where(inside, device, me), inside))
    return out


def edge_rows(columns):
    rows = columns[0][0].shape[0]
    lane = lax.broadcasted_iota(jnp.int32, (rows, LANES), 1)
    halves = [jnp.zeros((rows, LANES), F32), jnp.zeros((rows, LANES), F32)]
    for value, source, half, row in columns:
        moved = pltpu.roll(value, (row - source) % LANES, 1)
        halves[half] = jnp.where(lane == row, moved, halves[half])
    return jnp.concatenate(halves, axis=0).T


def edge_columns(left_tile, right_tile):
    stacked = jnp.concatenate(
        [left_tile, right_tile, jnp.zeros((LANES - 16, LANES), F32)], axis=0
    )
    turned = stacked.T
    return turned[: LANES // 2], turned[LANES // 2 :]


def edge_block(pieces):
    rows = pieces[0][0].shape[0]
    lane = lax.broadcasted_iota(jnp.int32, (rows, LANES), 1)
    block = jnp.zeros((rows, LANES), F32)
    for value, source, target in pieces:
        block = jnp.where(lane == target, pltpu.roll(value, (target - source) % LANES, 1), block)
    return block


def row_chunk(ref, f, start):
    count = ref.shape[1]
    if start < 0:
        return jnp.concatenate([ref[f, count + start : count, :], ref[f, 0 : 8 + start, :]], axis=0)
    if start + 8 > count:
        return jnp.concatenate([ref[f, start:count, :], ref[f, 0 : start + 8 - count, :]], axis=0)
    return ref[f, start : start + 8, :]


def difference_x(ref, f, start):
    return row_chunk(ref, f, start + 1) - row_chunk(ref, f, start - 1)


def difference_y(value):
    lanes = value.shape[1]
    return pltpu.roll(value, lanes - 1, 1) - pltpu.roll(value, 1, 1)


def radial_return(xx, yy, xy):
    offset = xx - 0.5 * yy
    square = offset * offset + 0.75 * yy * yy + 3.0 * xy * xy
    scale = lax.rsqrt(jnp.maximum(square, 1.0))
    return xx * scale, yy * scale, xy * scale


def stress_chunk(vel_ref, stress, plate, start):
    current = [vel_ref[f, start : start + 8, :] for f in range(FIELDS)]
    along_x = [difference_x(vel_ref, f, start) for f in range(FIELDS)]
    along_y = [difference_y(value) for value in current]
    normal = 0.5 * time_step * plate_modulus
    skew = 0.5 * time_step * shear_modulus
    arm = 0.5 * plate
    membrane = radial_return(
        stress[0] + normal * (along_x[0] + poisson_ratio * along_y[1]),
        stress[1] + normal * (along_y[1] + poisson_ratio * along_x[0]),
        stress[2] + skew * (along_y[0] + along_x[1]),
    )
    bending = radial_return(
        stress[3] + (normal * arm) * (along_x[3] + poisson_ratio * along_y[4]),
        stress[4] + (normal * arm) * (along_y[4] + poisson_ratio * along_x[3]),
        stress[5] + (skew * arm) * (along_y[3] + along_x[4]),
    )
    shear = (
        stress[6] + skew * (along_x[2] + 2.0 * current[3]),
        stress[7] + skew * (along_y[2] + 2.0 * current[4]),
    )
    return membrane + bending + shear


def resultants(stress, plate):
    arm = plate * plate * (1.0 / 6.0)
    shear = shear_factor * plate
    return (
        [plate * value for value in stress[0:3]]
        + [arm * value for value in stress[3:6]]
        + [shear * value for value in stress[6:8]]
    )


def force_chunk(res_ref, start, cols):
    def both(x, y):
        along_x = difference_x(res_ref, x, start)[:, :cols]
        along_y = difference_y(res_ref[y, start : start + 8, :])[:, :cols]
        return 0.5 * (along_x + along_y)

    return [
        both(0, 2),
        both(2, 1),
        both(6, 7),
        both(3, 5) - res_ref[6, start : start + 8, :cols],
        both(5, 4) - res_ref[7, start : start + 8, :cols],
    ]


def send_joints(payload, near, far, corners):
    devices = payload.shape[0] // 2
    payload[pl.ds(0, devices, stride=2), :] = near
    payload[pl.ds(1, devices, stride=2), :] = far
    row = lax.broadcasted_iota(jnp.int32, (8, LANES), 0)
    lane = lax.broadcasted_iota(jnp.int32, (8, LANES), 1)
    free = jnp.logical_and(lane >= CORNER_LANE, lane < CORNER_LANE + FIELDS)
    for (device, _), corner in zip(corner_neighbours(), corners):
        tile = lax.div(device, 4)
        here = jnp.logical_and(free, row == 2 * lax.rem(device, 4))
        set_tile(payload, tile, jnp.where(here, corner, tile_of(payload, tile)))


def in_order(axis, low, high):
    even = lax.rem(lax.axis_index(axis), 2) == 0
    return jnp.where(even, high, low), jnp.where(even, low, high)


def send_sides(pair, halo_rows):
    for ref, value in zip(pair, in_order("girth", halo_rows[0:8], halo_rows[8:16])):
        ref[...] = value


def send_ends(pair, low, high):
    for ref in pair:
        ref[...] = jnp.zeros(ref.shape, F32)
    start = 0
    for top, bottom in zip(low, high):
        count = top.shape[0]
        for ref, value in zip(pair, in_order("sec", top, bottom)):
            ref[start : start + count, :] = value
        start += count


def corner_of(incoming, device):
    row = lax.broadcasted_iota(jnp.int32, (8, LANES), 0)
    tile = tile_of(incoming, lax.div(device, 4))
    return jnp.sum(jnp.where(row == 2 * lax.rem(device, 4), tile, 0.0), axis=0, keepdims=True)


def fetch(done, pairs):
    copies = [
        pltpu.make_async_copy(source, target, done.at[k])
        for k, (source, target) in enumerate(pairs)
    ]
    for copy in copies:
        copy.start()
    return copies


def pieces(rows):
    return [slice(0, PIECE), slice(PIECE, 2 * PIECE), slice(2 * PIECE, rows)]


def start_kernel(
    disp_in, stress_in, thickness_in, from_in, to_in, stiff_in,
    payload, sec_first, sec_second, girth_first, girth_second,
    column_marks, row_marks, picked, spring,
    disp, stress_left, stress_right, stress_top, stress_bottom, thickness,
    weld_from, weld_to, weld_stiff, done,
):
    rows, cols = thickness.shape
    _, slots, devices = weld_from.shape
    sec_pair, girth_pair = (sec_first, sec_second), (girth_first, girth_second)
    copies = fetch(
        done,
        [
            (from_in, weld_from),
            (to_in, weld_to),
            (stiff_in, weld_stiff),
            (disp_in, disp),
            (thickness_in, thickness),
            (stress_in.at[:, :, 0:LANES], stress_left),
            (stress_in.at[:, :, cols - LANES : cols], stress_right),
            (stress_in.at[:, 0:8, :], stress_top),
            (stress_in.at[:, rows - 8 : rows, :], stress_bottom),
        ],
    )
    shift = cols.bit_length() - 1
    by_device, by_place = slot_marks(devices, slots)
    for copy in copies[:3]:
        copy.wait()
    near, far = weld_from[0], weld_to[0]
    stiff = jnp.where(near >= 0, weld_stiff[0], 0.0)
    index_parts = []
    for index in (near, far):
        index = jnp.maximum(index, 0)
        column = index & (cols - 1)
        index_parts += [index >> shift, column >> 1, column & 1]
    index_parts = [part.astype(F32).astype(BF16) for part in index_parts]
    index_parts += list(split(stiff))
    wide = [expand(part, by_device, by_place, turned=True) for part in index_parts]
    row_index = jnp.concatenate([wide[0], wide[3]], axis=1)
    column_index = jnp.concatenate([2.0 * wide[1] + wide[2], 2.0 * wide[4] + wide[5]], axis=1)
    stiff_row = wide[6] + wide[7]
    total = row_index.shape[1]
    spring[...] = jnp.broadcast_to(stiff_row, spring.shape)
    row_iota = lax.broadcasted_iota(jnp.int32, (rows, total), 0).astype(F32)
    row_hits = (row_iota == row_index).astype(F32).astype(BF16)
    row_marks[...] = row_hits
    for start in range(0, cols, 64):
        iota = (lax.broadcasted_iota(jnp.int32, (64, total), 0) + start).astype(F32)
        column_marks[start : start + 64, :] = (iota == column_index).astype(F32).astype(BF16)
    copies[3].wait()
    values = pick([disp[f] for f in range(FIELDS)], column_marks[...], row_hits)
    picked[...] = jnp.concatenate(values + [values[0]] * 3, axis=0)
    half = total // 2
    near_out = collapse([value[:, :half] for value in values] + [stiff_row], by_device, by_place)
    far_out = collapse([value[:, half:] for value in values], by_device, by_place)

    for copy in copies[4:]:
        copy.wait()
    plate = thickness[...].astype(F32) * (1.0 / spacing_mm)
    columns = []
    for f in range(RESULTS + 1):
        left = stress_left[f] if f < RESULTS else plate[:, 0:LANES]
        right = stress_right[f] if f < RESULTS else plate[:, cols - LANES :]
        columns.append((left, 0, f // 5, 2 + f % 5))
        columns.append((right, LANES - 1, f // 5, 10 + f % 5))
    send_sides(girth_pair, edge_rows(columns))
    send_joints(payload, near_out, far_out, [])
    send_ends(
        sec_pair,
        [stress_top[f, 0:1, :] for f in range(RESULTS)] + [plate[0:1, :]],
        [stress_bottom[f, 7:8, :] for f in range(RESULTS)] + [plate[rows - 1 : rows, :]],
    )


def fill_halo(ref, f, above, below, sides, corner):
    rows, cols = ref.shape[1] - PAD_ROWS, ref.shape[2] - LANES
    depth = above.shape[0]
    ref[f, rows:, :cols] = jnp.concatenate(
        [below, jnp.zeros((PAD_ROWS - 2 * depth, cols), F32), above], axis=0
    )
    ref[f, :rows, cols:] = sides
    ref[f, rows:, cols:] = corner


def load_velocity(vel_ext, incoming, above, below, left, right):
    first, second = edge_columns(left, right)
    row = lax.broadcasted_iota(jnp.int32, (8, LANES), 0)
    corner_tiles = [
        jnp.broadcast_to(jnp.where(inside, corner_of(incoming, device), 0.0), (8, LANES))
        for device, inside in corner_neighbours()
    ]
    for f in range(FIELDS):
        sides = edge_block(
            [
                (first, 2 + f, LANES - 2),
                (second, 2 + f, LANES - 1),
                (first, 10 + f, 0),
                (second, 10 + f, 1),
            ]
        )
        upper = edge_block([(corner_tiles[0], CORNER_LANE + f, LANES - 1), (corner_tiles[1], CORNER_LANE + f, 0)])
        lower = edge_block([(corner_tiles[2], CORNER_LANE + f, LANES - 1), (corner_tiles[3], CORNER_LANE + f, 0)])
        corner = jnp.where(row == 0, lower, jnp.where(row == 7, upper, 0.0))
        fill_halo(
            vel_ext, f, above[2 * f : 2 * f + 2, :], below[2 * f : 2 * f + 2, :], sides, corner
        )


def load_stress(stress_ext, plate_ext, thickness, above, below, left, right):
    rows, cols = thickness.shape
    halves = edge_columns(left, right)
    plate_ext[0, :rows, :cols] = thickness[...].astype(F32) * (1.0 / spacing_mm)
    empty = jnp.zeros((PAD_ROWS, LANES), F32)
    for f in range(RESULTS + 1):
        lane = 2 + f % 5
        half = halves[f // 5]
        sides = edge_block([(half, lane, LANES - 1), (half, 8 + lane, 0)])
        ref, k = (stress_ext, f) if f < RESULTS else (plate_ext, 0)
        fill_halo(ref, k, above[f : f + 1, :], below[f : f + 1, :], sides, empty)


def step_kernel(first, last, *refs):
    (stress_in, velocity_in, disp_in, thickness_in, pressure_in) = refs[:5]
    if first:
        out = refs[14:]
    else:
        plate_ext = refs[14]
        out = refs[15:]
    (incoming, sec_first, sec_second, girth_first, girth_second,
     column_marks, row_marks, picked, spring) = refs[5:14]
    stress_out, velocity_out, disp_out = out[:3]
    out = out[3:]
    if first:
        plate_ext, spring_out = out[:2]
        out = out[2:]
    girth_pair, sec_pair = out[0:2], out[2:4]
    out = out[4:]
    if not last:
        picked_out, payload = out[:2]
        out = out[2:]
    (stress_ext, res_ext, vel_ext, weld, velocity, disp, thickness, pressure,
     got, sent) = out

    _, rows, cols = velocity.shape
    devices = incoming.shape[0] // 2
    total = picked.shape[1]
    half = total // 2
    by_device, by_place = slot_marks(devices, half // devices)
    if first:
        pairs = [(thickness_in, thickness)]
        pairs += [
            (stress_in.at[:, part, :], stress_ext.at[:, part, 0:cols]) for part in pieces(rows)
        ]
        pairs += [(velocity_in, velocity)]
    else:
        pairs = [(velocity_in, vel_ext.at[:, 0:rows, 0:cols])]
        pairs += [
            (stress_in.at[:, part, :], stress_ext.at[:, part, :])
            for part in pieces(rows + PAD_ROWS)
        ]
    pairs += [(disp_in, disp), (pressure_in, pressure)]
    copies = fetch(got, pairs)
    sends = []

    def send(source, target):
        copy = pltpu.make_async_copy(source, target, sent.at[len(sends)])
        copy.start()
        sends.append(copy)

    other = []
    for row in (1, 0):
        high, low = split(incoming[pl.ds(row, devices, stride=2), :])
        other.append(expand(high, by_device, by_place) + expand(low, by_device, by_place))
    if first:
        stiffness = jnp.concatenate([spring[0:1, :], other[1][5:6]], axis=1)
        spring_out[...] = jnp.broadcast_to(stiffness, spring_out.shape)
    else:
        stiffness = spring[0:1, :]
    field = lax.broadcasted_iota(jnp.int32, (8, total), 0)
    scale = jnp.where(field < 3, 1.0, rotary_share) * stiffness
    pulls = scale * (jnp.concatenate(other, axis=1) - picked[...])
    weld[...] = spread(pulls, column_marks[...], row_marks[...])

    above, below = in_order("sec", sec_first[...], sec_second[...])
    left, right = in_order("girth", girth_first[...], girth_second[...])
    copies[0].wait()
    if first:
        load_stress(stress_ext, plate_ext, thickness, above, below, left, right)
    else:
        load_velocity(vel_ext, incoming, above, below, left, right)
    for start in range(0, rows + PAD_ROWS, 8):
        if start in (0, PIECE, 2 * PIECE):
            copies[1 + start // PIECE].wait()
        plate = plate_ext[0, start : start + 8, :]
        chunk = [stress_ext[k, start : start + 8, :] for k in range(RESULTS)]
        if not first:
            chunk = stress_chunk(vel_ext, chunk, plate, start)
            for k, value in enumerate(chunk):
                stress_ext[k, start : start + 8, :] = value
        for k, value in enumerate(resultants(chunk, plate)):
            res_ext[k, start : start + 8, :] = value
        for part in pieces(rows + PAD_ROWS):
            if part.stop == start + 8:
                send(stress_ext.at[:, part, :], stress_out.at[:, part, :])
    for copy in copies[4:]:
        copy.wait()

    for start in range(0, rows, 8):
        part = slice(start, start + 8)
        plate = plate_ext[0, part, :cols]
        linear = time_step / plate
        angular = (12.0 * linear) / (1.0 + plate * plate)
        force = force_chunk(res_ext, start, cols)
        force[2] = force[2] + pressure[part, :]
        for f in range(FIELDS):
            joined = force[f] + weld[f * rows + start : f * rows + start + 8, :]
            before = velocity[f, part, :] if first else vel_ext[f, part, :cols]
            speed = before + (linear if f < 3 else angular) * joined
            velocity[f, part, :] = speed
            disp[f, part, :] = disp[f, part, :] + time_step * speed
        if start % 32 == 24:
            done = slice(start - 24, start + 8)
            for source, target in ((velocity, velocity_out), (disp, disp_out)):
                send(source.at[:, done, :], target.at[:, done, :])

    ends = (cols - LANES, cols)
    if last:
        columns = []
        for f in range(FIELDS):
            columns.append((velocity[f, :, 0:LANES], 0, 0, f))
            columns.append((velocity[f, :, ends[0] : ends[1]], LANES - 1, 0, 8 + f))
        send_sides(girth_pair, edge_rows(columns))
        send_ends(
            sec_pair,
            [velocity[f, 0:1, :] for f in range(FIELDS)],
            [velocity[f, rows - 1 : rows, :] for f in range(FIELDS)],
        )
        for copy in sends:
            copy.wait()
        return
    values = pick([disp[f] for f in range(FIELDS)], column_marks[...], row_marks[...])
    picked_out[...] = jnp.concatenate(values + [values[0]] * 3, axis=0)
    near_out = collapse([value[:, :half] for value in values], by_device, by_place)
    far_out = collapse([value[:, half:] for value in values], by_device, by_place)
    columns = []
    for f in range(FIELDS):
        left_lanes = velocity[f, :, 0:LANES]
        right_lanes = velocity[f, :, ends[0] : ends[1]]
        for depth in (0, 1):
            columns.append((left_lanes, depth, depth, 2 + f))
            columns.append((right_lanes, LANES - 2 + depth, depth, 10 + f))
    corners = []
    lane = lax.broadcasted_iota(jnp.int32, (8, LANES), 1)
    for row in (0, rows - 1):
        tile = slice(row // 8 * 8, row // 8 * 8 + 8)
        for side in (0, 1):
            value = jnp.zeros((8, LANES), F32)
            for f in range(FIELDS):
                part = velocity[f, tile, ends[0] : ends[1]] if side else velocity[f, tile, 0:LANES]
                source = LANES - 1 if side else 0
                target = CORNER_LANE + f
                value = jnp.where(lane == target, pltpu.roll(part, (target - source) % LANES, 1), value)
            corners.append(jnp.broadcast_to(value[row % 8 : row % 8 + 1], (8, LANES)))
    send_sides(girth_pair, edge_rows(columns))
    send_joints(payload, near_out, far_out, corners)
    send_ends(
        sec_pair,
        [velocity[f, 0:2, :] for f in range(FIELDS)],
        [velocity[f, rows - 2 : rows, :] for f in range(FIELDS)],
    )
    for copy in sends:
        copy.wait()


def final_kernel(
    stress_in, velocity_in, sec_first, sec_second, girth_first, girth_second, plate_ext, height,
    stress_out, moment, stress, vel_ext, got, sent,
):
    rows, cols = vel_ext.shape[1] - PAD_ROWS, vel_ext.shape[2] - LANES
    pairs = [(velocity_in, vel_ext.at[:, 0:rows, 0:cols])]
    pairs += [(stress_in.at[:, part, :], stress.at[:, part, :]) for part in pieces(rows)]
    copies = fetch(got, pairs)
    above, below = in_order("sec", sec_first[...], sec_second[...])
    left, right = in_order("girth", girth_first[...], girth_second[...])
    first, _ = edge_columns(left, right)
    empty = jnp.zeros((PAD_ROWS, LANES), F32)
    for f in range(FIELDS):
        sides = edge_block([(first, f, LANES - 1), (first, 8 + f, 0)])
        fill_halo(vel_ext, f, above[f : f + 1, :], below[f : f + 1, :], sides, empty)
    copies[0].wait()
    weight = height[0:1, :]
    parts = []
    sends = []
    for start in range(0, rows, 8):
        if start in (0, PIECE, 2 * PIECE):
            copies[1 + start // PIECE].wait()
        part = slice(start, start + 8)
        chunk = [stress[k, part, :] for k in range(RESULTS)]
        plate = plate_ext[0, part, :]
        chunk = stress_chunk(vel_ext, chunk, plate, start)
        for k, value in enumerate(chunk):
            stress[k, part, :] = value
        if start % 16 == 8:
            done = slice(start - 8, start + 8)
            copy = pltpu.make_async_copy(
                stress.at[:, done, :cols], stress_out.at[:, done, :], sent.at[len(sends)]
            )
            copy.start()
            sends.append(copy)
        weighted = plate[:, :cols] * chunk[0][:, :cols] * weight
        parts.append(jnp.sum(weighted, axis=1, keepdims=True))
    column = jnp.broadcast_to(jnp.concatenate(parts, axis=0), (rows, LANES))
    if rows < LANES:
        column = jnp.concatenate([column, jnp.zeros((LANES - rows, LANES), F32)], axis=0)
    moment[...] = column.T[0:8, :rows]
    for copy in sends:
        copy.wait()


def call(kernel, vmem_bytes, outs, scratch, *operands, far=0, far_out=0, copies=(1,)):
    operands = [
        pltpu.with_memory_space_constraint(value, pltpu.HBM) if k < far else value
        for k, value in enumerate(operands)
    ]
    whole = pl.BlockSpec(memory_space=pltpu.VMEM)
    away = pl.BlockSpec(memory_space=pltpu.HBM)
    scratch = [pltpu.VMEM(shape, dtype) for shape, dtype in scratch]
    scratch += [pltpu.SemaphoreType.DMA((count,)) for count in copies]
    return pl.pallas_call(
        kernel,
        out_shape=[
            pltpu.HBM(shape, dtype) if k < far_out else jax.ShapeDtypeStruct(shape, dtype)
            for k, (shape, dtype) in enumerate(outs)
        ],
        in_specs=[away] * far + [whole] * (len(operands) - far),
        out_specs=[away] * far_out + [whole] * (len(outs) - far_out),
        scratch_shapes=scratch,
        compiler_params=pltpu.CompilerParams(vmem_limit_bytes=vmem_bytes),
    )(*operands)


def swap(pair, axis, around):
    count = lax.axis_size(axis)
    out = []
    for start, value in enumerate(pair):
        couples = [(i, (i + 1) % count) for i in range(start, count, 2)]
        couples = [(i, j) for i, j in couples if j > i or around]
        out.append(lax.ppermute(value, axis, couples + [(j, i) for i, j in couples]))
    return out


def sum_over(value, axis):
    count = lax.axis_size(axis)
    if count & (count - 1):
        return lax.psum(value, axis)
    parts = [value] + [
        lax.ppermute(value, axis, [(i, i ^ step) for i in range(count)]) for step in range(1, count)
    ]
    while len(parts) > 1:
        parts = [a + b for a, b in zip(parts[0::2], parts[1::2])]
    return parts[0]


def exchange(joints):
    blocks = joints.reshape(joints.shape[0] // 2, 2, LANES)
    blocks = lax.all_to_all(blocks, ("sec", "girth"), 0, 0, tiled=True)
    return blocks.reshape(joints.shape)


def local(displacement, velocity, stress, thickness, pressure, weld_from, weld_to, weld_stiff):
    rows, cols = thickness.shape
    _, devices, slots = weld_from.shape
    total = 2 * devices * slots
    girth_total = cols * lax.axis_size("girth")
    column = (lax.axis_index("girth") * cols + lax.iota(jnp.int32, cols)).astype(F32)
    height = jnp.sin(2.0 * jnp.pi / girth_total * (column + 0.5)) / girth_total
    height = jnp.broadcast_to(height[None, :], (8, cols))

    vmem_bytes = 8 * 1024 * 1024 + total * VMEM_PER_SLOT
    message = (devices * 2, LANES)
    edge = (8, LANES)
    strip = (16, cols)
    block = (FIELDS, rows, cols)
    stress_shape = (RESULTS, rows + PAD_ROWS, cols + LANES)
    plate_shape = (1, rows + PAD_ROWS, cols + LANES)
    slot_rows = (8, total)
    scratch = [
        (stress_shape, F32),
        (stress_shape, F32),
        ((FIELDS, rows + PAD_ROWS, cols + LANES), F32),
        ((FIELDS * rows, cols), F32),
        (block, F32),
        (block, F32),
        ((rows, cols), jnp.int32),
        ((rows, cols), F32),
    ]

    (payload, sec_first, sec_second, girth_first, girth_second,
     column_marks, row_marks, picked, spring) = call(
        start_kernel,
        vmem_bytes,
        [
            (message, F32), (strip, F32), (strip, F32), (edge, F32), (edge, F32),
            ((cols, total), BF16), ((rows, total), BF16), (slot_rows, F32), ((8, total // 2), F32),
        ],
        [
            (block, F32), ((RESULTS, rows, LANES), F32), ((RESULTS, rows, LANES), F32),
            ((RESULTS, 8, cols), F32), ((RESULTS, 8, cols), F32), ((rows, cols), jnp.int32),
            ((1, slots, devices), jnp.int32), ((1, slots, devices), jnp.int32),
            ((1, slots, devices), F32),
        ],
        displacement, stress, thickness,
        *[jnp.swapaxes(array, 1, 2) for array in (weld_from, weld_to, weld_stiff)],
        far=6,
        copies=(9,),
    )
    plate = None
    for step in range(STEPS):
        first, last = step == 0, step == STEPS - 1
        incoming = exchange(payload)
        ends = swap((sec_first, sec_second), "sec", False)
        sides = swap((girth_first, girth_second), "girth", True)
        outs = [(stress_shape, F32), (block, F32), (block, F32)]
        if first:
            outs += [(plate_shape, F32), (slot_rows, F32)]
        halo = (8, cols) if last else strip
        outs += [(edge, F32), (edge, F32), (halo, F32), (halo, F32)]
        if not last:
            outs += [(slot_rows, F32), (message, F32)]
        results = call(
            functools.partial(step_kernel, first, last),
            vmem_bytes,
            outs,
            scratch,
            stress, velocity, displacement, thickness, pressure,
            incoming, *ends, *sides,
            column_marks, row_marks, picked, spring,
            *([] if first else [plate]),
            far=5,
            far_out=3,
            copies=(7, 3 + 2 * (rows // 32)),
        )
        stress, velocity, displacement = results[:3]
        results = results[3:]
        if first:
            plate, spring = results[:2]
            results = results[2:]
        girth_first, girth_second, sec_first, sec_second = results[:4]
        if not last:
            picked, payload = results[4:]

    ends = swap((sec_first, sec_second), "sec", False)
    sides = swap((girth_first, girth_second), "girth", True)
    stress, partial_moment = call(
        final_kernel,
        vmem_bytes,
        [((RESULTS, rows, cols), F32), ((8, rows), F32)],
        [(stress_shape, F32), ((FIELDS, rows + PAD_ROWS, cols + LANES), F32)],
        stress, velocity, *ends, *sides, plate, height,
        far=2,
        far_out=1,
        copies=(4, rows // 16),
    )
    moment = sum_over(partial_moment, "girth")[0]
    return (displacement, velocity, stress, moment)


def solution(mesh):
    in_specs = (
        P(None, "sec", "girth"),
        P(None, "sec", "girth"),
        P(None, "sec", "girth"),
        P("sec", "girth"),
        P("sec", "girth"),
        P(("sec", "girth"), None, None),
        P(("sec", "girth"), None, None),
        P(("sec", "girth"), None, None),
    )
    out_specs = (
        P(None, "sec", "girth"),
        P(None, "sec", "girth"),
        P(None, "sec", "girth"),
        P("sec"),
    )
    return jax.shard_map(local, mesh=mesh, in_specs=in_specs, out_specs=out_specs, check_vma=False)
```

```python
import functools

import jax
import jax.numpy as jnp
from jax import lax
from jax.experimental import pallas as pl
from jax.experimental.pallas import tpu as pltpu
from jax.sharding import PartitionSpec as P

STEPS = 3
CORNER_LANE = 112
PIECE = 24
FIELDS = 5
RESULTS = 8
PAD_ROWS = 8
LANES = 128
VMEM_PER_SLOT = 5 * 1024

young_modulus = 4.0
poisson_ratio = 0.3
plate_modulus = young_modulus / (1.0 - poisson_ratio * poisson_ratio)
shear_modulus = young_modulus / (2.0 * (1.0 + poisson_ratio))
shear_factor = 5.0 / 6.0
time_step = 0.2
spacing_mm = 50.0
rotary_share = 1.0 / 12.0

F32 = jnp.float32
BF16 = jnp.bfloat16


def split(values):
    high = values.astype(BF16)
    low = (values - high.astype(F32)).astype(BF16)
    return high, low


def dot(a, b, contract):
    return lax.dot_general(a, b, (contract, ((), ())), preferred_element_type=F32)


def slot_marks(devices, slots):
    total = devices * slots
    lane = lax.broadcasted_iota(jnp.int32, (devices, total), 1)
    device = lax.broadcasted_iota(jnp.int32, (devices, total), 0)
    by_device = (lane // slots == device).astype(F32).astype(BF16)
    lane = lax.broadcasted_iota(jnp.int32, (slots, total), 1)
    place = lax.broadcasted_iota(jnp.int32, (slots, total), 0)
    by_place = (lane % slots == place).astype(F32)
    return by_device, by_place


def expand(blocks, by_device, by_place, turned=False):
    slots, total = by_place.shape
    wide = dot(blocks, by_device, ((1 if turned else 0,), (0,)))
    wide = wide.reshape(wide.shape[0] // slots, slots, total) * by_place[None]
    return jnp.sum(wide, axis=1)


def collapse(rows, by_device, by_place):
    slots, _ = by_place.shape
    marks = by_place.astype(BF16)
    pieces = []
    for part in (0, 1):
        blocks = [split(row)[part] * marks for row in rows]
        blocks += [jnp.zeros_like(marks)] * (LANES // slots - len(rows))
        pieces.append(jnp.concatenate(blocks, axis=0))
    return dot(by_device, pieces[0], ((1,), (1,))) + dot(by_device, pieces[1], ((1,), (1,)))


def pick(fields, column_marks, row_marks):
    rows = fields[0].shape[0]
    parts = [split(field) for field in fields]
    high = jnp.concatenate([part[0] for part in parts], axis=0)
    low = jnp.concatenate([part[1] for part in parts], axis=0)
    by_column = dot(high, column_marks, ((1,), (0,))) + dot(low, column_marks, ((1,), (0,)))
    marks = row_marks.astype(F32)
    return [
        jnp.sum(by_column[rows * f : rows * (f + 1)] * marks, axis=0, keepdims=True)
        for f in range(len(fields))
    ]


def spread(pulls, column_marks, row_marks):
    high, low = split(pulls)
    total = None
    for part in (high, low):
        marked = jnp.concatenate(
            [part[f : f + 1] * row_marks for f in range(FIELDS)], axis=0
        )
        summed = dot(marked, column_marks, ((1,), (1,)))
        total = summed if total is None else total + summed
    return total


def place():
    sec, girth = lax.axis_index("sec"), lax.axis_index("girth")
    return sec, girth, lax.axis_size("sec"), lax.axis_size("girth")


def tile_of(ref, device):
    return ref[pl.ds(pl.multiple_of(device * 8, 8), 8), :]


def set_tile(ref, device, value):
    ref[pl.ds(pl.multiple_of(device * 8, 8), 8), :] = value


def corner_neighbours():
    sec, girth, secs, girths = place()
    me = sec * girths + girth
    out = []
    for step in (-1, 1):
        row = sec + step
        inside = jnp.logical_and(row >= 0, row < secs)
        for turn in (girths - 1, 1):
            device = row * girths + lax.rem(girth + turn, girths)
            out.append((jnp.where(inside, device, me), inside))
    return out


def edge_rows(columns):
    rows = columns[0][0].shape[0]
    lane = lax.broadcasted_iota(jnp.int32, (rows, LANES), 1)
    halves = [jnp.zeros((rows, LANES), F32), jnp.zeros((rows, LANES), F32)]
    for value, source, half, row in columns:
        moved = pltpu.roll(value, (row - source) % LANES, 1)
        halves[half] = jnp.where(lane == row, moved, halves[half])
    return jnp.concatenate(halves, axis=0).T


def edge_columns(left_tile, right_tile):
    stacked = jnp.concatenate(
        [left_tile, right_tile, jnp.zeros((LANES - 16, LANES), F32)], axis=0
    )
    turned = stacked.T
    return turned[: LANES // 2], turned[LANES // 2 :]


def edge_block(pieces):
    rows = pieces[0][0].shape[0]
    lane = lax.broadcasted_iota(jnp.int32, (rows, LANES), 1)
    block = jnp.zeros((rows, LANES), F32)
    for value, source, target in pieces:
        block = jnp.where(lane == target, pltpu.roll(value, (target - source) % LANES, 1), block)
    return block


def row_chunk(ref, f, start):
    count = ref.shape[1]
    if start < 0:
        return jnp.concatenate([ref[f, count + start : count, :], ref[f, 0 : 8 + start, :]], axis=0)
    if start + 8 > count:
        return jnp.concatenate([ref[f, start:count, :], ref[f, 0 : start + 8 - count, :]], axis=0)
    return ref[f, start : start + 8, :]


def difference_x(ref, f, start):
    return row_chunk(ref, f, start + 1) - row_chunk(ref, f, start - 1)


def difference_y(value):
    lanes = value.shape[1]
    return pltpu.roll(value, lanes - 1, 1) - pltpu.roll(value, 1, 1)


def radial_return(xx, yy, xy):
    offset = xx - 0.5 * yy
    square = offset * offset + 0.75 * yy * yy + 3.0 * xy * xy
    scale = lax.rsqrt(jnp.maximum(square, 1.0))
    return xx * scale, yy * scale, xy * scale


def stress_chunk(vel_ref, stress, plate, start):
    current = [vel_ref[f, start : start + 8, :] for f in range(FIELDS)]
    along_x = [difference_x(vel_ref, f, start) for f in range(FIELDS)]
    along_y = [difference_y(value) for value in current]
    normal = 0.5 * time_step * plate_modulus
    skew = 0.5 * time_step * shear_modulus
    arm = 0.5 * plate
    membrane = radial_return(
        stress[0] + normal * (along_x[0] + poisson_ratio * along_y[1]),
        stress[1] + normal * (along_y[1] + poisson_ratio * along_x[0]),
        stress[2] + skew * (along_y[0] + along_x[1]),
    )
    bending = radial_return(
        stress[3] + (normal * arm) * (along_x[3] + poisson_ratio * along_y[4]),
        stress[4] + (normal * arm) * (along_y[4] + poisson_ratio * along_x[3]),
        stress[5] + (skew * arm) * (along_y[3] + along_x[4]),
    )
    shear = (
        stress[6] + skew * (along_x[2] + 2.0 * current[3]),
        stress[7] + skew * (along_y[2] + 2.0 * current[4]),
    )
    return membrane + bending + shear


def resultants(stress, plate):
    arm = plate * plate * (1.0 / 6.0)
    shear = shear_factor * plate
    return (
        [plate * value for value in stress[0:3]]
        + [arm * value for value in stress[3:6]]
        + [shear * value for value in stress[6:8]]
    )


def force_chunk(res_ref, start, cols):
    def both(x, y):
        along_x = difference_x(res_ref, x, start)[:, :cols]
        along_y = difference_y(res_ref[y, start : start + 8, :])[:, :cols]
        return 0.5 * (along_x + along_y)

    return [
        both(0, 2),
        both(2, 1),
        both(6, 7),
        both(3, 5) - res_ref[6, start : start + 8, :cols],
        both(5, 4) - res_ref[7, start : start + 8, :cols],
    ]


def send_joints(payload, near, far, corners):
    payload[0] = near
    payload[1] = far
    row = lax.broadcasted_iota(jnp.int32, near.shape, 0)
    lane = lax.broadcasted_iota(jnp.int32, near.shape, 1)
    free = jnp.logical_and(lane >= CORNER_LANE, lane < CORNER_LANE + FIELDS)
    for (device, _), corner in zip(corner_neighbours(), corners):
        here = jnp.logical_and(free, row == device)
        payload[0] = jnp.where(here, corner, payload[0])


def in_order(axis, low, high):
    even = lax.rem(lax.axis_index(axis), 2) == 0
    return jnp.where(even, high, low), jnp.where(even, low, high)


def send_sides(pair, halo_rows):
    for ref, value in zip(pair, in_order("girth", halo_rows[0:8], halo_rows[8:16])):
        ref[...] = value


def send_ends(pair, low, high):
    for ref in pair:
        ref[...] = jnp.zeros(ref.shape, F32)
    start = 0
    for top, bottom in zip(low, high):
        count = top.shape[0]
        for ref, value in zip(pair, in_order("sec", top, bottom)):
            ref[start : start + count, :] = value
        start += count


def corner_of(incoming, device):
    near = incoming[0]
    row = lax.broadcasted_iota(jnp.int32, near.shape, 0)
    return jnp.sum(jnp.where(row == device, near, 0.0), axis=0, keepdims=True)


def fetch(done, pairs):
    copies = [
        pltpu.make_async_copy(source, target, done.at[k])
        for k, (source, target) in enumerate(pairs)
    ]
    for copy in copies:
        copy.start()
    return copies


def pieces(rows):
    return [slice(0, PIECE), slice(PIECE, 2 * PIECE), slice(2 * PIECE, rows)]


def start_kernel(
    disp_in, stress_in, thickness_in, from_in, to_in, stiff_in,
    payload, sec_first, sec_second, girth_first, girth_second,
    column_marks, row_marks, picked, spring,
    disp, stress_left, stress_right, stress_top, stress_bottom, thickness,
    weld_from, weld_to, weld_stiff, done,
):
    rows, cols = thickness.shape
    _, slots, devices = weld_from.shape
    sec_pair, girth_pair = (sec_first, sec_second), (girth_first, girth_second)
    copies = fetch(
        done,
        [
            (from_in, weld_from),
            (to_in, weld_to),
            (stiff_in, weld_stiff),
            (disp_in, disp),
            (thickness_in, thickness),
            (stress_in.at[:, :, 0:LANES], stress_left),
            (stress_in.at[:, :, cols - LANES : cols], stress_right),
            (stress_in.at[:, 0:8, :], stress_top),
            (stress_in.at[:, rows - 8 : rows, :], stress_bottom),
        ],
    )
    shift = cols.bit_length() - 1
    by_device, by_place = slot_marks(devices, slots)
    for copy in copies[:3]:
        copy.wait()
    near, far = weld_from[0], weld_to[0]
    stiff = jnp.where(near >= 0, weld_stiff[0], 0.0)
    index_parts = []
    for index in (near, far):
        index = jnp.maximum(index, 0)
        column = index & (cols - 1)
        index_parts += [index >> shift, column >> 1, column & 1]
    index_parts = [part.astype(F32).astype(BF16) for part in index_parts]
    index_parts += list(split(stiff))
    wide = [expand(part, by_device, by_place, turned=True) for part in index_parts]
    row_index = jnp.concatenate([wide[0], wide[3]], axis=1)
    column_index = jnp.concatenate([2.0 * wide[1] + wide[2], 2.0 * wide[4] + wide[5]], axis=1)
    stiff_row = wide[6] + wide[7]
    total = row_index.shape[1]
    spring[...] = jnp.broadcast_to(stiff_row, spring.shape)
    row_iota = lax.broadcasted_iota(jnp.int32, (rows, total), 0).astype(F32)
    row_hits = (row_iota == row_index).astype(F32).astype(BF16)
    row_marks[...] = row_hits
    for start in range(0, cols, 64):
        iota = (lax.broadcasted_iota(jnp.int32, (64, total), 0) + start).astype(F32)
        column_marks[start : start + 64, :] = (iota == column_index).astype(F32).astype(BF16)
    copies[3].wait()
    values = pick([disp[f] for f in range(FIELDS)], column_marks[...], row_hits)
    picked[...] = jnp.concatenate(values + [values[0]] * 3, axis=0)
    half = total // 2
    near_out = collapse([value[:, :half] for value in values] + [stiff_row], by_device, by_place)
    far_out = collapse([value[:, half:] for value in values], by_device, by_place)

    for copy in copies[4:]:
        copy.wait()
    plate = thickness[...].astype(F32) * (1.0 / spacing_mm)
    columns = []
    for f in range(RESULTS + 1):
        left = stress_left[f] if f < RESULTS else plate[:, 0:LANES]
        right = stress_right[f] if f < RESULTS else plate[:, cols - LANES :]
        columns.append((left, 0, f // 5, 2 + f % 5))
        columns.append((right, LANES - 1, f // 5, 10 + f % 5))
    send_sides(girth_pair, edge_rows(columns))
    send_joints(payload, near_out, far_out, [])
    send_ends(
        sec_pair,
        [stress_top[f, 0:1, :] for f in range(RESULTS)] + [plate[0:1, :]],
        [stress_bottom[f, 7:8, :] for f in range(RESULTS)] + [plate[rows - 1 : rows, :]],
    )


def fill_halo(ref, f, above, below, sides, corner):
    rows, cols = ref.shape[1] - PAD_ROWS, ref.shape[2] - LANES
    depth = above.shape[0]
    ref[f, rows:, :cols] = jnp.concatenate(
        [below, jnp.zeros((PAD_ROWS - 2 * depth, cols), F32), above], axis=0
    )
    ref[f, :rows, cols:] = sides
    ref[f, rows:, cols:] = corner


def load_velocity(vel_ext, incoming, above, below, left, right):
    first, second = edge_columns(left, right)
    row = lax.broadcasted_iota(jnp.int32, (8, LANES), 0)
    corner_tiles = [
        jnp.broadcast_to(jnp.where(inside, corner_of(incoming, device), 0.0), (8, LANES))
        for device, inside in corner_neighbours()
    ]
    for f in range(FIELDS):
        sides = edge_block(
            [
                (first, 2 + f, LANES - 2),
                (second, 2 + f, LANES - 1),
                (first, 10 + f, 0),
                (second, 10 + f, 1),
            ]
        )
        upper = edge_block([(corner_tiles[0], CORNER_LANE + f, LANES - 1), (corner_tiles[1], CORNER_LANE + f, 0)])
        lower = edge_block([(corner_tiles[2], CORNER_LANE + f, LANES - 1), (corner_tiles[3], CORNER_LANE + f, 0)])
        corner = jnp.where(row == 0, lower, jnp.where(row == 7, upper, 0.0))
        fill_halo(
            vel_ext, f, above[2 * f : 2 * f + 2, :], below[2 * f : 2 * f + 2, :], sides, corner
        )


def load_stress(stress_ext, plate_ext, thickness, above, below, left, right):
    rows, cols = thickness.shape
    halves = edge_columns(left, right)
    plate_ext[0, :rows, :cols] = thickness[...].astype(F32) * (1.0 / spacing_mm)
    empty = jnp.zeros((PAD_ROWS, LANES), F32)
    for f in range(RESULTS + 1):
        lane = 2 + f % 5
        half = halves[f // 5]
        sides = edge_block([(half, lane, LANES - 1), (half, 8 + lane, 0)])
        ref, k = (stress_ext, f) if f < RESULTS else (plate_ext, 0)
        fill_halo(ref, k, above[f : f + 1, :], below[f : f + 1, :], sides, empty)


def step_kernel(first, last, *refs):
    (stress_in, velocity_in, disp_in, thickness_in, pressure_in) = refs[:5]
    if first:
        out = refs[14:]
    else:
        plate_ext = refs[14]
        out = refs[15:]
    gathered = refs[5]
    (sec_first, sec_second, girth_first, girth_second,
     column_marks, row_marks, picked, spring) = refs[6:14]
    stress_out, velocity_out, disp_out = out[:3]
    out = out[3:]
    if first:
        plate_ext, spring_out = out[:2]
        out = out[2:]
    girth_pair, sec_pair = out[0:2], out[2:4]
    out = out[4:]
    if not last:
        picked_out, payload = out[:2]
        out = out[2:]
    (stress_ext, res_ext, vel_ext, weld, velocity, disp, thickness, pressure, gathered_tile,
     got, sent) = out

    _, rows, cols = velocity.shape
    devices = gathered.shape[0]
    total = picked.shape[1]
    half = total // 2
    by_device, by_place = slot_marks(devices, half // devices)
    if first:
        pairs = [(thickness_in, thickness)]
        pairs += [
            (stress_in.at[:, part, :], stress_ext.at[:, part, 0:cols]) for part in pieces(rows)
        ]
        pairs += [(velocity_in, velocity)]
    else:
        pairs = [(velocity_in, vel_ext.at[:, 0:rows, 0:cols])]
        pairs += [
            (stress_in.at[:, part, :], stress_ext.at[:, part, :])
            for part in pieces(rows + PAD_ROWS)
        ]
    pairs += [(disp_in, disp), (pressure_in, pressure)]
    sec, girth, _, girths = place()
    me = sec * girths + girth
    tile = pl.ds(pl.multiple_of(lax.div(me, 8) * 8, 8), 8)
    pairs = [(gathered.at[:, :, tile, :], gathered_tile)] + pairs
    message, *copies = fetch(got, pairs)
    message.wait()
    row = lax.broadcasted_iota(jnp.int32, (devices, 8, LANES), 1)
    incoming = [
        jnp.sum(jnp.where(row == lax.rem(me, 8), gathered_tile[:, end], 0.0), axis=1)
        for end in (0, 1)
    ]
    sends = []

    def send(source, target):
        copy = pltpu.make_async_copy(source, target, sent.at[len(sends)])
        copy.start()
        sends.append(copy)

    other = []
    for row in (1, 0):
        high, low = split(incoming[row])
        other.append(expand(high, by_device, by_place) + expand(low, by_device, by_place))
    if first:
        stiffness = jnp.concatenate([spring[0:1, :], other[1][5:6]], axis=1)
        spring_out[...] = jnp.broadcast_to(stiffness, spring_out.shape)
    else:
        stiffness = spring[0:1, :]
    field = lax.broadcasted_iota(jnp.int32, (8, total), 0)
    scale = jnp.where(field < 3, 1.0, rotary_share) * stiffness
    pulls = scale * (jnp.concatenate(other, axis=1) - picked[...])
    weld[...] = spread(pulls, column_marks[...], row_marks[...])

    above, below = in_order("sec", sec_first[...], sec_second[...])
    left, right = in_order("girth", girth_first[...], girth_second[...])
    copies[0].wait()
    if first:
        load_stress(stress_ext, plate_ext, thickness, above, below, left, right)
    else:
        load_velocity(vel_ext, incoming, above, below, left, right)
    for start in range(0, rows + PAD_ROWS, 8):
        if start in (0, PIECE, 2 * PIECE):
            copies[1 + start // PIECE].wait()
        plate = plate_ext[0, start : start + 8, :]
        chunk = [stress_ext[k, start : start + 8, :] for k in range(RESULTS)]
        if not first:
            chunk = stress_chunk(vel_ext, chunk, plate, start)
            for k, value in enumerate(chunk):
                stress_ext[k, start : start + 8, :] = value
        for k, value in enumerate(resultants(chunk, plate)):
            res_ext[k, start : start + 8, :] = value
        for part in pieces(rows + PAD_ROWS):
            if part.stop == start + 8:
                send(stress_ext.at[:, part, :], stress_out.at[:, part, :])
    for copy in copies[4:]:
        copy.wait()

    for start in range(0, rows, 8):
        part = slice(start, start + 8)
        plate = plate_ext[0, part, :cols]
        linear = time_step / plate
        angular = (12.0 * linear) / (1.0 + plate * plate)
        force = force_chunk(res_ext, start, cols)
        force[2] = force[2] + pressure[part, :]
        for f in range(FIELDS):
            joined = force[f] + weld[f * rows + start : f * rows + start + 8, :]
            before = velocity[f, part, :] if first else vel_ext[f, part, :cols]
            speed = before + (linear if f < 3 else angular) * joined
            velocity[f, part, :] = speed
            disp[f, part, :] = disp[f, part, :] + time_step * speed
        if start % 32 == 24:
            done = slice(start - 24, start + 8)
            for source, target in ((velocity, velocity_out), (disp, disp_out)):
                send(source.at[:, done, :], target.at[:, done, :])

    ends = (cols - LANES, cols)
    if last:
        columns = []
        for f in range(FIELDS):
            columns.append((velocity[f, :, 0:LANES], 0, 0, f))
            columns.append((velocity[f, :, ends[0] : ends[1]], LANES - 1, 0, 8 + f))
        send_sides(girth_pair, edge_rows(columns))
        send_ends(
            sec_pair,
            [velocity[f, 0:1, :] for f in range(FIELDS)],
            [velocity[f, rows - 1 : rows, :] for f in range(FIELDS)],
        )
        for copy in sends:
            copy.wait()
        return
    values = pick([disp[f] for f in range(FIELDS)], column_marks[...], row_marks[...])
    picked_out[...] = jnp.concatenate(values + [values[0]] * 3, axis=0)
    near_out = collapse([value[:, :half] for value in values], by_device, by_place)
    far_out = collapse([value[:, half:] for value in values], by_device, by_place)
    columns = []
    for f in range(FIELDS):
        left_lanes = velocity[f, :, 0:LANES]
        right_lanes = velocity[f, :, ends[0] : ends[1]]
        for depth in (0, 1):
            columns.append((left_lanes, depth, depth, 2 + f))
            columns.append((right_lanes, LANES - 2 + depth, depth, 10 + f))
    corners = []
    lane = lax.broadcasted_iota(jnp.int32, (8, LANES), 1)
    for row in (0, rows - 1):
        tile = slice(row // 8 * 8, row // 8 * 8 + 8)
        for side in (0, 1):
            value = jnp.zeros((8, LANES), F32)
            for f in range(FIELDS):
                part = velocity[f, tile, ends[0] : ends[1]] if side else velocity[f, tile, 0:LANES]
                source = LANES - 1 if side else 0
                target = CORNER_LANE + f
                value = jnp.where(lane == target, pltpu.roll(part, (target - source) % LANES, 1), value)
            corners.append(value[row % 8 : row % 8 + 1])
    send_sides(girth_pair, edge_rows(columns))
    send_joints(payload, near_out, far_out, corners)
    send_ends(
        sec_pair,
        [velocity[f, 0:2, :] for f in range(FIELDS)],
        [velocity[f, rows - 2 : rows, :] for f in range(FIELDS)],
    )
    for copy in sends:
        copy.wait()


def final_kernel(
    stress_in, velocity_in, sec_first, sec_second, girth_first, girth_second, plate_ext, height,
    stress_out, moment, stress, vel_ext, got, sent,
):
    rows, cols = vel_ext.shape[1] - PAD_ROWS, vel_ext.shape[2] - LANES
    pairs = [(velocity_in, vel_ext.at[:, 0:rows, 0:cols])]
    pairs += [(stress_in.at[:, part, :], stress.at[:, part, :]) for part in pieces(rows)]
    copies = fetch(got, pairs)
    above, below = in_order("sec", sec_first[...], sec_second[...])
    left, right = in_order("girth", girth_first[...], girth_second[...])
    first, _ = edge_columns(left, right)
    empty = jnp.zeros((PAD_ROWS, LANES), F32)
    for f in range(FIELDS):
        sides = edge_block([(first, f, LANES - 1), (first, 8 + f, 0)])
        fill_halo(vel_ext, f, above[f : f + 1, :], below[f : f + 1, :], sides, empty)
    copies[0].wait()
    weight = height[0:1, :]
    parts = []
    sends = []
    for start in range(0, rows, 8):
        if start in (0, PIECE, 2 * PIECE):
            copies[1 + start // PIECE].wait()
        part = slice(start, start + 8)
        chunk = [stress[k, part, :] for k in range(RESULTS)]
        plate = plate_ext[0, part, :]
        chunk = stress_chunk(vel_ext, chunk, plate, start)
        for k, value in enumerate(chunk):
            stress[k, part, :] = value
        if start % 16 == 8:
            done = slice(start - 8, start + 8)
            copy = pltpu.make_async_copy(
                stress.at[:, done, :cols], stress_out.at[:, done, :], sent.at[len(sends)]
            )
            copy.start()
            sends.append(copy)
        weighted = plate[:, :cols] * chunk[0][:, :cols] * weight
        parts.append(jnp.sum(weighted, axis=1, keepdims=True))
    column = jnp.broadcast_to(jnp.concatenate(parts, axis=0), (rows, LANES))
    if rows < LANES:
        column = jnp.concatenate([column, jnp.zeros((LANES - rows, LANES), F32)], axis=0)
    moment[...] = column.T[0:8, :rows]
    for copy in sends:
        copy.wait()


def call(kernel, vmem_bytes, outs, scratch, *operands, far=0, far_out=0, copies=(1,)):
    operands = [
        pltpu.with_memory_space_constraint(value, pltpu.HBM) if k < far else value
        for k, value in enumerate(operands)
    ]
    whole = pl.BlockSpec(memory_space=pltpu.VMEM)
    away = pl.BlockSpec(memory_space=pltpu.HBM)
    scratch = [pltpu.VMEM(shape, dtype) for shape, dtype in scratch]
    scratch += [pltpu.SemaphoreType.DMA((count,)) for count in copies]
    return pl.pallas_call(
        kernel,
        out_shape=[
            pltpu.HBM(shape, dtype) if k < far_out else jax.ShapeDtypeStruct(shape, dtype)
            for k, (shape, dtype) in enumerate(outs)
        ],
        in_specs=[away] * far + [whole] * (len(operands) - far),
        out_specs=[away] * far_out + [whole] * (len(outs) - far_out),
        scratch_shapes=scratch,
        compiler_params=pltpu.CompilerParams(vmem_limit_bytes=vmem_bytes),
    )(*operands)


def swap(pair, axis, around):
    count = lax.axis_size(axis)
    out = []
    for start, value in enumerate(pair):
        couples = [(i, (i + 1) % count) for i in range(start, count, 2)]
        couples = [(i, j) for i, j in couples if j > i or around]
        out.append(lax.ppermute(value, axis, couples + [(j, i) for i, j in couples]))
    return out


def sum_over(value, axis):
    count = lax.axis_size(axis)
    if count & (count - 1):
        return lax.psum(value, axis)
    parts = [value] + [
        lax.ppermute(value, axis, [(i, i ^ step) for i in range(count)]) for step in range(1, count)
    ]
    while len(parts) > 1:
        parts = [a + b for a, b in zip(parts[0::2], parts[1::2])]
    return parts[0]


def exchange(joints):
    return lax.all_gather(joints, ("sec", "girth"), axis=0)


def local(displacement, velocity, stress, thickness, pressure, weld_from, weld_to, weld_stiff):
    rows, cols = thickness.shape
    _, devices, slots = weld_from.shape
    total = 2 * devices * slots
    girth_total = cols * lax.axis_size("girth")
    column = (lax.axis_index("girth") * cols + lax.iota(jnp.int32, cols)).astype(F32)
    height = jnp.sin(2.0 * jnp.pi / girth_total * (column + 0.5)) / girth_total
    height = jnp.broadcast_to(height[None, :], (8, cols))

    vmem_bytes = 8 * 1024 * 1024 + total * VMEM_PER_SLOT
    message = (2, devices, LANES)
    edge = (8, LANES)
    strip = (16, cols)
    block = (FIELDS, rows, cols)
    stress_shape = (RESULTS, rows + PAD_ROWS, cols + LANES)
    plate_shape = (1, rows + PAD_ROWS, cols + LANES)
    slot_rows = (8, total)
    scratch = [
        (stress_shape, F32),
        (stress_shape, F32),
        ((FIELDS, rows + PAD_ROWS, cols + LANES), F32),
        ((FIELDS * rows, cols), F32),
        (block, F32),
        (block, F32),
        ((rows, cols), jnp.int32),
        ((rows, cols), F32),
        ((devices, 2, 8, LANES), F32),
    ]

    (payload, sec_first, sec_second, girth_first, girth_second,
     column_marks, row_marks, picked, spring) = call(
        start_kernel,
        vmem_bytes,
        [
            (message, F32), (strip, F32), (strip, F32), (edge, F32), (edge, F32),
            ((cols, total), BF16), ((rows, total), BF16), (slot_rows, F32), ((8, total // 2), F32),
        ],
        [
            (block, F32), ((RESULTS, rows, LANES), F32), ((RESULTS, rows, LANES), F32),
            ((RESULTS, 8, cols), F32), ((RESULTS, 8, cols), F32), ((rows, cols), jnp.int32),
            ((1, slots, devices), jnp.int32), ((1, slots, devices), jnp.int32),
            ((1, slots, devices), F32),
        ],
        displacement, stress, thickness,
        *[jnp.swapaxes(array, 1, 2) for array in (weld_from, weld_to, weld_stiff)],
        far=6,
        copies=(9,),
    )
    plate = None
    for step in range(STEPS):
        first, last = step == 0, step == STEPS - 1
        incoming = exchange(payload)
        ends = swap((sec_first, sec_second), "sec", False)
        sides = swap((girth_first, girth_second), "girth", True)
        outs = [(stress_shape, F32), (block, F32), (block, F32)]
        if first:
            outs += [(plate_shape, F32), (slot_rows, F32)]
        halo = (8, cols) if last else strip
        outs += [(edge, F32), (edge, F32), (halo, F32), (halo, F32)]
        if not last:
            outs += [(slot_rows, F32), (message, F32)]
        results = call(
            functools.partial(step_kernel, first, last),
            vmem_bytes,
            outs,
            scratch,
            stress, velocity, displacement, thickness, pressure,
            incoming, *ends, *sides,
            column_marks, row_marks, picked, spring,
            *([] if first else [plate]),
            far=6,
            far_out=3,
            copies=(8, 3 + 2 * (rows // 32)),
        )
        stress, velocity, displacement = results[:3]
        results = results[3:]
        if first:
            plate, spring = results[:2]
            results = results[2:]
        girth_first, girth_second, sec_first, sec_second = results[:4]
        if not last:
            picked, payload = results[4:]

    ends = swap((sec_first, sec_second), "sec", False)
    sides = swap((girth_first, girth_second), "girth", True)
    stress, partial_moment = call(
        final_kernel,
        vmem_bytes,
        [((RESULTS, rows, cols), F32), ((8, rows), F32)],
        [(stress_shape, F32), ((FIELDS, rows + PAD_ROWS, cols + LANES), F32)],
        stress, velocity, *ends, *sides, plate, height,
        far=2,
        far_out=1,
        copies=(4, rows // 16),
    )
    moment = sum_over(partial_moment, "girth")[0]
    return (displacement, velocity, stress, moment)


def solution(mesh):
    in_specs = (
        P(None, "sec", "girth"),
        P(None, "sec", "girth"),
        P(None, "sec", "girth"),
        P("sec", "girth"),
        P("sec", "girth"),
        P(("sec", "girth"), None, None),
        P(("sec", "girth"), None, None),
        P(("sec", "girth"), None, None),
    )
    out_specs = (
        P(None, "sec", "girth"),
        P(None, "sec", "girth"),
        P(None, "sec", "girth"),
        P("sec"),
    )
    return jax.shard_map(local, mesh=mesh, in_specs=in_specs, out_specs=out_specs, check_vma=False)
```

```python
import functools

import jax
import jax.numpy as jnp
from jax import lax
from jax.experimental import pallas as pl
from jax.experimental.pallas import tpu as pltpu
from jax.sharding import PartitionSpec as P

STEPS = 3
CORNER_LANE = 112
PIECE = 24
FIELDS = 5
RESULTS = 8
PAD_ROWS = 8
LANES = 128
VMEM_PER_SLOT = 5 * 1024

young_modulus = 4.0
poisson_ratio = 0.3
plate_modulus = young_modulus / (1.0 - poisson_ratio * poisson_ratio)
shear_modulus = young_modulus / (2.0 * (1.0 + poisson_ratio))
shear_factor = 5.0 / 6.0
time_step = 0.2
spacing_mm = 50.0
rotary_share = 1.0 / 12.0

F32 = jnp.float32
BF16 = jnp.bfloat16


def split(values):
    high = values.astype(BF16)
    low = (values - high.astype(F32)).astype(BF16)
    return high, low


def dot(a, b, contract):
    return lax.dot_general(a, b, (contract, ((), ())), preferred_element_type=F32)


def slot_marks(devices, slots):
    total = devices * slots
    lane = lax.broadcasted_iota(jnp.int32, (devices, total), 1)
    device = lax.broadcasted_iota(jnp.int32, (devices, total), 0)
    by_device = (lane // slots == device).astype(F32).astype(BF16)
    lane = lax.broadcasted_iota(jnp.int32, (slots, total), 1)
    place = lax.broadcasted_iota(jnp.int32, (slots, total), 0)
    by_place = (lane % slots == place).astype(F32)
    return by_device, by_place


def expand(blocks, by_device, by_place, turned=False):
    slots, total = by_place.shape
    wide = dot(blocks, by_device, ((1 if turned else 0,), (0,)))
    wide = wide.reshape(wide.shape[0] // slots, slots, total) * by_place[None]
    return jnp.sum(wide, axis=1)


def collapse(rows, by_device, by_place):
    slots, _ = by_place.shape
    marks = by_place.astype(BF16)
    pieces = []
    for part in (0, 1):
        blocks = [split(row)[part] * marks for row in rows]
        blocks += [jnp.zeros_like(marks)] * (LANES // slots - len(rows))
        pieces.append(jnp.concatenate(blocks, axis=0))
    return dot(by_device, pieces[0], ((1,), (1,))) + dot(by_device, pieces[1], ((1,), (1,)))


def pick(fields, column_marks, row_marks):
    rows = fields[0].shape[0]
    parts = [split(field) for field in fields]
    high = jnp.concatenate([part[0] for part in parts], axis=0)
    low = jnp.concatenate([part[1] for part in parts], axis=0)
    by_column = dot(high, column_marks, ((1,), (0,))) + dot(low, column_marks, ((1,), (0,)))
    marks = row_marks.astype(F32)
    return [
        jnp.sum(by_column[rows * f : rows * (f + 1)] * marks, axis=0, keepdims=True)
        for f in range(len(fields))
    ]


def spread(pulls, column_marks, row_marks):
    high, low = split(pulls)
    total = None
    for part in (high, low):
        marked = jnp.concatenate(
            [part[f : f + 1] * row_marks for f in range(FIELDS)], axis=0
        )
        summed = dot(marked, column_marks, ((1,), (1,)))
        total = summed if total is None else total + summed
    return total


def place():
    sec, girth = lax.axis_index("sec"), lax.axis_index("girth")
    return sec, girth, lax.axis_size("sec"), lax.axis_size("girth")


def tile_of(ref, device):
    return ref[pl.ds(pl.multiple_of(device * 8, 8), 8), :]


def set_tile(ref, device, value):
    ref[pl.ds(pl.multiple_of(device * 8, 8), 8), :] = value


def corner_neighbours():
    sec, girth, secs, girths = place()
    me = sec * girths + girth
    out = []
    for step in (-1, 1):
        row = sec + step
        inside = jnp.logical_and(row >= 0, row < secs)
        for turn in (girths - 1, 1):
            device = row * girths + lax.rem(girth + turn, girths)
            out.append((jnp.where(inside, device, me), inside))
    return out


def edge_rows(columns):
    rows = columns[0][0].shape[0]
    lane = lax.broadcasted_iota(jnp.int32, (rows, LANES), 1)
    halves = [jnp.zeros((rows, LANES), F32), jnp.zeros((rows, LANES), F32)]
    for value, source, half, row in columns:
        moved = pltpu.roll(value, (row - source) % LANES, 1)
        halves[half] = jnp.where(lane == row, moved, halves[half])
    return jnp.concatenate(halves, axis=0).T


def edge_columns(left_tile, right_tile):
    stacked = jnp.concatenate(
        [left_tile, right_tile, jnp.zeros((LANES - 16, LANES), F32)], axis=0
    )
    turned = stacked.T
    return turned[: LANES // 2], turned[LANES // 2 :]


def edge_block(pieces):
    rows = pieces[0][0].shape[0]
    lane = lax.broadcasted_iota(jnp.int32, (rows, LANES), 1)
    block = jnp.zeros((rows, LANES), F32)
    for value, source, target in pieces:
        block = jnp.where(lane == target, pltpu.roll(value, (target - source) % LANES, 1), block)
    return block


def row_chunk(ref, f, start):
    count = ref.shape[1]
    if start < 0:
        return jnp.concatenate([ref[f, count + start : count, :], ref[f, 0 : 8 + start, :]], axis=0)
    if start + 8 > count:
        return jnp.concatenate([ref[f, start:count, :], ref[f, 0 : start + 8 - count, :]], axis=0)
    return ref[f, start : start + 8, :]


def difference_x(ref, f, start):
    return row_chunk(ref, f, start + 1) - row_chunk(ref, f, start - 1)


def difference_y(value):
    lanes = value.shape[1]
    return pltpu.roll(value, lanes - 1, 1) - pltpu.roll(value, 1, 1)


def radial_return(xx, yy, xy):
    offset = xx - 0.5 * yy
    square = offset * offset + 0.75 * yy * yy + 3.0 * xy * xy
    scale = lax.rsqrt(jnp.maximum(square, 1.0))
    return xx * scale, yy * scale, xy * scale


def membrane_chunk(along_x, along_y, stress):
    normal = 0.5 * time_step * plate_modulus
    skew = 0.5 * time_step * shear_modulus
    return radial_return(
        stress[0] + normal * (along_x[0] + poisson_ratio * along_y[1]),
        stress[1] + normal * (along_y[1] + poisson_ratio * along_x[0]),
        stress[2] + skew * (along_y[0] + along_x[1]),
    )


def plate_chunk(along_x, along_y, turns, stress, plate):
    arm = 0.5 * plate
    normal = 0.5 * time_step * plate_modulus * arm
    skew = 0.5 * time_step * shear_modulus
    bending = radial_return(
        stress[0] + normal * (along_x[1] + poisson_ratio * along_y[2]),
        stress[1] + normal * (along_y[2] + poisson_ratio * along_x[1]),
        stress[2] + (skew * arm) * (along_y[1] + along_x[2]),
    )
    return bending + (
        stress[3] + skew * (along_x[0] + 2.0 * turns[0]),
        stress[4] + skew * (along_y[0] + 2.0 * turns[1]),
    )


def differences(vel_ref, fields, start):
    current = [vel_ref[f, start : start + 8, :] for f in fields]
    along_x = [difference_x(vel_ref, f, start) for f in fields]
    return current, along_x, [difference_y(value) for value in current]


def stress_chunk(vel_ref, stress, plate, start):
    current, along_x, along_y = differences(vel_ref, range(FIELDS), start)
    membrane = membrane_chunk(along_x[:2], along_y[:2], stress[:3])
    return membrane + plate_chunk(along_x[2:], along_y[2:], current[3:], stress[3:], plate)


def resultants(stress, plate):
    arm = plate * plate * (1.0 / 6.0)
    shear = shear_factor * plate
    return (
        [plate * value for value in stress[0:3]]
        + [arm * value for value in stress[3:6]]
        + [shear * value for value in stress[6:8]]
    )


def force_chunk(res_ref, start, cols):
    def both(x, y):
        along_x = difference_x(res_ref, x, start)[:, :cols]
        along_y = difference_y(res_ref[y, start : start + 8, :])[:, :cols]
        return 0.5 * (along_x + along_y)

    return [
        both(0, 2),
        both(2, 1),
        both(6, 7),
        both(3, 5) - res_ref[6, start : start + 8, :cols],
        both(5, 4) - res_ref[7, start : start + 8, :cols],
    ]


def send_joints(payload, near, far, corners):
    devices = payload.shape[0] // 2
    payload[pl.ds(0, devices, stride=2), :] = near
    payload[pl.ds(1, devices, stride=2), :] = far
    row = lax.broadcasted_iota(jnp.int32, (8, LANES), 0)
    lane = lax.broadcasted_iota(jnp.int32, (8, LANES), 1)
    free = jnp.logical_and(lane >= CORNER_LANE, lane < CORNER_LANE + FIELDS)
    for (device, _), corner in zip(corner_neighbours(), corners):
        tile = lax.div(device, 4)
        here = jnp.logical_and(free, row == 2 * lax.rem(device, 4))
        set_tile(payload, tile, jnp.where(here, corner, tile_of(payload, tile)))


def in_order(axis, low, high):
    even = lax.rem(lax.axis_index(axis), 2) == 0
    return jnp.where(even, high, low), jnp.where(even, low, high)


def send_sides(pair, halo_rows):
    for ref, value in zip(pair, in_order("girth", halo_rows[0:8], halo_rows[8:16])):
        ref[...] = value


def send_ends(pair, low, high):
    for ref in pair:
        ref[...] = jnp.zeros(ref.shape, F32)
    start = 0
    for top, bottom in zip(low, high):
        count = top.shape[0]
        for ref, value in zip(pair, in_order("sec", top, bottom)):
            ref[start : start + count, :] = value
        start += count


def corner_of(incoming, device):
    row = lax.broadcasted_iota(jnp.int32, (8, LANES), 0)
    tile = tile_of(incoming, lax.div(device, 4))
    return jnp.sum(jnp.where(row == 2 * lax.rem(device, 4), tile, 0.0), axis=0, keepdims=True)


def fetch(done, pairs):
    copies = [
        pltpu.make_async_copy(source, target, done.at[k])
        for k, (source, target) in enumerate(pairs)
    ]
    for copy in copies:
        copy.start()
    return copies


def pieces(rows):
    return [slice(0, PIECE), slice(PIECE, 2 * PIECE), slice(2 * PIECE, rows)]


def start_kernel(
    disp_in, stress_in, thickness_in, from_in, to_in, stiff_in,
    payload, sec_first, sec_second, girth_first, girth_second,
    column_marks, row_marks, picked, spring,
    disp, stress_left, stress_right, stress_top, stress_bottom, thickness,
    weld_from, weld_to, weld_stiff, done,
):
    rows, cols = thickness.shape
    _, slots, devices = weld_from.shape
    sec_pair, girth_pair = (sec_first, sec_second), (girth_first, girth_second)
    copies = fetch(
        done,
        [
            (from_in, weld_from),
            (to_in, weld_to),
            (stiff_in, weld_stiff),
            (disp_in, disp),
            (thickness_in, thickness),
            (stress_in.at[:, :, 0:LANES], stress_left),
            (stress_in.at[:, :, cols - LANES : cols], stress_right),
            (stress_in.at[:, 0:8, :], stress_top),
            (stress_in.at[:, rows - 8 : rows, :], stress_bottom),
        ],
    )
    shift = cols.bit_length() - 1
    by_device, by_place = slot_marks(devices, slots)
    for copy in copies[:3]:
        copy.wait()
    near, far = weld_from[0], weld_to[0]
    stiff = jnp.where(near >= 0, weld_stiff[0], 0.0)
    index_parts = []
    for index in (near, far):
        index = jnp.maximum(index, 0)
        column = index & (cols - 1)
        index_parts += [index >> shift, column >> 1, column & 1]
    index_parts = [part.astype(F32).astype(BF16) for part in index_parts]
    index_parts += list(split(stiff))
    wide = [expand(part, by_device, by_place, turned=True) for part in index_parts]
    row_index = jnp.concatenate([wide[0], wide[3]], axis=1)
    column_index = jnp.concatenate([2.0 * wide[1] + wide[2], 2.0 * wide[4] + wide[5]], axis=1)
    stiff_row = wide[6] + wide[7]
    total = row_index.shape[1]
    spring[...] = jnp.broadcast_to(stiff_row, spring.shape)
    row_iota = lax.broadcasted_iota(jnp.int32, (rows, total), 0).astype(F32)
    row_hits = (row_iota == row_index).astype(F32).astype(BF16)
    row_marks[...] = row_hits
    for start in range(0, cols, 64):
        iota = (lax.broadcasted_iota(jnp.int32, (64, total), 0) + start).astype(F32)
        column_marks[start : start + 64, :] = (iota == column_index).astype(F32).astype(BF16)
    copies[3].wait()
    values = pick([disp[f] for f in range(FIELDS)], column_marks[...], row_hits)
    picked[...] = jnp.concatenate(values + [values[0]] * 3, axis=0)
    half = total // 2
    near_out = collapse([value[:, :half] for value in values] + [stiff_row], by_device, by_place)
    far_out = collapse([value[:, half:] for value in values], by_device, by_place)

    for copy in copies[4:]:
        copy.wait()
    plate = thickness[...].astype(F32) * (1.0 / spacing_mm)
    columns = []
    for f in range(RESULTS + 1):
        left = stress_left[f] if f < RESULTS else plate[:, 0:LANES]
        right = stress_right[f] if f < RESULTS else plate[:, cols - LANES :]
        columns.append((left, 0, f // 5, 2 + f % 5))
        columns.append((right, LANES - 1, f // 5, 10 + f % 5))
    send_sides(girth_pair, edge_rows(columns))
    send_joints(payload, near_out, far_out, [])
    send_ends(
        sec_pair,
        [stress_top[f, 0:1, :] for f in range(RESULTS)] + [plate[0:1, :]],
        [stress_bottom[f, 7:8, :] for f in range(RESULTS)] + [plate[rows - 1 : rows, :]],
    )


def fill_halo(ref, f, above, below, sides, corner):
    rows, cols = ref.shape[1] - PAD_ROWS, ref.shape[2] - LANES
    depth = above.shape[0]
    ref[f, rows:, :cols] = jnp.concatenate(
        [below, jnp.zeros((PAD_ROWS - 2 * depth, cols), F32), above], axis=0
    )
    ref[f, :rows, cols:] = sides
    ref[f, rows:, cols:] = corner


def load_velocity(vel_ext, incoming, above, below, left, right):
    first, second = edge_columns(left, right)
    row = lax.broadcasted_iota(jnp.int32, (8, LANES), 0)
    corner_tiles = [
        jnp.broadcast_to(jnp.where(inside, corner_of(incoming, device), 0.0), (8, LANES))
        for device, inside in corner_neighbours()
    ]
    for f in range(FIELDS):
        sides = edge_block(
            [
                (first, 2 + f, LANES - 2),
                (second, 2 + f, LANES - 1),
                (first, 10 + f, 0),
                (second, 10 + f, 1),
            ]
        )
        upper = edge_block([(corner_tiles[0], CORNER_LANE + f, LANES - 1), (corner_tiles[1], CORNER_LANE + f, 0)])
        lower = edge_block([(corner_tiles[2], CORNER_LANE + f, LANES - 1), (corner_tiles[3], CORNER_LANE + f, 0)])
        corner = jnp.where(row == 0, lower, jnp.where(row == 7, upper, 0.0))
        fill_halo(
            vel_ext, f, above[2 * f : 2 * f + 2, :], below[2 * f : 2 * f + 2, :], sides, corner
        )


def load_stress(stress_ext, plate_ext, thickness, above, below, left, right):
    rows, cols = thickness.shape
    halves = edge_columns(left, right)
    plate_ext[0, :rows, :cols] = thickness[...].astype(F32) * (1.0 / spacing_mm)
    empty = jnp.zeros((PAD_ROWS, LANES), F32)
    for f in range(RESULTS + 1):
        lane = 2 + f % 5
        half = halves[f // 5]
        sides = edge_block([(half, lane, LANES - 1), (half, 8 + lane, 0)])
        ref, k = (stress_ext, f) if f < RESULTS else (plate_ext, 0)
        fill_halo(ref, k, above[f : f + 1, :], below[f : f + 1, :], sides, empty)


def step_kernel(first, last, *refs):
    (stress_in, velocity_in, disp_in, thickness_in, pressure_in) = refs[:5]
    if first:
        out = refs[14:]
    else:
        plate_ext = refs[14]
        out = refs[15:]
    (incoming, sec_second, sec_first, girth_second, girth_first,
     column_marks, row_marks, picked, spring) = refs[5:14]
    stress_out, velocity_out, disp_out = out[:3]
    out = out[3:]
    if first:
        plate_ext, spring_out = out[:2]
        out = out[2:]
    girth_pair, sec_pair = out[0:2], out[2:4]
    out = out[4:]
    if not last:
        picked_out, payload = out[:2]
        out = out[2:]
    (stress_ext, res_ext, vel_ext, weld, velocity, disp, thickness, pressure,
     got, sent) = out

    _, rows, cols = velocity.shape
    devices = incoming.shape[0] // 2
    total = picked.shape[1]
    half = total // 2
    by_device, by_place = slot_marks(devices, half // devices)
    if first:
        pairs = [(thickness_in, thickness)]
        pairs += [
            (stress_in.at[:, part, :], stress_ext.at[:, part, 0:cols]) for part in pieces(rows)
        ]
        pairs += [(velocity_in, velocity)]
    else:
        pairs = [(velocity_in, vel_ext.at[:, 0:rows, 0:cols])]
        pairs += [
            (stress_in.at[:, part, :], stress_ext.at[:, part, :])
            for part in pieces(rows + PAD_ROWS)
        ]
    pairs += [(disp_in, disp), (pressure_in, pressure)]
    copies = fetch(got, pairs)
    sends = []

    def send(source, target):
        copy = pltpu.make_async_copy(source, target, sent.at[len(sends)])
        copy.start()
        sends.append(copy)

    other = []
    for row in (1, 0):
        high, low = split(incoming[pl.ds(row, devices, stride=2), :])
        other.append(expand(high, by_device, by_place) + expand(low, by_device, by_place))
    if first:
        stiffness = jnp.concatenate([spring[0:1, :], other[1][5:6]], axis=1)
        spring_out[...] = jnp.broadcast_to(stiffness, spring_out.shape)
    else:
        stiffness = spring[0:1, :]
    field = lax.broadcasted_iota(jnp.int32, (8, total), 0)
    scale = jnp.where(field < 3, 1.0, rotary_share) * stiffness
    pulls = scale * (jnp.concatenate(other, axis=1) - picked[...])
    weld[...] = spread(pulls, column_marks[...], row_marks[...])

    above, below = in_order("sec", sec_first[...], sec_second[...])
    left, right = in_order("girth", girth_first[...], girth_second[...])
    copies[0].wait()
    if first:
        load_stress(stress_ext, plate_ext, thickness, above, below, left, right)
    else:
        load_velocity(vel_ext, incoming, above, below, left, right)
    for start in range(0, rows + PAD_ROWS, 8):
        if start in (0, PIECE, 2 * PIECE):
            copies[1 + start // PIECE].wait()
        plate = plate_ext[0, start : start + 8, :]
        chunk = [stress_ext[k, start : start + 8, :] for k in range(RESULTS)]
        if not first:
            chunk = stress_chunk(vel_ext, chunk, plate, start)
            for k, value in enumerate(chunk):
                stress_ext[k, start : start + 8, :] = value
        for k, value in enumerate(resultants(chunk, plate)):
            res_ext[k, start : start + 8, :] = value
        for part in pieces(rows + PAD_ROWS):
            if part.stop == start + 8:
                send(stress_ext.at[:, part, :], stress_out.at[:, part, :])
    for copy in copies[4:]:
        copy.wait()

    for start in range(0, rows, 8):
        part = slice(start, start + 8)
        plate = plate_ext[0, part, :cols]
        linear = time_step / plate
        angular = (12.0 * linear) / (1.0 + plate * plate)
        force = force_chunk(res_ext, start, cols)
        force[2] = force[2] + pressure[part, :]
        for f in range(FIELDS):
            joined = force[f] + weld[f * rows + start : f * rows + start + 8, :]
            before = velocity[f, part, :] if first else vel_ext[f, part, :cols]
            speed = before + (linear if f < 3 else angular) * joined
            velocity[f, part, :] = speed
            disp[f, part, :] = disp[f, part, :] + time_step * speed
        if start % 32 == 24:
            done = slice(start - 24, start + 8)
            for source, target in ((velocity, velocity_out), (disp, disp_out)):
                send(source.at[:, done, :], target.at[:, done, :])

    ends = (cols - LANES, cols)
    if last:
        columns = []
        for f in range(FIELDS):
            columns.append((velocity[f, :, 0:LANES], 0, 0, f))
            columns.append((velocity[f, :, ends[0] : ends[1]], LANES - 1, 0, 8 + f))
        send_sides(girth_pair, edge_rows(columns))
        send_ends(
            sec_pair,
            [velocity[f, 0:1, :] for f in range(FIELDS)],
            [velocity[f, rows - 1 : rows, :] for f in range(FIELDS)],
        )
        for copy in sends:
            copy.wait()
        return
    values = pick([disp[f] for f in range(FIELDS)], column_marks[...], row_marks[...])
    picked_out[...] = jnp.concatenate(values + [values[0]] * 3, axis=0)
    near_out = collapse([value[:, :half] for value in values], by_device, by_place)
    far_out = collapse([value[:, half:] for value in values], by_device, by_place)
    columns = []
    for f in range(FIELDS):
        left_lanes = velocity[f, :, 0:LANES]
        right_lanes = velocity[f, :, ends[0] : ends[1]]
        for depth in (0, 1):
            columns.append((left_lanes, depth, depth, 2 + f))
            columns.append((right_lanes, LANES - 2 + depth, depth, 10 + f))
    corners = []
    lane = lax.broadcasted_iota(jnp.int32, (8, LANES), 1)
    for row in (0, rows - 1):
        tile = slice(row // 8 * 8, row // 8 * 8 + 8)
        for side in (0, 1):
            value = jnp.zeros((8, LANES), F32)
            for f in range(FIELDS):
                part = velocity[f, tile, ends[0] : ends[1]] if side else velocity[f, tile, 0:LANES]
                source = LANES - 1 if side else 0
                target = CORNER_LANE + f
                value = jnp.where(lane == target, pltpu.roll(part, (target - source) % LANES, 1), value)
            corners.append(jnp.broadcast_to(value[row % 8 : row % 8 + 1], (8, LANES)))
    send_sides(girth_pair, edge_rows(columns))
    send_joints(payload, near_out, far_out, corners)
    send_ends(
        sec_pair,
        [velocity[f, 0:2, :] for f in range(FIELDS)],
        [velocity[f, rows - 2 : rows, :] for f in range(FIELDS)],
    )
    for copy in sends:
        copy.wait()


def final_kernel(membrane, *refs):
    (stress_in, velocity_in), refs = refs[:2], refs[2:]
    if membrane:
        sec_second, sec_first, girth_second, girth_first, plate_ext, height = refs[:6]
        stress_out, moment = refs[6:8]
        refs = refs[8:]
    else:
        sec_second, sec_first, girth_second, girth_first, plate_ext = refs[1:6]
        stress_out = refs[6]
        refs = refs[7:]
    stress, made, vel_ext, got, sent = refs
    rows, cols = vel_ext.shape[1] - PAD_ROWS, vel_ext.shape[2] - LANES
    fields = range(0, 2) if membrane else range(2, FIELDS)
    kinds = slice(0, 3) if membrane else slice(3, RESULTS)
    pairs = [(velocity_in.at[fields.start : fields.stop], vel_ext.at[:, 0:rows, 0:cols])]
    pairs += [(stress_in.at[kinds, part, 0:cols], stress.at[:, part, :]) for part in pieces(rows)]
    copies = fetch(got, pairs)
    above, below = in_order("sec", sec_first[...], sec_second[...])
    left, right = in_order("girth", girth_first[...], girth_second[...])
    first, _ = edge_columns(left, right)
    empty = jnp.zeros((PAD_ROWS, LANES), F32)
    for k, f in enumerate(fields):
        sides = edge_block([(first, f, LANES - 1), (first, 8 + f, 0)])
        fill_halo(vel_ext, k, above[f : f + 1, :], below[f : f + 1, :], sides, empty)
    copies[0].wait()
    parts = []
    sends = []
    for start in range(0, rows, 8):
        if start in (0, PIECE, 2 * PIECE):
            copies[1 + start // PIECE].wait()
        part = slice(start, start + 8)
        chunk = [stress[k, part, :] for k in range(stress.shape[0])]
        plate = plate_ext[0, part, :cols]
        current, along_x, along_y = [
            [value[:, :cols] for value in values]
            for values in differences(vel_ext, range(len(fields)), start)
        ]
        if membrane:
            chunk = membrane_chunk(along_x, along_y, chunk)
            weighted = plate * chunk[0] * height[0:1, :]
            parts.append(jnp.sum(weighted, axis=1, keepdims=True))
        else:
            chunk = plate_chunk(along_x, along_y, current[1:], chunk, plate)
        for k, value in enumerate(chunk):
            made[k, part, :] = value
        if start % 16 == 8:
            done = slice(start - 8, start + 8)
            copy = pltpu.make_async_copy(
                made.at[:, done, :], stress_out.at[kinds, done, :], sent.at[len(sends)]
            )
            copy.start()
            sends.append(copy)
    if membrane:
        column = jnp.broadcast_to(jnp.concatenate(parts, axis=0), (rows, LANES))
        if rows < LANES:
            column = jnp.concatenate([column, jnp.zeros((LANES - rows, LANES), F32)], axis=0)
        moment[...] = column.T[0:8, :rows]
    for copy in sends:
        copy.wait()


def call(kernel, vmem_bytes, outs, scratch, *operands, far=0, far_out=0, copies=(1,), alias=None):
    operands = [
        pltpu.with_memory_space_constraint(value, pltpu.HBM) if k < far else value
        for k, value in enumerate(operands)
    ]
    whole = pl.BlockSpec(memory_space=pltpu.VMEM)
    away = pl.BlockSpec(memory_space=pltpu.HBM)
    scratch = [pltpu.VMEM(shape, dtype) for shape, dtype in scratch]
    scratch += [pltpu.SemaphoreType.DMA((count,)) for count in copies]
    return pl.pallas_call(
        kernel,
        out_shape=[
            pltpu.HBM(shape, dtype) if k < far_out else jax.ShapeDtypeStruct(shape, dtype)
            for k, (shape, dtype) in enumerate(outs)
        ],
        in_specs=[away] * far + [whole] * (len(operands) - far),
        out_specs=[away] * far_out + [whole] * (len(outs) - far_out),
        scratch_shapes=scratch,
        input_output_aliases=alias or {},
        compiler_params=pltpu.CompilerParams(vmem_limit_bytes=vmem_bytes),
    )(*operands)


def swap(pair, axis, around):
    count = lax.axis_size(axis)
    out = []
    for start, value in reversed(list(enumerate(pair))):
        couples = [(i, (i + 1) % count) for i in range(start, count, 2)]
        couples = [(i, j) for i, j in couples if j > i or around]
        out.append(lax.ppermute(value, axis, couples + [(j, i) for i, j in couples]))
    return out


def sum_over(value, axis):
    count = lax.axis_size(axis)
    if count & (count - 1):
        return lax.psum(value, axis)
    parts = [
        lax.ppermute(value, axis, [(i, i ^ step) for i in range(count)])
        for step in range(count - 1, 0, -1)
    ]
    parts = [value] + parts[::-1]
    while len(parts) > 1:
        parts = [a + b for a, b in zip(parts[0::2], parts[1::2])]
    return parts[0]


def exchange(joints):
    blocks = joints.reshape(joints.shape[0] // 2, 2, LANES)
    blocks = lax.all_to_all(blocks, ("sec", "girth"), 0, 0, tiled=True)
    return blocks.reshape(joints.shape)


def local(displacement, velocity, stress, thickness, pressure, weld_from, weld_to, weld_stiff):
    rows, cols = thickness.shape
    _, devices, slots = weld_from.shape
    total = 2 * devices * slots
    girth_total = cols * lax.axis_size("girth")
    column = (lax.axis_index("girth") * cols + lax.iota(jnp.int32, cols)).astype(F32)
    height = jnp.sin(2.0 * jnp.pi / girth_total * (column + 0.5)) / girth_total
    height = jnp.broadcast_to(height[None, :], (8, cols))

    vmem_bytes = 8 * 1024 * 1024 + total * VMEM_PER_SLOT
    message = (devices * 2, LANES)
    edge = (8, LANES)
    strip = (16, cols)
    block = (FIELDS, rows, cols)
    stress_shape = (RESULTS, rows + PAD_ROWS, cols + LANES)
    plate_shape = (1, rows + PAD_ROWS, cols + LANES)
    slot_rows = (8, total)
    scratch = [
        (stress_shape, F32),
        (stress_shape, F32),
        ((FIELDS, rows + PAD_ROWS, cols + LANES), F32),
        ((FIELDS * rows, cols), F32),
        (block, F32),
        (block, F32),
        ((rows, cols), jnp.int32),
        ((rows, cols), F32),
    ]

    (payload, sec_first, sec_second, girth_first, girth_second,
     column_marks, row_marks, picked, spring) = call(
        start_kernel,
        vmem_bytes,
        [
            (message, F32), (strip, F32), (strip, F32), (edge, F32), (edge, F32),
            ((cols, total), BF16), ((rows, total), BF16), (slot_rows, F32), ((8, total // 2), F32),
        ],
        [
            (block, F32), ((RESULTS, rows, LANES), F32), ((RESULTS, rows, LANES), F32),
            ((RESULTS, 8, cols), F32), ((RESULTS, 8, cols), F32), ((rows, cols), jnp.int32),
            ((1, slots, devices), jnp.int32), ((1, slots, devices), jnp.int32),
            ((1, slots, devices), F32),
        ],
        displacement, stress, thickness,
        *[jnp.swapaxes(array, 1, 2) for array in (weld_from, weld_to, weld_stiff)],
        far=6,
        copies=(9,),
    )
    plate = None
    for step in range(STEPS):
        first, last = step == 0, step == STEPS - 1
        incoming = exchange(payload)
        ends = swap((sec_first, sec_second), "sec", False)
        sides = swap((girth_first, girth_second), "girth", True)
        outs = [(stress_shape, F32), (block, F32), (block, F32)]
        if first:
            outs += [(plate_shape, F32), (slot_rows, F32)]
        halo = (8, cols) if last else strip
        outs += [(edge, F32), (edge, F32), (halo, F32), (halo, F32)]
        if not last:
            outs += [(slot_rows, F32), (message, F32)]
        results = call(
            functools.partial(step_kernel, first, last),
            vmem_bytes,
            outs,
            scratch,
            stress, velocity, displacement, thickness, pressure,
            incoming, *ends, *sides,
            column_marks, row_marks, picked, spring,
            *([] if first else [plate]),
            far=5,
            far_out=3,
            copies=(7, 3 + 2 * (rows // 32)),
        )
        stress, velocity, displacement = results[:3]
        results = results[3:]
        if first:
            plate, spring = results[:2]
            results = results[2:]
        girth_first, girth_second, sec_first, sec_second = results[:4]
        if not last:
            picked, payload = results[4:]

    ends = swap((sec_first, sec_second), "sec", False)
    sides = swap((girth_first, girth_second), "girth", True)
    membrane, partial_moment = call(
        functools.partial(final_kernel, True),
        vmem_bytes,
        [((RESULTS, rows, cols), F32), ((8, rows), F32)],
        [
            ((3, rows, cols), F32), ((3, rows, cols), F32),
            ((2, rows + PAD_ROWS, cols + LANES), F32),
        ],
        stress, velocity, *ends, *sides, plate, height,
        far=2,
        far_out=1,
        copies=(4, rows // 16),
    )
    (stress,) = call(
        functools.partial(final_kernel, False),
        vmem_bytes,
        [((RESULTS, rows, cols), F32)],
        [
            ((5, rows, cols), F32), ((5, rows, cols), F32),
            ((3, rows + PAD_ROWS, cols + LANES), F32),
        ],
        stress, velocity, membrane, *ends, *sides, plate,
        far=3,
        far_out=1,
        copies=(4, rows // 16),
        alias={2: 0},
    )
    moment = sum_over(partial_moment, "girth")[0]
    return (displacement, velocity, stress, moment)


def solution(mesh):
    in_specs = (
        P(None, "sec", "girth"),
        P(None, "sec", "girth"),
        P(None, "sec", "girth"),
        P("sec", "girth"),
        P("sec", "girth"),
        P(("sec", "girth"), None, None),
        P(("sec", "girth"), None, None),
        P(("sec", "girth"), None, None),
    )
    out_specs = (
        P(None, "sec", "girth"),
        P(None, "sec", "girth"),
        P(None, "sec", "girth"),
        P("sec"),
    )
    return jax.shard_map(local, mesh=mesh, in_specs=in_specs, out_specs=out_specs, check_vma=False)
```

```python
import functools

import jax
import jax.numpy as jnp
from jax import lax
from jax.experimental import pallas as pl
from jax.experimental.pallas import tpu as pltpu
from jax.sharding import PartitionSpec as P

STEPS = 3
CORNER_LANE = 112
PIECE = 24
FIELDS = 5
RESULTS = 8
PAD_ROWS = 8
LANES = 128
VMEM_PER_SLOT = 5 * 1024

young_modulus = 4.0
poisson_ratio = 0.3
plate_modulus = young_modulus / (1.0 - poisson_ratio * poisson_ratio)
shear_modulus = young_modulus / (2.0 * (1.0 + poisson_ratio))
shear_factor = 5.0 / 6.0
time_step = 0.2
spacing_mm = 50.0
rotary_share = 1.0 / 12.0

F32 = jnp.float32
BF16 = jnp.bfloat16


def split(values):
    high = values.astype(BF16)
    low = (values - high.astype(F32)).astype(BF16)
    return high, low


def dot(a, b, contract):
    return lax.dot_general(a, b, (contract, ((), ())), preferred_element_type=F32)


def slot_marks(devices, slots):
    total = devices * slots
    lane = lax.broadcasted_iota(jnp.int32, (devices, total), 1)
    device = lax.broadcasted_iota(jnp.int32, (devices, total), 0)
    by_device = (lane // slots == device).astype(F32).astype(BF16)
    lane = lax.broadcasted_iota(jnp.int32, (slots, total), 1)
    place = lax.broadcasted_iota(jnp.int32, (slots, total), 0)
    by_place = (lane % slots == place).astype(F32)
    return by_device, by_place


def expand(blocks, by_device, by_place, turned=False):
    slots, total = by_place.shape
    wide = dot(blocks, by_device, ((1 if turned else 0,), (0,)))
    wide = wide.reshape(wide.shape[0] // slots, slots, total) * by_place[None]
    return jnp.sum(wide, axis=1)


def collapse(rows, by_device, by_place):
    slots, _ = by_place.shape
    marks = by_place.astype(BF16)
    pieces = []
    for part in (0, 1):
        blocks = [split(row)[part] * marks for row in rows]
        blocks += [jnp.zeros_like(marks)] * (LANES // slots - len(rows))
        pieces.append(jnp.concatenate(blocks, axis=0))
    return dot(by_device, pieces[0], ((1,), (1,))) + dot(by_device, pieces[1], ((1,), (1,)))


def pick(fields, column_marks, row_marks):
    rows = fields[0].shape[0]
    parts = [split(field) for field in fields]
    high = jnp.concatenate([part[0] for part in parts], axis=0)
    low = jnp.concatenate([part[1] for part in parts], axis=0)
    by_column = dot(high, column_marks, ((1,), (0,))) + dot(low, column_marks, ((1,), (0,)))
    marks = row_marks.astype(F32)
    return [
        jnp.sum(by_column[rows * f : rows * (f + 1)] * marks, axis=0, keepdims=True)
        for f in range(len(fields))
    ]


def spread(pulls, column_marks, row_marks):
    high, low = split(pulls)
    total = None
    for part in (high, low):
        marked = jnp.concatenate(
            [part[f : f + 1] * row_marks for f in range(FIELDS)], axis=0
        )
        summed = dot(marked, column_marks, ((1,), (1,)))
        total = summed if total is None else total + summed
    return total


def place():
    sec, girth = lax.axis_index("sec"), lax.axis_index("girth")
    return sec, girth, lax.axis_size("sec"), lax.axis_size("girth")


def tile_of(ref, device):
    return ref[pl.ds(pl.multiple_of(device * 8, 8), 8), :]


def set_tile(ref, device, value):
    ref[pl.ds(pl.multiple_of(device * 8, 8), 8), :] = value


def corner_neighbours():
    sec, girth, secs, girths = place()
    me = sec * girths + girth
    out = []
    for step in (-1, 1):
        row = sec + step
        inside = jnp.logical_and(row >= 0, row < secs)
        for turn in (girths - 1, 1):
            device = row * girths + lax.rem(girth + turn, girths)
            out.append((jnp.where(inside, device, me), inside))
    return out


def edge_rows(columns):
    rows = columns[0][0].shape[0]
    lane = lax.broadcasted_iota(jnp.int32, (rows, LANES), 1)
    halves = [jnp.zeros((rows, LANES), F32), jnp.zeros((rows, LANES), F32)]
    for value, source, half, row in columns:
        moved = pltpu.roll(value, (row - source) % LANES, 1)
        halves[half] = jnp.where(lane == row, moved, halves[half])
    return jnp.concatenate(halves, axis=0).T


def edge_columns(left_tile, right_tile):
    stacked = jnp.concatenate(
        [left_tile, right_tile, jnp.zeros((LANES - 16, LANES), F32)], axis=0
    )
    turned = stacked.T
    return turned[: LANES // 2], turned[LANES // 2 :]


def edge_block(pieces):
    rows = pieces[0][0].shape[0]
    lane = lax.broadcasted_iota(jnp.int32, (rows, LANES), 1)
    block = jnp.zeros((rows, LANES), F32)
    for value, source, target in pieces:
        block = jnp.where(lane == target, pltpu.roll(value, (target - source) % LANES, 1), block)
    return block


def row_chunk(ref, f, start):
    count = ref.shape[1]
    if start < 0:
        return jnp.concatenate([ref[f, count + start : count, :], ref[f, 0 : 8 + start, :]], axis=0)
    if start + 8 > count:
        return jnp.concatenate([ref[f, start:count, :], ref[f, 0 : start + 8 - count, :]], axis=0)
    return ref[f, start : start + 8, :]


def difference_x(ref, f, start):
    return row_chunk(ref, f, start + 1) - row_chunk(ref, f, start - 1)


def difference_y(value):
    lanes = value.shape[1]
    return pltpu.roll(value, lanes - 1, 1) - pltpu.roll(value, 1, 1)


def radial_return(xx, yy, xy):
    offset = xx - 0.5 * yy
    square = offset * offset + 0.75 * yy * yy + 3.0 * xy * xy
    scale = lax.rsqrt(jnp.maximum(square, 1.0))
    return xx * scale, yy * scale, xy * scale


def membrane_chunk(along_x, along_y, stress):
    normal = 0.5 * time_step * plate_modulus
    skew = 0.5 * time_step * shear_modulus
    return radial_return(
        stress[0] + normal * (along_x[0] + poisson_ratio * along_y[1]),
        stress[1] + normal * (along_y[1] + poisson_ratio * along_x[0]),
        stress[2] + skew * (along_y[0] + along_x[1]),
    )


def plate_chunk(along_x, along_y, turns, stress, plate):
    arm = 0.5 * plate
    normal = 0.5 * time_step * plate_modulus * arm
    skew = 0.5 * time_step * shear_modulus
    bending = radial_return(
        stress[0] + normal * (along_x[1] + poisson_ratio * along_y[2]),
        stress[1] + normal * (along_y[2] + poisson_ratio * along_x[1]),
        stress[2] + (skew * arm) * (along_y[1] + along_x[2]),
    )
    return bending + (
        stress[3] + skew * (along_x[0] + 2.0 * turns[0]),
        stress[4] + skew * (along_y[0] + 2.0 * turns[1]),
    )


def differences(vel_ref, fields, start):
    current = [vel_ref[f, start : start + 8, :] for f in fields]
    along_x = [difference_x(vel_ref, f, start) for f in fields]
    return current, along_x, [difference_y(value) for value in current]


def stress_chunk(vel_ref, stress, plate, start):
    current, along_x, along_y = differences(vel_ref, range(FIELDS), start)
    membrane = membrane_chunk(along_x[:2], along_y[:2], stress[:3])
    return membrane + plate_chunk(along_x[2:], along_y[2:], current[3:], stress[3:], plate)


def resultants(stress, plate):
    arm = plate * plate * (1.0 / 6.0)
    shear = shear_factor * plate
    return (
        [plate * value for value in stress[0:3]]
        + [arm * value for value in stress[3:6]]
        + [shear * value for value in stress[6:8]]
    )


def force_chunk(res_ref, start, cols):
    def both(x, y):
        along_x = difference_x(res_ref, x, start)[:, :cols]
        along_y = difference_y(res_ref[y, start : start + 8, :])[:, :cols]
        return 0.5 * (along_x + along_y)

    return [
        both(0, 2),
        both(2, 1),
        both(6, 7),
        both(3, 5) - res_ref[6, start : start + 8, :cols],
        both(5, 4) - res_ref[7, start : start + 8, :cols],
    ]


def send_joints(payload, near, far, corners):
    devices = payload.shape[0] // 2
    payload[pl.ds(0, devices, stride=2), :] = near
    payload[pl.ds(1, devices, stride=2), :] = far
    row = lax.broadcasted_iota(jnp.int32, (8, LANES), 0)
    lane = lax.broadcasted_iota(jnp.int32, (8, LANES), 1)
    free = jnp.logical_and(lane >= CORNER_LANE, lane < CORNER_LANE + FIELDS)
    for (device, _), corner in zip(corner_neighbours(), corners):
        tile = lax.div(device, 4)
        here = jnp.logical_and(free, row == 2 * lax.rem(device, 4))
        set_tile(payload, tile, jnp.where(here, corner, tile_of(payload, tile)))


def in_order(axis, low, high):
    even = lax.rem(lax.axis_index(axis), 2) == 0
    return jnp.where(even, high, low), jnp.where(even, low, high)


def send_sides(pair, halo_rows):
    for ref, value in zip(pair, in_order("girth", halo_rows[0:8], halo_rows[8:16])):
        ref[...] = value


def send_ends(pair, low, high):
    for ref in pair:
        ref[...] = jnp.zeros(ref.shape, F32)
    start = 0
    for top, bottom in zip(low, high):
        count = top.shape[0]
        for ref, value in zip(pair, in_order("sec", top, bottom)):
            ref[start : start + count, :] = value
        start += count


def corner_of(incoming, device):
    row = lax.broadcasted_iota(jnp.int32, (8, LANES), 0)
    tile = tile_of(incoming, lax.div(device, 4))
    return jnp.sum(jnp.where(row == 2 * lax.rem(device, 4), tile, 0.0), axis=0, keepdims=True)


def fetch(done, pairs):
    copies = [
        pltpu.make_async_copy(source, target, done.at[k])
        for k, (source, target) in enumerate(pairs)
    ]
    for copy in copies:
        copy.start()
    return copies


def pieces(rows):
    return [slice(0, PIECE), slice(PIECE, 2 * PIECE), slice(2 * PIECE, rows)]


def start_kernel(
    disp_in, stress_in, thickness_in, from_in, to_in, stiff_in,
    payload, sec_first, sec_second, girth_first, girth_second,
    column_marks, row_marks, picked, spring,
    disp, stress_left, stress_right, stress_top, stress_bottom, thickness,
    weld_from, weld_to, weld_stiff, done,
):
    rows, cols = thickness.shape
    _, slots, devices = weld_from.shape
    sec_pair, girth_pair = (sec_first, sec_second), (girth_first, girth_second)
    copies = fetch(
        done,
        [
            (from_in, weld_from),
            (to_in, weld_to),
            (stiff_in, weld_stiff),
            (disp_in, disp),
            (thickness_in, thickness),
            (stress_in.at[:, :, 0:LANES], stress_left),
            (stress_in.at[:, :, cols - LANES : cols], stress_right),
            (stress_in.at[:, 0:8, :], stress_top),
            (stress_in.at[:, rows - 8 : rows, :], stress_bottom),
        ],
    )
    shift = cols.bit_length() - 1
    by_device, by_place = slot_marks(devices, slots)
    for copy in copies[:3]:
        copy.wait()
    near, far = weld_from[0], weld_to[0]
    stiff = jnp.where(near >= 0, weld_stiff[0], 0.0)
    index_parts = []
    for index in (near, far):
        index = jnp.maximum(index, 0)
        column = index & (cols - 1)
        index_parts += [index >> shift, column >> 1, column & 1]
    index_parts = [part.astype(F32).astype(BF16) for part in index_parts]
    index_parts += list(split(stiff))
    wide = [expand(part, by_device, by_place, turned=True) for part in index_parts]
    row_index = jnp.concatenate([wide[0], wide[3]], axis=1)
    column_index = jnp.concatenate([2.0 * wide[1] + wide[2], 2.0 * wide[4] + wide[5]], axis=1)
    stiff_row = wide[6] + wide[7]
    total = row_index.shape[1]
    spring[...] = jnp.broadcast_to(stiff_row, spring.shape)
    row_iota = lax.broadcasted_iota(jnp.int32, (rows, total), 0).astype(F32)
    row_hits = (row_iota == row_index).astype(F32).astype(BF16)
    row_marks[...] = row_hits
    for start in range(0, cols, 64):
        iota = (lax.broadcasted_iota(jnp.int32, (64, total), 0) + start).astype(F32)
        column_marks[start : start + 64, :] = (iota == column_index).astype(F32).astype(BF16)
    copies[3].wait()
    values = pick([disp[f] for f in range(FIELDS)], column_marks[...], row_hits)
    picked[...] = jnp.concatenate(values + [values[0]] * 3, axis=0)
    half = total // 2
    near_out = collapse([value[:, :half] for value in values] + [stiff_row], by_device, by_place)
    far_out = collapse([value[:, half:] for value in values], by_device, by_place)

    for copy in copies[4:]:
        copy.wait()
    plate = thickness[...].astype(F32) * (1.0 / spacing_mm)
    columns = []
    for f in range(RESULTS + 1):
        left = stress_left[f] if f < RESULTS else plate[:, 0:LANES]
        right = stress_right[f] if f < RESULTS else plate[:, cols - LANES :]
        columns.append((left, 0, f // 5, 2 + f % 5))
        columns.append((right, LANES - 1, f // 5, 10 + f % 5))
    send_sides(girth_pair, edge_rows(columns))
    send_joints(payload, near_out, far_out, [])
    send_ends(
        sec_pair,
        [stress_top[f, 0:1, :] for f in range(RESULTS)] + [plate[0:1, :]],
        [stress_bottom[f, 7:8, :] for f in range(RESULTS)] + [plate[rows - 1 : rows, :]],
    )


def fill_halo(ref, f, above, below, sides, corner):
    rows, cols = ref.shape[1] - PAD_ROWS, ref.shape[2] - LANES
    depth = above.shape[0]
    ref[f, rows:, :cols] = jnp.concatenate(
        [below, jnp.zeros((PAD_ROWS - 2 * depth, cols), F32), above], axis=0
    )
    ref[f, :rows, cols:] = sides
    ref[f, rows:, cols:] = corner


def load_velocity(vel_ext, incoming, above, below, left, right):
    first, second = edge_columns(left, right)
    row = lax.broadcasted_iota(jnp.int32, (8, LANES), 0)
    corner_tiles = [
        jnp.broadcast_to(jnp.where(inside, corner_of(incoming, device), 0.0), (8, LANES))
        for device, inside in corner_neighbours()
    ]
    for f in range(FIELDS):
        sides = edge_block(
            [
                (first, 2 + f, LANES - 2),
                (second, 2 + f, LANES - 1),
                (first, 10 + f, 0),
                (second, 10 + f, 1),
            ]
        )
        upper = edge_block([(corner_tiles[0], CORNER_LANE + f, LANES - 1), (corner_tiles[1], CORNER_LANE + f, 0)])
        lower = edge_block([(corner_tiles[2], CORNER_LANE + f, LANES - 1), (corner_tiles[3], CORNER_LANE + f, 0)])
        corner = jnp.where(row == 0, lower, jnp.where(row == 7, upper, 0.0))
        fill_halo(
            vel_ext, f, above[2 * f : 2 * f + 2, :], below[2 * f : 2 * f + 2, :], sides, corner
        )


def load_stress(stress_ext, plate_ext, thickness, above, below, left, right):
    rows, cols = thickness.shape
    halves = edge_columns(left, right)
    plate_ext[0, :rows, :cols] = thickness[...].astype(F32) * (1.0 / spacing_mm)
    empty = jnp.zeros((PAD_ROWS, LANES), F32)
    for f in range(RESULTS + 1):
        lane = 2 + f % 5
        half = halves[f // 5]
        sides = edge_block([(half, lane, LANES - 1), (half, 8 + lane, 0)])
        ref, k = (stress_ext, f) if f < RESULTS else (plate_ext, 0)
        fill_halo(ref, k, above[f : f + 1, :], below[f : f + 1, :], sides, empty)


def step_kernel(first, last, *refs):
    (stress_in, velocity_in, thickness_in, pressure_in) = refs[:4]
    if first:
        out = refs[13:]
    else:
        plate_ext = refs[13]
        out = refs[14:]
    (incoming, girth_second, sec_first, sec_second, girth_first,
     column_marks, row_marks, picked, spring) = refs[4:13]
    stress_out, velocity_out = out[:2]
    out = out[2:]
    if first:
        plate_ext, spring_out = out[:2]
        out = out[2:]
    girth_pair, sec_pair = out[0:2], out[2:4]
    out = out[4:]
    if not last:
        picked_out, payload = out[:2]
        out = out[2:]
    (stress_ext, res_ext, vel_ext, weld, velocity, thickness, pressure, got, sent) = out

    _, rows, cols = velocity.shape
    devices = incoming.shape[0] // 2
    total = picked.shape[1]
    half = total // 2
    by_device, by_place = slot_marks(devices, half // devices)
    if first:
        pairs = [(thickness_in, thickness)]
        pairs += [
            (stress_in.at[:, part, :], stress_ext.at[:, part, 0:cols]) for part in pieces(rows)
        ]
        pairs += [(velocity_in, velocity)]
    else:
        pairs = [(velocity_in, vel_ext.at[:, 0:rows, 0:cols])]
        pairs += [
            (stress_in.at[:, part, :], stress_ext.at[:, part, :])
            for part in pieces(rows + PAD_ROWS)
        ]
    pairs += [(pressure_in, pressure)]
    copies = fetch(got, pairs)
    sends = []

    def send(source, target):
        copy = pltpu.make_async_copy(source, target, sent.at[len(sends)])
        copy.start()
        sends.append(copy)

    other = []
    for row in (1, 0):
        high, low = split(incoming[pl.ds(row, devices, stride=2), :])
        other.append(expand(high, by_device, by_place) + expand(low, by_device, by_place))
    if first:
        stiffness = jnp.concatenate([spring[0:1, :], other[1][5:6]], axis=1)
        spring_out[...] = jnp.broadcast_to(stiffness, spring_out.shape)
    else:
        stiffness = spring[0:1, :]
    field = lax.broadcasted_iota(jnp.int32, (8, total), 0)
    scale = jnp.where(field < 3, 1.0, rotary_share) * stiffness
    pulls = scale * (jnp.concatenate(other, axis=1) - picked[...])
    weld[...] = spread(pulls, column_marks[...], row_marks[...])

    above, below = in_order("sec", sec_first[...], sec_second[...])
    left, right = in_order("girth", girth_first[...], girth_second[...])
    copies[0].wait()
    if first:
        load_stress(stress_ext, plate_ext, thickness, above, below, left, right)
    else:
        load_velocity(vel_ext, incoming, above, below, left, right)
    for start in range(0, rows + PAD_ROWS, 8):
        if start in (0, PIECE, 2 * PIECE):
            copies[1 + start // PIECE].wait()
        plate = plate_ext[0, start : start + 8, :]
        chunk = [stress_ext[k, start : start + 8, :] for k in range(RESULTS)]
        if not first:
            chunk = stress_chunk(vel_ext, chunk, plate, start)
            for k, value in enumerate(chunk):
                stress_ext[k, start : start + 8, :] = value
        for k, value in enumerate(resultants(chunk, plate)):
            res_ext[k, start : start + 8, :] = value
        for part in pieces(rows + PAD_ROWS):
            if part.stop == start + 8:
                send(stress_ext.at[:, part, :], stress_out.at[:, part, :])
    for copy in copies[4:]:
        copy.wait()

    for start in range(0, rows, 8):
        part = slice(start, start + 8)
        plate = plate_ext[0, part, :cols]
        linear = time_step / plate
        angular = (12.0 * linear) / (1.0 + plate * plate)
        force = force_chunk(res_ext, start, cols)
        force[2] = force[2] + pressure[part, :]
        for f in range(FIELDS):
            joined = force[f] + weld[f * rows + start : f * rows + start + 8, :]
            before = velocity[f, part, :] if first else vel_ext[f, part, :cols]
            speed = before + (linear if f < 3 else angular) * joined
            velocity[f, part, :] = speed
        if start % 32 == 24:
            done = slice(start - 24, start + 8)
            send(velocity.at[:, done, :], velocity_out.at[:, done, :])

    ends = (cols - LANES, cols)
    if last:
        columns = []
        for f in range(FIELDS):
            columns.append((velocity[f, :, 0:LANES], 0, 0, f))
            columns.append((velocity[f, :, ends[0] : ends[1]], LANES - 1, 0, 8 + f))
        send_sides(girth_pair, edge_rows(columns))
        send_ends(
            sec_pair,
            [velocity[f, 0:1, :] for f in range(FIELDS)],
            [velocity[f, rows - 1 : rows, :] for f in range(FIELDS)],
        )
        for copy in sends:
            copy.wait()
        return
    moves = pick([velocity[f] for f in range(FIELDS)], column_marks[...], row_marks[...])
    values = [picked[f : f + 1, :] + time_step * moves[f] for f in range(FIELDS)]
    picked_out[...] = jnp.concatenate(values + [values[0]] * 3, axis=0)
    near_out = collapse([value[:, :half] for value in values], by_device, by_place)
    far_out = collapse([value[:, half:] for value in values], by_device, by_place)
    columns = []
    for f in range(FIELDS):
        left_lanes = velocity[f, :, 0:LANES]
        right_lanes = velocity[f, :, ends[0] : ends[1]]
        for depth in (0, 1):
            columns.append((left_lanes, depth, depth, 2 + f))
            columns.append((right_lanes, LANES - 2 + depth, depth, 10 + f))
    corners = []
    lane = lax.broadcasted_iota(jnp.int32, (8, LANES), 1)
    for row in (0, rows - 1):
        tile = slice(row // 8 * 8, row // 8 * 8 + 8)
        for side in (0, 1):
            value = jnp.zeros((8, LANES), F32)
            for f in range(FIELDS):
                part = velocity[f, tile, ends[0] : ends[1]] if side else velocity[f, tile, 0:LANES]
                source = LANES - 1 if side else 0
                target = CORNER_LANE + f
                value = jnp.where(lane == target, pltpu.roll(part, (target - source) % LANES, 1), value)
            corners.append(jnp.broadcast_to(value[row % 8 : row % 8 + 1], (8, LANES)))
    send_sides(girth_pair, edge_rows(columns))
    send_joints(payload, near_out, far_out, corners)
    send_ends(
        sec_pair,
        [velocity[f, 0:2, :] for f in range(FIELDS)],
        [velocity[f, rows - 2 : rows, :] for f in range(FIELDS)],
    )
    for copy in sends:
        copy.wait()


def final_kernel(membrane, *refs):
    (stress_in, velocity_in), refs = refs[:2], refs[2:]
    if membrane:
        girth_second, sec_first, sec_second, girth_first, plate_ext, height = refs[:6]
        stress_out, moment = refs[6:8]
        refs = refs[8:]
    else:
        girth_second, sec_first, sec_second, girth_first, plate_ext = refs[1:6]
        stress_out = refs[6]
        refs = refs[7:]
    stress, made, vel_ext, got, sent = refs
    rows, cols = vel_ext.shape[1] - PAD_ROWS, vel_ext.shape[2] - LANES
    fields = range(0, 2) if membrane else range(2, FIELDS)
    kinds = slice(0, 3) if membrane else slice(3, RESULTS)
    pairs = [(velocity_in.at[fields.start : fields.stop], vel_ext.at[:, 0:rows, 0:cols])]
    pairs += [(stress_in.at[kinds, part, 0:cols], stress.at[:, part, :]) for part in pieces(rows)]
    copies = fetch(got, pairs)
    above, below = in_order("sec", sec_first[...], sec_second[...])
    left, right = in_order("girth", girth_first[...], girth_second[...])
    first, _ = edge_columns(left, right)
    empty = jnp.zeros((PAD_ROWS, LANES), F32)
    for k, f in enumerate(fields):
        sides = edge_block([(first, f, LANES - 1), (first, 8 + f, 0)])
        fill_halo(vel_ext, k, above[f : f + 1, :], below[f : f + 1, :], sides, empty)
    copies[0].wait()
    parts = []
    sends = []
    for start in range(0, rows, 8):
        if start in (0, PIECE, 2 * PIECE):
            copies[1 + start // PIECE].wait()
        part = slice(start, start + 8)
        chunk = [stress[k, part, :] for k in range(stress.shape[0])]
        plate = plate_ext[0, part, :cols]
        current, along_x, along_y = [
            [value[:, :cols] for value in values]
            for values in differences(vel_ext, range(len(fields)), start)
        ]
        if membrane:
            chunk = membrane_chunk(along_x, along_y, chunk)
            weighted = plate * chunk[0] * height[0:1, :]
            parts.append(jnp.sum(weighted, axis=1, keepdims=True))
        else:
            chunk = plate_chunk(along_x, along_y, current[1:], chunk, plate)
        for k, value in enumerate(chunk):
            made[k, part, :] = value
        if start % 16 == 8:
            done = slice(start - 8, start + 8)
            copy = pltpu.make_async_copy(
                made.at[:, done, :], stress_out.at[kinds, done, :], sent.at[len(sends)]
            )
            copy.start()
            sends.append(copy)
    if membrane:
        column = jnp.broadcast_to(jnp.concatenate(parts, axis=0), (rows, LANES))
        if rows < LANES:
            column = jnp.concatenate([column, jnp.zeros((LANES - rows, LANES), F32)], axis=0)
        moment[...] = column.T[0:8, :rows]
    for copy in sends:
        copy.wait()


def call(kernel, vmem_bytes, outs, scratch, *operands, far=0, far_out=0, copies=(1,), alias=None):
    operands = [
        pltpu.with_memory_space_constraint(value, pltpu.HBM) if k < far else value
        for k, value in enumerate(operands)
    ]
    whole = pl.BlockSpec(memory_space=pltpu.VMEM)
    away = pl.BlockSpec(memory_space=pltpu.HBM)
    scratch = [pltpu.VMEM(shape, dtype) for shape, dtype in scratch]
    scratch += [pltpu.SemaphoreType.DMA((count,)) for count in copies]
    return pl.pallas_call(
        kernel,
        out_shape=[
            pltpu.HBM(shape, dtype) if k < far_out else jax.ShapeDtypeStruct(shape, dtype)
            for k, (shape, dtype) in enumerate(outs)
        ],
        in_specs=[away] * far + [whole] * (len(operands) - far),
        out_specs=[away] * far_out + [whole] * (len(outs) - far_out),
        scratch_shapes=scratch,
        input_output_aliases=alias or {},
        compiler_params=pltpu.CompilerParams(vmem_limit_bytes=vmem_bytes),
    )(*operands)


def swap(value, axis, start, around):
    count = lax.axis_size(axis)
    couples = [(i, (i + 1) % count) for i in range(start, count, 2)]
    couples = [(i, j) for i, j in couples if j > i or around]
    return lax.ppermute(value, axis, couples + [(j, i) for i, j in couples])


def swap_halos(sec_first, sec_second, girth_first, girth_second):
    return (
        swap(girth_second, "girth", 1, True),
        swap(sec_first, "sec", 0, False),
        swap(sec_second, "sec", 1, False),
        swap(girth_first, "girth", 0, True),
    )


def sum_over(value, axis):
    count = lax.axis_size(axis)
    if count & (count - 1):
        return lax.psum(value, axis)
    parts = [
        lax.ppermute(value, axis, [(i, i ^ step) for i in range(count)])
        for step in range(count - 1, 0, -1)
    ]
    parts = [value] + parts[::-1]
    while len(parts) > 1:
        parts = [a + b for a, b in zip(parts[0::2], parts[1::2])]
    return parts[0]


def exchange(joints):
    blocks = joints.reshape(joints.shape[0] // 2, 2, LANES)
    blocks = lax.all_to_all(blocks, ("sec", "girth"), 0, 0, tiled=True)
    return blocks.reshape(joints.shape)


def local(displacement, velocity, stress, thickness, pressure, weld_from, weld_to, weld_stiff):
    rows, cols = thickness.shape
    _, devices, slots = weld_from.shape
    total = 2 * devices * slots
    girth_total = cols * lax.axis_size("girth")
    column = (lax.axis_index("girth") * cols + lax.iota(jnp.int32, cols)).astype(F32)
    height = jnp.sin(2.0 * jnp.pi / girth_total * (column + 0.5)) / girth_total
    height = jnp.broadcast_to(height[None, :], (8, cols))

    vmem_bytes = 8 * 1024 * 1024 + total * VMEM_PER_SLOT
    message = (devices * 2, LANES)
    edge = (8, LANES)
    strip = (16, cols)
    block = (FIELDS, rows, cols)
    stress_shape = (RESULTS, rows + PAD_ROWS, cols + LANES)
    plate_shape = (1, rows + PAD_ROWS, cols + LANES)
    slot_rows = (8, total)
    scratch = [
        (stress_shape, F32),
        (stress_shape, F32),
        ((FIELDS, rows + PAD_ROWS, cols + LANES), F32),
        ((FIELDS * rows, cols), F32),
        (block, F32),
        ((rows, cols), jnp.int32),
        ((rows, cols), F32),
    ]

    (payload, sec_first, sec_second, girth_first, girth_second,
     column_marks, row_marks, picked, spring) = call(
        start_kernel,
        vmem_bytes,
        [
            (message, F32), (strip, F32), (strip, F32), (edge, F32), (edge, F32),
            ((cols, total), BF16), ((rows, total), BF16), (slot_rows, F32), ((8, total // 2), F32),
        ],
        [
            (block, F32), ((RESULTS, rows, LANES), F32), ((RESULTS, rows, LANES), F32),
            ((RESULTS, 8, cols), F32), ((RESULTS, 8, cols), F32), ((rows, cols), jnp.int32),
            ((1, slots, devices), jnp.int32), ((1, slots, devices), jnp.int32),
            ((1, slots, devices), F32),
        ],
        displacement, stress, thickness,
        *[jnp.swapaxes(array, 1, 2) for array in (weld_from, weld_to, weld_stiff)],
        far=6,
        copies=(9,),
    )
    plate = None
    moved = 0.0
    for step in range(STEPS):
        first, last = step == 0, step == STEPS - 1
        incoming = exchange(payload)
        halos = swap_halos(sec_first, sec_second, girth_first, girth_second)
        outs = [(stress_shape, F32), (block, F32)]
        if first:
            outs += [(plate_shape, F32), (slot_rows, F32)]
        halo = (8, cols) if last else strip
        outs += [(edge, F32), (edge, F32), (halo, F32), (halo, F32)]
        if not last:
            outs += [(slot_rows, F32), (message, F32)]
        results = call(
            functools.partial(step_kernel, first, last),
            vmem_bytes,
            outs,
            scratch,
            stress, velocity, thickness, pressure,
            incoming, *halos,
            column_marks, row_marks, picked, spring,
            *([] if first else [plate]),
            far=4,
            far_out=2,
            copies=(6, 3 + rows // 32),
        )
        stress, velocity = results[:2]
        results = results[2:]
        moved = moved + velocity
        if first:
            plate, spring = results[:2]
            results = results[2:]
        girth_first, girth_second, sec_first, sec_second = results[:4]
        if not last:
            picked, payload = results[4:]

    halos = swap_halos(sec_first, sec_second, girth_first, girth_second)
    moved = displacement + time_step * moved
    velocity, moved = lax.optimization_barrier((velocity, moved))
    membrane, partial_moment = call(
        functools.partial(final_kernel, True),
        vmem_bytes,
        [((RESULTS, rows, cols), F32), ((8, rows), F32)],
        [
            ((3, rows, cols), F32), ((3, rows, cols), F32),
            ((2, rows + PAD_ROWS, cols + LANES), F32),
        ],
        stress, velocity, *halos, plate, height,
        far=2,
        far_out=1,
        copies=(4, rows // 16),
    )
    (stress,) = call(
        functools.partial(final_kernel, False),
        vmem_bytes,
        [((RESULTS, rows, cols), F32)],
        [
            ((5, rows, cols), F32), ((5, rows, cols), F32),
            ((3, rows + PAD_ROWS, cols + LANES), F32),
        ],
        stress, velocity, membrane, *halos, plate,
        far=3,
        far_out=1,
        copies=(4, rows // 16),
        alias={2: 0},
    )
    moment = sum_over(partial_moment, "girth")[0]
    return (moved, velocity, stress, moment)


def solution(mesh):
    in_specs = (
        P(None, "sec", "girth"),
        P(None, "sec", "girth"),
        P(None, "sec", "girth"),
        P("sec", "girth"),
        P("sec", "girth"),
        P(("sec", "girth"), None, None),
        P(("sec", "girth"), None, None),
        P(("sec", "girth"), None, None),
    )
    out_specs = (
        P(None, "sec", "girth"),
        P(None, "sec", "girth"),
        P(None, "sec", "girth"),
        P("sec"),
    )
    return jax.shard_map(local, mesh=mesh, in_specs=in_specs, out_specs=out_specs, check_vma=False)
```

```python
import functools

import jax
import jax.numpy as jnp
from jax import lax
from jax.experimental import pallas as pl
from jax.experimental.pallas import tpu as pltpu
from jax.sharding import PartitionSpec as P

STEPS = 3
CORNER_LANE = 112
PIECE = 24
FIELDS = 5
RESULTS = 8
PAD_ROWS = 8
LANES = 128
VMEM_PER_SLOT = 5 * 1024

young_modulus = 4.0
poisson_ratio = 0.3
plate_modulus = young_modulus / (1.0 - poisson_ratio * poisson_ratio)
shear_modulus = young_modulus / (2.0 * (1.0 + poisson_ratio))
shear_factor = 5.0 / 6.0
time_step = 0.2
spacing_mm = 50.0
rotary_share = 1.0 / 12.0

F32 = jnp.float32
BF16 = jnp.bfloat16


def split(values):
    high = values.astype(BF16)
    low = (values - high.astype(F32)).astype(BF16)
    return high, low


def dot(a, b, contract):
    return lax.dot_general(a, b, (contract, ((), ())), preferred_element_type=F32)


def slot_marks(devices, slots):
    total = devices * slots
    lane = lax.broadcasted_iota(jnp.int32, (devices, total), 1)
    device = lax.broadcasted_iota(jnp.int32, (devices, total), 0)
    by_device = (lane // slots == device).astype(F32).astype(BF16)
    lane = lax.broadcasted_iota(jnp.int32, (slots, total), 1)
    place = lax.broadcasted_iota(jnp.int32, (slots, total), 0)
    by_place = (lane % slots == place).astype(F32)
    return by_device, by_place


def expand(blocks, by_device, by_place, turned=False):
    slots, total = by_place.shape
    wide = dot(blocks, by_device, ((1 if turned else 0,), (0,)))
    wide = wide.reshape(wide.shape[0] // slots, slots, total) * by_place[None]
    return jnp.sum(wide, axis=1)


def collapse(rows, by_device, by_place):
    slots, _ = by_place.shape
    marks = by_place.astype(BF16)
    pieces = []
    for part in (0, 1):
        blocks = [split(row)[part] * marks for row in rows]
        blocks += [jnp.zeros_like(marks)] * (LANES // slots - len(rows))
        pieces.append(jnp.concatenate(blocks, axis=0))
    return dot(by_device, pieces[0], ((1,), (1,))) + dot(by_device, pieces[1], ((1,), (1,)))


def pick(fields, column_marks, row_marks):
    rows = fields[0].shape[0]
    parts = [split(field) for field in fields]
    high = jnp.concatenate([part[0] for part in parts], axis=0)
    low = jnp.concatenate([part[1] for part in parts], axis=0)
    by_column = dot(high, column_marks, ((1,), (0,))) + dot(low, column_marks, ((1,), (0,)))
    marks = row_marks.astype(F32)
    return [
        jnp.sum(by_column[rows * f : rows * (f + 1)] * marks, axis=0, keepdims=True)
        for f in range(len(fields))
    ]


def spread(pulls, column_marks, row_marks):
    high, low = split(pulls)
    total = None
    for part in (high, low):
        marked = jnp.concatenate(
            [part[f : f + 1] * row_marks for f in range(FIELDS)], axis=0
        )
        summed = dot(marked, column_marks, ((1,), (1,)))
        total = summed if total is None else total + summed
    return total


def place():
    sec, girth = lax.axis_index("sec"), lax.axis_index("girth")
    return sec, girth, lax.axis_size("sec"), lax.axis_size("girth")


def tile_of(ref, device):
    return ref[pl.ds(pl.multiple_of(device * 8, 8), 8), :]


def set_tile(ref, device, value):
    ref[pl.ds(pl.multiple_of(device * 8, 8), 8), :] = value


def corner_neighbours():
    sec, girth, secs, girths = place()
    me = sec * girths + girth
    out = []
    for step in (-1, 1):
        row = sec + step
        inside = jnp.logical_and(row >= 0, row < secs)
        for turn in (girths - 1, 1):
            device = row * girths + lax.rem(girth + turn, girths)
            out.append((jnp.where(inside, device, me), inside))
    return out


def edge_rows(columns):
    rows = columns[0][0].shape[0]
    lane = lax.broadcasted_iota(jnp.int32, (rows, LANES), 1)
    halves = [jnp.zeros((rows, LANES), F32), jnp.zeros((rows, LANES), F32)]
    for value, source, half, row in columns:
        moved = pltpu.roll(value, (row - source) % LANES, 1)
        halves[half] = jnp.where(lane == row, moved, halves[half])
    return jnp.concatenate(halves, axis=0).T


def edge_columns(left_tile, right_tile):
    stacked = jnp.concatenate(
        [left_tile, right_tile, jnp.zeros((LANES - 16, LANES), F32)], axis=0
    )
    turned = stacked.T
    return turned[: LANES // 2], turned[LANES // 2 :]


def edge_block(pieces):
    rows = pieces[0][0].shape[0]
    lane = lax.broadcasted_iota(jnp.int32, (rows, LANES), 1)
    block = jnp.zeros((rows, LANES), F32)
    for value, source, target in pieces:
        block = jnp.where(lane == target, pltpu.roll(value, (target - source) % LANES, 1), block)
    return block


def row_chunk(ref, f, start):
    count = ref.shape[1]
    if start < 0:
        return jnp.concatenate([ref[f, count + start : count, :], ref[f, 0 : 8 + start, :]], axis=0)
    if start + 8 > count:
        return jnp.concatenate([ref[f, start:count, :], ref[f, 0 : start + 8 - count, :]], axis=0)
    return ref[f, start : start + 8, :]


def difference_x(ref, f, start):
    return row_chunk(ref, f, start + 1) - row_chunk(ref, f, start - 1)


def difference_y(value):
    lanes = value.shape[1]
    return pltpu.roll(value, lanes - 1, 1) - pltpu.roll(value, 1, 1)


def radial_return(xx, yy, xy):
    offset = xx - 0.5 * yy
    square = offset * offset + 0.75 * yy * yy + 3.0 * xy * xy
    scale = lax.rsqrt(jnp.maximum(square, 1.0))
    return xx * scale, yy * scale, xy * scale


def membrane_chunk(along_x, along_y, stress):
    normal = 0.5 * time_step * plate_modulus
    skew = 0.5 * time_step * shear_modulus
    return radial_return(
        stress[0] + normal * (along_x[0] + poisson_ratio * along_y[1]),
        stress[1] + normal * (along_y[1] + poisson_ratio * along_x[0]),
        stress[2] + skew * (along_y[0] + along_x[1]),
    )


def plate_chunk(along_x, along_y, turns, stress, plate):
    arm = 0.5 * plate
    normal = 0.5 * time_step * plate_modulus * arm
    skew = 0.5 * time_step * shear_modulus
    bending = radial_return(
        stress[0] + normal * (along_x[1] + poisson_ratio * along_y[2]),
        stress[1] + normal * (along_y[2] + poisson_ratio * along_x[1]),
        stress[2] + (skew * arm) * (along_y[1] + along_x[2]),
    )
    return bending + (
        stress[3] + skew * (along_x[0] + 2.0 * turns[0]),
        stress[4] + skew * (along_y[0] + 2.0 * turns[1]),
    )


def differences(vel_ref, fields, start):
    current = [vel_ref[f, start : start + 8, :] for f in fields]
    along_x = [difference_x(vel_ref, f, start) for f in fields]
    return current, along_x, [difference_y(value) for value in current]


def stress_chunk(vel_ref, stress, plate, start):
    current, along_x, along_y = differences(vel_ref, range(FIELDS), start)
    membrane = membrane_chunk(along_x[:2], along_y[:2], stress[:3])
    return membrane + plate_chunk(along_x[2:], along_y[2:], current[3:], stress[3:], plate)


def resultants(stress, plate):
    arm = plate * plate * (1.0 / 6.0)
    shear = shear_factor * plate
    return (
        [plate * value for value in stress[0:3]]
        + [arm * value for value in stress[3:6]]
        + [shear * value for value in stress[6:8]]
    )


def force_chunk(res_ref, start, cols):
    def both(x, y):
        along_x = difference_x(res_ref, x, start)[:, :cols]
        along_y = difference_y(res_ref[y, start : start + 8, :])[:, :cols]
        return 0.5 * (along_x + along_y)

    return [
        both(0, 2),
        both(2, 1),
        both(6, 7),
        both(3, 5) - res_ref[6, start : start + 8, :cols],
        both(5, 4) - res_ref[7, start : start + 8, :cols],
    ]


def send_joints(payload, near, far, corners):
    devices = payload.shape[0] // 2
    payload[pl.ds(0, devices, stride=2), :] = near
    payload[pl.ds(1, devices, stride=2), :] = far
    row = lax.broadcasted_iota(jnp.int32, (8, LANES), 0)
    lane = lax.broadcasted_iota(jnp.int32, (8, LANES), 1)
    free = jnp.logical_and(lane >= CORNER_LANE, lane < CORNER_LANE + FIELDS)
    for (device, _), corner in zip(corner_neighbours(), corners):
        tile = lax.div(device, 4)
        here = jnp.logical_and(free, row == 2 * lax.rem(device, 4))
        set_tile(payload, tile, jnp.where(here, corner, tile_of(payload, tile)))


def in_order(axis, low, high):
    even = lax.rem(lax.axis_index(axis), 2) == 0
    return jnp.where(even, high, low), jnp.where(even, low, high)


def send_sides(pair, halo_rows):
    for ref, value in zip(pair, in_order("girth", halo_rows[0:8], halo_rows[8:16])):
        ref[...] = value


def send_ends(pair, low, high):
    for ref in pair:
        ref[...] = jnp.zeros(ref.shape, F32)
    start = 0
    for top, bottom in zip(low, high):
        count = top.shape[0]
        for ref, value in zip(pair, in_order("sec", top, bottom)):
            ref[start : start + count, :] = value
        start += count


def corner_of(incoming, device):
    row = lax.broadcasted_iota(jnp.int32, (8, LANES), 0)
    tile = tile_of(incoming, lax.div(device, 4))
    return jnp.sum(jnp.where(row == 2 * lax.rem(device, 4), tile, 0.0), axis=0, keepdims=True)


def fetch(done, pairs):
    copies = [
        pltpu.make_async_copy(source, target, done.at[k])
        for k, (source, target) in enumerate(pairs)
    ]
    for copy in copies:
        copy.start()
    return copies


def pieces(rows):
    return [slice(0, PIECE), slice(PIECE, 2 * PIECE), slice(2 * PIECE, rows)]


def start_kernel(
    disp_in, stress_in, thickness_in, from_in, to_in, stiff_in,
    payload, sec_first, sec_second, girth_first, girth_second,
    column_marks, row_marks, picked, spring,
    disp, stress_left, stress_right, stress_top, stress_bottom, thickness,
    weld_from, weld_to, weld_stiff, done,
):
    rows, cols = thickness.shape
    _, slots, devices = weld_from.shape
    sec_pair, girth_pair = (sec_first, sec_second), (girth_first, girth_second)
    copies = fetch(
        done,
        [
            (from_in, weld_from),
            (to_in, weld_to),
            (stiff_in, weld_stiff),
            (disp_in, disp),
            (thickness_in, thickness),
            (stress_in.at[:, :, 0:LANES], stress_left),
            (stress_in.at[:, :, cols - LANES : cols], stress_right),
            (stress_in.at[:, 0:8, :], stress_top),
            (stress_in.at[:, rows - 8 : rows, :], stress_bottom),
        ],
    )
    shift = cols.bit_length() - 1
    by_device, by_place = slot_marks(devices, slots)
    for copy in copies[:3]:
        copy.wait()
    near, far = weld_from[0], weld_to[0]
    stiff = jnp.where(near >= 0, weld_stiff[0], 0.0)
    index_parts = []
    for index in (near, far):
        index = jnp.maximum(index, 0)
        column = index & (cols - 1)
        index_parts += [index >> shift, column >> 1, column & 1]
    index_parts = [part.astype(F32).astype(BF16) for part in index_parts]
    index_parts += list(split(stiff))
    wide = [expand(part, by_device, by_place, turned=True) for part in index_parts]
    row_index = jnp.concatenate([wide[0], wide[3]], axis=1)
    column_index = jnp.concatenate([2.0 * wide[1] + wide[2], 2.0 * wide[4] + wide[5]], axis=1)
    stiff_row = wide[6] + wide[7]
    total = row_index.shape[1]
    spring[...] = jnp.broadcast_to(stiff_row, spring.shape)
    row_iota = lax.broadcasted_iota(jnp.int32, (rows, total), 0).astype(F32)
    row_hits = (row_iota == row_index).astype(F32).astype(BF16)
    row_marks[...] = row_hits
    for start in range(0, cols, 64):
        iota = (lax.broadcasted_iota(jnp.int32, (64, total), 0) + start).astype(F32)
        column_marks[start : start + 64, :] = (iota == column_index).astype(F32).astype(BF16)
    copies[3].wait()
    values = pick([disp[f] for f in range(FIELDS)], column_marks[...], row_hits)
    picked[...] = jnp.concatenate(values + [values[0]] * 3, axis=0)
    half = total // 2
    near_out = collapse([value[:, :half] for value in values] + [stiff_row], by_device, by_place)
    far_out = collapse([value[:, half:] for value in values], by_device, by_place)

    for copy in copies[4:]:
        copy.wait()
    plate = thickness[...].astype(F32) * (1.0 / spacing_mm)
    columns = []
    for f in range(RESULTS + 1):
        left = stress_left[f] if f < RESULTS else plate[:, 0:LANES]
        right = stress_right[f] if f < RESULTS else plate[:, cols - LANES :]
        columns.append((left, 0, f // 5, 2 + f % 5))
        columns.append((right, LANES - 1, f // 5, 10 + f % 5))
    send_sides(girth_pair, edge_rows(columns))
    send_joints(payload, near_out, far_out, [])
    send_ends(
        sec_pair,
        [stress_top[f, 0:1, :] for f in range(RESULTS)] + [plate[0:1, :]],
        [stress_bottom[f, 7:8, :] for f in range(RESULTS)] + [plate[rows - 1 : rows, :]],
    )


def fill_halo(ref, f, above, below, sides, corner):
    rows, cols = ref.shape[1] - PAD_ROWS, ref.shape[2] - LANES
    depth = above.shape[0]
    ref[f, rows:, :cols] = jnp.concatenate(
        [below, jnp.zeros((PAD_ROWS - 2 * depth, cols), F32), above], axis=0
    )
    ref[f, :rows, cols:] = sides
    ref[f, rows:, cols:] = corner


def load_velocity(vel_ext, incoming, above, below, left, right):
    first, second = edge_columns(left, right)
    row = lax.broadcasted_iota(jnp.int32, (8, LANES), 0)
    corner_tiles = [
        jnp.broadcast_to(jnp.where(inside, corner_of(incoming, device), 0.0), (8, LANES))
        for device, inside in corner_neighbours()
    ]
    for f in range(FIELDS):
        sides = edge_block(
            [
                (first, 2 + f, LANES - 2),
                (second, 2 + f, LANES - 1),
                (first, 10 + f, 0),
                (second, 10 + f, 1),
            ]
        )
        upper = edge_block([(corner_tiles[0], CORNER_LANE + f, LANES - 1), (corner_tiles[1], CORNER_LANE + f, 0)])
        lower = edge_block([(corner_tiles[2], CORNER_LANE + f, LANES - 1), (corner_tiles[3], CORNER_LANE + f, 0)])
        corner = jnp.where(row == 0, lower, jnp.where(row == 7, upper, 0.0))
        fill_halo(
            vel_ext, f, above[2 * f : 2 * f + 2, :], below[2 * f : 2 * f + 2, :], sides, corner
        )


def load_stress(stress_ext, plate_ext, thickness, above, below, left, right):
    rows, cols = thickness.shape
    halves = edge_columns(left, right)
    plate_ext[0, :rows, :cols] = thickness[...].astype(F32) * (1.0 / spacing_mm)
    empty = jnp.zeros((PAD_ROWS, LANES), F32)
    for f in range(RESULTS + 1):
        lane = 2 + f % 5
        half = halves[f // 5]
        sides = edge_block([(half, lane, LANES - 1), (half, 8 + lane, 0)])
        ref, k = (stress_ext, f) if f < RESULTS else (plate_ext, 0)
        fill_halo(ref, k, above[f : f + 1, :], below[f : f + 1, :], sides, empty)


def step_kernel(first, last, *refs):
    (stress_in, velocity_in, disp_in, thickness_in, pressure_in) = refs[:5]
    if first:
        out = refs[14:]
    else:
        plate_ext = refs[14]
        out = refs[15:]
    (incoming, sec_second, sec_first, girth_second, girth_first,
     column_marks, row_marks, picked, spring) = refs[5:14]
    stress_out, velocity_out, disp_out = out[:3]
    out = out[3:]
    if first:
        plate_ext, spring_out = out[:2]
        out = out[2:]
    girth_pair, sec_pair = out[0:2], out[2:4]
    out = out[4:]
    if not last:
        picked_out, payload = out[:2]
        out = out[2:]
    res_ext, vel_ext, weld, thickness, pressure = out[:5]
    out = out[5:]
    if last:
        stress_ext, velocity, disp = stress_out, velocity_out, disp_out
    else:
        stress_ext, velocity, disp = out[:3]
        out = out[3:]
    got, sent = out

    _, rows, cols = velocity.shape
    devices = incoming.shape[0] // 2
    total = picked.shape[1]
    half = total // 2
    by_device, by_place = slot_marks(devices, half // devices)
    if first:
        pairs = [(thickness_in, thickness)]
        pairs += [
            (stress_in.at[:, part, :], stress_ext.at[:, part, 0:cols]) for part in pieces(rows)
        ]
        pairs += [(velocity_in, velocity)]
    else:
        pairs = [(velocity_in, vel_ext.at[:, 0:rows, 0:cols])]
        pairs += [
            (stress_in.at[:, part, :], stress_ext.at[:, part, :])
            for part in pieces(rows + PAD_ROWS)
        ]
    pairs += [(disp_in, disp), (pressure_in, pressure)]
    copies = fetch(got, pairs)
    sends = []

    def send(source, target):
        if last:
            return
        copy = pltpu.make_async_copy(source, target, sent.at[len(sends)])
        copy.start()
        sends.append(copy)

    other = []
    for row in (1, 0):
        high, low = split(incoming[pl.ds(row, devices, stride=2), :])
        other.append(expand(high, by_device, by_place) + expand(low, by_device, by_place))
    if first:
        stiffness = jnp.concatenate([spring[0:1, :], other[1][5:6]], axis=1)
        spring_out[...] = jnp.broadcast_to(stiffness, spring_out.shape)
    else:
        stiffness = spring[0:1, :]
    field = lax.broadcasted_iota(jnp.int32, (8, total), 0)
    scale = jnp.where(field < 3, 1.0, rotary_share) * stiffness
    pulls = scale * (jnp.concatenate(other, axis=1) - picked[...])
    weld[...] = spread(pulls, column_marks[...], row_marks[...])

    above, below = in_order("sec", sec_first[...], sec_second[...])
    left, right = in_order("girth", girth_first[...], girth_second[...])
    copies[0].wait()
    if first:
        load_stress(stress_ext, plate_ext, thickness, above, below, left, right)
    else:
        load_velocity(vel_ext, incoming, above, below, left, right)
    for start in range(0, rows + PAD_ROWS, 8):
        if start in (0, PIECE, 2 * PIECE):
            copies[1 + start // PIECE].wait()
        plate = plate_ext[0, start : start + 8, :]
        chunk = [stress_ext[k, start : start + 8, :] for k in range(RESULTS)]
        if not first:
            chunk = stress_chunk(vel_ext, chunk, plate, start)
            for k, value in enumerate(chunk):
                stress_ext[k, start : start + 8, :] = value
        for k, value in enumerate(resultants(chunk, plate)):
            res_ext[k, start : start + 8, :] = value
        for part in pieces(rows + PAD_ROWS):
            if part.stop == start + 8:
                send(stress_ext.at[:, part, :], stress_out.at[:, part, :])
    for copy in copies[4:]:
        copy.wait()

    for start in range(0, rows, 8):
        part = slice(start, start + 8)
        plate = plate_ext[0, part, :cols]
        linear = time_step / plate
        angular = (12.0 * linear) / (1.0 + plate * plate)
        force = force_chunk(res_ext, start, cols)
        force[2] = force[2] + pressure[part, :]
        for f in range(FIELDS):
            joined = force[f] + weld[f * rows + start : f * rows + start + 8, :]
            before = velocity[f, part, :] if first else vel_ext[f, part, :cols]
            speed = before + (linear if f < 3 else angular) * joined
            velocity[f, part, :] = speed
            disp[f, part, :] = disp[f, part, :] + time_step * speed
        if start % 32 == 24:
            done = slice(start - 24, start + 8)
            for source, target in ((velocity, velocity_out), (disp, disp_out)):
                send(source.at[:, done, :], target.at[:, done, :])

    ends = (cols - LANES, cols)
    if last:
        columns = []
        for f in range(FIELDS):
            columns.append((velocity[f, :, 0:LANES], 0, 0, f))
            columns.append((velocity[f, :, ends[0] : ends[1]], LANES - 1, 0, 8 + f))
        send_sides(girth_pair, edge_rows(columns))
        send_ends(
            sec_pair,
            [velocity[f, 0:1, :] for f in range(FIELDS)],
            [velocity[f, rows - 1 : rows, :] for f in range(FIELDS)],
        )
        for copy in sends:
            copy.wait()
        return
    values = pick([disp[f] for f in range(FIELDS)], column_marks[...], row_marks[...])
    picked_out[...] = jnp.concatenate(values + [values[0]] * 3, axis=0)
    near_out = collapse([value[:, :half] for value in values], by_device, by_place)
    far_out = collapse([value[:, half:] for value in values], by_device, by_place)
    columns = []
    for f in range(FIELDS):
        left_lanes = velocity[f, :, 0:LANES]
        right_lanes = velocity[f, :, ends[0] : ends[1]]
        for depth in (0, 1):
            columns.append((left_lanes, depth, depth, 2 + f))
            columns.append((right_lanes, LANES - 2 + depth, depth, 10 + f))
    corners = []
    lane = lax.broadcasted_iota(jnp.int32, (8, LANES), 1)
    for row in (0, rows - 1):
        tile = slice(row // 8 * 8, row // 8 * 8 + 8)
        for side in (0, 1):
            value = jnp.zeros((8, LANES), F32)
            for f in range(FIELDS):
                part = velocity[f, tile, ends[0] : ends[1]] if side else velocity[f, tile, 0:LANES]
                source = LANES - 1 if side else 0
                target = CORNER_LANE + f
                value = jnp.where(lane == target, pltpu.roll(part, (target - source) % LANES, 1), value)
            corners.append(jnp.broadcast_to(value[row % 8 : row % 8 + 1], (8, LANES)))
    send_sides(girth_pair, edge_rows(columns))
    send_joints(payload, near_out, far_out, corners)
    send_ends(
        sec_pair,
        [velocity[f, 0:2, :] for f in range(FIELDS)],
        [velocity[f, rows - 2 : rows, :] for f in range(FIELDS)],
    )
    for copy in sends:
        copy.wait()


def final_kernel(membrane, *refs):
    if membrane:
        stress, velocity = refs[:2]
        sec_second, sec_first, girth_second, girth_first, plate_ext, height = refs[2:8]
        stress_out, moment = refs[8:10]
        refs = refs[10:]
    else:
        stress, velocity, disp = refs[1:4]
        sec_second, sec_first, girth_second, girth_first, plate_ext = refs[4:9]
        stress_out, velocity_out, disp_out = refs[9:12]
        refs = refs[12:]
    made, vel_ext, sent = refs
    _, rows, cols = velocity.shape
    fields = range(0, 2) if membrane else range(2, FIELDS)
    kinds = range(0, 3) if membrane else range(3, RESULTS)
    sends = []

    def send(source, target):
        copy = pltpu.make_async_copy(source, target, sent.at[len(sends)])
        copy.start()
        sends.append(copy)

    if not membrane:
        send(velocity, velocity_out)
        send(disp, disp_out)
    above, below = in_order("sec", sec_first[...], sec_second[...])
    left, right = in_order("girth", girth_first[...], girth_second[...])
    first, _ = edge_columns(left, right)
    empty = jnp.zeros((PAD_ROWS, LANES), F32)
    for k, f in enumerate(fields):
        vel_ext[k, :rows, :cols] = velocity[f]
        sides = edge_block([(first, f, LANES - 1), (first, 8 + f, 0)])
        fill_halo(vel_ext, k, above[f : f + 1, :], below[f : f + 1, :], sides, empty)
    parts = []
    for start in range(0, rows, 8):
        part = slice(start, start + 8)
        chunk = [stress[k, part, :cols] for k in kinds]
        plate = plate_ext[0, part, :cols]
        current, along_x, along_y = [
            [value[:, :cols] for value in values]
            for values in differences(vel_ext, range(len(fields)), start)
        ]
        if membrane:
            chunk = membrane_chunk(along_x, along_y, chunk)
            weighted = plate * chunk[0] * height[0:1, :]
            parts.append(jnp.sum(weighted, axis=1, keepdims=True))
        else:
            chunk = plate_chunk(along_x, along_y, current[1:], chunk, plate)
        for k, value in enumerate(chunk):
            made[k, part, :] = value
        if start % 16 == 8:
            done = slice(start - 8, start + 8)
            send(made.at[:, done, :], stress_out.at[kinds.start : kinds.stop, done, :])
    if membrane:
        column = jnp.broadcast_to(jnp.concatenate(parts, axis=0), (rows, LANES))
        if rows < LANES:
            column = jnp.concatenate([column, jnp.zeros((LANES - rows, LANES), F32)], axis=0)
        moment[...] = column.T[0:1, :rows]
    for copy in sends:
        copy.wait()


def call(
    kernel, vmem_bytes, outs, scratch, *operands, far=0, kept=0, far_out=0, kept_out=0,
    copies=(1,), alias=None,
):
    def placed(k, away, here):
        return pltpu.HBM if k < away else pltpu.VMEM if k < away + here else None

    operands = [
        value if placed(k, far, kept) is None
        else pltpu.with_memory_space_constraint(value, placed(k, far, kept))
        for k, value in enumerate(operands)
    ]
    results = [
        (placed(k, far_out, kept_out) or jax.ShapeDtypeStruct)(shape, dtype)
        for k, (shape, dtype) in enumerate(outs)
    ]
    whole = pl.BlockSpec(memory_space=pltpu.VMEM)
    away = pl.BlockSpec(memory_space=pltpu.HBM)
    scratch = [pltpu.VMEM(shape, dtype) for shape, dtype in scratch]
    scratch += [pltpu.SemaphoreType.DMA((count,)) for count in copies]
    return pl.pallas_call(
        kernel,
        out_shape=results,
        in_specs=[away] * far + [whole] * (len(operands) - far),
        out_specs=[away] * far_out + [whole] * (len(outs) - far_out),
        scratch_shapes=scratch,
        input_output_aliases=alias or {},
        compiler_params=pltpu.CompilerParams(vmem_limit_bytes=vmem_bytes),
    )(*operands)


def swap(pair, axis, around):
    count = lax.axis_size(axis)
    out = []
    for start, value in reversed(list(enumerate(pair))):
        couples = [(i, (i + 1) % count) for i in range(start, count, 2)]
        couples = [(i, j) for i, j in couples if j > i or around]
        out.append(lax.ppermute(value, axis, couples + [(j, i) for i, j in couples]))
    return out


def sum_over(value, axis):
    count = lax.axis_size(axis)
    if count & (count - 1):
        return lax.psum(value, axis)
    parts = [
        lax.ppermute(value, axis, [(i, i ^ step) for i in range(count)])
        for step in range(count - 1, 0, -1)
    ]
    parts = [value] + parts[::-1]
    while len(parts) > 1:
        parts = [a + b for a, b in zip(parts[0::2], parts[1::2])]
    return parts[0]


def exchange(joints):
    blocks = joints.reshape(joints.shape[0] // 2, 2, LANES)
    blocks = lax.all_to_all(blocks, ("sec", "girth"), 0, 0, tiled=True)
    return blocks.reshape(joints.shape)


def local(displacement, velocity, stress, thickness, pressure, weld_from, weld_to, weld_stiff):
    rows, cols = thickness.shape
    _, devices, slots = weld_from.shape
    total = 2 * devices * slots
    girth_total = cols * lax.axis_size("girth")
    column = (lax.axis_index("girth") * cols + lax.iota(jnp.int32, cols)).astype(F32)
    height = jnp.sin(2.0 * jnp.pi / girth_total * (column + 0.5)) / girth_total
    height = jnp.broadcast_to(height[None, :], (8, cols))

    vmem_bytes = 8 * 1024 * 1024 + total * VMEM_PER_SLOT
    message = (devices * 2, LANES)
    edge = (8, LANES)
    strip = (16, cols)
    block = (FIELDS, rows, cols)
    stress_shape = (RESULTS, rows + PAD_ROWS, cols + LANES)
    plate_shape = (1, rows + PAD_ROWS, cols + LANES)
    slot_rows = (8, total)
    scratch = [
        (stress_shape, F32),
        ((FIELDS, rows + PAD_ROWS, cols + LANES), F32),
        ((FIELDS * rows, cols), F32),
        ((rows, cols), jnp.int32),
        ((rows, cols), F32),
    ]

    (payload, sec_first, sec_second, girth_first, girth_second,
     column_marks, row_marks, picked, spring) = call(
        start_kernel,
        vmem_bytes,
        [
            (message, F32), (strip, F32), (strip, F32), (edge, F32), (edge, F32),
            ((cols, total), BF16), ((rows, total), BF16), (slot_rows, F32), ((8, total // 2), F32),
        ],
        [
            (block, F32), ((RESULTS, rows, LANES), F32), ((RESULTS, rows, LANES), F32),
            ((RESULTS, 8, cols), F32), ((RESULTS, 8, cols), F32), ((rows, cols), jnp.int32),
            ((1, slots, devices), jnp.int32), ((1, slots, devices), jnp.int32),
            ((1, slots, devices), F32),
        ],
        displacement, stress, thickness,
        *[jnp.swapaxes(array, 1, 2) for array in (weld_from, weld_to, weld_stiff)],
        far=6,
        copies=(9,),
    )
    plate = None
    for step in range(STEPS):
        first, last = step == 0, step == STEPS - 1
        incoming = exchange(payload)
        ends = swap((sec_first, sec_second), "sec", False)
        sides = swap((girth_first, girth_second), "girth", True)
        outs = [(stress_shape, F32), (block, F32), (block, F32)]
        if first:
            outs += [(plate_shape, F32), (slot_rows, F32)]
        halo = (8, cols) if last else strip
        outs += [(edge, F32), (edge, F32), (halo, F32), (halo, F32)]
        if not last:
            outs += [(slot_rows, F32), (message, F32)]
        results = call(
            functools.partial(step_kernel, first, last),
            vmem_bytes,
            outs,
            scratch + ([] if last else outs[:3]),
            stress, velocity, displacement, thickness, pressure,
            incoming, *ends, *sides,
            column_marks, row_marks, picked, spring,
            *([] if first else [plate]),
            far=5,
            far_out=0 if last else 3,
            kept_out=3 if last else 0,
            copies=(7, 3 + 2 * (rows // 32)),
        )
        stress, velocity, displacement = results[:3]
        results = results[3:]
        if first:
            plate, spring = results[:2]
            results = results[2:]
        girth_first, girth_second, sec_first, sec_second = results[:4]
        if not last:
            picked, payload = results[4:]

    ends = swap((sec_first, sec_second), "sec", False)
    sides = swap((girth_first, girth_second), "girth", True)
    membrane, partial_moment = call(
        functools.partial(final_kernel, True),
        vmem_bytes,
        [((RESULTS, rows, cols), F32), ((1, rows), F32)],
        [((3, rows, cols), F32), ((2, rows + PAD_ROWS, cols + LANES), F32)],
        stress, velocity, *ends, *sides, plate, height,
        kept=2,
        far_out=1,
        copies=(rows // 16,),
    )
    stress, velocity, displacement = call(
        functools.partial(final_kernel, False),
        vmem_bytes,
        [((RESULTS, rows, cols), F32), (block, F32), (block, F32)],
        [((5, rows, cols), F32), ((3, rows + PAD_ROWS, cols + LANES), F32)],
        membrane, stress, velocity, displacement, *ends, *sides, plate,
        far=1,
        kept=3,
        far_out=3,
        copies=(2 + rows // 16,),
        alias={0: 0},
    )
    moment = sum_over(partial_moment, "girth")[0]
    return (displacement, velocity, stress, moment)


def solution(mesh):
    in_specs = (
        P(None, "sec", "girth"),
        P(None, "sec", "girth"),
        P(None, "sec", "girth"),
        P("sec", "girth"),
        P("sec", "girth"),
        P(("sec", "girth"), None, None),
        P(("sec", "girth"), None, None),
        P(("sec", "girth"), None, None),
    )
    out_specs = (
        P(None, "sec", "girth"),
        P(None, "sec", "girth"),
        P(None, "sec", "girth"),
        P("sec"),
    )
    return jax.shard_map(local, mesh=mesh, in_specs=in_specs, out_specs=out_specs, check_vma=False)
```

```python
import functools

import jax
import jax.numpy as jnp
from jax import lax
from jax.experimental import pallas as pl
from jax.experimental.pallas import tpu as pltpu
from jax.sharding import PartitionSpec as P

STEPS = 3
CORNER_LANE = 112
PIECE = 24
FIELDS = 5
RESULTS = 8
PAD_ROWS = 8
LANES = 128
VMEM_PER_SLOT = 5 * 1024

young_modulus = 4.0
poisson_ratio = 0.3
plate_modulus = young_modulus / (1.0 - poisson_ratio * poisson_ratio)
shear_modulus = young_modulus / (2.0 * (1.0 + poisson_ratio))
shear_factor = 5.0 / 6.0
time_step = 0.2
spacing_mm = 50.0
rotary_share = 1.0 / 12.0

F32 = jnp.float32
BF16 = jnp.bfloat16


def split(values):
    high = values.astype(BF16)
    low = (values - high.astype(F32)).astype(BF16)
    return high, low


def dot(a, b, contract):
    return lax.dot_general(a, b, (contract, ((), ())), preferred_element_type=F32)


def slot_marks(devices, slots):
    total = devices * slots
    lane = lax.broadcasted_iota(jnp.int32, (devices, total), 1)
    device = lax.broadcasted_iota(jnp.int32, (devices, total), 0)
    by_device = (lane // slots == device).astype(F32).astype(BF16)
    lane = lax.broadcasted_iota(jnp.int32, (slots, total), 1)
    place = lax.broadcasted_iota(jnp.int32, (slots, total), 0)
    by_place = (lane % slots == place).astype(F32)
    return by_device, by_place


def expand(blocks, by_device, by_place, turned=False):
    slots, total = by_place.shape
    wide = dot(blocks, by_device, ((1 if turned else 0,), (0,)))
    wide = wide.reshape(wide.shape[0] // slots, slots, total) * by_place[None]
    return jnp.sum(wide, axis=1)


def collapse(rows, by_device, by_place):
    slots, _ = by_place.shape
    marks = by_place.astype(BF16)
    pieces = []
    for part in (0, 1):
        blocks = [split(row)[part] * marks for row in rows]
        blocks += [jnp.zeros_like(marks)] * (LANES // slots - len(rows))
        pieces.append(jnp.concatenate(blocks, axis=0))
    return dot(by_device, pieces[0], ((1,), (1,))) + dot(by_device, pieces[1], ((1,), (1,)))


def pick(fields, column_marks, row_marks):
    rows = fields[0].shape[0]
    parts = [split(field) for field in fields]
    high = jnp.concatenate([part[0] for part in parts], axis=0)
    low = jnp.concatenate([part[1] for part in parts], axis=0)
    by_column = dot(high, column_marks, ((1,), (0,))) + dot(low, column_marks, ((1,), (0,)))
    marks = row_marks.astype(F32)
    return [
        jnp.sum(by_column[rows * f : rows * (f + 1)] * marks, axis=0, keepdims=True)
        for f in range(len(fields))
    ]


def spread(pulls, column_marks, row_marks):
    high, low = split(pulls)
    total = None
    for part in (high, low):
        marked = jnp.concatenate(
            [part[f : f + 1] * row_marks for f in range(FIELDS)], axis=0
        )
        summed = dot(marked, column_marks, ((1,), (1,)))
        total = summed if total is None else total + summed
    return total


def place():
    sec, girth = lax.axis_index("sec"), lax.axis_index("girth")
    return sec, girth, lax.axis_size("sec"), lax.axis_size("girth")


def tile_of(ref, device):
    return ref[pl.ds(pl.multiple_of(device * 8, 8), 8), :]


def set_tile(ref, device, value):
    ref[pl.ds(pl.multiple_of(device * 8, 8), 8), :] = value


def corner_neighbours():
    sec, girth, secs, girths = place()
    me = sec * girths + girth
    out = []
    for step in (-1, 1):
        row = sec + step
        inside = jnp.logical_and(row >= 0, row < secs)
        for turn in (girths - 1, 1):
            device = row * girths + lax.rem(girth + turn, girths)
            out.append((jnp.where(inside, device, me), inside))
    return out


def edge_rows(columns):
    rows = columns[0][0].shape[0]
    lane = lax.broadcasted_iota(jnp.int32, (rows, LANES), 1)
    halves = [jnp.zeros((rows, LANES), F32), jnp.zeros((rows, LANES), F32)]
    for value, source, half, row in columns:
        moved = pltpu.roll(value, (row - source) % LANES, 1)
        halves[half] = jnp.where(lane == row, moved, halves[half])
    return jnp.concatenate(halves, axis=0).T


def edge_columns(left_tile, right_tile):
    stacked = jnp.concatenate(
        [left_tile, right_tile, jnp.zeros((LANES - 16, LANES), F32)], axis=0
    )
    turned = stacked.T
    return turned[: LANES // 2], turned[LANES // 2 :]


def edge_block(pieces):
    rows = pieces[0][0].shape[0]
    lane = lax.broadcasted_iota(jnp.int32, (rows, LANES), 1)
    block = jnp.zeros((rows, LANES), F32)
    for value, source, target in pieces:
        block = jnp.where(lane == target, pltpu.roll(value, (target - source) % LANES, 1), block)
    return block


def row_chunk(ref, f, start):
    count = ref.shape[1]
    if start < 0:
        return jnp.concatenate([ref[f, count + start : count, :], ref[f, 0 : 8 + start, :]], axis=0)
    if start + 8 > count:
        return jnp.concatenate([ref[f, start:count, :], ref[f, 0 : start + 8 - count, :]], axis=0)
    return ref[f, start : start + 8, :]


def difference_x(ref, f, start):
    return row_chunk(ref, f, start + 1) - row_chunk(ref, f, start - 1)


def difference_y(value):
    lanes = value.shape[1]
    return pltpu.roll(value, lanes - 1, 1) - pltpu.roll(value, 1, 1)


def radial_return(xx, yy, xy):
    offset = xx - 0.5 * yy
    square = offset * offset + 0.75 * yy * yy + 3.0 * xy * xy
    scale = lax.rsqrt(jnp.maximum(square, 1.0))
    return xx * scale, yy * scale, xy * scale


def membrane_chunk(along_x, along_y, stress):
    normal = 0.5 * time_step * plate_modulus
    skew = 0.5 * time_step * shear_modulus
    return radial_return(
        stress[0] + normal * (along_x[0] + poisson_ratio * along_y[1]),
        stress[1] + normal * (along_y[1] + poisson_ratio * along_x[0]),
        stress[2] + skew * (along_y[0] + along_x[1]),
    )


def plate_chunk(along_x, along_y, turns, stress, plate):
    arm = 0.5 * plate
    normal = 0.5 * time_step * plate_modulus * arm
    skew = 0.5 * time_step * shear_modulus
    bending = radial_return(
        stress[0] + normal * (along_x[1] + poisson_ratio * along_y[2]),
        stress[1] + normal * (along_y[2] + poisson_ratio * along_x[1]),
        stress[2] + (skew * arm) * (along_y[1] + along_x[2]),
    )
    return bending + (
        stress[3] + skew * (along_x[0] + 2.0 * turns[0]),
        stress[4] + skew * (along_y[0] + 2.0 * turns[1]),
    )


def differences(vel_ref, fields, start):
    current = [vel_ref[f, start : start + 8, :] for f in fields]
    along_x = [difference_x(vel_ref, f, start) for f in fields]
    return current, along_x, [difference_y(value) for value in current]


def stress_chunk(vel_ref, stress, plate, start):
    current, along_x, along_y = differences(vel_ref, range(FIELDS), start)
    membrane = membrane_chunk(along_x[:2], along_y[:2], stress[:3])
    return membrane + plate_chunk(along_x[2:], along_y[2:], current[3:], stress[3:], plate)


def resultants(stress, plate):
    arm = plate * plate * (1.0 / 6.0)
    shear = shear_factor * plate
    return (
        [plate * value for value in stress[0:3]]
        + [arm * value for value in stress[3:6]]
        + [shear * value for value in stress[6:8]]
    )


def force_chunk(res_ref, start, cols):
    def both(x, y):
        along_x = difference_x(res_ref, x, start)[:, :cols]
        along_y = difference_y(res_ref[y, start : start + 8, :])[:, :cols]
        return 0.5 * (along_x + along_y)

    return [
        both(0, 2),
        both(2, 1),
        both(6, 7),
        both(3, 5) - res_ref[6, start : start + 8, :cols],
        both(5, 4) - res_ref[7, start : start + 8, :cols],
    ]


def send_joints(payload, near, far, corners):
    devices = payload.shape[0] // 2
    payload[pl.ds(0, devices, stride=2), :] = near
    payload[pl.ds(1, devices, stride=2), :] = far
    row = lax.broadcasted_iota(jnp.int32, (8, LANES), 0)
    lane = lax.broadcasted_iota(jnp.int32, (8, LANES), 1)
    free = jnp.logical_and(lane >= CORNER_LANE, lane < CORNER_LANE + FIELDS)
    for (device, _), corner in zip(corner_neighbours(), corners):
        tile = lax.div(device, 4)
        here = jnp.logical_and(free, row == 2 * lax.rem(device, 4))
        set_tile(payload, tile, jnp.where(here, corner, tile_of(payload, tile)))


def in_order(axis, low, high):
    even = lax.rem(lax.axis_index(axis), 2) == 0
    return jnp.where(even, high, low), jnp.where(even, low, high)


def send_sides(pair, halo_rows):
    for ref, value in zip(pair, in_order("girth", halo_rows[0:8], halo_rows[8:16])):
        ref[...] = value


def send_ends(pair, low, high):
    for ref in pair:
        ref[...] = jnp.zeros(ref.shape, F32)
    start = 0
    for top, bottom in zip(low, high):
        count = top.shape[0]
        for ref, value in zip(pair, in_order("sec", top, bottom)):
            ref[start : start + count, :] = value
        start += count


def corner_of(incoming, device):
    row = lax.broadcasted_iota(jnp.int32, (8, LANES), 0)
    tile = tile_of(incoming, lax.div(device, 4))
    return jnp.sum(jnp.where(row == 2 * lax.rem(device, 4), tile, 0.0), axis=0, keepdims=True)


def fetch(done, pairs):
    copies = [
        pltpu.make_async_copy(source, target, done.at[k])
        for k, (source, target) in enumerate(pairs)
    ]
    for copy in copies:
        copy.start()
    return copies


def pieces(rows):
    return [slice(0, PIECE), slice(PIECE, 2 * PIECE), slice(2 * PIECE, rows)]


def start_kernel(
    disp_in, stress_in, thickness_in, from_in, to_in, stiff_in,
    payload, sec_first, sec_second, girth_first, girth_second,
    column_marks, row_marks, picked, spring,
    disp, stress_left, stress_right, stress_top, stress_bottom, thickness,
    weld_from, weld_to, weld_stiff, done,
):
    rows, cols = thickness.shape
    _, slots, devices = weld_from.shape
    sec_pair, girth_pair = (sec_first, sec_second), (girth_first, girth_second)
    copies = fetch(
        done,
        [
            (from_in, weld_from),
            (to_in, weld_to),
            (stiff_in, weld_stiff),
            (disp_in, disp),
            (thickness_in, thickness),
            (stress_in.at[:, :, 0:LANES], stress_left),
            (stress_in.at[:, :, cols - LANES : cols], stress_right),
            (stress_in.at[:, 0:8, :], stress_top),
            (stress_in.at[:, rows - 8 : rows, :], stress_bottom),
        ],
    )
    shift = cols.bit_length() - 1
    by_device, by_place = slot_marks(devices, slots)
    for copy in copies[:3]:
        copy.wait()
    near, far = weld_from[0], weld_to[0]
    stiff = jnp.where(near >= 0, weld_stiff[0], 0.0)
    index_parts = []
    for index in (near, far):
        index = jnp.maximum(index, 0)
        column = index & (cols - 1)
        index_parts += [index >> shift, column >> 1, column & 1]
    index_parts = [part.astype(F32).astype(BF16) for part in index_parts]
    index_parts += list(split(stiff))
    wide = [expand(part, by_device, by_place, turned=True) for part in index_parts]
    row_index = jnp.concatenate([wide[0], wide[3]], axis=1)
    column_index = jnp.concatenate([2.0 * wide[1] + wide[2], 2.0 * wide[4] + wide[5]], axis=1)
    stiff_row = wide[6] + wide[7]
    total = row_index.shape[1]
    spring[...] = jnp.broadcast_to(stiff_row, spring.shape)
    row_iota = lax.broadcasted_iota(jnp.int32, (rows, total), 0).astype(F32)
    row_hits = (row_iota == row_index).astype(F32).astype(BF16)
    row_marks[...] = row_hits
    for start in range(0, cols, 64):
        iota = (lax.broadcasted_iota(jnp.int32, (64, total), 0) + start).astype(F32)
        column_marks[start : start + 64, :] = (iota == column_index).astype(F32).astype(BF16)
    copies[3].wait()
    values = pick([disp[f] for f in range(FIELDS)], column_marks[...], row_hits)
    picked[...] = jnp.concatenate(values + [values[0]] * 3, axis=0)
    half = total // 2
    near_out = collapse([value[:, :half] for value in values] + [stiff_row], by_device, by_place)
    far_out = collapse([value[:, half:] for value in values], by_device, by_place)

    for copy in copies[4:]:
        copy.wait()
    plate = thickness[...].astype(F32) * (1.0 / spacing_mm)
    columns = []
    for f in range(RESULTS + 1):
        left = stress_left[f] if f < RESULTS else plate[:, 0:LANES]
        right = stress_right[f] if f < RESULTS else plate[:, cols - LANES :]
        columns.append((left, 0, f // 5, 2 + f % 5))
        columns.append((right, LANES - 1, f // 5, 10 + f % 5))
    send_sides(girth_pair, edge_rows(columns))
    send_joints(payload, near_out, far_out, [])
    send_ends(
        sec_pair,
        [stress_top[f, 0:1, :] for f in range(RESULTS)] + [plate[0:1, :]],
        [stress_bottom[f, 7:8, :] for f in range(RESULTS)] + [plate[rows - 1 : rows, :]],
    )


def fill_halo(ref, f, above, below, sides, corner):
    rows, cols = ref.shape[1] - PAD_ROWS, ref.shape[2] - LANES
    depth = above.shape[0]
    ref[f, rows:, :cols] = jnp.concatenate(
        [below, jnp.zeros((PAD_ROWS - 2 * depth, cols), F32), above], axis=0
    )
    ref[f, :rows, cols:] = sides
    ref[f, rows:, cols:] = corner


def load_velocity(vel_ext, velocity, incoming, above, below, left, right):
    first, second = edge_columns(left, right)
    row = lax.broadcasted_iota(jnp.int32, (8, LANES), 0)
    corner_tiles = [
        jnp.broadcast_to(jnp.where(inside, corner_of(incoming, device), 0.0), (8, LANES))
        for device, inside in corner_neighbours()
    ]
    for f in range(FIELDS):
        vel_ext[f, : velocity.shape[1], : velocity.shape[2]] = velocity[f]
        sides = edge_block(
            [
                (first, 2 + f, LANES - 2),
                (second, 2 + f, LANES - 1),
                (first, 10 + f, 0),
                (second, 10 + f, 1),
            ]
        )
        upper = edge_block([(corner_tiles[0], CORNER_LANE + f, LANES - 1), (corner_tiles[1], CORNER_LANE + f, 0)])
        lower = edge_block([(corner_tiles[2], CORNER_LANE + f, LANES - 1), (corner_tiles[3], CORNER_LANE + f, 0)])
        corner = jnp.where(row == 0, lower, jnp.where(row == 7, upper, 0.0))
        fill_halo(
            vel_ext, f, above[2 * f : 2 * f + 2, :], below[2 * f : 2 * f + 2, :], sides, corner
        )


def load_stress(stress_ext, plate_ext, thickness, above, below, left, right):
    rows, cols = thickness.shape
    halves = edge_columns(left, right)
    plate_ext[0, :rows, :cols] = thickness[...].astype(F32) * (1.0 / spacing_mm)
    empty = jnp.zeros((PAD_ROWS, LANES), F32)
    for f in range(RESULTS + 1):
        lane = 2 + f % 5
        half = halves[f // 5]
        sides = edge_block([(half, lane, LANES - 1), (half, 8 + lane, 0)])
        ref, k = (stress_ext, f) if f < RESULTS else (plate_ext, 0)
        fill_halo(ref, k, above[f : f + 1, :], below[f : f + 1, :], sides, empty)


def joint_kernel(first, *refs):
    far = refs[: 4 + first]
    incoming, column_marks, row_marks, picked, spring = refs[4 + first : 9 + first]
    refs = refs[9 + first :]
    near = refs[: 4 + first]
    weld = refs[4 + first]
    copies = fetch(refs[-1], list(zip(far, near)))
    devices = incoming.shape[0] // 2
    total = picked.shape[1]
    by_device, by_place = slot_marks(devices, total // 2 // devices)
    other = []
    for row in (1, 0):
        high, low = split(incoming[pl.ds(row, devices, stride=2), :])
        other.append(expand(high, by_device, by_place) + expand(low, by_device, by_place))
    if first:
        stiffness = jnp.concatenate([spring[0:1, :], other[1][5:6]], axis=1)
        spring_out = refs[5 + first]
        spring_out[...] = jnp.broadcast_to(stiffness, spring_out.shape)
    else:
        stiffness = spring[0:1, :]
    field = lax.broadcasted_iota(jnp.int32, (8, total), 0)
    scale = jnp.where(field < 3, 1.0, rotary_share) * stiffness
    pulls = scale * (jnp.concatenate(other, axis=1) - picked[...])
    weld[...] = spread(pulls, column_marks[...], row_marks[...])
    for copy in copies:
        copy.wait()


def step_kernel(first, last, *refs):
    stress_in, velocity_in, disp_in, pressure = refs[:4]
    if first:
        thickness, refs = refs[4], refs[5:]
    else:
        refs = refs[4:]
    (weld, incoming, sec_second, sec_first, girth_second, girth_first,
     column_marks, row_marks, picked) = refs[:9]
    out = refs[9:]
    if not first:
        plate_ext, out = out[0], out[1:]
    stress_out, velocity_out, disp_out = out[:3]
    out = out[3:]
    if first:
        plate_ext, out = out[0], out[1:]
    girth_pair, sec_pair = out[0:2], out[2:4]
    out = out[4:]
    if not last:
        picked_out, payload = out[:2]
        out = out[2:]
    res_ext, vel_ext = out[:2]
    if last:
        stress_ext, velocity, disp = stress_out, velocity_out, disp_out
    else:
        stress_ext, velocity, disp = out[2:5]
    sent = out[-1]

    _, rows, cols = velocity.shape
    devices = incoming.shape[0] // 2
    total = picked.shape[1]
    half = total // 2
    by_device, by_place = slot_marks(devices, half // devices)
    sends = []

    def send(source, target):
        if last:
            return
        copy = pltpu.make_async_copy(source, target, sent.at[len(sends)])
        copy.start()
        sends.append(copy)

    above, below = in_order("sec", sec_first[...], sec_second[...])
    left, right = in_order("girth", girth_first[...], girth_second[...])
    if first:
        for k in range(RESULTS):
            stress_ext[k, :rows, :cols] = stress_in[k]
        load_stress(stress_ext, plate_ext, thickness, above, below, left, right)
    else:
        load_velocity(vel_ext, velocity_in, incoming, above, below, left, right)
    for start in range(0, rows + PAD_ROWS, 8):
        plate = plate_ext[0, start : start + 8, :]
        source = stress_ext if first else stress_in
        chunk = [source[k, start : start + 8, :] for k in range(RESULTS)]
        if not first:
            chunk = stress_chunk(vel_ext, chunk, plate, start)
            for k, value in enumerate(chunk):
                stress_ext[k, start : start + 8, :] = value
        for k, value in enumerate(resultants(chunk, plate)):
            res_ext[k, start : start + 8, :] = value
        for part in pieces(rows + PAD_ROWS):
            if part.stop == start + 8:
                send(stress_ext.at[:, part, :], stress_out.at[:, part, :])

    for start in range(0, rows, 8):
        part = slice(start, start + 8)
        plate = plate_ext[0, part, :cols]
        linear = time_step / plate
        angular = (12.0 * linear) / (1.0 + plate * plate)
        force = force_chunk(res_ext, start, cols)
        force[2] = force[2] + pressure[part, :]
        for f in range(FIELDS):
            joined = force[f] + weld[f * rows + start : f * rows + start + 8, :]
            speed = velocity_in[f, part, :] + (linear if f < 3 else angular) * joined
            velocity[f, part, :] = speed
            disp[f, part, :] = disp_in[f, part, :] + time_step * speed
        if start % 32 == 24:
            done = slice(start - 24, start + 8)
            for source, target in ((velocity, velocity_out), (disp, disp_out)):
                send(source.at[:, done, :], target.at[:, done, :])

    ends = (cols - LANES, cols)
    if last:
        columns = []
        for f in range(FIELDS):
            columns.append((velocity[f, :, 0:LANES], 0, 0, f))
            columns.append((velocity[f, :, ends[0] : ends[1]], LANES - 1, 0, 8 + f))
        send_sides(girth_pair, edge_rows(columns))
        send_ends(
            sec_pair,
            [velocity[f, 0:1, :] for f in range(FIELDS)],
            [velocity[f, rows - 1 : rows, :] for f in range(FIELDS)],
        )
        for copy in sends:
            copy.wait()
        return
    values = pick([disp[f] for f in range(FIELDS)], column_marks[...], row_marks[...])
    picked_out[...] = jnp.concatenate(values + [values[0]] * 3, axis=0)
    near_out = collapse([value[:, :half] for value in values], by_device, by_place)
    far_out = collapse([value[:, half:] for value in values], by_device, by_place)
    columns = []
    for f in range(FIELDS):
        left_lanes = velocity[f, :, 0:LANES]
        right_lanes = velocity[f, :, ends[0] : ends[1]]
        for depth in (0, 1):
            columns.append((left_lanes, depth, depth, 2 + f))
            columns.append((right_lanes, LANES - 2 + depth, depth, 10 + f))
    corners = []
    lane = lax.broadcasted_iota(jnp.int32, (8, LANES), 1)
    for row in (0, rows - 1):
        tile = slice(row // 8 * 8, row // 8 * 8 + 8)
        for side in (0, 1):
            value = jnp.zeros((8, LANES), F32)
            for f in range(FIELDS):
                part = velocity[f, tile, ends[0] : ends[1]] if side else velocity[f, tile, 0:LANES]
                source = LANES - 1 if side else 0
                target = CORNER_LANE + f
                value = jnp.where(lane == target, pltpu.roll(part, (target - source) % LANES, 1), value)
            corners.append(jnp.broadcast_to(value[row % 8 : row % 8 + 1], (8, LANES)))
    send_sides(girth_pair, edge_rows(columns))
    send_joints(payload, near_out, far_out, corners)
    send_ends(
        sec_pair,
        [velocity[f, 0:2, :] for f in range(FIELDS)],
        [velocity[f, rows - 2 : rows, :] for f in range(FIELDS)],
    )
    for copy in sends:
        copy.wait()


def final_kernel(membrane, *refs):
    if membrane:
        stress, velocity = refs[:2]
        sec_second, sec_first, girth_second, girth_first, plate_ext, height = refs[2:8]
        stress_out, moment = refs[8:10]
        refs = refs[10:]
    else:
        stress, velocity, disp = refs[1:4]
        sec_second, sec_first, girth_second, girth_first, plate_ext = refs[4:9]
        stress_out, velocity_out, disp_out = refs[9:12]
        refs = refs[12:]
    made, vel_ext, sent = refs
    _, rows, cols = velocity.shape
    fields = range(0, 2) if membrane else range(2, FIELDS)
    kinds = range(0, 3) if membrane else range(3, RESULTS)
    sends = []

    def send(source, target):
        copy = pltpu.make_async_copy(source, target, sent.at[len(sends)])
        copy.start()
        sends.append(copy)

    if not membrane:
        send(velocity, velocity_out)
        send(disp, disp_out)
    above, below = in_order("sec", sec_first[...], sec_second[...])
    left, right = in_order("girth", girth_first[...], girth_second[...])
    first, _ = edge_columns(left, right)
    empty = jnp.zeros((PAD_ROWS, LANES), F32)
    for k, f in enumerate(fields):
        vel_ext[k, :rows, :cols] = velocity[f]
        sides = edge_block([(first, f, LANES - 1), (first, 8 + f, 0)])
        fill_halo(vel_ext, k, above[f : f + 1, :], below[f : f + 1, :], sides, empty)
    parts = []
    for start in range(0, rows, 8):
        part = slice(start, start + 8)
        chunk = [stress[k, part, :cols] for k in kinds]
        plate = plate_ext[0, part, :cols]
        current, along_x, along_y = [
            [value[:, :cols] for value in values]
            for values in differences(vel_ext, range(len(fields)), start)
        ]
        if membrane:
            chunk = membrane_chunk(along_x, along_y, chunk)
            weighted = plate * chunk[0] * height[0:1, :]
            parts.append(jnp.sum(weighted, axis=1, keepdims=True))
        else:
            chunk = plate_chunk(along_x, along_y, current[1:], chunk, plate)
        for k, value in enumerate(chunk):
            made[k, part, :] = value
        if start % 16 == 8:
            done = slice(start - 8, start + 8)
            send(made.at[:, done, :], stress_out.at[kinds.start : kinds.stop, done, :])
    if membrane:
        column = jnp.broadcast_to(jnp.concatenate(parts, axis=0), (rows, LANES))
        if rows < LANES:
            column = jnp.concatenate([column, jnp.zeros((LANES - rows, LANES), F32)], axis=0)
        moment[...] = column.T[0:1, :rows]
    for copy in sends:
        copy.wait()


def call(
    kernel, vmem_bytes, outs, scratch, *operands, far=0, kept=0, far_out=0, kept_out=0,
    copies=(1,), alias=None,
):
    def placed(k, away, here):
        return pltpu.HBM if k < away else pltpu.VMEM if k < away + here else None

    operands = [
        value if placed(k, far, kept) is None
        else pltpu.with_memory_space_constraint(value, placed(k, far, kept))
        for k, value in enumerate(operands)
    ]
    results = [
        (placed(k, far_out, kept_out) or jax.ShapeDtypeStruct)(shape, dtype)
        for k, (shape, dtype) in enumerate(outs)
    ]
    whole = pl.BlockSpec(memory_space=pltpu.VMEM)
    away = pl.BlockSpec(memory_space=pltpu.HBM)
    scratch = [pltpu.VMEM(shape, dtype) for shape, dtype in scratch]
    scratch += [pltpu.SemaphoreType.DMA((count,)) for count in copies]
    return pl.pallas_call(
        kernel,
        out_shape=results,
        in_specs=[away] * far + [whole] * (len(operands) - far),
        out_specs=[away] * far_out + [whole] * (len(outs) - far_out),
        scratch_shapes=scratch,
        input_output_aliases=alias or {},
        compiler_params=pltpu.CompilerParams(vmem_limit_bytes=vmem_bytes),
    )(*operands)


def swap(pair, axis, around):
    count = lax.axis_size(axis)
    out = []
    for start, value in reversed(list(enumerate(pair))):
        couples = [(i, (i + 1) % count) for i in range(start, count, 2)]
        couples = [(i, j) for i, j in couples if j > i or around]
        out.append(lax.ppermute(value, axis, couples + [(j, i) for i, j in couples]))
    return out


def sum_over(value, axis):
    count = lax.axis_size(axis)
    if count & (count - 1):
        return lax.psum(value, axis)
    parts = [
        lax.ppermute(value, axis, [(i, i ^ step) for i in range(count)])
        for step in range(count - 1, 0, -1)
    ]
    parts = [value] + parts[::-1]
    while len(parts) > 1:
        parts = [a + b for a, b in zip(parts[0::2], parts[1::2])]
    return parts[0]


def exchange(joints):
    blocks = joints.reshape(joints.shape[0] // 2, 2, LANES)
    blocks = lax.all_to_all(blocks, ("sec", "girth"), 0, 0, tiled=True)
    return blocks.reshape(joints.shape)


def local(displacement, velocity, stress, thickness, pressure, weld_from, weld_to, weld_stiff):
    rows, cols = thickness.shape
    _, devices, slots = weld_from.shape
    total = 2 * devices * slots
    girth_total = cols * lax.axis_size("girth")
    column = (lax.axis_index("girth") * cols + lax.iota(jnp.int32, cols)).astype(F32)
    height = jnp.sin(2.0 * jnp.pi / girth_total * (column + 0.5)) / girth_total
    height = jnp.broadcast_to(height[None, :], (8, cols))

    vmem_bytes = 8 * 1024 * 1024 + total * VMEM_PER_SLOT
    message = (devices * 2, LANES)
    edge = (8, LANES)
    strip = (16, cols)
    block = (FIELDS, rows, cols)
    stress_shape = (RESULTS, rows + PAD_ROWS, cols + LANES)
    plate_shape = (1, rows + PAD_ROWS, cols + LANES)
    slot_rows = (8, total)
    scratch = [(stress_shape, F32), ((FIELDS, rows + PAD_ROWS, cols + LANES), F32)]

    (payload, sec_first, sec_second, girth_first, girth_second,
     column_marks, row_marks, picked, spring) = call(
        start_kernel,
        vmem_bytes,
        [
            (message, F32), (strip, F32), (strip, F32), (edge, F32), (edge, F32),
            ((cols, total), BF16), ((rows, total), BF16), (slot_rows, F32), ((8, total // 2), F32),
        ],
        [
            (block, F32), ((RESULTS, rows, LANES), F32), ((RESULTS, rows, LANES), F32),
            ((RESULTS, 8, cols), F32), ((RESULTS, 8, cols), F32), ((rows, cols), jnp.int32),
            ((1, slots, devices), jnp.int32), ((1, slots, devices), jnp.int32),
            ((1, slots, devices), F32),
        ],
        displacement, stress, thickness,
        *[jnp.swapaxes(array, 1, 2) for array in (weld_from, weld_to, weld_stiff)],
        far=6,
        copies=(9,),
    )
    plate = None
    for step in range(STEPS):
        first, last = step == 0, step == STEPS - 1
        incoming = exchange(payload)
        ends = swap((sec_first, sec_second), "sec", False)
        sides = swap((girth_first, girth_second), "girth", True)
        state = [stress, velocity, displacement, pressure] + [thickness] * first
        *state, weld = call(
            functools.partial(joint_kernel, first),
            vmem_bytes,
            [(value.shape, value.dtype) for value in state]
            + [((FIELDS * rows, cols), F32)]
            + [(slot_rows, F32)] * first,
            [],
            *state, incoming, column_marks, row_marks, picked, spring,
            far=len(state),
            kept_out=len(state) + 1,
            copies=(len(state),),
        )
        if first:
            spring, weld, state = weld, state[-1], state[:-1]
        halo = (8, cols) if last else strip
        outs = [(stress_shape, F32), (block, F32), (block, F32)] + [(plate_shape, F32)] * first
        outs += [(edge, F32), (edge, F32), (halo, F32), (halo, F32)]
        if not last:
            outs += [(slot_rows, F32), (message, F32)]
        results = call(
            functools.partial(step_kernel, first, last),
            vmem_bytes,
            outs,
            scratch + ([] if last else outs[:3]),
            *state, weld, incoming, *ends, *sides, column_marks, row_marks, picked,
            *([] if first else [plate]),
            kept=len(state) + 1,
            far_out=0 if last else 3,
            kept_out=3 if last else 0,
            copies=(3 + 2 * (rows // 32),),
        )
        stress, velocity, displacement = results[:3]
        results = results[3:]
        if first:
            plate, results = results[0], results[1:]
        girth_first, girth_second, sec_first, sec_second = results[:4]
        if not last:
            picked, payload = results[4:]

    ends = swap((sec_first, sec_second), "sec", False)
    sides = swap((girth_first, girth_second), "girth", True)
    membrane, partial_moment = call(
        functools.partial(final_kernel, True),
        vmem_bytes,
        [((RESULTS, rows, cols), F32), ((1, rows), F32)],
        [((3, rows, cols), F32), ((2, rows + PAD_ROWS, cols + LANES), F32)],
        stress, velocity, *ends, *sides, plate, height,
        kept=2,
        far_out=1,
        copies=(rows // 16,),
    )
    stress, velocity, displacement = call(
        functools.partial(final_kernel, False),
        vmem_bytes,
        [((RESULTS, rows, cols), F32), (block, F32), (block, F32)],
        [((5, rows, cols), F32), ((3, rows + PAD_ROWS, cols + LANES), F32)],
        membrane, stress, velocity, displacement, *ends, *sides, plate,
        far=1,
        kept=3,
        far_out=3,
        copies=(2 + rows // 16,),
        alias={0: 0},
    )
    moment = sum_over(partial_moment, "girth")[0]
    return (displacement, velocity, stress, moment)


def solution(mesh):
    in_specs = (
        P(None, "sec", "girth"),
        P(None, "sec", "girth"),
        P(None, "sec", "girth"),
        P("sec", "girth"),
        P("sec", "girth"),
        P(("sec", "girth"), None, None),
        P(("sec", "girth"), None, None),
        P(("sec", "girth"), None, None),
    )
    out_specs = (
        P(None, "sec", "girth"),
        P(None, "sec", "girth"),
        P(None, "sec", "girth"),
        P("sec"),
    )
    return jax.shard_map(local, mesh=mesh, in_specs=in_specs, out_specs=out_specs, check_vma=False)
```

```python
import functools

import jax
import jax.numpy as jnp
from jax import lax
from jax.experimental import pallas as pl
from jax.experimental.pallas import tpu as pltpu
from jax.sharding import PartitionSpec as P

STEPS = 3
CORNER_LANE = 112
PIECE = 24
FIELDS = 5
RESULTS = 8
PAD_ROWS = 8
LANES = 128
VMEM_PER_SLOT = 5 * 1024

young_modulus = 4.0
poisson_ratio = 0.3
plate_modulus = young_modulus / (1.0 - poisson_ratio * poisson_ratio)
shear_modulus = young_modulus / (2.0 * (1.0 + poisson_ratio))
shear_factor = 5.0 / 6.0
time_step = 0.2
spacing_mm = 50.0
rotary_share = 1.0 / 12.0

F32 = jnp.float32
BF16 = jnp.bfloat16


def split(values):
    high = values.astype(BF16)
    low = (values - high.astype(F32)).astype(BF16)
    return high, low


def dot(a, b, contract):
    return lax.dot_general(a, b, (contract, ((), ())), preferred_element_type=F32)


def slot_marks(devices, slots):
    total = devices * slots
    lane = lax.broadcasted_iota(jnp.int32, (devices, total), 1)
    device = lax.broadcasted_iota(jnp.int32, (devices, total), 0)
    by_device = (lane // slots == device).astype(F32).astype(BF16)
    lane = lax.broadcasted_iota(jnp.int32, (slots, total), 1)
    place = lax.broadcasted_iota(jnp.int32, (slots, total), 0)
    by_place = (lane % slots == place).astype(F32)
    return by_device, by_place


def expand(blocks, by_device, by_place, turned=False):
    slots, total = by_place.shape
    wide = dot(blocks, by_device, ((1 if turned else 0,), (0,)))
    wide = wide.reshape(wide.shape[0] // slots, slots, total) * by_place[None]
    return jnp.sum(wide, axis=1)


def collapse(rows, by_device, by_place):
    slots, _ = by_place.shape
    marks = by_place.astype(BF16)
    pieces = []
    for part in (0, 1):
        blocks = [split(row)[part] * marks for row in rows]
        blocks += [jnp.zeros_like(marks)] * (LANES // slots - len(rows))
        pieces.append(jnp.concatenate(blocks, axis=0))
    return dot(by_device, pieces[0], ((1,), (1,))) + dot(by_device, pieces[1], ((1,), (1,)))


def pick(fields, column_marks, row_marks):
    rows = fields[0].shape[0]
    parts = [split(field) for field in fields]
    high = jnp.concatenate([part[0] for part in parts], axis=0)
    low = jnp.concatenate([part[1] for part in parts], axis=0)
    by_column = dot(high, column_marks, ((1,), (0,))) + dot(low, column_marks, ((1,), (0,)))
    marks = row_marks.astype(F32)
    return [
        jnp.sum(by_column[rows * f : rows * (f + 1)] * marks, axis=0, keepdims=True)
        for f in range(len(fields))
    ]


def spread(pulls, column_marks, row_marks):
    high, low = split(pulls)
    total = None
    for part in (high, low):
        marked = jnp.concatenate(
            [part[f : f + 1] * row_marks for f in range(FIELDS)], axis=0
        )
        summed = dot(marked, column_marks, ((1,), (1,)))
        total = summed if total is None else total + summed
    return total


def place():
    sec, girth = lax.axis_index("sec"), lax.axis_index("girth")
    return sec, girth, lax.axis_size("sec"), lax.axis_size("girth")


def tile_of(ref, device):
    return ref[pl.ds(pl.multiple_of(device * 8, 8), 8), :]


def set_tile(ref, device, value):
    ref[pl.ds(pl.multiple_of(device * 8, 8), 8), :] = value


def corner_neighbours():
    sec, girth, secs, girths = place()
    me = sec * girths + girth
    out = []
    for step in (-1, 1):
        row = sec + step
        inside = jnp.logical_and(row >= 0, row < secs)
        for turn in (girths - 1, 1):
            device = row * girths + lax.rem(girth + turn, girths)
            out.append((jnp.where(inside, device, me), inside))
    return out


def edge_rows(columns):
    rows = columns[0][0].shape[0]
    lane = lax.broadcasted_iota(jnp.int32, (rows, LANES), 1)
    halves = [jnp.zeros((rows, LANES), F32), jnp.zeros((rows, LANES), F32)]
    for value, source, half, row in columns:
        moved = pltpu.roll(value, (row - source) % LANES, 1)
        halves[half] = jnp.where(lane == row, moved, halves[half])
    return jnp.concatenate(halves, axis=0).T


def edge_columns(left_tile, right_tile):
    stacked = jnp.concatenate(
        [left_tile, right_tile, jnp.zeros((LANES - 16, LANES), F32)], axis=0
    )
    turned = stacked.T
    return turned[: LANES // 2], turned[LANES // 2 :]


def edge_block(pieces):
    rows = pieces[0][0].shape[0]
    lane = lax.broadcasted_iota(jnp.int32, (rows, LANES), 1)
    block = jnp.zeros((rows, LANES), F32)
    for value, source, target in pieces:
        block = jnp.where(lane == target, pltpu.roll(value, (target - source) % LANES, 1), block)
    return block


def row_chunk(ref, f, start):
    count = ref.shape[1]
    if start < 0:
        return jnp.concatenate([ref[f, count + start : count, :], ref[f, 0 : 8 + start, :]], axis=0)
    if start + 8 > count:
        return jnp.concatenate([ref[f, start:count, :], ref[f, 0 : start + 8 - count, :]], axis=0)
    return ref[f, start : start + 8, :]


def difference_x(ref, f, start):
    return row_chunk(ref, f, start + 1) - row_chunk(ref, f, start - 1)


def difference_y(value):
    lanes = value.shape[1]
    return pltpu.roll(value, lanes - 1, 1) - pltpu.roll(value, 1, 1)


def radial_return(xx, yy, xy):
    offset = xx - 0.5 * yy
    square = offset * offset + 0.75 * yy * yy + 3.0 * xy * xy
    scale = lax.rsqrt(jnp.maximum(square, 1.0))
    return xx * scale, yy * scale, xy * scale


def membrane_chunk(along_x, along_y, stress):
    normal = 0.5 * time_step * plate_modulus
    skew = 0.5 * time_step * shear_modulus
    return radial_return(
        stress[0] + normal * (along_x[0] + poisson_ratio * along_y[1]),
        stress[1] + normal * (along_y[1] + poisson_ratio * along_x[0]),
        stress[2] + skew * (along_y[0] + along_x[1]),
    )


def plate_chunk(along_x, along_y, turns, stress, plate):
    arm = 0.5 * plate
    normal = 0.5 * time_step * plate_modulus * arm
    skew = 0.5 * time_step * shear_modulus
    bending = radial_return(
        stress[0] + normal * (along_x[1] + poisson_ratio * along_y[2]),
        stress[1] + normal * (along_y[2] + poisson_ratio * along_x[1]),
        stress[2] + (skew * arm) * (along_y[1] + along_x[2]),
    )
    return bending + (
        stress[3] + skew * (along_x[0] + 2.0 * turns[0]),
        stress[4] + skew * (along_y[0] + 2.0 * turns[1]),
    )


def differences(vel_ref, fields, start):
    current = [vel_ref[f, start : start + 8, :] for f in fields]
    along_x = [difference_x(vel_ref, f, start) for f in fields]
    return current, along_x, [difference_y(value) for value in current]


def stress_chunk(vel_ref, stress, plate, start):
    current, along_x, along_y = differences(vel_ref, range(FIELDS), start)
    membrane = membrane_chunk(along_x[:2], along_y[:2], stress[:3])
    return membrane + plate_chunk(along_x[2:], along_y[2:], current[3:], stress[3:], plate)


def resultants(stress, plate):
    arm = plate * plate * (1.0 / 6.0)
    shear = shear_factor * plate
    return (
        [plate * value for value in stress[0:3]]
        + [arm * value for value in stress[3:6]]
        + [shear * value for value in stress[6:8]]
    )


def force_chunk(res_ref, start, cols):
    def both(x, y):
        along_x = difference_x(res_ref, x, start)[:, :cols]
        along_y = difference_y(res_ref[y, start : start + 8, :])[:, :cols]
        return 0.5 * (along_x + along_y)

    return [
        both(0, 2),
        both(2, 1),
        both(6, 7),
        both(3, 5) - res_ref[6, start : start + 8, :cols],
        both(5, 4) - res_ref[7, start : start + 8, :cols],
    ]


def send_joints(payload, near, far, corners):
    devices = payload.shape[0] // 2
    payload[pl.ds(0, devices, stride=2), :] = near
    payload[pl.ds(1, devices, stride=2), :] = far
    row = lax.broadcasted_iota(jnp.int32, (8, LANES), 0)
    lane = lax.broadcasted_iota(jnp.int32, (8, LANES), 1)
    free = jnp.logical_and(lane >= CORNER_LANE, lane < CORNER_LANE + FIELDS)
    for (device, _), corner in zip(corner_neighbours(), corners):
        tile = lax.div(device, 4)
        here = jnp.logical_and(free, row == 2 * lax.rem(device, 4))
        set_tile(payload, tile, jnp.where(here, corner, tile_of(payload, tile)))


def in_order(axis, low, high):
    even = lax.rem(lax.axis_index(axis), 2) == 0
    return jnp.where(even, high, low), jnp.where(even, low, high)


def send_sides(pair, halo_rows):
    for ref, value in zip(pair, in_order("girth", halo_rows[0:8], halo_rows[8:16])):
        ref[...] = value


def send_ends(pair, low, high):
    for ref in pair:
        ref[...] = jnp.zeros(ref.shape, F32)
    start = 0
    for top, bottom in zip(low, high):
        count = top.shape[0]
        for ref, value in zip(pair, in_order("sec", top, bottom)):
            ref[start : start + count, :] = value
        start += count


def corner_of(incoming, device):
    row = lax.broadcasted_iota(jnp.int32, (8, LANES), 0)
    tile = tile_of(incoming, lax.div(device, 4))
    return jnp.sum(jnp.where(row == 2 * lax.rem(device, 4), tile, 0.0), axis=0, keepdims=True)


def fetch(done, pairs):
    copies = [
        pltpu.make_async_copy(source, target, done.at[k])
        for k, (source, target) in enumerate(pairs)
    ]
    for copy in copies:
        copy.start()
    return copies


def pieces(rows):
    return [slice(0, PIECE), slice(PIECE, 2 * PIECE), slice(2 * PIECE, rows)]


def start_kernel(
    disp_in, stress_in, thickness_in, from_in, to_in, stiff_in,
    payload, sec_first, sec_second, girth_first, girth_second,
    column_marks, row_marks, picked, spring,
    disp, stress_left, stress_right, stress_top, stress_bottom, thickness,
    weld_from, weld_to, weld_stiff, done,
):
    rows, cols = thickness.shape
    _, slots, devices = weld_from.shape
    sec_pair, girth_pair = (sec_first, sec_second), (girth_first, girth_second)
    copies = fetch(
        done,
        [
            (from_in, weld_from),
            (to_in, weld_to),
            (stiff_in, weld_stiff),
            (disp_in, disp),
            (thickness_in, thickness),
            (stress_in.at[:, :, 0:LANES], stress_left),
            (stress_in.at[:, :, cols - LANES : cols], stress_right),
            (stress_in.at[:, 0:8, :], stress_top),
            (stress_in.at[:, rows - 8 : rows, :], stress_bottom),
        ],
    )
    shift = cols.bit_length() - 1
    by_device, by_place = slot_marks(devices, slots)
    for copy in copies[:3]:
        copy.wait()
    near, far = weld_from[0], weld_to[0]
    stiff = jnp.where(near >= 0, weld_stiff[0], 0.0)
    index_parts = []
    for index in (near, far):
        index = jnp.maximum(index, 0)
        column = index & (cols - 1)
        index_parts += [index >> shift, column >> 1, column & 1]
    index_parts = [part.astype(F32).astype(BF16) for part in index_parts]
    index_parts += list(split(stiff))
    wide = [expand(part, by_device, by_place, turned=True) for part in index_parts]
    row_index = jnp.concatenate([wide[0], wide[3]], axis=1)
    column_index = jnp.concatenate([2.0 * wide[1] + wide[2], 2.0 * wide[4] + wide[5]], axis=1)
    stiff_row = wide[6] + wide[7]
    total = row_index.shape[1]
    spring[...] = jnp.broadcast_to(stiff_row, spring.shape)
    row_iota = lax.broadcasted_iota(jnp.int32, (rows, total), 0).astype(F32)
    row_hits = (row_iota == row_index).astype(F32).astype(BF16)
    row_marks[...] = row_hits
    for start in range(0, cols, 64):
        iota = (lax.broadcasted_iota(jnp.int32, (64, total), 0) + start).astype(F32)
        column_marks[start : start + 64, :] = (iota == column_index).astype(F32).astype(BF16)
    copies[3].wait()
    values = pick([disp[f] for f in range(FIELDS)], column_marks[...], row_hits)
    picked[...] = jnp.concatenate(values + [values[0]] * 3, axis=0)
    half = total // 2
    near_out = collapse([value[:, :half] for value in values] + [stiff_row], by_device, by_place)
    far_out = collapse([value[:, half:] for value in values], by_device, by_place)

    for copy in copies[4:]:
        copy.wait()
    plate = thickness[...].astype(F32) * (1.0 / spacing_mm)
    columns = []
    for f in range(RESULTS + 1):
        left = stress_left[f] if f < RESULTS else plate[:, 0:LANES]
        right = stress_right[f] if f < RESULTS else plate[:, cols - LANES :]
        columns.append((left, 0, f // 5, 2 + f % 5))
        columns.append((right, LANES - 1, f // 5, 10 + f % 5))
    send_sides(girth_pair, edge_rows(columns))
    send_joints(payload, near_out, far_out, [])
    send_ends(
        sec_pair,
        [stress_top[f, 0:1, :] for f in range(RESULTS)] + [plate[0:1, :]],
        [stress_bottom[f, 7:8, :] for f in range(RESULTS)] + [plate[rows - 1 : rows, :]],
    )


def fill_halo(ref, f, above, below, sides, corner):
    rows, cols = ref.shape[1] - PAD_ROWS, ref.shape[2] - LANES
    depth = above.shape[0]
    ref[f, rows:, :cols] = jnp.concatenate(
        [below, jnp.zeros((PAD_ROWS - 2 * depth, cols), F32), above], axis=0
    )
    ref[f, :rows, cols:] = sides
    ref[f, rows:, cols:] = corner


def load_velocity(vel_ext, velocity, incoming, above, below, left, right):
    first, second = edge_columns(left, right)
    row = lax.broadcasted_iota(jnp.int32, (8, LANES), 0)
    corner_tiles = [
        jnp.broadcast_to(jnp.where(inside, corner_of(incoming, device), 0.0), (8, LANES))
        for device, inside in corner_neighbours()
    ]
    for f in range(FIELDS):
        vel_ext[f, : velocity.shape[1], : velocity.shape[2]] = velocity[f]
        sides = edge_block(
            [
                (first, 2 + f, LANES - 2),
                (second, 2 + f, LANES - 1),
                (first, 10 + f, 0),
                (second, 10 + f, 1),
            ]
        )
        upper = edge_block([(corner_tiles[0], CORNER_LANE + f, LANES - 1), (corner_tiles[1], CORNER_LANE + f, 0)])
        lower = edge_block([(corner_tiles[2], CORNER_LANE + f, LANES - 1), (corner_tiles[3], CORNER_LANE + f, 0)])
        corner = jnp.where(row == 0, lower, jnp.where(row == 7, upper, 0.0))
        fill_halo(
            vel_ext, f, above[2 * f : 2 * f + 2, :], below[2 * f : 2 * f + 2, :], sides, corner
        )


def load_stress(stress_ext, plate_ext, thickness, above, below, left, right):
    rows, cols = thickness.shape
    halves = edge_columns(left, right)
    plate_ext[0, :rows, :cols] = thickness[...].astype(F32) * (1.0 / spacing_mm)
    empty = jnp.zeros((PAD_ROWS, LANES), F32)
    for f in range(RESULTS + 1):
        lane = 2 + f % 5
        half = halves[f // 5]
        sides = edge_block([(half, lane, LANES - 1), (half, 8 + lane, 0)])
        ref, k = (stress_ext, f) if f < RESULTS else (plate_ext, 0)
        fill_halo(ref, k, above[f : f + 1, :], below[f : f + 1, :], sides, empty)


def joint_kernel(first, *refs):
    far = refs[: 4 + first]
    incoming, column_marks, row_marks, picked, spring = refs[4 + first : 9 + first]
    refs = refs[9 + first :]
    near = refs[: 4 + first]
    weld = refs[4 + first]
    copies = fetch(refs[-1], list(zip(far, near)))
    devices = incoming.shape[0] // 2
    total = picked.shape[1]
    by_device, by_place = slot_marks(devices, total // 2 // devices)
    other = []
    for row in (1, 0):
        high, low = split(incoming[pl.ds(row, devices, stride=2), :])
        other.append(expand(high, by_device, by_place) + expand(low, by_device, by_place))
    if first:
        stiffness = jnp.concatenate([spring[0:1, :], other[1][5:6]], axis=1)
        spring_out = refs[5 + first]
        spring_out[...] = jnp.broadcast_to(stiffness, spring_out.shape)
    else:
        stiffness = spring[0:1, :]
    field = lax.broadcasted_iota(jnp.int32, (8, total), 0)
    scale = jnp.where(field < 3, 1.0, rotary_share) * stiffness
    pulls = scale * (jnp.concatenate(other, axis=1) - picked[...])
    weld[...] = spread(pulls, column_marks[...], row_marks[...])
    for copy in copies:
        copy.wait()


def step_kernel(first, last, *refs):
    stress_in, velocity_in, disp_in, pressure = refs[:4]
    if first:
        thickness, refs = refs[4], refs[5:]
    else:
        refs = refs[4:]
    (weld, incoming, sec_second, sec_first, girth_second, girth_first,
     column_marks, row_marks, picked) = refs[:9]
    out = refs[9:]
    if not first:
        plate_ext, out = out[0], out[1:]
    stress_out, velocity_out, disp_out = out[:3]
    out = out[3:]
    if first:
        plate_ext, out = out[0], out[1:]
    girth_pair, sec_pair = out[0:2], out[2:4]
    out = out[4:]
    if not last:
        picked_out, payload = out[:2]
        out = out[2:]
    res_ext, vel_ext = out[:2]
    if last:
        stress_ext, velocity, disp = stress_out, velocity_out, disp_out
    else:
        stress_ext, velocity, disp = out[2:5]
    sent = out[-1]

    _, rows, cols = velocity.shape
    devices = incoming.shape[0] // 2
    total = picked.shape[1]
    half = total // 2
    by_device, by_place = slot_marks(devices, half // devices)
    sends = []

    def send(source, target):
        if last:
            return
        copy = pltpu.make_async_copy(source, target, sent.at[len(sends)])
        copy.start()
        sends.append(copy)

    above, below = in_order("sec", sec_first[...], second_of(sec_second))
    left, right = in_order("girth", girth_first[...], girth_second[...])
    if first:
        for k in range(RESULTS):
            stress_ext[k, :rows, :cols] = stress_in[k]
        load_stress(stress_ext, plate_ext, thickness, above, below, left, right)
    else:
        load_velocity(vel_ext, velocity_in, incoming, above, below, left, right)
    for start in range(0, rows + PAD_ROWS, 8):
        plate = plate_ext[0, start : start + 8, :]
        source = stress_ext if first else stress_in
        chunk = [source[k, start : start + 8, :] for k in range(RESULTS)]
        if not first:
            chunk = stress_chunk(vel_ext, chunk, plate, start)
            for k, value in enumerate(chunk):
                stress_ext[k, start : start + 8, :] = value
        for k, value in enumerate(resultants(chunk, plate)):
            res_ext[k, start : start + 8, :] = value
        for part in pieces(rows + PAD_ROWS):
            if part.stop == start + 8:
                send(stress_ext.at[:, part, :], stress_out.at[:, part, :])

    for start in range(0, rows, 8):
        part = slice(start, start + 8)
        plate = plate_ext[0, part, :cols]
        linear = time_step / plate
        angular = (12.0 * linear) / (1.0 + plate * plate)
        force = force_chunk(res_ext, start, cols)
        force[2] = force[2] + pressure[part, :]
        for f in range(FIELDS):
            joined = force[f] + weld[f * rows + start : f * rows + start + 8, :]
            speed = velocity_in[f, part, :] + (linear if f < 3 else angular) * joined
            velocity[f, part, :] = speed
            disp[f, part, :] = disp_in[f, part, :] + time_step * speed
        if start % 32 == 24:
            done = slice(start - 24, start + 8)
            for source, target in ((velocity, velocity_out), (disp, disp_out)):
                send(source.at[:, done, :], target.at[:, done, :])

    ends = (cols - LANES, cols)
    if last:
        columns = []
        for f in range(FIELDS):
            columns.append((velocity[f, :, 0:LANES], 0, 0, f))
            columns.append((velocity[f, :, ends[0] : ends[1]], LANES - 1, 0, 8 + f))
        send_sides(girth_pair, edge_rows(columns))
        send_ends(
            sec_pair,
            [velocity[f, 0:1, :] for f in range(FIELDS)],
            [velocity[f, rows - 1 : rows, :] for f in range(FIELDS)],
        )
        for copy in sends:
            copy.wait()
        return
    values = pick([disp[f] for f in range(FIELDS)], column_marks[...], row_marks[...])
    picked_out[...] = jnp.concatenate(values + [values[0]] * 3, axis=0)
    near_out = collapse([value[:, :half] for value in values], by_device, by_place)
    far_out = collapse([value[:, half:] for value in values], by_device, by_place)
    columns = []
    for f in range(FIELDS):
        left_lanes = velocity[f, :, 0:LANES]
        right_lanes = velocity[f, :, ends[0] : ends[1]]
        for depth in (0, 1):
            columns.append((left_lanes, depth, depth, 2 + f))
            columns.append((right_lanes, LANES - 2 + depth, depth, 10 + f))
    corners = []
    lane = lax.broadcasted_iota(jnp.int32, (8, LANES), 1)
    for row in (0, rows - 1):
        tile = slice(row // 8 * 8, row // 8 * 8 + 8)
        for side in (0, 1):
            value = jnp.zeros((8, LANES), F32)
            for f in range(FIELDS):
                part = velocity[f, tile, ends[0] : ends[1]] if side else velocity[f, tile, 0:LANES]
                source = LANES - 1 if side else 0
                target = CORNER_LANE + f
                value = jnp.where(lane == target, pltpu.roll(part, (target - source) % LANES, 1), value)
            corners.append(jnp.broadcast_to(value[row % 8 : row % 8 + 1], (8, LANES)))
    send_sides(girth_pair, edge_rows(columns))
    send_joints(payload, near_out, far_out, corners)
    send_ends(
        sec_pair,
        [velocity[f, 0:2, :] for f in range(FIELDS)],
        [velocity[f, rows - 2 : rows, :] for f in range(FIELDS)],
    )
    for copy in sends:
        copy.wait()


def final_kernel(membrane, *refs):
    if membrane:
        stress, velocity = refs[:2]
        sec_second, sec_first, girth_second, girth_first, plate_ext, height = refs[2:8]
        stress_out, moment = refs[8:10]
        refs = refs[10:]
    else:
        stress, velocity, disp = refs[1:4]
        sec_second, sec_first, girth_second, girth_first, plate_ext = refs[4:9]
        stress_out, velocity_out, disp_out = refs[9:12]
        refs = refs[12:]
    made, vel_ext, sent = refs
    _, rows, cols = velocity.shape
    fields = range(0, 2) if membrane else range(2, FIELDS)
    kinds = range(0, 3) if membrane else range(3, RESULTS)
    sends = []

    def send(source, target):
        copy = pltpu.make_async_copy(source, target, sent.at[len(sends)])
        copy.start()
        sends.append(copy)

    if not membrane:
        send(velocity, velocity_out)
        send(disp, disp_out)
    above, below = in_order("sec", sec_first[...], sec_second[...])
    left, right = in_order("girth", girth_first[...], girth_second[...])
    first, _ = edge_columns(left, right)
    empty = jnp.zeros((PAD_ROWS, LANES), F32)
    for k, f in enumerate(fields):
        vel_ext[k, :rows, :cols] = velocity[f]
        sides = edge_block([(first, f, LANES - 1), (first, 8 + f, 0)])
        fill_halo(vel_ext, k, above[f : f + 1, :], below[f : f + 1, :], sides, empty)
    parts = []
    for start in range(0, rows, 8):
        part = slice(start, start + 8)
        chunk = [stress[k, part, :cols] for k in kinds]
        plate = plate_ext[0, part, :cols]
        current, along_x, along_y = [
            [value[:, :cols] for value in values]
            for values in differences(vel_ext, range(len(fields)), start)
        ]
        if membrane:
            chunk = membrane_chunk(along_x, along_y, chunk)
            weighted = plate * chunk[0] * height[0:1, :]
            parts.append(jnp.sum(weighted, axis=1, keepdims=True))
        else:
            chunk = plate_chunk(along_x, along_y, current[1:], chunk, plate)
        for k, value in enumerate(chunk):
            made[k, part, :] = value
        if start % 16 == 8:
            done = slice(start - 8, start + 8)
            send(made.at[:, done, :], stress_out.at[kinds.start : kinds.stop, done, :])
    if membrane:
        column = jnp.broadcast_to(jnp.concatenate(parts, axis=0), (rows, LANES))
        if rows < LANES:
            column = jnp.concatenate([column, jnp.zeros((LANES - rows, LANES), F32)], axis=0)
        moment[...] = column.T[0:1, :rows]
    for copy in sends:
        copy.wait()


def call(
    kernel, vmem_bytes, outs, scratch, *operands, far=0, kept=0, far_out=0, kept_out=0,
    copies=(1,), alias=None,
):
    def placed(k, away, here):
        return pltpu.HBM if k < away else pltpu.VMEM if k < away + here else None

    operands = [
        value if placed(k, far, kept) is None
        else pltpu.with_memory_space_constraint(value, placed(k, far, kept))
        for k, value in enumerate(operands)
    ]
    results = [
        (placed(k, far_out, kept_out) or jax.ShapeDtypeStruct)(shape, dtype)
        for k, (shape, dtype) in enumerate(outs)
    ]
    whole = pl.BlockSpec(memory_space=pltpu.VMEM)
    away = pl.BlockSpec(memory_space=pltpu.HBM)
    scratch = [pltpu.VMEM(shape, dtype) for shape, dtype in scratch]
    scratch += [pltpu.SemaphoreType.DMA((count,)) for count in copies]
    return pl.pallas_call(
        kernel,
        out_shape=results,
        in_specs=[away] * far + [whole] * (len(operands) - far),
        out_specs=[away] * far_out + [whole] * (len(outs) - far_out),
        scratch_shapes=scratch,
        input_output_aliases=alias or {},
        compiler_params=pltpu.CompilerParams(vmem_limit_bytes=vmem_bytes),
    )(*operands)


def swap(pair, axis, around):
    count = lax.axis_size(axis)
    out = []
    for start, value in reversed(list(enumerate(pair))):
        couples = [(i, (i + 1) % count) for i in range(start, count, 2)]
        couples = [(i, j) for i, j in couples if j > i or around]
        out.append(lax.ppermute(value, axis, couples + [(j, i) for i, j in couples]))
    return out


def gather_second(value, axis):
    count = lax.axis_size(axis)
    pairs = [[i, (i + 1) % count] for i in range(1, count, 2)]
    return lax.all_gather(value, axis, axis_index_groups=pairs)


def second_of(gathered):
    sec, _, secs, _ = place()
    value = jnp.where(lax.rem(sec, 2) == 0, gathered[0], gathered[1])
    return jnp.where(jnp.logical_or(sec == 0, sec == secs - 1), 0.0, value)


def sum_over(value, axis):
    count = lax.axis_size(axis)
    if count & (count - 1):
        return lax.psum(value, axis)
    parts = [
        lax.ppermute(value, axis, [(i, i ^ step) for i in range(count)])
        for step in range(count - 1, 0, -1)
    ]
    parts = [value] + parts[::-1]
    while len(parts) > 1:
        parts = [a + b for a, b in zip(parts[0::2], parts[1::2])]
    return parts[0]


def exchange(joints):
    blocks = joints.reshape(joints.shape[0] // 2, 2, LANES)
    blocks = lax.all_to_all(blocks, ("sec", "girth"), 0, 0, tiled=True)
    return blocks.reshape(joints.shape)


def local(displacement, velocity, stress, thickness, pressure, weld_from, weld_to, weld_stiff):
    rows, cols = thickness.shape
    _, devices, slots = weld_from.shape
    total = 2 * devices * slots
    girth_total = cols * lax.axis_size("girth")
    column = (lax.axis_index("girth") * cols + lax.iota(jnp.int32, cols)).astype(F32)
    height = jnp.sin(2.0 * jnp.pi / girth_total * (column + 0.5)) / girth_total
    height = jnp.broadcast_to(height[None, :], (8, cols))

    vmem_bytes = 8 * 1024 * 1024 + total * VMEM_PER_SLOT
    message = (devices * 2, LANES)
    edge = (8, LANES)
    strip = (16, cols)
    block = (FIELDS, rows, cols)
    stress_shape = (RESULTS, rows + PAD_ROWS, cols + LANES)
    plate_shape = (1, rows + PAD_ROWS, cols + LANES)
    slot_rows = (8, total)
    scratch = [(stress_shape, F32), ((FIELDS, rows + PAD_ROWS, cols + LANES), F32)]

    (payload, sec_first, sec_second, girth_first, girth_second,
     column_marks, row_marks, picked, spring) = call(
        start_kernel,
        vmem_bytes,
        [
            (message, F32), (strip, F32), (strip, F32), (edge, F32), (edge, F32),
            ((cols, total), BF16), ((rows, total), BF16), (slot_rows, F32), ((8, total // 2), F32),
        ],
        [
            (block, F32), ((RESULTS, rows, LANES), F32), ((RESULTS, rows, LANES), F32),
            ((RESULTS, 8, cols), F32), ((RESULTS, 8, cols), F32), ((rows, cols), jnp.int32),
            ((1, slots, devices), jnp.int32), ((1, slots, devices), jnp.int32),
            ((1, slots, devices), F32),
        ],
        displacement, stress, thickness,
        *[jnp.swapaxes(array, 1, 2) for array in (weld_from, weld_to, weld_stiff)],
        far=6,
        copies=(9,),
    )
    plate = None
    for step in range(STEPS):
        first, last = step == 0, step == STEPS - 1
        incoming = exchange(payload)
        ends = (gather_second(sec_second, "sec"), swap((sec_first,), "sec", False)[0])
        sides = swap((girth_first, girth_second), "girth", True)
        state = [stress, velocity, displacement, pressure] + [thickness] * first
        *state, weld = call(
            functools.partial(joint_kernel, first),
            vmem_bytes,
            [(value.shape, value.dtype) for value in state]
            + [((FIELDS * rows, cols), F32)]
            + [(slot_rows, F32)] * first,
            [],
            *state, incoming, column_marks, row_marks, picked, spring,
            far=len(state),
            kept_out=len(state) + 1,
            copies=(len(state),),
        )
        if first:
            spring, weld, state = weld, state[-1], state[:-1]
        halo = (8, cols) if last else strip
        outs = [(stress_shape, F32), (block, F32), (block, F32)] + [(plate_shape, F32)] * first
        outs += [(edge, F32), (edge, F32), (halo, F32), (halo, F32)]
        if not last:
            outs += [(slot_rows, F32), (message, F32)]
        results = call(
            functools.partial(step_kernel, first, last),
            vmem_bytes,
            outs,
            scratch + ([] if last else outs[:3]),
            *state, weld, incoming, *ends, *sides, column_marks, row_marks, picked,
            *([] if first else [plate]),
            kept=len(state) + 1,
            far_out=0 if last else 3,
            kept_out=3 if last else 0,
            copies=(3 + 2 * (rows // 32),),
        )
        stress, velocity, displacement = results[:3]
        results = results[3:]
        if first:
            plate, results = results[0], results[1:]
        girth_first, girth_second, sec_first, sec_second = results[:4]
        if not last:
            picked, payload = results[4:]

    ends = swap((sec_first, sec_second), "sec", False)
    sides = swap((girth_first, girth_second), "girth", True)
    membrane, partial_moment = call(
        functools.partial(final_kernel, True),
        vmem_bytes,
        [((RESULTS, rows, cols), F32), ((1, rows), F32)],
        [((3, rows, cols), F32), ((2, rows + PAD_ROWS, cols + LANES), F32)],
        stress, velocity, *ends, *sides, plate, height,
        kept=2,
        far_out=1,
        copies=(rows // 16,),
    )
    stress, velocity, displacement = call(
        functools.partial(final_kernel, False),
        vmem_bytes,
        [((RESULTS, rows, cols), F32), (block, F32), (block, F32)],
        [((5, rows, cols), F32), ((3, rows + PAD_ROWS, cols + LANES), F32)],
        membrane, stress, velocity, displacement, *ends, *sides, plate,
        far=1,
        kept=3,
        far_out=3,
        copies=(2 + rows // 16,),
        alias={0: 0},
    )
    moment = sum_over(partial_moment, "girth")[0]
    return (displacement, velocity, stress, moment)


def solution(mesh):
    in_specs = (
        P(None, "sec", "girth"),
        P(None, "sec", "girth"),
        P(None, "sec", "girth"),
        P("sec", "girth"),
        P("sec", "girth"),
        P(("sec", "girth"), None, None),
        P(("sec", "girth"), None, None),
        P(("sec", "girth"), None, None),
    )
    out_specs = (
        P(None, "sec", "girth"),
        P(None, "sec", "girth"),
        P(None, "sec", "girth"),
        P("sec"),
    )
    return jax.shard_map(local, mesh=mesh, in_specs=in_specs, out_specs=out_specs, check_vma=False)
```

```python
import functools

import jax
import jax.numpy as jnp
from jax import lax
from jax.experimental import pallas as pl
from jax.experimental.pallas import tpu as pltpu
from jax.sharding import PartitionSpec as P

STEPS = 3
CORNER_LANE = 112
SIDE_ROWS = 24
PIECE = 24
FIELDS = 5
RESULTS = 8
PAD_ROWS = 8
LANES = 128
VMEM_PER_SLOT = 5 * 1024

young_modulus = 4.0
poisson_ratio = 0.3
plate_modulus = young_modulus / (1.0 - poisson_ratio * poisson_ratio)
shear_modulus = young_modulus / (2.0 * (1.0 + poisson_ratio))
shear_factor = 5.0 / 6.0
time_step = 0.2
spacing_mm = 50.0
rotary_share = 1.0 / 12.0

F32 = jnp.float32
BF16 = jnp.bfloat16


def split(values):
    high = values.astype(BF16)
    low = (values - high.astype(F32)).astype(BF16)
    return high, low


def dot(a, b, contract):
    return lax.dot_general(a, b, (contract, ((), ())), preferred_element_type=F32)


def slot_marks(devices, slots):
    total = devices * slots
    lane = lax.broadcasted_iota(jnp.int32, (devices, total), 1)
    device = lax.broadcasted_iota(jnp.int32, (devices, total), 0)
    by_device = (lane // slots == device).astype(F32).astype(BF16)
    lane = lax.broadcasted_iota(jnp.int32, (slots, total), 1)
    place = lax.broadcasted_iota(jnp.int32, (slots, total), 0)
    by_place = (lane % slots == place).astype(F32)
    return by_device, by_place


def expand(blocks, by_device, by_place, turned=False):
    slots, total = by_place.shape
    wide = dot(blocks, by_device, ((1 if turned else 0,), (0,)))
    wide = wide.reshape(wide.shape[0] // slots, slots, total) * by_place[None]
    return jnp.sum(wide, axis=1)


def collapse(rows, by_device, by_place):
    slots, _ = by_place.shape
    marks = by_place.astype(BF16)
    pieces = []
    for part in (0, 1):
        blocks = [split(row)[part] * marks for row in rows]
        blocks += [jnp.zeros_like(marks)] * (LANES // slots - len(rows))
        pieces.append(jnp.concatenate(blocks, axis=0))
    return dot(by_device, pieces[0], ((1,), (1,))) + dot(by_device, pieces[1], ((1,), (1,)))


def pick(fields, column_marks, row_marks):
    rows = fields[0].shape[0]
    parts = [split(field) for field in fields]
    high = jnp.concatenate([part[0] for part in parts], axis=0)
    low = jnp.concatenate([part[1] for part in parts], axis=0)
    by_column = dot(high, column_marks, ((1,), (0,))) + dot(low, column_marks, ((1,), (0,)))
    marks = row_marks.astype(F32)
    return [
        jnp.sum(by_column[rows * f : rows * (f + 1)] * marks, axis=0, keepdims=True)
        for f in range(len(fields))
    ]


def spread(pulls, column_marks, row_marks):
    high, low = split(pulls)
    total = None
    for part in (high, low):
        marked = jnp.concatenate(
            [part[f : f + 1] * row_marks for f in range(FIELDS)], axis=0
        )
        summed = dot(marked, column_marks, ((1,), (1,)))
        total = summed if total is None else total + summed
    return total


def place():
    sec, girth = lax.axis_index("sec"), lax.axis_index("girth")
    return sec, girth, lax.axis_size("sec"), lax.axis_size("girth")


def tile_of(ref, device):
    return ref[pl.ds(pl.multiple_of(device * 8, 8), 8), :]


def set_tile(ref, device, value):
    ref[pl.ds(pl.multiple_of(device * 8, 8), 8), :] = value


def corner_neighbours():
    sec, girth, secs, girths = place()
    me = sec * girths + girth
    out = []
    for step in (-1, 1):
        row = sec + step
        inside = jnp.logical_and(row >= 0, row < secs)
        for turn in (girths - 1, 1):
            device = row * girths + lax.rem(girth + turn, girths)
            out.append((jnp.where(inside, device, me), inside))
    return out


def place_lanes(pieces):
    shape = pieces[0][0].shape
    lane = lax.broadcasted_iota(jnp.int32, shape, 1)
    block = jnp.zeros(shape, F32)
    for value, source, target, count in pieces:
        moved = value if source == target else pltpu.roll(value, (target - source) % LANES, 1)
        inside = jnp.logical_and(lane >= target, lane < target + count)
        if target + count > LANES:
            inside = jnp.logical_or(inside, lane < target + count - LANES)
        block = jnp.where(inside, moved, block)
    return block


def edge_rows(left, right, depth):
    pieces = []
    for k, (low, high) in enumerate(zip(left, right)):
        pieces.append((high, LANES - depth, 2 * depth * k, depth))
        pieces.append((low, 0, 2 * depth * k + depth, depth))
    block = place_lanes(pieces)
    rows = block.shape[0]
    if rows < LANES:
        block = jnp.concatenate([block, jnp.zeros((LANES - rows, LANES), F32)], axis=0)
    return block.T[:SIDE_ROWS]


def edge_columns(left, right, depth, rows):
    row = lax.broadcasted_iota(jnp.int32, left.shape, 0)
    both = jnp.where(lax.rem(row, 2 * depth) < depth, left, right)
    both = jnp.concatenate([both, jnp.zeros((LANES - SIDE_ROWS, LANES), F32)], axis=0)
    return both.T[:rows]


def side_block(columns, k, depth):
    return place_lanes([(columns, 2 * depth * k, LANES - depth, 2 * depth)])


def row_chunk(ref, f, start):
    count = ref.shape[1]
    if start < 0:
        return jnp.concatenate([ref[f, count + start : count, :], ref[f, 0 : 8 + start, :]], axis=0)
    if start + 8 > count:
        return jnp.concatenate([ref[f, start:count, :], ref[f, 0 : start + 8 - count, :]], axis=0)
    return ref[f, start : start + 8, :]


def difference_x(ref, f, start):
    return row_chunk(ref, f, start + 1) - row_chunk(ref, f, start - 1)


def difference_y(value):
    lanes = value.shape[1]
    return pltpu.roll(value, lanes - 1, 1) - pltpu.roll(value, 1, 1)


def radial_return(xx, yy, xy):
    offset = xx - 0.5 * yy
    square = offset * offset + 0.75 * yy * yy + 3.0 * xy * xy
    scale = lax.rsqrt(jnp.maximum(square, 1.0))
    return xx * scale, yy * scale, xy * scale


def membrane_chunk(along_x, along_y, stress):
    normal = 0.5 * time_step * plate_modulus
    skew = 0.5 * time_step * shear_modulus
    return radial_return(
        stress[0] + normal * (along_x[0] + poisson_ratio * along_y[1]),
        stress[1] + normal * (along_y[1] + poisson_ratio * along_x[0]),
        stress[2] + skew * (along_y[0] + along_x[1]),
    )


def plate_chunk(along_x, along_y, turns, stress, plate):
    arm = 0.5 * plate
    normal = 0.5 * time_step * plate_modulus * arm
    skew = 0.5 * time_step * shear_modulus
    bending = radial_return(
        stress[0] + normal * (along_x[1] + poisson_ratio * along_y[2]),
        stress[1] + normal * (along_y[2] + poisson_ratio * along_x[1]),
        stress[2] + (skew * arm) * (along_y[1] + along_x[2]),
    )
    return bending + (
        stress[3] + skew * (along_x[0] + 2.0 * turns[0]),
        stress[4] + skew * (along_y[0] + 2.0 * turns[1]),
    )


def differences(vel_ref, fields, start):
    current = [vel_ref[f, start : start + 8, :] for f in fields]
    along_x = [difference_x(vel_ref, f, start) for f in fields]
    return current, along_x, [difference_y(value) for value in current]


def stress_chunk(vel_ref, stress, plate, start):
    current, along_x, along_y = differences(vel_ref, range(FIELDS), start)
    membrane = membrane_chunk(along_x[:2], along_y[:2], stress[:3])
    return membrane + plate_chunk(along_x[2:], along_y[2:], current[3:], stress[3:], plate)


def resultants(stress, plate):
    arm = plate * plate * (1.0 / 6.0)
    shear = shear_factor * plate
    return (
        [plate * value for value in stress[0:3]]
        + [arm * value for value in stress[3:6]]
        + [shear * value for value in stress[6:8]]
    )


def force_chunk(res_ref, start, cols):
    def both(x, y):
        along_x = difference_x(res_ref, x, start)[:, :cols]
        along_y = difference_y(res_ref[y, start : start + 8, :])[:, :cols]
        return 0.5 * (along_x + along_y)

    return [
        both(0, 2),
        both(2, 1),
        both(6, 7),
        both(3, 5) - res_ref[6, start : start + 8, :cols],
        both(5, 4) - res_ref[7, start : start + 8, :cols],
    ]


def send_joints(payload, near, far, corners):
    devices = payload.shape[0] // 2
    payload[pl.ds(0, devices, stride=2), :] = near
    payload[pl.ds(1, devices, stride=2), :] = far
    row = lax.broadcasted_iota(jnp.int32, (8, LANES), 0)
    lane = lax.broadcasted_iota(jnp.int32, (8, LANES), 1)
    free = jnp.logical_and(lane >= CORNER_LANE, lane < CORNER_LANE + FIELDS)
    for (device, _), corner in zip(corner_neighbours(), corners):
        tile = lax.div(device, 4)
        here = jnp.logical_and(free, row == 2 * lax.rem(device, 4))
        set_tile(payload, tile, jnp.where(here, corner, tile_of(payload, tile)))


def in_order(axis, low, high):
    even = lax.rem(lax.axis_index(axis), 2) == 0
    return jnp.where(even, high, low), jnp.where(even, low, high)


def send_ends(pair, low, high):
    for ref in pair:
        ref[...] = jnp.zeros(ref.shape, F32)
    start = 0
    for top, bottom in zip(low, high):
        count = top.shape[0]
        for ref, value in zip(pair, in_order("sec", top, bottom)):
            ref[start : start + count, :] = value
        start += count


def corner_of(incoming, device):
    row = lax.broadcasted_iota(jnp.int32, (8, LANES), 0)
    tile = tile_of(incoming, lax.div(device, 4))
    return jnp.sum(jnp.where(row == 2 * lax.rem(device, 4), tile, 0.0), axis=0, keepdims=True)


def fetch(done, pairs):
    copies = [
        pltpu.make_async_copy(source, target, done.at[k])
        for k, (source, target) in enumerate(pairs)
    ]
    for copy in copies:
        copy.start()
    return copies


def pieces(rows):
    return [slice(0, PIECE), slice(PIECE, 2 * PIECE), slice(2 * PIECE, rows)]


def start_kernel(
    disp_in, stress_in, thickness_in, from_in, to_in, stiff_in,
    payload, sec_first, sec_second, sides,
    column_marks, row_marks, picked, spring,
    disp, stress_left, stress_right, stress_top, stress_bottom, thickness,
    weld_from, weld_to, weld_stiff, done,
):
    rows, cols = thickness.shape
    _, slots, devices = weld_from.shape
    sec_pair = (sec_first, sec_second)
    copies = fetch(
        done,
        [
            (from_in, weld_from),
            (to_in, weld_to),
            (stiff_in, weld_stiff),
            (disp_in, disp),
            (thickness_in, thickness),
            (stress_in.at[:, :, 0:LANES], stress_left),
            (stress_in.at[:, :, cols - LANES : cols], stress_right),
            (stress_in.at[:, 0:8, :], stress_top),
            (stress_in.at[:, rows - 8 : rows, :], stress_bottom),
        ],
    )
    shift = cols.bit_length() - 1
    by_device, by_place = slot_marks(devices, slots)
    for copy in copies[:3]:
        copy.wait()
    near, far = weld_from[0], weld_to[0]
    stiff = jnp.where(near >= 0, weld_stiff[0], 0.0)
    index_parts = []
    for index in (near, far):
        index = jnp.maximum(index, 0)
        column = index & (cols - 1)
        index_parts += [index >> shift, column >> 1, column & 1]
    index_parts = [part.astype(F32).astype(BF16) for part in index_parts]
    index_parts += list(split(stiff))
    wide = [expand(part, by_device, by_place, turned=True) for part in index_parts]
    row_index = jnp.concatenate([wide[0], wide[3]], axis=1)
    column_index = jnp.concatenate([2.0 * wide[1] + wide[2], 2.0 * wide[4] + wide[5]], axis=1)
    stiff_row = wide[6] + wide[7]
    total = row_index.shape[1]
    spring[...] = jnp.broadcast_to(stiff_row, spring.shape)
    row_iota = lax.broadcasted_iota(jnp.int32, (rows, total), 0).astype(F32)
    row_hits = (row_iota == row_index).astype(F32).astype(BF16)
    row_marks[...] = row_hits
    for start in range(0, cols, 64):
        iota = (lax.broadcasted_iota(jnp.int32, (64, total), 0) + start).astype(F32)
        column_marks[start : start + 64, :] = (iota == column_index).astype(F32).astype(BF16)
    copies[3].wait()
    values = pick([disp[f] for f in range(FIELDS)], column_marks[...], row_hits)
    picked[...] = jnp.concatenate(values + [values[0]] * 3, axis=0)
    half = total // 2
    near_out = collapse([value[:, :half] for value in values] + [stiff_row], by_device, by_place)
    far_out = collapse([value[:, half:] for value in values], by_device, by_place)

    for copy in copies[4:]:
        copy.wait()
    plate = thickness[...].astype(F32) * (1.0 / spacing_mm)
    sides[...] = edge_rows(
        [stress_left[f] for f in range(RESULTS)] + [plate[:, 0:LANES]],
        [stress_right[f] for f in range(RESULTS)] + [plate[:, cols - LANES :]],
        1,
    )
    send_joints(payload, near_out, far_out, [])
    send_ends(
        sec_pair,
        [stress_top[f, 0:1, :] for f in range(RESULTS)] + [plate[0:1, :]],
        [stress_bottom[f, 7:8, :] for f in range(RESULTS)] + [plate[rows - 1 : rows, :]],
    )


def fill_halo(ref, f, above, below, sides, corner):
    rows, cols = ref.shape[1] - PAD_ROWS, ref.shape[2] - LANES
    depth = above.shape[0]
    ref[f, rows:, :cols] = jnp.concatenate(
        [below, jnp.zeros((PAD_ROWS - 2 * depth, cols), F32), above], axis=0
    )
    ref[f, :rows, cols:] = sides
    ref[f, rows:, cols:] = corner


def load_velocity(vel_ext, velocity, incoming, above, below, left, right):
    columns = edge_columns(left, right, 2, velocity.shape[1])
    row = lax.broadcasted_iota(jnp.int32, (8, LANES), 0)
    corner_tiles = [
        jnp.broadcast_to(jnp.where(inside, corner_of(incoming, device), 0.0), (8, LANES))
        for device, inside in corner_neighbours()
    ]
    for f in range(FIELDS):
        vel_ext[f, : velocity.shape[1], : velocity.shape[2]] = velocity[f]
        sides = side_block(columns, f, 2)
        corner_lane = CORNER_LANE + f
        upper, lower = [
            place_lanes([(low, corner_lane, LANES - 1, 1), (high, corner_lane, 0, 1)])
            for low, high in (corner_tiles[0:2], corner_tiles[2:4])
        ]
        corner = jnp.where(row == 0, lower, jnp.where(row == 7, upper, 0.0))
        fill_halo(
            vel_ext, f, above[2 * f : 2 * f + 2, :], below[2 * f : 2 * f + 2, :], sides, corner
        )


def load_stress(stress_ext, plate_ext, thickness, above, below, left, right):
    rows, cols = thickness.shape
    columns = edge_columns(left, right, 1, rows)
    plate_ext[0, :rows, :cols] = thickness[...].astype(F32) * (1.0 / spacing_mm)
    empty = jnp.zeros((PAD_ROWS, LANES), F32)
    for f in range(RESULTS + 1):
        sides = side_block(columns, f, 1)
        ref, k = (stress_ext, f) if f < RESULTS else (plate_ext, 0)
        fill_halo(ref, k, above[f : f + 1, :], below[f : f + 1, :], sides, empty)


def set_rates(linear, angular, plate):
    rate = time_step / plate
    linear[...] = rate
    angular[...] = (12.0 * rate) / (1.0 + plate * plate)


def joint_kernel(first, *refs):
    far = refs[: 4 + first]
    incoming, column_marks, row_marks, picked, spring = refs[4 + first : 9 + first]
    refs = refs[9 + first :]
    if not first:
        plate_ext, refs = refs[0], refs[1:]
    near = refs[: 4 + first]
    weld, linear, angular = refs[4 + first : 7 + first]
    copies = fetch(refs[-1], list(zip(far, near)))
    devices = incoming.shape[0] // 2
    total = picked.shape[1]
    by_device, by_place = slot_marks(devices, total // 2 // devices)
    other = []
    for row in (1, 0):
        high, low = split(incoming[pl.ds(row, devices, stride=2), :])
        other.append(expand(high, by_device, by_place) + expand(low, by_device, by_place))
    if first:
        stiffness = jnp.concatenate([spring[0:1, :], other[1][5:6]], axis=1)
        spring_out = refs[8]
        spring_out[...] = jnp.broadcast_to(stiffness, spring_out.shape)
    else:
        stiffness = spring[0:1, :]
    field = lax.broadcasted_iota(jnp.int32, (8, total), 0)
    scale = jnp.where(field < 3, 1.0, rotary_share) * stiffness
    pulls = scale * (jnp.concatenate(other, axis=1) - picked[...])
    weld[...] = spread(pulls, column_marks[...], row_marks[...])
    rows, cols = linear.shape
    if not first:
        set_rates(linear, angular, plate_ext[0, :rows, :cols])
    for copy in copies:
        copy.wait()
    if first:
        set_rates(linear, angular, near[-1][...].astype(F32) * (1.0 / spacing_mm))


def step_kernel(first, last, *refs):
    stress_in, velocity_in, disp_in, pressure = refs[:4]
    if first:
        thickness, refs = refs[4], refs[5:]
    else:
        refs = refs[4:]
    (weld, linear, angular, incoming, sec_second, sec_first, girth_second, girth_first,
     column_marks, row_marks, picked) = refs[:11]
    out = refs[11:]
    if not first:
        plate_ext, out = out[0], out[1:]
    stress_out, velocity_out, disp_out = out[:3]
    out = out[3:]
    if first:
        plate_ext, out = out[0], out[1:]
    sides, sec_pair = out[0], out[1:3]
    out = out[3:]
    if not last:
        picked_out, payload = out[:2]
        out = out[2:]
    res_ext, vel_ext = out[:2]
    if last:
        stress_ext, velocity, disp = stress_out, velocity_out, disp_out
    else:
        stress_ext, velocity, disp = out[2:5]
    sent = out[-1]

    _, rows, cols = velocity.shape
    devices = incoming.shape[0] // 2
    total = picked.shape[1]
    half = total // 2
    by_device, by_place = slot_marks(devices, half // devices)
    sends = []

    def send(source, target):
        if last:
            return
        copy = pltpu.make_async_copy(source, target, sent.at[len(sends)])
        copy.start()
        sends.append(copy)

    above, below = in_order("sec", sec_first[...], sec_second[...])
    left, right = in_order("girth", girth_first[...], girth_second[...])
    if first:
        for k in range(RESULTS):
            stress_ext[k, :rows, :cols] = stress_in[k]
        load_stress(stress_ext, plate_ext, thickness, above, below, left, right)
    else:
        load_velocity(vel_ext, velocity_in, incoming, above, below, left, right)
    for start in range(0, rows + PAD_ROWS, 8):
        plate = plate_ext[0, start : start + 8, :]
        source = stress_ext if first else stress_in
        chunk = [source[k, start : start + 8, :] for k in range(RESULTS)]
        if not first:
            chunk = stress_chunk(vel_ext, chunk, plate, start)
            for k, value in enumerate(chunk):
                stress_ext[k, start : start + 8, :] = value
        for k, value in enumerate(resultants(chunk, plate)):
            res_ext[k, start : start + 8, :] = value
        for part in pieces(rows + PAD_ROWS):
            if part.stop == start + 8:
                send(stress_ext.at[:, part, :], stress_out.at[:, part, :])

    for start in range(0, rows, 8):
        part = slice(start, start + 8)
        rates = [linear[part, :]] * 3 + [angular[part, :]] * 2
        force = force_chunk(res_ext, start, cols)
        force[2] = force[2] + pressure[part, :]
        for f in range(FIELDS):
            joined = force[f] + weld[f * rows + start : f * rows + start + 8, :]
            speed = velocity_in[f, part, :] + rates[f] * joined
            velocity[f, part, :] = speed
            disp[f, part, :] = disp_in[f, part, :] + time_step * speed
        if start % 32 == 24:
            done = slice(start - 24, start + 8)
            for source, target in ((velocity, velocity_out), (disp, disp_out)):
                send(source.at[:, done, :], target.at[:, done, :])

    ends = (cols - LANES, cols)
    left_lanes = [velocity[f, :, 0:LANES] for f in range(FIELDS)]
    right_lanes = [velocity[f, :, ends[0] : ends[1]] for f in range(FIELDS)]
    sides[...] = edge_rows(left_lanes, right_lanes, 1 if last else 2)
    if last:
        send_ends(
            sec_pair,
            [velocity[f, 0:1, :] for f in range(FIELDS)],
            [velocity[f, rows - 1 : rows, :] for f in range(FIELDS)],
        )
        for copy in sends:
            copy.wait()
        return
    values = pick([disp[f] for f in range(FIELDS)], column_marks[...], row_marks[...])
    picked_out[...] = jnp.concatenate(values + [values[0]] * 3, axis=0)
    near_out = collapse([value[:, :half] for value in values], by_device, by_place)
    far_out = collapse([value[:, half:] for value in values], by_device, by_place)
    corners = []
    lane = lax.broadcasted_iota(jnp.int32, (8, LANES), 1)
    for row in (0, rows - 1):
        tile = slice(row // 8 * 8, row // 8 * 8 + 8)
        for side in (0, 1):
            value = jnp.zeros((8, LANES), F32)
            for f in range(FIELDS):
                part = velocity[f, tile, ends[0] : ends[1]] if side else velocity[f, tile, 0:LANES]
                source = LANES - 1 if side else 0
                target = CORNER_LANE + f
                value = jnp.where(lane == target, pltpu.roll(part, (target - source) % LANES, 1), value)
            corners.append(jnp.broadcast_to(value[row % 8 : row % 8 + 1], (8, LANES)))
    send_joints(payload, near_out, far_out, corners)
    send_ends(
        sec_pair,
        [velocity[f, 0:2, :] for f in range(FIELDS)],
        [velocity[f, rows - 2 : rows, :] for f in range(FIELDS)],
    )
    for copy in sends:
        copy.wait()


def final_kernel(membrane, *refs):
    if membrane:
        stress, velocity = refs[:2]
        sec_second, sec_first, girth_second, girth_first, plate_ext, height = refs[2:8]
        stress_out, moment = refs[8:10]
        refs = refs[10:]
    else:
        stress, velocity, disp = refs[1:4]
        sec_second, sec_first, girth_second, girth_first, plate_ext = refs[4:9]
        stress_out, velocity_out, disp_out = refs[9:12]
        refs = refs[12:]
    made, vel_ext, sent = refs
    _, rows, cols = velocity.shape
    fields = range(0, 2) if membrane else range(2, FIELDS)
    kinds = range(0, 3) if membrane else range(3, RESULTS)
    sends = []

    def send(source, target):
        copy = pltpu.make_async_copy(source, target, sent.at[len(sends)])
        copy.start()
        sends.append(copy)

    if not membrane:
        send(velocity, velocity_out)
        send(disp, disp_out)
    above, below = in_order("sec", sec_first[...], sec_second[...])
    left, right = in_order("girth", girth_first[...], girth_second[...])
    columns = edge_columns(left, right, 1, rows)
    empty = jnp.zeros((PAD_ROWS, LANES), F32)
    for k, f in enumerate(fields):
        vel_ext[k, :rows, :cols] = velocity[f]
        sides = side_block(columns, f, 1)
        fill_halo(vel_ext, k, above[f : f + 1, :], below[f : f + 1, :], sides, empty)
    parts = []
    for start in range(0, rows, 8):
        part = slice(start, start + 8)
        chunk = [stress[k, part, :cols] for k in kinds]
        plate = plate_ext[0, part, :cols]
        current, along_x, along_y = [
            [value[:, :cols] for value in values]
            for values in differences(vel_ext, range(len(fields)), start)
        ]
        if membrane:
            chunk = membrane_chunk(along_x, along_y, chunk)
            weighted = plate * chunk[0] * height[0:1, :]
            parts.append(jnp.sum(weighted, axis=1, keepdims=True))
        else:
            chunk = plate_chunk(along_x, along_y, current[1:], chunk, plate)
        for k, value in enumerate(chunk):
            made[k, part, :] = value
        if start % 16 == 8:
            done = slice(start - 8, start + 8)
            send(made.at[:, done, :], stress_out.at[kinds.start : kinds.stop, done, :])
    if membrane:
        column = jnp.broadcast_to(jnp.concatenate(parts, axis=0), (rows, LANES))
        if rows < LANES:
            column = jnp.concatenate([column, jnp.zeros((LANES - rows, LANES), F32)], axis=0)
        moment[...] = column.T[0:1, :rows]
    for copy in sends:
        copy.wait()


def call(
    kernel, vmem_bytes, outs, scratch, *operands, far=0, kept=0, far_out=0, kept_out=0,
    copies=(1,), alias=None,
):
    def placed(k, away, here):
        return pltpu.HBM if k < away else pltpu.VMEM if k < away + here else None

    operands = [
        value if placed(k, far, kept) is None
        else pltpu.with_memory_space_constraint(value, placed(k, far, kept))
        for k, value in enumerate(operands)
    ]
    results = [
        (placed(k, far_out, kept_out) or jax.ShapeDtypeStruct)(shape, dtype)
        for k, (shape, dtype) in enumerate(outs)
    ]
    whole = pl.BlockSpec(memory_space=pltpu.VMEM)
    away = pl.BlockSpec(memory_space=pltpu.HBM)
    scratch = [pltpu.VMEM(shape, dtype) for shape, dtype in scratch]
    scratch += [pltpu.SemaphoreType.DMA((count,)) for count in copies]
    return pl.pallas_call(
        kernel,
        out_shape=results,
        in_specs=[away] * far + [whole] * (len(operands) - far),
        out_specs=[away] * far_out + [whole] * (len(outs) - far_out),
        scratch_shapes=scratch,
        input_output_aliases=alias or {},
        compiler_params=pltpu.CompilerParams(vmem_limit_bytes=vmem_bytes),
    )(*operands)


def swap(pair, axis, around):
    count = lax.axis_size(axis)
    out = []
    for start, value in reversed(list(enumerate(pair))):
        couples = [(i, (i + 1) % count) for i in range(start, count, 2)]
        couples = [(i, j) for i, j in couples if j > i or around]
        out.append(lax.ppermute(value, axis, couples + [(j, i) for i, j in couples]))
    return out


def sum_over(value, axis):
    count = lax.axis_size(axis)
    if count & (count - 1):
        return lax.psum(value, axis)
    parts = [
        lax.ppermute(value, axis, [(i, i ^ step) for i in range(count)])
        for step in range(count - 1, 0, -1)
    ]
    parts = parts + [value]
    while len(parts) > 1:
        parts = [a + b for a, b in zip(parts[0::2], parts[1::2])]
    return parts[0]


def exchange(joints):
    blocks = joints.reshape(joints.shape[0] // 2, 2, LANES)
    blocks = lax.all_to_all(blocks, ("sec", "girth"), 0, 0, tiled=True)
    return blocks.reshape(joints.shape)


def local(displacement, velocity, stress, thickness, pressure, weld_from, weld_to, weld_stiff):
    rows, cols = thickness.shape
    _, devices, slots = weld_from.shape
    total = 2 * devices * slots
    girth_total = cols * lax.axis_size("girth")
    column = (lax.axis_index("girth") * cols + lax.iota(jnp.int32, cols)).astype(F32)
    height = jnp.sin(2.0 * jnp.pi / girth_total * (column + 0.5)) / girth_total
    height = jnp.broadcast_to(height[None, :], (8, cols))

    vmem_bytes = 8 * 1024 * 1024 + total * VMEM_PER_SLOT
    message = (devices * 2, LANES)
    edge = (SIDE_ROWS, LANES)
    strip = (16, cols)
    block = (FIELDS, rows, cols)
    stress_shape = (RESULTS, rows + PAD_ROWS, cols + LANES)
    plate_shape = (1, rows + PAD_ROWS, cols + LANES)
    slot_rows = (8, total)
    scratch = [(stress_shape, F32), ((FIELDS, rows + PAD_ROWS, cols + LANES), F32)]

    (payload, sec_first, sec_second, sides,
     column_marks, row_marks, picked, spring) = call(
        start_kernel,
        vmem_bytes,
        [
            (message, F32), (strip, F32), (strip, F32), (edge, F32),
            ((cols, total), BF16), ((rows, total), BF16), (slot_rows, F32), ((8, total // 2), F32),
        ],
        [
            (block, F32), ((RESULTS, rows, LANES), F32), ((RESULTS, rows, LANES), F32),
            ((RESULTS, 8, cols), F32), ((RESULTS, 8, cols), F32), ((rows, cols), jnp.int32),
            ((1, slots, devices), jnp.int32), ((1, slots, devices), jnp.int32),
            ((1, slots, devices), F32),
        ],
        displacement, stress, thickness,
        *[jnp.swapaxes(array, 1, 2) for array in (weld_from, weld_to, weld_stiff)],
        far=6,
        copies=(9,),
    )
    plate = None
    for step in range(STEPS):
        first, last = step == 0, step == STEPS - 1
        incoming = exchange(payload)
        ends = swap((sec_first, sec_second), "sec", False)
        sides = swap((sides, sides), "girth", True)
        state = [stress, velocity, displacement, pressure] + [thickness] * first
        *state, weld, linear, angular = call(
            functools.partial(joint_kernel, first),
            vmem_bytes,
            [(value.shape, value.dtype) for value in state]
            + [((FIELDS * rows, cols), F32), ((rows, cols), F32), ((rows, cols), F32)]
            + [(slot_rows, F32)] * first,
            [],
            *state, incoming, column_marks, row_marks, picked, spring,
            *([] if first else [plate]),
            far=len(state),
            kept_out=len(state) + 3,
            copies=(len(state),),
        )
        if first:
            *state, weld, linear, angular, spring = *state, weld, linear, angular
        halo = (8, cols) if last else strip
        outs = [(stress_shape, F32), (block, F32), (block, F32)] + [(plate_shape, F32)] * first
        outs += [(edge, F32), (halo, F32), (halo, F32)]
        if not last:
            outs += [(slot_rows, F32), (message, F32)]
        results = call(
            functools.partial(step_kernel, first, last),
            vmem_bytes,
            outs,
            scratch + ([] if last else outs[:3]),
            *state, weld, linear, angular, incoming, *ends, *sides, column_marks, row_marks, picked,
            *([] if first else [plate]),
            kept=len(state) + 3,
            far_out=0 if last else 3,
            kept_out=3 if last else 0,
            copies=(3 + 2 * (rows // 32),),
        )
        stress, velocity, displacement = results[:3]
        results = results[3:]
        if first:
            plate, results = results[0], results[1:]
        sides, sec_first, sec_second = results[:3]
        if not last:
            picked, payload = results[3:]

    ends = swap((sec_first, sec_second), "sec", False)
    sides = swap((sides, sides), "girth", True)
    membrane, partial_moment = call(
        functools.partial(final_kernel, True),
        vmem_bytes,
        [((RESULTS, rows, cols), F32), ((1, rows), F32)],
        [((3, rows, cols), F32), ((2, rows + PAD_ROWS, cols + LANES), F32)],
        stress, velocity, *ends, *sides, plate, height,
        kept=2,
        far_out=1,
        copies=(rows // 16,),
    )
    stress, velocity, displacement = call(
        functools.partial(final_kernel, False),
        vmem_bytes,
        [((RESULTS, rows, cols), F32), (block, F32), (block, F32)],
        [((5, rows, cols), F32), ((3, rows + PAD_ROWS, cols + LANES), F32)],
        membrane, stress, velocity, displacement, *ends, *sides, plate,
        far=1,
        kept=3,
        far_out=3,
        copies=(2 + rows // 16,),
        alias={0: 0},
    )
    moment = sum_over(partial_moment, "girth")[0]
    return (displacement, velocity, stress, moment)


def solution(mesh):
    in_specs = (
        P(None, "sec", "girth"),
        P(None, "sec", "girth"),
        P(None, "sec", "girth"),
        P("sec", "girth"),
        P("sec", "girth"),
        P(("sec", "girth"), None, None),
        P(("sec", "girth"), None, None),
        P(("sec", "girth"), None, None),
    )
    out_specs = (
        P(None, "sec", "girth"),
        P(None, "sec", "girth"),
        P(None, "sec", "girth"),
        P("sec"),
    )
    return jax.shard_map(local, mesh=mesh, in_specs=in_specs, out_specs=out_specs, check_vma=False)
```

```python
import functools

import jax
import jax.numpy as jnp
from jax import lax
from jax.experimental import pallas as pl
from jax.experimental.pallas import tpu as pltpu
from jax.sharding import PartitionSpec as P

STEPS = 3
CORNER_LANE = 112
SIDE_ROWS = 24
PIECE = 24
FIELDS = 5
RESULTS = 8
PAD_ROWS = 8
LANES = 128
VMEM_PER_SLOT = 5 * 1024

young_modulus = 4.0
poisson_ratio = 0.3
plate_modulus = young_modulus / (1.0 - poisson_ratio * poisson_ratio)
shear_modulus = young_modulus / (2.0 * (1.0 + poisson_ratio))
shear_factor = 5.0 / 6.0
time_step = 0.2
spacing_mm = 50.0
rotary_share = 1.0 / 12.0

F32 = jnp.float32
BF16 = jnp.bfloat16


def split(values):
    high = values.astype(BF16)
    low = (values - high.astype(F32)).astype(BF16)
    return high, low


def dot(a, b, contract):
    return lax.dot_general(a, b, (contract, ((), ())), preferred_element_type=F32)


def slot_marks(devices, slots):
    total = devices * slots
    lane = lax.broadcasted_iota(jnp.int32, (devices, total), 1)
    device = lax.broadcasted_iota(jnp.int32, (devices, total), 0)
    by_device = (lane // slots == device).astype(F32).astype(BF16)
    lane = lax.broadcasted_iota(jnp.int32, (slots, total), 1)
    place = lax.broadcasted_iota(jnp.int32, (slots, total), 0)
    by_place = (lane % slots == place).astype(F32)
    return by_device, by_place


def expand(blocks, by_device, by_place, turned=False):
    slots, total = by_place.shape
    wide = dot(blocks, by_device, ((1 if turned else 0,), (0,)))
    wide = wide.reshape(wide.shape[0] // slots, slots, total) * by_place[None]
    return jnp.sum(wide, axis=1)


def collapse(rows, by_device, by_place):
    slots, _ = by_place.shape
    marks = by_place.astype(BF16)
    pieces = []
    for part in (0, 1):
        blocks = [split(row)[part] * marks for row in rows]
        blocks += [jnp.zeros_like(marks)] * (LANES // slots - len(rows))
        pieces.append(jnp.concatenate(blocks, axis=0))
    return dot(by_device, pieces[0], ((1,), (1,))) + dot(by_device, pieces[1], ((1,), (1,)))


def pick(fields, column_marks, row_marks):
    rows = fields[0].shape[0]
    parts = [split(field) for field in fields]
    high = jnp.concatenate([part[0] for part in parts], axis=0)
    low = jnp.concatenate([part[1] for part in parts], axis=0)
    by_column = dot(high, column_marks, ((1,), (0,))) + dot(low, column_marks, ((1,), (0,)))
    marks = row_marks.astype(F32)
    return [
        jnp.sum(by_column[rows * f : rows * (f + 1)] * marks, axis=0, keepdims=True)
        for f in range(len(fields))
    ]


def spread(pulls, column_marks, row_marks):
    high, low = split(pulls)
    total = None
    for part in (high, low):
        marked = jnp.concatenate(
            [part[f : f + 1] * row_marks for f in range(FIELDS)], axis=0
        )
        summed = dot(marked, column_marks, ((1,), (1,)))
        total = summed if total is None else total + summed
    return total


def place():
    sec, girth = lax.axis_index("sec"), lax.axis_index("girth")
    return sec, girth, lax.axis_size("sec"), lax.axis_size("girth")


def tile_of(ref, device):
    return ref[pl.ds(pl.multiple_of(device * 8, 8), 8), :]


def set_tile(ref, device, value):
    ref[pl.ds(pl.multiple_of(device * 8, 8), 8), :] = value


def corner_neighbours():
    sec, girth, secs, girths = place()
    me = sec * girths + girth
    out = []
    for step in (-1, 1):
        row = sec + step
        inside = jnp.logical_and(row >= 0, row < secs)
        for turn in (girths - 1, 1):
            device = row * girths + lax.rem(girth + turn, girths)
            out.append((jnp.where(inside, device, me), inside))
    return out


def place_lanes(pieces):
    shape = pieces[0][0].shape
    lane = lax.broadcasted_iota(jnp.int32, shape, 1)
    block = jnp.zeros(shape, F32)
    for value, source, target, count in pieces:
        moved = value if source == target else pltpu.roll(value, (target - source) % LANES, 1)
        inside = jnp.logical_and(lane >= target, lane < target + count)
        if target + count > LANES:
            inside = jnp.logical_or(inside, lane < target + count - LANES)
        block = jnp.where(inside, moved, block)
    return block


def edge_rows(left, right, depth):
    pieces = []
    for k, (low, high) in enumerate(zip(left, right)):
        pieces.append((high, LANES - depth, 2 * depth * k, depth))
        pieces.append((low, 0, 2 * depth * k + depth, depth))
    block = place_lanes(pieces)
    rows = block.shape[0]
    if rows < LANES:
        block = jnp.concatenate([block, jnp.zeros((LANES - rows, LANES), F32)], axis=0)
    return block.T[:SIDE_ROWS]


def edge_columns(left, right, depth, rows):
    row = lax.broadcasted_iota(jnp.int32, left.shape, 0)
    both = jnp.where(lax.rem(row, 2 * depth) < depth, left, right)
    both = jnp.concatenate([both, jnp.zeros((LANES - SIDE_ROWS, LANES), F32)], axis=0)
    return both.T[:rows]


def side_block(columns, k, depth):
    return place_lanes([(columns, 2 * depth * k, LANES - depth, 2 * depth)])


def row_chunk(ref, f, start):
    count = ref.shape[1]
    if start < 0:
        return jnp.concatenate([ref[f, count + start : count, :], ref[f, 0 : 8 + start, :]], axis=0)
    if start + 8 > count:
        return jnp.concatenate([ref[f, start:count, :], ref[f, 0 : start + 8 - count, :]], axis=0)
    return ref[f, start : start + 8, :]


def difference_x(ref, f, start):
    return row_chunk(ref, f, start + 1) - row_chunk(ref, f, start - 1)


def difference_y(value):
    lanes = value.shape[1]
    return pltpu.roll(value, lanes - 1, 1) - pltpu.roll(value, 1, 1)


def radial_return(xx, yy, xy):
    offset = xx - 0.5 * yy
    square = offset * offset + 0.75 * yy * yy + 3.0 * xy * xy
    scale = lax.rsqrt(jnp.maximum(square, 1.0))
    return xx * scale, yy * scale, xy * scale


def membrane_chunk(along_x, along_y, stress):
    normal = 0.5 * time_step * plate_modulus
    skew = 0.5 * time_step * shear_modulus
    return radial_return(
        stress[0] + normal * (along_x[0] + poisson_ratio * along_y[1]),
        stress[1] + normal * (along_y[1] + poisson_ratio * along_x[0]),
        stress[2] + skew * (along_y[0] + along_x[1]),
    )


def plate_chunk(along_x, along_y, turns, stress, plate):
    arm = 0.5 * plate
    normal = 0.5 * time_step * plate_modulus * arm
    skew = 0.5 * time_step * shear_modulus
    bending = radial_return(
        stress[0] + normal * (along_x[1] + poisson_ratio * along_y[2]),
        stress[1] + normal * (along_y[2] + poisson_ratio * along_x[1]),
        stress[2] + (skew * arm) * (along_y[1] + along_x[2]),
    )
    return bending + (
        stress[3] + skew * (along_x[0] + 2.0 * turns[0]),
        stress[4] + skew * (along_y[0] + 2.0 * turns[1]),
    )


def differences(vel_ref, fields, start):
    current = [vel_ref[f, start : start + 8, :] for f in fields]
    along_x = [difference_x(vel_ref, f, start) for f in fields]
    return current, along_x, [difference_y(value) for value in current]


def stress_chunk(vel_ref, stress, plate, start):
    current, along_x, along_y = differences(vel_ref, range(FIELDS), start)
    membrane = membrane_chunk(along_x[:2], along_y[:2], stress[:3])
    return membrane + plate_chunk(along_x[2:], along_y[2:], current[3:], stress[3:], plate)


def resultants(stress, plate):
    arm = plate * plate * (1.0 / 6.0)
    shear = shear_factor * plate
    return (
        [plate * value for value in stress[0:3]]
        + [arm * value for value in stress[3:6]]
        + [shear * value for value in stress[6:8]]
    )


def force_chunk(res_ref, start, cols):
    def both(x, y):
        along_x = difference_x(res_ref, x, start)[:, :cols]
        along_y = difference_y(res_ref[y, start : start + 8, :])[:, :cols]
        return 0.5 * (along_x + along_y)

    return [
        both(0, 2),
        both(2, 1),
        both(6, 7),
        both(3, 5) - res_ref[6, start : start + 8, :cols],
        both(5, 4) - res_ref[7, start : start + 8, :cols],
    ]


def send_joints(payload, near, far, corners):
    devices = payload.shape[0] // 2
    payload[pl.ds(0, devices, stride=2), :] = near
    payload[pl.ds(1, devices, stride=2), :] = far
    row = lax.broadcasted_iota(jnp.int32, (8, LANES), 0)
    lane = lax.broadcasted_iota(jnp.int32, (8, LANES), 1)
    free = jnp.logical_and(lane >= CORNER_LANE, lane < CORNER_LANE + FIELDS)
    for (device, _), corner in zip(corner_neighbours(), corners):
        tile = lax.div(device, 4)
        here = jnp.logical_and(free, row == 2 * lax.rem(device, 4))
        set_tile(payload, tile, jnp.where(here, corner, tile_of(payload, tile)))


def in_order(axis, low, high):
    even = lax.rem(lax.axis_index(axis), 2) == 0
    return jnp.where(even, high, low), jnp.where(even, low, high)


def send_ends(pair, low, high):
    for ref in pair:
        ref[...] = jnp.zeros(ref.shape, F32)
    start = 0
    for top, bottom in zip(low, high):
        count = top.shape[0]
        for ref, value in zip(pair, in_order("sec", top, bottom)):
            ref[start : start + count, :] = value
        start += count


def corner_of(incoming, device):
    row = lax.broadcasted_iota(jnp.int32, (8, LANES), 0)
    tile = tile_of(incoming, lax.div(device, 4))
    return jnp.sum(jnp.where(row == 2 * lax.rem(device, 4), tile, 0.0), axis=0, keepdims=True)


def fetch(done, pairs):
    copies = [
        pltpu.make_async_copy(source, target, done.at[k])
        for k, (source, target) in enumerate(pairs)
    ]
    for copy in copies:
        copy.start()
    return copies


def pieces(rows):
    return [slice(0, PIECE), slice(PIECE, 2 * PIECE), slice(2 * PIECE, rows)]


def start_kernel(
    disp_in, stress_in, thickness_in, from_in, to_in, stiff_in,
    payload_out, sec_first, sec_second, sides,
    column_marks, row_marks, picked, spring,
    disp, stress_left, stress_right, stress_top, stress_bottom, thickness,
    weld_from, weld_to, weld_stiff, payload, done,
):
    rows, cols = thickness.shape
    _, slots, devices = weld_from.shape
    sec_pair = (sec_first, sec_second)
    copies = fetch(
        done,
        [
            (from_in, weld_from),
            (to_in, weld_to),
            (stiff_in, weld_stiff),
            (disp_in, disp),
            (thickness_in, thickness),
            (stress_in.at[:, :, 0:LANES], stress_left),
            (stress_in.at[:, :, cols - LANES : cols], stress_right),
            (stress_in.at[:, 0:8, :], stress_top),
            (stress_in.at[:, rows - 8 : rows, :], stress_bottom),
        ],
    )
    shift = cols.bit_length() - 1
    by_device, by_place = slot_marks(devices, slots)
    for copy in copies[:3]:
        copy.wait()
    near, far = weld_from[0], weld_to[0]
    stiff = jnp.where(near >= 0, weld_stiff[0], 0.0)
    index_parts = []
    for index in (near, far):
        index = jnp.maximum(index, 0)
        column = index & (cols - 1)
        index_parts += [index >> shift, column >> 1, column & 1]
    index_parts = [part.astype(F32).astype(BF16) for part in index_parts]
    index_parts += list(split(stiff))
    wide = [expand(part, by_device, by_place, turned=True) for part in index_parts]
    row_index = jnp.concatenate([wide[0], wide[3]], axis=1)
    column_index = jnp.concatenate([2.0 * wide[1] + wide[2], 2.0 * wide[4] + wide[5]], axis=1)
    stiff_row = wide[6] + wide[7]
    total = row_index.shape[1]
    spring[...] = jnp.broadcast_to(stiff_row, spring.shape)
    row_iota = lax.broadcasted_iota(jnp.int32, (rows, total), 0).astype(F32)
    row_hits = (row_iota == row_index).astype(F32).astype(BF16)
    row_marks[...] = row_hits
    for start in range(0, cols, 64):
        iota = (lax.broadcasted_iota(jnp.int32, (64, total), 0) + start).astype(F32)
        column_marks[start : start + 64, :] = (iota == column_index).astype(F32).astype(BF16)
    copies[3].wait()
    values = pick([disp[f] for f in range(FIELDS)], column_marks[...], row_hits)
    picked[...] = jnp.concatenate(values + [values[0]] * 3, axis=0)
    half = total // 2
    near_out = collapse([value[:, :half] for value in values] + [stiff_row], by_device, by_place)
    far_out = collapse([value[:, half:] for value in values], by_device, by_place)

    send_joints(payload, near_out, far_out, [])
    message = pltpu.make_async_copy(payload, payload_out, done.at[len(copies)])
    message.start()
    for copy in copies[4:]:
        copy.wait()
    plate = thickness[...].astype(F32) * (1.0 / spacing_mm)
    sides[...] = edge_rows(
        [stress_left[f] for f in range(RESULTS)] + [plate[:, 0:LANES]],
        [stress_right[f] for f in range(RESULTS)] + [plate[:, cols - LANES :]],
        1,
    )
    send_ends(
        sec_pair,
        [stress_top[f, 0:1, :] for f in range(RESULTS)] + [plate[0:1, :]],
        [stress_bottom[f, 7:8, :] for f in range(RESULTS)] + [plate[rows - 1 : rows, :]],
    )
    message.wait()


def fill_halo(ref, f, above, below, sides, corner):
    rows, cols = ref.shape[1] - PAD_ROWS, ref.shape[2] - LANES
    depth = above.shape[0]
    ref[f, rows:, :cols] = jnp.concatenate(
        [below, jnp.zeros((PAD_ROWS - 2 * depth, cols), F32), above], axis=0
    )
    ref[f, :rows, cols:] = sides
    ref[f, rows:, cols:] = corner


def load_velocity(vel_ext, velocity, incoming, above, below, left, right):
    columns = edge_columns(left, right, 2, velocity.shape[1])
    row = lax.broadcasted_iota(jnp.int32, (8, LANES), 0)
    corner_tiles = [
        jnp.broadcast_to(jnp.where(inside, corner_of(incoming, device), 0.0), (8, LANES))
        for device, inside in corner_neighbours()
    ]
    for f in range(FIELDS):
        vel_ext[f, : velocity.shape[1], : velocity.shape[2]] = velocity[f]
        sides = side_block(columns, f, 2)
        corner_lane = CORNER_LANE + f
        upper, lower = [
            place_lanes([(low, corner_lane, LANES - 1, 1), (high, corner_lane, 0, 1)])
            for low, high in (corner_tiles[0:2], corner_tiles[2:4])
        ]
        corner = jnp.where(row == 0, lower, jnp.where(row == 7, upper, 0.0))
        fill_halo(
            vel_ext, f, above[2 * f : 2 * f + 2, :], below[2 * f : 2 * f + 2, :], sides, corner
        )


def load_stress(stress_ext, plate_ext, thickness, above, below, left, right):
    rows, cols = thickness.shape
    columns = edge_columns(left, right, 1, rows)
    plate_ext[0, :rows, :cols] = thickness[...].astype(F32) * (1.0 / spacing_mm)
    empty = jnp.zeros((PAD_ROWS, LANES), F32)
    for f in range(RESULTS + 1):
        sides = side_block(columns, f, 1)
        ref, k = (stress_ext, f) if f < RESULTS else (plate_ext, 0)
        fill_halo(ref, k, above[f : f + 1, :], below[f : f + 1, :], sides, empty)


def set_rates(linear, angular, plate):
    rate = time_step / plate
    linear[...] = rate
    angular[...] = (12.0 * rate) / (1.0 + plate * plate)


def joint_kernel(first, *refs):
    far = refs[: 4 + first]
    incoming, column_marks, row_marks, picked, spring = refs[4 + first : 9 + first]
    refs = refs[9 + first :]
    if not first:
        plate_ext, refs = refs[0], refs[1:]
    near = refs[: 4 + first]
    weld, linear, angular = refs[4 + first : 7 + first]
    copies = fetch(refs[-1], list(zip(far, near)))
    devices = incoming.shape[0] // 2
    total = picked.shape[1]
    by_device, by_place = slot_marks(devices, total // 2 // devices)
    other = []
    for row in (1, 0):
        high, low = split(incoming[pl.ds(row, devices, stride=2), :])
        other.append(expand(high, by_device, by_place) + expand(low, by_device, by_place))
    if first:
        stiffness = jnp.concatenate([spring[0:1, :], other[1][5:6]], axis=1)
        spring_out = refs[8]
        spring_out[...] = jnp.broadcast_to(stiffness, spring_out.shape)
    else:
        stiffness = spring[0:1, :]
    field = lax.broadcasted_iota(jnp.int32, (8, total), 0)
    scale = jnp.where(field < 3, 1.0, rotary_share) * stiffness
    pulls = scale * (jnp.concatenate(other, axis=1) - picked[...])
    weld[...] = spread(pulls, column_marks[...], row_marks[...])
    rows, cols = linear.shape
    if not first:
        set_rates(linear, angular, plate_ext[0, :rows, :cols])
    for copy in copies:
        copy.wait()
    if first:
        set_rates(linear, angular, near[-1][...].astype(F32) * (1.0 / spacing_mm))


def step_kernel(first, last, *refs):
    stress_in, velocity_in, disp_in, pressure = refs[:4]
    if first:
        thickness, refs = refs[4], refs[5:]
    else:
        refs = refs[4:]
    (weld, linear, angular, incoming, sec_second, sec_first, girth_second, girth_first,
     column_marks, row_marks, picked) = refs[:11]
    out = refs[11:]
    if not first:
        plate_ext, out = out[0], out[1:]
    stress_out, velocity_out, disp_out = out[:3]
    out = out[3:]
    if not last:
        payload_out, out = out[0], out[1:]
    if first:
        plate_ext, out = out[0], out[1:]
    sides, sec_pair = out[0], out[1:3]
    out = out[3:]
    if not last:
        picked_out, out = out[0], out[1:]
    res_ext, vel_ext = out[:2]
    if last:
        stress_ext, velocity, disp = stress_out, velocity_out, disp_out
    else:
        stress_ext, velocity, disp, payload = out[2:6]
    sent = out[-1]

    _, rows, cols = velocity.shape
    devices = incoming.shape[0] // 2
    total = picked.shape[1]
    half = total // 2
    by_device, by_place = slot_marks(devices, half // devices)
    sends = []

    def send(source, target):
        if last:
            return
        copy = pltpu.make_async_copy(source, target, sent.at[len(sends)])
        copy.start()
        sends.append(copy)

    above, below = in_order("sec", sec_first[...], sec_second[...])
    left, right = in_order("girth", girth_first[...], girth_second[...])
    if first:
        for k in range(RESULTS):
            stress_ext[k, :rows, :cols] = stress_in[k]
        load_stress(stress_ext, plate_ext, thickness, above, below, left, right)
    else:
        load_velocity(vel_ext, velocity_in, incoming, above, below, left, right)
    for start in range(0, rows + PAD_ROWS, 8):
        plate = plate_ext[0, start : start + 8, :]
        source = stress_ext if first else stress_in
        chunk = [source[k, start : start + 8, :] for k in range(RESULTS)]
        if not first:
            chunk = stress_chunk(vel_ext, chunk, plate, start)
            for k, value in enumerate(chunk):
                stress_ext[k, start : start + 8, :] = value
        for k, value in enumerate(resultants(chunk, plate)):
            res_ext[k, start : start + 8, :] = value
        for part in pieces(rows + PAD_ROWS):
            if part.stop == start + 8:
                send(stress_ext.at[:, part, :], stress_out.at[:, part, :])

    for start in range(0, rows, 8):
        part = slice(start, start + 8)
        rates = [linear[part, :]] * 3 + [angular[part, :]] * 2
        force = force_chunk(res_ext, start, cols)
        force[2] = force[2] + pressure[part, :]
        for f in range(FIELDS):
            joined = force[f] + weld[f * rows + start : f * rows + start + 8, :]
            speed = velocity_in[f, part, :] + rates[f] * joined
            velocity[f, part, :] = speed
            disp[f, part, :] = disp_in[f, part, :] + time_step * speed
        if start % 32 == 24:
            done = slice(start - 24, start + 8)
            for source, target in ((velocity, velocity_out), (disp, disp_out)):
                send(source.at[:, done, :], target.at[:, done, :])

    ends = (cols - LANES, cols)
    left_lanes = [velocity[f, :, 0:LANES] for f in range(FIELDS)]
    right_lanes = [velocity[f, :, ends[0] : ends[1]] for f in range(FIELDS)]
    if last:
        sides[...] = edge_rows(left_lanes, right_lanes, 1)
        send_ends(
            sec_pair,
            [velocity[f, 0:1, :] for f in range(FIELDS)],
            [velocity[f, rows - 1 : rows, :] for f in range(FIELDS)],
        )
        for copy in sends:
            copy.wait()
        return
    values = pick([disp[f] for f in range(FIELDS)], column_marks[...], row_marks[...])
    picked_out[...] = jnp.concatenate(values + [values[0]] * 3, axis=0)
    near_out = collapse([value[:, :half] for value in values], by_device, by_place)
    far_out = collapse([value[:, half:] for value in values], by_device, by_place)
    corners = []
    lane = lax.broadcasted_iota(jnp.int32, (8, LANES), 1)
    for row in (0, rows - 1):
        tile = slice(row // 8 * 8, row // 8 * 8 + 8)
        for side in (0, 1):
            value = jnp.zeros((8, LANES), F32)
            for f in range(FIELDS):
                part = velocity[f, tile, ends[0] : ends[1]] if side else velocity[f, tile, 0:LANES]
                source = LANES - 1 if side else 0
                target = CORNER_LANE + f
                value = jnp.where(lane == target, pltpu.roll(part, (target - source) % LANES, 1), value)
            corners.append(jnp.broadcast_to(value[row % 8 : row % 8 + 1], (8, LANES)))
    send_joints(payload, near_out, far_out, corners)
    send(payload, payload_out)
    sides[...] = edge_rows(left_lanes, right_lanes, 2)
    send_ends(
        sec_pair,
        [velocity[f, 0:2, :] for f in range(FIELDS)],
        [velocity[f, rows - 2 : rows, :] for f in range(FIELDS)],
    )
    for copy in sends:
        copy.wait()


def final_kernel(membrane, *refs):
    if membrane:
        stress, velocity = refs[:2]
        sec_second, sec_first, girth_second, girth_first, plate_ext, height = refs[2:8]
        made, moment, vel_ext = refs[8:11]
    else:
        stress, velocity, disp, ready = refs[:4]
        sec_second, sec_first, girth_second, girth_first, plate_ext = refs[4:9]
        stress_out, velocity_out, disp_out = refs[9:12]
        made, vel_ext, sent = refs[12:]
    _, rows, cols = velocity.shape
    fields = range(0, 2) if membrane else range(2, FIELDS)
    kinds = range(0, 3) if membrane else range(3, RESULTS)
    sends = []

    def send(source, target):
        copy = pltpu.make_async_copy(source, target, sent.at[len(sends)])
        copy.start()
        sends.append(copy)

    if not membrane:
        send(ready, stress_out.at[0:3])
        send(velocity, velocity_out)
        send(disp, disp_out)
    above, below = in_order("sec", sec_first[...], sec_second[...])
    left, right = in_order("girth", girth_first[...], girth_second[...])
    columns = edge_columns(left, right, 1, rows)
    empty = jnp.zeros((PAD_ROWS, LANES), F32)
    for k, f in enumerate(fields):
        vel_ext[k, :rows, :cols] = velocity[f]
        sides = side_block(columns, f, 1)
        fill_halo(vel_ext, k, above[f : f + 1, :], below[f : f + 1, :], sides, empty)
    parts = []
    for start in range(0, rows, 8):
        part = slice(start, start + 8)
        chunk = [stress[k, part, :cols] for k in kinds]
        plate = plate_ext[0, part, :cols]
        current, along_x, along_y = [
            [value[:, :cols] for value in values]
            for values in differences(vel_ext, range(len(fields)), start)
        ]
        if membrane:
            chunk = membrane_chunk(along_x, along_y, chunk)
            weighted = plate * chunk[0] * height[0:1, :]
            parts.append(jnp.sum(weighted, axis=1, keepdims=True))
        else:
            chunk = plate_chunk(along_x, along_y, current[1:], chunk, plate)
        for k, value in enumerate(chunk):
            made[k, part, :] = value
        if not membrane and start % 16 == 8:
            done = slice(start - 8, start + 8)
            send(made.at[:, done, :], stress_out.at[kinds.start : kinds.stop, done, :])
    if membrane:
        column = jnp.broadcast_to(jnp.concatenate(parts, axis=0), (rows, LANES))
        if rows < LANES:
            column = jnp.concatenate([column, jnp.zeros((LANES - rows, LANES), F32)], axis=0)
        moment[...] = column.T[0:1, :rows]
    for copy in sends:
        copy.wait()


def call(
    kernel, vmem_bytes, outs, scratch, *operands, far=0, kept=0, far_out=0, kept_out=0,
    copies=(1,),
):
    def placed(k, away, here):
        return pltpu.HBM if k < away else pltpu.VMEM if k < away + here else None

    operands = [
        value if placed(k, far, kept) is None
        else pltpu.with_memory_space_constraint(value, placed(k, far, kept))
        for k, value in enumerate(operands)
    ]
    results = [
        (placed(k, far_out, kept_out) or jax.ShapeDtypeStruct)(shape, dtype)
        for k, (shape, dtype) in enumerate(outs)
    ]
    whole = pl.BlockSpec(memory_space=pltpu.VMEM)
    away = pl.BlockSpec(memory_space=pltpu.HBM)
    scratch = [pltpu.VMEM(shape, dtype) for shape, dtype in scratch]
    scratch += [pltpu.SemaphoreType.DMA((count,)) for count in copies]
    return pl.pallas_call(
        kernel,
        out_shape=results,
        in_specs=[away] * far + [whole] * (len(operands) - far),
        out_specs=[away] * far_out + [whole] * (len(outs) - far_out),
        scratch_shapes=scratch,
        compiler_params=pltpu.CompilerParams(vmem_limit_bytes=vmem_bytes),
    )(*operands)


def swap(pair, axis, around):
    count = lax.axis_size(axis)
    out = []
    for start, value in reversed(list(enumerate(pair))):
        couples = [(i, (i + 1) % count) for i in range(start, count, 2)]
        couples = [(i, j) for i, j in couples if j > i or around]
        out.append(lax.ppermute(value, axis, couples + [(j, i) for i, j in couples]))
    return out


def sum_over(value, axis):
    count = lax.axis_size(axis)
    if count & (count - 1):
        return lax.psum(value, axis)
    parts = [
        lax.ppermute(value, axis, [(i, i ^ step) for i in range(count)])
        for step in range(count - 1, 0, -1)
    ]
    parts = parts + [value]
    while len(parts) > 1:
        parts = [a + b for a, b in zip(parts[0::2], parts[1::2])]
    return parts[0]


def exchange(joints):
    blocks = joints.reshape(joints.shape[0] // 2, 2, LANES)
    blocks = lax.all_to_all(blocks, ("sec", "girth"), 0, 0, tiled=True)
    return blocks.reshape(joints.shape)


def local(displacement, velocity, stress, thickness, pressure, weld_from, weld_to, weld_stiff):
    rows, cols = thickness.shape
    _, devices, slots = weld_from.shape
    total = 2 * devices * slots
    girth_total = cols * lax.axis_size("girth")
    column = (lax.axis_index("girth") * cols + lax.iota(jnp.int32, cols)).astype(F32)
    height = jnp.sin(2.0 * jnp.pi / girth_total * (column + 0.5)) / girth_total
    height = jnp.broadcast_to(height[None, :], (8, cols))

    vmem_bytes = 8 * 1024 * 1024 + total * VMEM_PER_SLOT
    message = (devices * 2, LANES)
    edge = (SIDE_ROWS, LANES)
    strip = (16, cols)
    block = (FIELDS, rows, cols)
    stress_shape = (RESULTS, rows + PAD_ROWS, cols + LANES)
    plate_shape = (1, rows + PAD_ROWS, cols + LANES)
    slot_rows = (8, total)
    scratch = [(stress_shape, F32), ((FIELDS, rows + PAD_ROWS, cols + LANES), F32)]

    (payload, sec_first, sec_second, sides,
     column_marks, row_marks, picked, spring) = call(
        start_kernel,
        vmem_bytes,
        [
            (message, F32), (strip, F32), (strip, F32), (edge, F32),
            ((cols, total), BF16), ((rows, total), BF16), (slot_rows, F32), ((8, total // 2), F32),
        ],
        [
            (block, F32), ((RESULTS, rows, LANES), F32), ((RESULTS, rows, LANES), F32),
            ((RESULTS, 8, cols), F32), ((RESULTS, 8, cols), F32), ((rows, cols), jnp.int32),
            ((1, slots, devices), jnp.int32), ((1, slots, devices), jnp.int32),
            ((1, slots, devices), F32), (message, F32),
        ],
        displacement, stress, thickness,
        *[jnp.swapaxes(array, 1, 2) for array in (weld_from, weld_to, weld_stiff)],
        far=6,
        far_out=1,
        copies=(10,),
    )
    plate = None
    for step in range(STEPS):
        first, last = step == 0, step == STEPS - 1
        incoming = exchange(payload)
        ends = swap((sec_first, sec_second), "sec", False)
        sides = swap((sides, sides), "girth", True)
        state = [stress, velocity, displacement, pressure] + [thickness] * first
        *state, weld, linear, angular = call(
            functools.partial(joint_kernel, first),
            vmem_bytes,
            [(value.shape, value.dtype) for value in state]
            + [((FIELDS * rows, cols), F32), ((rows, cols), F32), ((rows, cols), F32)]
            + [(slot_rows, F32)] * first,
            [],
            *state, incoming, column_marks, row_marks, picked, spring,
            *([] if first else [plate]),
            far=len(state),
            kept_out=len(state) + 3,
            copies=(len(state),),
        )
        if first:
            *state, weld, linear, angular, spring = *state, weld, linear, angular
        outs = [(stress_shape, F32), (block, F32), (block, F32)] + [(message, F32)] * (not last)
        own = [] if last else outs
        outs = outs + [(plate_shape, F32)] * first
        outs += [(edge, F32), (strip, F32), (strip, F32)] + [(slot_rows, F32)] * (not last)
        results = call(
            functools.partial(step_kernel, first, last),
            vmem_bytes,
            outs,
            scratch + own,
            *state, weld, linear, angular, incoming, *ends, *sides, column_marks, row_marks, picked,
            *([] if first else [plate]),
            kept=len(state) + 3,
            far_out=0 if last else 4,
            kept_out=3 if last else 0,
            copies=(4 + 2 * (rows // 32),),
        )
        stress, velocity, displacement = results[:3]
        results = results[3:]
        if not last:
            payload, results = results[0], results[1:]
        if first:
            plate, results = results[0], results[1:]
        sides, sec_first, sec_second = results[:3]
        if not last:
            picked = results[3]

    ends = swap((sec_first, sec_second), "sec", False)
    sides = swap((sides, sides), "girth", True)
    membrane, partial_moment = call(
        functools.partial(final_kernel, True),
        vmem_bytes,
        [((3, rows, cols), F32), ((1, rows), F32)],
        [((2, rows + PAD_ROWS, cols + LANES), F32)],
        stress, velocity, *ends, *sides, plate, height,
        kept=2,
        kept_out=1,
        copies=(),
    )
    stress, velocity, displacement = call(
        functools.partial(final_kernel, False),
        vmem_bytes,
        [((RESULTS, rows, cols), F32), (block, F32), (block, F32)],
        [((5, rows, cols), F32), ((3, rows + PAD_ROWS, cols + LANES), F32)],
        stress, velocity, displacement, membrane, *ends, *sides, plate,
        kept=4,
        far_out=3,
        copies=(3 + rows // 16,),
    )
    moment = sum_over(partial_moment, "girth")[0]
    return (displacement, velocity, stress, moment)


def solution(mesh):
    in_specs = (
        P(None, "sec", "girth"),
        P(None, "sec", "girth"),
        P(None, "sec", "girth"),
        P("sec", "girth"),
        P("sec", "girth"),
        P(("sec", "girth"), None, None),
        P(("sec", "girth"), None, None),
        P(("sec", "girth"), None, None),
    )
    out_specs = (
        P(None, "sec", "girth"),
        P(None, "sec", "girth"),
        P(None, "sec", "girth"),
        P("sec"),
    )
    return jax.shard_map(local, mesh=mesh, in_specs=in_specs, out_specs=out_specs, check_vma=False)
```

```python
import functools

import jax
import jax.numpy as jnp
from jax import lax
from jax.experimental import pallas as pl
from jax.experimental.pallas import tpu as pltpu
from jax.sharding import PartitionSpec as P

STEPS = 3
CORNER_LANE = 112
SIDE_ROWS = 24
PIECE = 24
FIELDS = 5
RESULTS = 8
PAD_ROWS = 8
LANES = 128
VMEM_PER_SLOT = 5 * 1024

young_modulus = 4.0
poisson_ratio = 0.3
plate_modulus = young_modulus / (1.0 - poisson_ratio * poisson_ratio)
shear_modulus = young_modulus / (2.0 * (1.0 + poisson_ratio))
shear_factor = 5.0 / 6.0
time_step = 0.2
spacing_mm = 50.0
rotary_share = 1.0 / 12.0

F32 = jnp.float32
BF16 = jnp.bfloat16


def split(values):
    high = values.astype(BF16)
    low = (values - high.astype(F32)).astype(BF16)
    return high, low


def dot(a, b, contract):
    return lax.dot_general(a, b, (contract, ((), ())), preferred_element_type=F32)


def slot_marks(devices, slots):
    total = devices * slots
    lane = lax.broadcasted_iota(jnp.int32, (devices, total), 1)
    device = lax.broadcasted_iota(jnp.int32, (devices, total), 0)
    by_device = (lane // slots == device).astype(F32).astype(BF16)
    lane = lax.broadcasted_iota(jnp.int32, (slots, total), 1)
    place = lax.broadcasted_iota(jnp.int32, (slots, total), 0)
    by_place = (lane % slots == place).astype(F32)
    return by_device, by_place


def expand(blocks, by_device, by_place, turned=False):
    slots, total = by_place.shape
    wide = dot(blocks, by_device, ((1 if turned else 0,), (0,)))
    wide = wide.reshape(wide.shape[0] // slots, slots, total) * by_place[None]
    return jnp.sum(wide, axis=1)


def collapse(rows, by_device, by_place):
    slots, _ = by_place.shape
    marks = by_place.astype(BF16)
    pieces = []
    for part in (0, 1):
        blocks = [split(row)[part] * marks for row in rows]
        blocks += [jnp.zeros_like(marks)] * (LANES // slots - len(rows))
        pieces.append(jnp.concatenate(blocks, axis=0))
    return dot(by_device, pieces[0], ((1,), (1,))) + dot(by_device, pieces[1], ((1,), (1,)))


def pick(fields, column_marks, row_marks):
    rows = fields[0].shape[0]
    parts = [split(field) for field in fields]
    high = jnp.concatenate([part[0] for part in parts], axis=0)
    low = jnp.concatenate([part[1] for part in parts], axis=0)
    by_column = dot(high, column_marks, ((1,), (0,))) + dot(low, column_marks, ((1,), (0,)))
    marks = row_marks.astype(F32)
    return [
        jnp.sum(by_column[rows * f : rows * (f + 1)] * marks, axis=0, keepdims=True)
        for f in range(len(fields))
    ]


def spread(pulls, column_marks, row_marks):
    high, low = split(pulls)
    total = None
    for part in (high, low):
        marked = jnp.concatenate(
            [part[f : f + 1] * row_marks for f in range(FIELDS)], axis=0
        )
        summed = dot(marked, column_marks, ((1,), (1,)))
        total = summed if total is None else total + summed
    return total


def place():
    sec, girth = lax.axis_index("sec"), lax.axis_index("girth")
    return sec, girth, lax.axis_size("sec"), lax.axis_size("girth")


def tile_of(ref, device):
    return ref[pl.ds(pl.multiple_of(device * 8, 8), 8), :]


def set_tile(ref, device, value):
    ref[pl.ds(pl.multiple_of(device * 8, 8), 8), :] = value


def corner_neighbours():
    sec, girth, secs, girths = place()
    me = sec * girths + girth
    out = []
    for step in (-1, 1):
        row = sec + step
        inside = jnp.logical_and(row >= 0, row < secs)
        for turn in (girths - 1, 1):
            device = row * girths + lax.rem(girth + turn, girths)
            out.append((jnp.where(inside, device, me), inside))
    return out


def place_lanes(pieces):
    shape = pieces[0][0].shape
    lane = lax.broadcasted_iota(jnp.int32, shape, 1)
    block = jnp.zeros(shape, F32)
    for value, source, target, count in pieces:
        moved = value if source == target else pltpu.roll(value, (target - source) % LANES, 1)
        inside = jnp.logical_and(lane >= target, lane < target + count)
        if target + count > LANES:
            inside = jnp.logical_or(inside, lane < target + count - LANES)
        block = jnp.where(inside, moved, block)
    return block


def edge_rows(left, right, depth):
    pieces = []
    for k, (low, high) in enumerate(zip(left, right)):
        pieces.append((high, LANES - depth, 2 * depth * k, depth))
        pieces.append((low, 0, 2 * depth * k + depth, depth))
    block = place_lanes(pieces)
    rows = block.shape[0]
    if rows < LANES:
        block = jnp.concatenate([block, jnp.zeros((LANES - rows, LANES), F32)], axis=0)
    return block.T[:SIDE_ROWS]


def edge_columns(left, right, depth, rows):
    row = lax.broadcasted_iota(jnp.int32, left.shape, 0)
    both = jnp.where(lax.rem(row, 2 * depth) < depth, left, right)
    both = jnp.concatenate([both, jnp.zeros((LANES - SIDE_ROWS, LANES), F32)], axis=0)
    return both.T[:rows]


def side_block(columns, k, depth):
    return place_lanes([(columns, 2 * depth * k, LANES - depth, 2 * depth)])


def row_chunk(ref, f, start):
    count = ref.shape[1]
    if start < 0:
        return jnp.concatenate([ref[f, count + start : count, :], ref[f, 0 : 8 + start, :]], axis=0)
    if start + 8 > count:
        return jnp.concatenate([ref[f, start:count, :], ref[f, 0 : start + 8 - count, :]], axis=0)
    return ref[f, start : start + 8, :]


def difference_x(ref, f, start):
    return row_chunk(ref, f, start + 1) - row_chunk(ref, f, start - 1)


def difference_y(value):
    lanes = value.shape[1]
    return pltpu.roll(value, lanes - 1, 1) - pltpu.roll(value, 1, 1)


def radial_return(xx, yy, xy):
    offset = xx - 0.5 * yy
    square = offset * offset + 0.75 * yy * yy + 3.0 * xy * xy
    scale = lax.rsqrt(jnp.maximum(square, 1.0))
    return xx * scale, yy * scale, xy * scale


def membrane_chunk(along_x, along_y, stress):
    normal = 0.5 * time_step * plate_modulus
    skew = 0.5 * time_step * shear_modulus
    return radial_return(
        stress[0] + normal * (along_x[0] + poisson_ratio * along_y[1]),
        stress[1] + normal * (along_y[1] + poisson_ratio * along_x[0]),
        stress[2] + skew * (along_y[0] + along_x[1]),
    )


def plate_chunk(along_x, along_y, turns, stress, plate):
    arm = 0.5 * plate
    normal = 0.5 * time_step * plate_modulus * arm
    skew = 0.5 * time_step * shear_modulus
    bending = radial_return(
        stress[0] + normal * (along_x[1] + poisson_ratio * along_y[2]),
        stress[1] + normal * (along_y[2] + poisson_ratio * along_x[1]),
        stress[2] + (skew * arm) * (along_y[1] + along_x[2]),
    )
    return bending + (
        stress[3] + skew * (along_x[0] + 2.0 * turns[0]),
        stress[4] + skew * (along_y[0] + 2.0 * turns[1]),
    )


def differences(vel_ref, fields, start):
    current = [vel_ref[f, start : start + 8, :] for f in fields]
    along_x = [difference_x(vel_ref, f, start) for f in fields]
    return current, along_x, [difference_y(value) for value in current]


def stress_chunk(vel_ref, stress, plate, start):
    current, along_x, along_y = differences(vel_ref, range(FIELDS), start)
    membrane = membrane_chunk(along_x[:2], along_y[:2], stress[:3])
    return membrane + plate_chunk(along_x[2:], along_y[2:], current[3:], stress[3:], plate)


def resultants(stress, plate):
    arm = plate * plate * (1.0 / 6.0)
    shear = shear_factor * plate
    return (
        [plate * value for value in stress[0:3]]
        + [arm * value for value in stress[3:6]]
        + [shear * value for value in stress[6:8]]
    )


def force_chunk(res_ref, start, cols):
    def both(x, y):
        along_x = difference_x(res_ref, x, start)[:, :cols]
        along_y = difference_y(res_ref[y, start : start + 8, :])[:, :cols]
        return 0.5 * (along_x + along_y)

    return [
        both(0, 2),
        both(2, 1),
        both(6, 7),
        both(3, 5) - res_ref[6, start : start + 8, :cols],
        both(5, 4) - res_ref[7, start : start + 8, :cols],
    ]


def send_joints(payload, near, far, corners):
    devices = payload.shape[0] // 2
    payload[pl.ds(0, devices, stride=2), :] = near
    payload[pl.ds(1, devices, stride=2), :] = far
    row = lax.broadcasted_iota(jnp.int32, (8, LANES), 0)
    lane = lax.broadcasted_iota(jnp.int32, (8, LANES), 1)
    free = jnp.logical_and(lane >= CORNER_LANE, lane < CORNER_LANE + FIELDS)
    for (device, _), corner in zip(corner_neighbours(), corners):
        tile = lax.div(device, 4)
        here = jnp.logical_and(free, row == 2 * lax.rem(device, 4))
        set_tile(payload, tile, jnp.where(here, corner, tile_of(payload, tile)))


def in_order(axis, low, high):
    even = lax.rem(lax.axis_index(axis), 2) == 0
    return jnp.where(even, high, low), jnp.where(even, low, high)


def send_ends(pair, low, high):
    for ref in pair:
        ref[...] = jnp.zeros(ref.shape, F32)
    start = 0
    for top, bottom in zip(low, high):
        count = top.shape[0]
        for ref, value in zip(pair, in_order("sec", top, bottom)):
            ref[start : start + count, :] = value
        start += count


def corner_of(incoming, device):
    row = lax.broadcasted_iota(jnp.int32, (8, LANES), 0)
    tile = tile_of(incoming, lax.div(device, 4))
    return jnp.sum(jnp.where(row == 2 * lax.rem(device, 4), tile, 0.0), axis=0, keepdims=True)


def fetch(done, pairs):
    copies = [
        pltpu.make_async_copy(source, target, done.at[k])
        for k, (source, target) in enumerate(pairs)
    ]
    for copy in copies:
        copy.start()
    return copies


def pieces(rows):
    return [slice(0, PIECE), slice(PIECE, 2 * PIECE), slice(2 * PIECE, rows)]


def start_kernel(
    disp_in, stress_in, thickness_in, from_in, to_in, stiff_in,
    payload_out, sec_first, sec_second, sides,
    column_marks, row_marks, picked, spring,
    disp, stress_left, stress_right, stress_top, stress_bottom, thickness,
    weld_from, weld_to, weld_stiff, payload, done,
):
    rows, cols = thickness.shape
    _, slots, devices = weld_from.shape
    sec_pair = (sec_first, sec_second)
    copies = fetch(
        done,
        [
            (from_in, weld_from),
            (to_in, weld_to),
            (stiff_in, weld_stiff),
            (disp_in, disp),
            (thickness_in, thickness),
            (stress_in.at[:, :, 0:LANES], stress_left),
            (stress_in.at[:, :, cols - LANES : cols], stress_right),
            (stress_in.at[:, 0:8, :], stress_top),
            (stress_in.at[:, rows - 8 : rows, :], stress_bottom),
        ],
    )
    shift = cols.bit_length() - 1
    by_device, by_place = slot_marks(devices, slots)
    for copy in copies[:3]:
        copy.wait()
    near, far = weld_from[0], weld_to[0]
    stiff = jnp.where(near >= 0, weld_stiff[0], 0.0)
    index_parts = []
    for index in (near, far):
        index = jnp.maximum(index, 0)
        column = index & (cols - 1)
        index_parts += [index >> shift, column >> 1, column & 1]
    index_parts = [part.astype(F32).astype(BF16) for part in index_parts]
    index_parts += list(split(stiff))
    wide = [expand(part, by_device, by_place, turned=True) for part in index_parts]
    row_index = jnp.concatenate([wide[0], wide[3]], axis=1)
    column_index = jnp.concatenate([2.0 * wide[1] + wide[2], 2.0 * wide[4] + wide[5]], axis=1)
    stiff_row = wide[6] + wide[7]
    total = row_index.shape[1]
    spring[...] = jnp.broadcast_to(stiff_row, spring.shape)
    row_iota = lax.broadcasted_iota(jnp.int32, (rows, total), 0).astype(F32)
    row_hits = (row_iota == row_index).astype(F32).astype(BF16)
    row_marks[...] = row_hits
    for start in range(0, cols, 64):
        iota = (lax.broadcasted_iota(jnp.int32, (64, total), 0) + start).astype(F32)
        column_marks[start : start + 64, :] = (iota == column_index).astype(F32).astype(BF16)
    copies[3].wait()
    values = pick([disp[f] for f in range(FIELDS)], column_marks[...], row_hits)
    picked[...] = jnp.concatenate(values + [values[0]] * 3, axis=0)
    half = total // 2
    near_out = collapse([value[:, :half] for value in values] + [stiff_row], by_device, by_place)
    far_out = collapse([value[:, half:] for value in values], by_device, by_place)

    send_joints(payload, near_out, far_out, [])
    message = pltpu.make_async_copy(payload, payload_out, done.at[len(copies)])
    message.start()
    for copy in copies[4:]:
        copy.wait()
    plate = thickness[...].astype(F32) * (1.0 / spacing_mm)
    sides[...] = edge_rows(
        [stress_left[f] for f in range(RESULTS)] + [plate[:, 0:LANES]],
        [stress_right[f] for f in range(RESULTS)] + [plate[:, cols - LANES :]],
        1,
    )
    send_ends(
        sec_pair,
        [stress_top[f, 0:1, :] for f in range(RESULTS)] + [plate[0:1, :]],
        [stress_bottom[f, 7:8, :] for f in range(RESULTS)] + [plate[rows - 1 : rows, :]],
    )
    message.wait()


def fill_halo(ref, f, above, below, sides, corner):
    rows, cols = ref.shape[1] - PAD_ROWS, ref.shape[2] - LANES
    depth = above.shape[0]
    ref[f, rows:, :cols] = jnp.concatenate(
        [below, jnp.zeros((PAD_ROWS - 2 * depth, cols), F32), above], axis=0
    )
    ref[f, :rows, cols:] = sides
    ref[f, rows:, cols:] = corner


def load_velocity(vel_ext, velocity, incoming, above, below, left, right):
    columns = edge_columns(left, right, 2, velocity.shape[1])
    row = lax.broadcasted_iota(jnp.int32, (8, LANES), 0)
    corner_tiles = [
        jnp.broadcast_to(jnp.where(inside, corner_of(incoming, device), 0.0), (8, LANES))
        for device, inside in corner_neighbours()
    ]
    for f in range(FIELDS):
        vel_ext[f, : velocity.shape[1], : velocity.shape[2]] = velocity[f]
        sides = side_block(columns, f, 2)
        corner_lane = CORNER_LANE + f
        upper, lower = [
            place_lanes([(low, corner_lane, LANES - 1, 1), (high, corner_lane, 0, 1)])
            for low, high in (corner_tiles[0:2], corner_tiles[2:4])
        ]
        corner = jnp.where(row == 0, lower, jnp.where(row == 7, upper, 0.0))
        fill_halo(
            vel_ext, f, above[2 * f : 2 * f + 2, :], below[2 * f : 2 * f + 2, :], sides, corner
        )


def load_stress(stress_ext, plate_ext, thickness, above, below, left, right):
    rows, cols = thickness.shape
    columns = edge_columns(left, right, 1, rows)
    plate_ext[0, :rows, :cols] = thickness[...].astype(F32) * (1.0 / spacing_mm)
    empty = jnp.zeros((PAD_ROWS, LANES), F32)
    for f in range(RESULTS + 1):
        sides = side_block(columns, f, 1)
        ref, k = (stress_ext, f) if f < RESULTS else (plate_ext, 0)
        fill_halo(ref, k, above[f : f + 1, :], below[f : f + 1, :], sides, empty)


def set_rates(linear, angular, plate):
    square = 1.0 + plate * plate
    inverse = time_step / (plate * square)
    linear[...] = square * inverse
    angular[...] = 12.0 * inverse


def joint_kernel(first, *refs):
    far = refs[: 4 + first]
    incoming, column_marks, row_marks, picked, spring = refs[4 + first : 9 + first]
    refs = refs[9 + first :]
    if not first:
        plate_ext, refs = refs[0], refs[1:]
    near = refs[: 4 + first]
    weld, linear, angular = refs[4 + first : 7 + first]
    copies = fetch(refs[-1], list(zip(far, near)))
    devices = incoming.shape[0] // 2
    total = picked.shape[1]
    by_device, by_place = slot_marks(devices, total // 2 // devices)
    other = []
    for row in (1, 0):
        high, low = split(incoming[pl.ds(row, devices, stride=2), :])
        other.append(expand(high, by_device, by_place) + expand(low, by_device, by_place))
    if first:
        stiffness = jnp.concatenate([spring[0:1, :], other[1][5:6]], axis=1)
        spring_out = refs[8]
        spring_out[...] = jnp.broadcast_to(stiffness, spring_out.shape)
    else:
        stiffness = spring[0:1, :]
    field = lax.broadcasted_iota(jnp.int32, (8, total), 0)
    scale = jnp.where(field < 3, 1.0, rotary_share) * stiffness
    pulls = scale * (jnp.concatenate(other, axis=1) - picked[...])
    weld[...] = spread(pulls, column_marks[...], row_marks[...])
    rows, cols = linear.shape
    if not first:
        set_rates(linear, angular, plate_ext[0, :rows, :cols])
    for copy in copies:
        copy.wait()
    if first:
        set_rates(linear, angular, near[-1][...].astype(F32) * (1.0 / spacing_mm))


def step_kernel(first, last, *refs):
    stress_in, velocity_in, disp_in, pressure = refs[:4]
    if first:
        thickness, refs = refs[4], refs[5:]
    else:
        refs = refs[4:]
    (weld, linear, angular, incoming, sec_second, sec_first, girth_second, girth_first,
     column_marks, row_marks, picked) = refs[:11]
    out = refs[11:]
    if not first:
        plate_ext, out = out[0], out[1:]
    stress_out, velocity_out, disp_out = out[:3]
    out = out[3:]
    if not last:
        payload_out, out = out[0], out[1:]
    if first:
        plate_ext, out = out[0], out[1:]
    sides, sec_pair = out[0], out[1:3]
    out = out[3:]
    if last:
        sides_again, out = out[0], out[1:]
    else:
        picked_out, out = out[0], out[1:]
    res_ext, vel_ext = out[:2]
    if last:
        stress_ext, velocity, disp = stress_out, velocity_out, disp_out
    else:
        stress_ext, velocity, disp, payload = out[2:6]
    sent = out[-1]

    _, rows, cols = velocity.shape
    devices = incoming.shape[0] // 2
    total = picked.shape[1]
    half = total // 2
    by_device, by_place = slot_marks(devices, half // devices)
    sends = []

    def send(source, target):
        if last:
            return
        copy = pltpu.make_async_copy(source, target, sent.at[len(sends)])
        copy.start()
        sends.append(copy)

    above, below = in_order("sec", sec_first[...], sec_second[...])
    left, right = in_order("girth", girth_first[...], girth_second[...])
    if first:
        for k in range(RESULTS):
            stress_ext[k, :rows, :cols] = stress_in[k]
        load_stress(stress_ext, plate_ext, thickness, above, below, left, right)
    else:
        load_velocity(vel_ext, velocity_in, incoming, above, below, left, right)
    for start in range(0, rows + PAD_ROWS, 8):
        plate = plate_ext[0, start : start + 8, :]
        source = stress_ext if first else stress_in
        chunk = [source[k, start : start + 8, :] for k in range(RESULTS)]
        if not first:
            chunk = stress_chunk(vel_ext, chunk, plate, start)
            for k, value in enumerate(chunk):
                stress_ext[k, start : start + 8, :] = value
        for k, value in enumerate(resultants(chunk, plate)):
            res_ext[k, start : start + 8, :] = value
        for part in pieces(rows + PAD_ROWS):
            if part.stop == start + 8:
                send(stress_ext.at[:, part, :], stress_out.at[:, part, :])

    for start in range(0, rows, 8):
        part = slice(start, start + 8)
        rates = [linear[part, :]] * 3 + [angular[part, :]] * 2
        force = force_chunk(res_ext, start, cols)
        force[2] = force[2] + pressure[part, :]
        for f in range(FIELDS):
            joined = force[f] + weld[f * rows + start : f * rows + start + 8, :]
            speed = velocity_in[f, part, :] + rates[f] * joined
            velocity[f, part, :] = speed
            disp[f, part, :] = disp_in[f, part, :] + time_step * speed
        if start % 32 == 24:
            done = slice(start - 24, start + 8)
            for source, target in ((velocity, velocity_out), (disp, disp_out)):
                send(source.at[:, done, :], target.at[:, done, :])

    ends = (cols - LANES, cols)
    left_lanes = [velocity[f, :, 0:LANES] for f in range(FIELDS)]
    right_lanes = [velocity[f, :, ends[0] : ends[1]] for f in range(FIELDS)]
    if last:
        sides[...] = edge_rows(left_lanes, right_lanes, 1)
        sides_again[...] = sides[...]
        send_ends(
            sec_pair,
            [velocity[f, 0:1, :] for f in range(FIELDS)],
            [velocity[f, rows - 1 : rows, :] for f in range(FIELDS)],
        )
        for copy in sends:
            copy.wait()
        return
    values = pick([disp[f] for f in range(FIELDS)], column_marks[...], row_marks[...])
    picked_out[...] = jnp.concatenate(values + [values[0]] * 3, axis=0)
    near_out = collapse([value[:, :half] for value in values], by_device, by_place)
    far_out = collapse([value[:, half:] for value in values], by_device, by_place)
    corners = []
    lane = lax.broadcasted_iota(jnp.int32, (8, LANES), 1)
    for row in (0, rows - 1):
        tile = slice(row // 8 * 8, row // 8 * 8 + 8)
        for side in (0, 1):
            value = jnp.zeros((8, LANES), F32)
            for f in range(FIELDS):
                part = velocity[f, tile, ends[0] : ends[1]] if side else velocity[f, tile, 0:LANES]
                source = LANES - 1 if side else 0
                target = CORNER_LANE + f
                value = jnp.where(lane == target, pltpu.roll(part, (target - source) % LANES, 1), value)
            corners.append(jnp.broadcast_to(value[row % 8 : row % 8 + 1], (8, LANES)))
    send_joints(payload, near_out, far_out, corners)
    send(payload, payload_out)
    sides[...] = edge_rows(left_lanes, right_lanes, 2)
    send_ends(
        sec_pair,
        [velocity[f, 0:2, :] for f in range(FIELDS)],
        [velocity[f, rows - 2 : rows, :] for f in range(FIELDS)],
    )
    for copy in sends:
        copy.wait()


def final_kernel(membrane, *refs):
    if membrane:
        stress, velocity = refs[:2]
        sec_second, sec_first, girth_second, girth_first, plate_ext, height = refs[2:8]
        made, moment, vel_ext = refs[8:11]
    else:
        stress, velocity, disp, ready = refs[:4]
        sec_second, sec_first, girth_second, girth_first, plate_ext = refs[4:9]
        stress_out, velocity_out, disp_out = refs[9:12]
        made, vel_ext, sent = refs[12:]
    _, rows, cols = velocity.shape
    fields = range(0, 2) if membrane else range(2, FIELDS)
    kinds = range(0, 3) if membrane else range(3, RESULTS)
    sends = []

    def send(source, target):
        copy = pltpu.make_async_copy(source, target, sent.at[len(sends)])
        copy.start()
        sends.append(copy)

    if not membrane:
        send(ready, stress_out.at[0:3])
        send(velocity, velocity_out)
        send(disp, disp_out)
    above, below = in_order("sec", sec_first[...], sec_second[...])
    left, right = in_order("girth", girth_first[...], girth_second[...])
    columns = edge_columns(left, right, 1, rows)
    empty = jnp.zeros((PAD_ROWS, LANES), F32)
    for k, f in enumerate(fields):
        vel_ext[k, :rows, :cols] = velocity[f]
        sides = side_block(columns, f, 1)
        fill_halo(vel_ext, k, above[f : f + 1, :], below[f : f + 1, :], sides, empty)
    parts = []
    for start in range(0, rows, 8):
        part = slice(start, start + 8)
        chunk = [stress[k, part, :cols] for k in kinds]
        plate = plate_ext[0, part, :cols]
        current, along_x, along_y = [
            [value[:, :cols] for value in values]
            for values in differences(vel_ext, range(len(fields)), start)
        ]
        if membrane:
            chunk = membrane_chunk(along_x, along_y, chunk)
            weighted = plate * chunk[0] * height[0:1, :]
            parts.append(jnp.sum(weighted, axis=1, keepdims=True))
        else:
            chunk = plate_chunk(along_x, along_y, current[1:], chunk, plate)
        for k, value in enumerate(chunk):
            made[k, part, :] = value
        if not membrane and start % 16 == 8:
            done = slice(start - 8, start + 8)
            send(made.at[:, done, :], stress_out.at[kinds.start : kinds.stop, done, :])
    if membrane:
        column = jnp.broadcast_to(jnp.concatenate(parts, axis=0), (rows, LANES))
        if rows < LANES:
            column = jnp.concatenate([column, jnp.zeros((LANES - rows, LANES), F32)], axis=0)
        moment[...] = column.T[0:1, :rows]
    for copy in sends:
        copy.wait()


def call(
    kernel, vmem_bytes, outs, scratch, *operands, far=0, kept=0, far_out=0, kept_out=0,
    copies=(1,),
):
    def placed(k, away, here):
        return pltpu.HBM if k < away else pltpu.VMEM if k < away + here else None

    operands = [
        value if placed(k, far, kept) is None
        else pltpu.with_memory_space_constraint(value, placed(k, far, kept))
        for k, value in enumerate(operands)
    ]
    results = [
        (placed(k, far_out, kept_out) or jax.ShapeDtypeStruct)(shape, dtype)
        for k, (shape, dtype) in enumerate(outs)
    ]
    whole = pl.BlockSpec(memory_space=pltpu.VMEM)
    away = pl.BlockSpec(memory_space=pltpu.HBM)
    scratch = [pltpu.VMEM(shape, dtype) for shape, dtype in scratch]
    scratch += [pltpu.SemaphoreType.DMA((count,)) for count in copies]
    return pl.pallas_call(
        kernel,
        out_shape=results,
        in_specs=[away] * far + [whole] * (len(operands) - far),
        out_specs=[away] * far_out + [whole] * (len(outs) - far_out),
        scratch_shapes=scratch,
        compiler_params=pltpu.CompilerParams(vmem_limit_bytes=vmem_bytes),
    )(*operands)


def swap(pair, axis, around):
    count = lax.axis_size(axis)
    out = []
    for start, value in reversed(list(enumerate(pair))):
        couples = [(i, (i + 1) % count) for i in range(start, count, 2)]
        couples = [(i, j) for i, j in couples if j > i or around]
        out.append(lax.ppermute(value, axis, couples + [(j, i) for i, j in couples]))
    return out


def sum_over(value, axis):
    count = lax.axis_size(axis)
    if count & (count - 1):
        return lax.psum(value, axis)
    parts = [
        lax.ppermute(value, axis, [(i, i ^ step) for i in range(count)])
        for step in range(count - 1, 0, -1)
    ]
    parts = parts + [value]
    while len(parts) > 1:
        parts = [a + b for a, b in zip(parts[0::2], parts[1::2])]
    return parts[0]


def exchange(joints):
    blocks = joints.reshape(joints.shape[0] // 2, 2, LANES)
    blocks = lax.all_to_all(blocks, ("sec", "girth"), 0, 0, tiled=True)
    return blocks.reshape(joints.shape)


def local(displacement, velocity, stress, thickness, pressure, weld_from, weld_to, weld_stiff):
    rows, cols = thickness.shape
    _, devices, slots = weld_from.shape
    total = 2 * devices * slots
    girth_total = cols * lax.axis_size("girth")
    column = (lax.axis_index("girth") * cols + lax.iota(jnp.int32, cols)).astype(F32)
    height = jnp.sin(2.0 * jnp.pi / girth_total * (column + 0.5)) / girth_total
    height = jnp.broadcast_to(height[None, :], (8, cols))

    vmem_bytes = 8 * 1024 * 1024 + total * VMEM_PER_SLOT
    message = (devices * 2, LANES)
    edge = (SIDE_ROWS, LANES)
    strip = (16, cols)
    block = (FIELDS, rows, cols)
    stress_shape = (RESULTS, rows + PAD_ROWS, cols + LANES)
    plate_shape = (1, rows + PAD_ROWS, cols + LANES)
    slot_rows = (8, total)
    scratch = [(stress_shape, F32), ((FIELDS, rows + PAD_ROWS, cols + LANES), F32)]

    (payload, sec_first, sec_second, sides,
     column_marks, row_marks, picked, spring) = call(
        start_kernel,
        vmem_bytes,
        [
            (message, F32), (strip, F32), (strip, F32), (edge, F32),
            ((cols, total), BF16), ((rows, total), BF16), (slot_rows, F32), ((8, total // 2), F32),
        ],
        [
            (block, F32), ((RESULTS, rows, LANES), F32), ((RESULTS, rows, LANES), F32),
            ((RESULTS, 8, cols), F32), ((RESULTS, 8, cols), F32), ((rows, cols), jnp.int32),
            ((1, slots, devices), jnp.int32), ((1, slots, devices), jnp.int32),
            ((1, slots, devices), F32), (message, F32),
        ],
        displacement, stress, thickness,
        *[jnp.swapaxes(array, 1, 2) for array in (weld_from, weld_to, weld_stiff)],
        far=6,
        far_out=1,
        copies=(10,),
    )
    plate = None
    for step in range(STEPS):
        first, last = step == 0, step == STEPS - 1
        incoming = exchange(payload)
        ends = swap((sec_first, sec_second), "sec", False)
        sides = swap((sides, sides), "girth", True)
        state = [stress, velocity, displacement, pressure] + [thickness] * first
        *state, weld, linear, angular = call(
            functools.partial(joint_kernel, first),
            vmem_bytes,
            [(value.shape, value.dtype) for value in state]
            + [((FIELDS * rows, cols), F32), ((rows, cols), F32), ((rows, cols), F32)]
            + [(slot_rows, F32)] * first,
            [],
            *state, incoming, column_marks, row_marks, picked, spring,
            *([] if first else [plate]),
            far=len(state),
            kept_out=len(state) + 3,
            copies=(len(state),),
        )
        if first:
            *state, weld, linear, angular, spring = *state, weld, linear, angular
        outs = [(stress_shape, F32), (block, F32), (block, F32)] + [(message, F32)] * (not last)
        own = [] if last else outs
        outs = outs + [(plate_shape, F32)] * first
        outs += [(edge, F32), (strip, F32), (strip, F32), (edge if last else slot_rows, F32)]
        results = call(
            functools.partial(step_kernel, first, last),
            vmem_bytes,
            outs,
            scratch + own,
            *state, weld, linear, angular, incoming, *ends, *sides, column_marks, row_marks, picked,
            *([] if first else [plate]),
            kept=len(state) + 3,
            far_out=0 if last else 4,
            kept_out=3 if last else 0,
            copies=(4 + 2 * (rows // 32),),
        )
        stress, velocity, displacement = results[:3]
        results = results[3:]
        if not last:
            payload, results = results[0], results[1:]
        if first:
            plate, results = results[0], results[1:]
        sides, sec_first, sec_second = results[:3]
        if last:
            sides_again = results[3]
        else:
            picked = results[3]

    ends = swap((sec_first, sec_second), "sec", False)
    sides = swap((sides, sides_again), "girth", True)
    membrane, partial_moment = call(
        functools.partial(final_kernel, True),
        vmem_bytes,
        [((3, rows, cols), F32), ((1, rows), F32)],
        [((2, rows + PAD_ROWS, cols + LANES), F32)],
        stress, velocity, *ends, *sides, plate, height,
        kept=2,
        kept_out=1,
        copies=(),
    )
    stress, velocity, displacement = call(
        functools.partial(final_kernel, False),
        vmem_bytes,
        [((RESULTS, rows, cols), F32), (block, F32), (block, F32)],
        [((5, rows, cols), F32), ((3, rows + PAD_ROWS, cols + LANES), F32)],
        stress, velocity, displacement, membrane, *ends, *sides, plate,
        kept=4,
        far_out=3,
        copies=(3 + rows // 16,),
    )
    moment = sum_over(partial_moment, "girth")[0]
    return (displacement, velocity, stress, moment)


def solution(mesh):
    in_specs = (
        P(None, "sec", "girth"),
        P(None, "sec", "girth"),
        P(None, "sec", "girth"),
        P("sec", "girth"),
        P("sec", "girth"),
        P(("sec", "girth"), None, None),
        P(("sec", "girth"), None, None),
        P(("sec", "girth"), None, None),
    )
    out_specs = (
        P(None, "sec", "girth"),
        P(None, "sec", "girth"),
        P(None, "sec", "girth"),
        P("sec"),
    )
    return jax.shard_map(local, mesh=mesh, in_specs=in_specs, out_specs=out_specs, check_vma=False)
```

```python
import functools

import jax
import jax.numpy as jnp
from jax import lax
from jax.experimental import pallas as pl
from jax.experimental.pallas import tpu as pltpu
from jax.sharding import PartitionSpec as P

STEPS = 3
CORNER_LANE = 112
SIDE_ROWS = 24
PIECE = 24
FIELDS = 5
RESULTS = 8
PAD_ROWS = 8
LANES = 128
VMEM_PER_SLOT = 5 * 1024

young_modulus = 4.0
poisson_ratio = 0.3
plate_modulus = young_modulus / (1.0 - poisson_ratio * poisson_ratio)
shear_modulus = young_modulus / (2.0 * (1.0 + poisson_ratio))
shear_factor = 5.0 / 6.0
time_step = 0.2
spacing_mm = 50.0
rotary_share = 1.0 / 12.0

F32 = jnp.float32
BF16 = jnp.bfloat16


def split(values):
    high = values.astype(BF16)
    low = (values - high.astype(F32)).astype(BF16)
    return high, low


def dot(a, b, contract):
    return lax.dot_general(a, b, (contract, ((), ())), preferred_element_type=F32)


def slot_marks(devices, slots):
    total = devices * slots
    lane = lax.broadcasted_iota(jnp.int32, (devices, total), 1)
    device = lax.broadcasted_iota(jnp.int32, (devices, total), 0)
    by_device = (lane // slots == device).astype(F32).astype(BF16)
    lane = lax.broadcasted_iota(jnp.int32, (slots, total), 1)
    place = lax.broadcasted_iota(jnp.int32, (slots, total), 0)
    by_place = (lane % slots == place).astype(F32)
    return by_device, by_place


def expand(blocks, by_device, by_place, turned=False):
    slots, total = by_place.shape
    wide = dot(blocks, by_device, ((1 if turned else 0,), (0,)))
    wide = wide.reshape(wide.shape[0] // slots, slots, total) * by_place[None]
    return jnp.sum(wide, axis=1)


def collapse(rows, by_device, by_place):
    slots, _ = by_place.shape
    marks = by_place.astype(BF16)
    pieces = []
    for part in (0, 1):
        blocks = [split(row)[part] * marks for row in rows]
        blocks += [jnp.zeros_like(marks)] * (LANES // slots - len(rows))
        pieces.append(jnp.concatenate(blocks, axis=0))
    return dot(by_device, pieces[0], ((1,), (1,))) + dot(by_device, pieces[1], ((1,), (1,)))


def pick(fields, column_marks, row_marks):
    rows = fields[0].shape[0]
    parts = [split(field) for field in fields]
    both = jnp.concatenate([part[0] for part in parts] + [part[1] for part in parts], axis=0)
    by_column = dot(both, column_marks, ((1,), (0,)))
    by_column = by_column[: rows * len(fields)] + by_column[rows * len(fields) :]
    marks = row_marks.astype(F32)
    return [
        jnp.sum(by_column[rows * f : rows * (f + 1)] * marks, axis=0, keepdims=True)
        for f in range(len(fields))
    ]


def spread(pulls, column_marks, row_marks):
    marked = [
        part[f : f + 1] * row_marks for part in split(pulls) for f in range(FIELDS)
    ]
    summed = dot(jnp.concatenate(marked, axis=0), column_marks, ((1,), (1,)))
    half = summed.shape[0] // 2
    return summed[:half] + summed[half:]


def place():
    sec, girth = lax.axis_index("sec"), lax.axis_index("girth")
    return sec, girth, lax.axis_size("sec"), lax.axis_size("girth")


def tile_of(ref, device):
    return ref[pl.ds(pl.multiple_of(device * 8, 8), 8), :]


def set_tile(ref, device, value):
    ref[pl.ds(pl.multiple_of(device * 8, 8), 8), :] = value


def corner_neighbours():
    sec, girth, secs, girths = place()
    me = sec * girths + girth
    out = []
    for step in (-1, 1):
        row = sec + step
        inside = jnp.logical_and(row >= 0, row < secs)
        for turn in (girths - 1, 1):
            device = row * girths + lax.rem(girth + turn, girths)
            out.append((jnp.where(inside, device, me), inside))
    return out


def place_lanes(pieces):
    shape = pieces[0][0].shape
    lane = lax.broadcasted_iota(jnp.int32, shape, 1)
    block = jnp.zeros(shape, F32)
    for value, source, target, count in pieces:
        moved = value if source == target else pltpu.roll(value, (target - source) % LANES, 1)
        inside = jnp.logical_and(lane >= target, lane < target + count)
        if target + count > LANES:
            inside = jnp.logical_or(inside, lane < target + count - LANES)
        block = jnp.where(inside, moved, block)
    return block


def edge_rows(left, right, depth):
    pieces = []
    for k, (low, high) in enumerate(zip(left, right)):
        pieces.append((high, LANES - depth, 2 * depth * k, depth))
        pieces.append((low, 0, 2 * depth * k + depth, depth))
    block = place_lanes(pieces)
    rows = block.shape[0]
    if rows < LANES:
        block = jnp.concatenate([block, jnp.zeros((LANES - rows, LANES), F32)], axis=0)
    return block.T[:SIDE_ROWS]


def edge_columns(left, right, depth, rows):
    row = lax.broadcasted_iota(jnp.int32, left.shape, 0)
    both = jnp.where(lax.rem(row, 2 * depth) < depth, left, right)
    both = jnp.concatenate([both, jnp.zeros((LANES - SIDE_ROWS, LANES), F32)], axis=0)
    return both.T[:rows]


def side_block(columns, k, depth):
    return place_lanes([(columns, 2 * depth * k, LANES - depth, 2 * depth)])


def row_chunk(ref, f, start):
    count = ref.shape[1]
    if start < 0:
        return jnp.concatenate([ref[f, count + start : count, :], ref[f, 0 : 8 + start, :]], axis=0)
    if start + 8 > count:
        return jnp.concatenate([ref[f, start:count, :], ref[f, 0 : start + 8 - count, :]], axis=0)
    return ref[f, start : start + 8, :]


def difference_x(ref, f, start):
    return row_chunk(ref, f, start + 1) - row_chunk(ref, f, start - 1)


def difference_y(value):
    lanes = value.shape[1]
    return pltpu.roll(value, lanes - 1, 1) - pltpu.roll(value, 1, 1)


def radial_return(xx, yy, xy):
    offset = xx - 0.5 * yy
    square = offset * offset + 0.75 * yy * yy + 3.0 * xy * xy
    scale = lax.rsqrt(jnp.maximum(square, 1.0))
    return xx * scale, yy * scale, xy * scale


def membrane_chunk(along_x, along_y, stress):
    normal = 0.5 * time_step * plate_modulus
    skew = 0.5 * time_step * shear_modulus
    return radial_return(
        stress[0] + normal * (along_x[0] + poisson_ratio * along_y[1]),
        stress[1] + normal * (along_y[1] + poisson_ratio * along_x[0]),
        stress[2] + skew * (along_y[0] + along_x[1]),
    )


def plate_chunk(along_x, along_y, turns, stress, plate):
    arm = 0.5 * plate
    normal = 0.5 * time_step * plate_modulus * arm
    skew = 0.5 * time_step * shear_modulus
    bending = radial_return(
        stress[0] + normal * (along_x[1] + poisson_ratio * along_y[2]),
        stress[1] + normal * (along_y[2] + poisson_ratio * along_x[1]),
        stress[2] + (skew * arm) * (along_y[1] + along_x[2]),
    )
    return bending + (
        stress[3] + skew * (along_x[0] + 2.0 * turns[0]),
        stress[4] + skew * (along_y[0] + 2.0 * turns[1]),
    )


def differences(vel_ref, fields, start):
    current = [vel_ref[f, start : start + 8, :] for f in fields]
    along_x = [difference_x(vel_ref, f, start) for f in fields]
    return current, along_x, [difference_y(value) for value in current]


def stress_chunk(vel_ref, stress, plate, start):
    current, along_x, along_y = differences(vel_ref, range(FIELDS), start)
    membrane = membrane_chunk(along_x[:2], along_y[:2], stress[:3])
    return membrane + plate_chunk(along_x[2:], along_y[2:], current[3:], stress[3:], plate)


def resultants(stress, plate):
    arm = plate * plate * (1.0 / 6.0)
    shear = shear_factor * plate
    return (
        [plate * value for value in stress[0:3]]
        + [arm * value for value in stress[3:6]]
        + [shear * value for value in stress[6:8]]
    )


def force_chunk(res_ref, start, cols):
    def both(x, y):
        along_x = difference_x(res_ref, x, start)[:, :cols]
        along_y = difference_y(res_ref[y, start : start + 8, :])[:, :cols]
        return 0.5 * (along_x + along_y)

    return [
        both(0, 2),
        both(2, 1),
        both(6, 7),
        both(3, 5) - res_ref[6, start : start + 8, :cols],
        both(5, 4) - res_ref[7, start : start + 8, :cols],
    ]


def send_joints(payload, near, far, corners):
    devices = payload.shape[0] // 2
    payload[pl.ds(0, devices, stride=2), :] = near
    payload[pl.ds(1, devices, stride=2), :] = far
    row = lax.broadcasted_iota(jnp.int32, (8, LANES), 0)
    lane = lax.broadcasted_iota(jnp.int32, (8, LANES), 1)
    free = jnp.logical_and(lane >= CORNER_LANE, lane < CORNER_LANE + FIELDS)
    for (device, _), corner in zip(corner_neighbours(), corners):
        tile = lax.div(device, 4)
        here = jnp.logical_and(free, row == 2 * lax.rem(device, 4))
        set_tile(payload, tile, jnp.where(here, corner, tile_of(payload, tile)))


def in_order(axis, low, high):
    even = lax.rem(lax.axis_index(axis), 2) == 0
    return jnp.where(even, high, low), jnp.where(even, low, high)


def send_ends(pair, low, high):
    for ref in pair:
        ref[...] = jnp.zeros(ref.shape, F32)
    start = 0
    for top, bottom in zip(low, high):
        count = top.shape[0]
        for ref, value in zip(pair, in_order("sec", top, bottom)):
            ref[start : start + count, :] = value
        start += count


def corner_of(incoming, device):
    row = lax.broadcasted_iota(jnp.int32, (8, LANES), 0)
    tile = tile_of(incoming, lax.div(device, 4))
    return jnp.sum(jnp.where(row == 2 * lax.rem(device, 4), tile, 0.0), axis=0, keepdims=True)


def fetch(done, pairs):
    copies = [
        pltpu.make_async_copy(source, target, done.at[k])
        for k, (source, target) in enumerate(pairs)
    ]
    for copy in copies:
        copy.start()
    return copies


def pieces(rows):
    return [slice(0, PIECE), slice(PIECE, 2 * PIECE), slice(2 * PIECE, rows)]


def start_kernel(
    disp_in, stress_in, thickness_in, from_in, to_in, stiff_in,
    payload_out, sec_first, sec_second, sides,
    column_marks, row_marks, picked, spring,
    disp, stress_left, stress_right, stress_top, stress_bottom, thickness,
    weld_from, weld_to, weld_stiff, payload, done,
):
    rows, cols = thickness.shape
    _, slots, devices = weld_from.shape
    sec_pair = (sec_first, sec_second)
    copies = fetch(
        done,
        [
            (from_in, weld_from),
            (to_in, weld_to),
            (stiff_in, weld_stiff),
            (disp_in, disp),
            (thickness_in, thickness),
            (stress_in.at[:, :, 0:LANES], stress_left),
            (stress_in.at[:, :, cols - LANES : cols], stress_right),
            (stress_in.at[:, 0:8, :], stress_top),
            (stress_in.at[:, rows - 8 : rows, :], stress_bottom),
        ],
    )
    shift = cols.bit_length() - 1
    by_device, by_place = slot_marks(devices, slots)
    for copy in copies[:3]:
        copy.wait()
    near, far = weld_from[0], weld_to[0]
    stiff = jnp.where(near >= 0, weld_stiff[0], 0.0)
    index_parts = []
    for index in (near, far):
        index = jnp.maximum(index, 0)
        column = index & (cols - 1)
        index_parts += [index >> shift, column >> 1, column & 1]
    index_parts = [part.astype(F32).astype(BF16) for part in index_parts]
    index_parts += list(split(stiff))
    wide = [expand(part, by_device, by_place, turned=True) for part in index_parts]
    row_index = jnp.concatenate([wide[0], wide[3]], axis=1)
    column_index = jnp.concatenate([2.0 * wide[1] + wide[2], 2.0 * wide[4] + wide[5]], axis=1)
    stiff_row = wide[6] + wide[7]
    total = row_index.shape[1]
    spring[...] = jnp.broadcast_to(stiff_row, spring.shape)
    row_iota = lax.broadcasted_iota(jnp.int32, (rows, total), 0).astype(F32)
    row_hits = (row_iota == row_index).astype(F32).astype(BF16)
    row_marks[...] = row_hits
    for start in range(0, cols, 64):
        iota = (lax.broadcasted_iota(jnp.int32, (64, total), 0) + start).astype(F32)
        column_marks[start : start + 64, :] = (iota == column_index).astype(F32).astype(BF16)
    copies[3].wait()
    values = pick([disp[f] for f in range(FIELDS)], column_marks[...], row_hits)
    picked[...] = jnp.concatenate(values + [values[0]] * 3, axis=0)
    half = total // 2
    near_out = collapse([value[:, :half] for value in values] + [stiff_row], by_device, by_place)
    far_out = collapse([value[:, half:] for value in values], by_device, by_place)

    send_joints(payload, near_out, far_out, [])
    message = pltpu.make_async_copy(payload, payload_out, done.at[len(copies)])
    message.start()
    for copy in copies[4:]:
        copy.wait()
    plate = thickness[...].astype(F32) * (1.0 / spacing_mm)
    sides[...] = edge_rows(
        [stress_left[f] for f in range(RESULTS)] + [plate[:, 0:LANES]],
        [stress_right[f] for f in range(RESULTS)] + [plate[:, cols - LANES :]],
        1,
    )
    send_ends(
        sec_pair,
        [stress_top[f, 0:1, :] for f in range(RESULTS)] + [plate[0:1, :]],
        [stress_bottom[f, 7:8, :] for f in range(RESULTS)] + [plate[rows - 1 : rows, :]],
    )
    message.wait()


def fill_halo(ref, f, above, below, sides, corner):
    rows, cols = ref.shape[1] - PAD_ROWS, ref.shape[2] - LANES
    depth = above.shape[0]
    ref[f, rows:, :cols] = jnp.concatenate(
        [below, jnp.zeros((PAD_ROWS - 2 * depth, cols), F32), above], axis=0
    )
    ref[f, :rows, cols:] = sides
    ref[f, rows:, cols:] = corner


def load_velocity(vel_ext, velocity, incoming, above, below, left, right):
    columns = edge_columns(left, right, 2, velocity.shape[1])
    row = lax.broadcasted_iota(jnp.int32, (8, LANES), 0)
    corner_tiles = [
        jnp.broadcast_to(jnp.where(inside, corner_of(incoming, device), 0.0), (8, LANES))
        for device, inside in corner_neighbours()
    ]
    for f in range(FIELDS):
        vel_ext[f, : velocity.shape[1], : velocity.shape[2]] = velocity[f]
        sides = side_block(columns, f, 2)
        corner_lane = CORNER_LANE + f
        upper, lower = [
            place_lanes([(low, corner_lane, LANES - 1, 1), (high, corner_lane, 0, 1)])
            for low, high in (corner_tiles[0:2], corner_tiles[2:4])
        ]
        corner = jnp.where(row == 0, lower, jnp.where(row == 7, upper, 0.0))
        fill_halo(
            vel_ext, f, above[2 * f : 2 * f + 2, :], below[2 * f : 2 * f + 2, :], sides, corner
        )


def load_stress(stress_ext, plate_ext, thickness, above, below, left, right):
    rows, cols = thickness.shape
    columns = edge_columns(left, right, 1, rows)
    plate_ext[0, :rows, :cols] = thickness[...].astype(F32) * (1.0 / spacing_mm)
    empty = jnp.zeros((PAD_ROWS, LANES), F32)
    for f in range(RESULTS + 1):
        sides = side_block(columns, f, 1)
        ref, k = (stress_ext, f) if f < RESULTS else (plate_ext, 0)
        fill_halo(ref, k, above[f : f + 1, :], below[f : f + 1, :], sides, empty)


def set_rates(linear, angular, plate):
    square = 1.0 + plate * plate
    inverse = time_step / (plate * square)
    linear[...] = square * inverse
    angular[...] = 12.0 * inverse


def joint_kernel(first, *refs):
    far = refs[: 4 + first]
    incoming, column_marks, row_marks, picked, spring = refs[4 + first : 9 + first]
    refs = refs[9 + first :]
    if not first:
        plate_ext, refs = refs[0], refs[1:]
    near = refs[: 4 + first]
    weld, linear, angular = refs[4 + first : 7 + first]
    copies = fetch(refs[-1], list(zip(far, near)))
    devices = incoming.shape[0] // 2
    total = picked.shape[1]
    by_device, by_place = slot_marks(devices, total // 2 // devices)
    other = []
    for row in (1, 0):
        high, low = split(incoming[pl.ds(row, devices, stride=2), :])
        other.append(expand(high, by_device, by_place) + expand(low, by_device, by_place))
    if first:
        stiffness = jnp.concatenate([spring[0:1, :], other[1][5:6]], axis=1)
        spring_out = refs[8]
        spring_out[...] = jnp.broadcast_to(stiffness, spring_out.shape)
    else:
        stiffness = spring[0:1, :]
    field = lax.broadcasted_iota(jnp.int32, (8, total), 0)
    scale = jnp.where(field < 3, 1.0, rotary_share) * stiffness
    pulls = scale * (jnp.concatenate(other, axis=1) - picked[...])
    weld[...] = spread(pulls, column_marks[...], row_marks[...])
    rows, cols = linear.shape
    if not first:
        set_rates(linear, angular, plate_ext[0, :rows, :cols])
    for copy in copies:
        copy.wait()
    if first:
        set_rates(linear, angular, near[-1][...].astype(F32) * (1.0 / spacing_mm))


def step_kernel(first, last, *refs):
    stress_in, velocity_in, disp_in, pressure = refs[:4]
    if first:
        thickness, refs = refs[4], refs[5:]
    else:
        refs = refs[4:]
    (weld, linear, angular, incoming, sec_second, sec_first, girth_second, girth_first,
     column_marks, row_marks, picked) = refs[:11]
    out = refs[11:]
    if not first:
        plate_ext, out = out[0], out[1:]
    stress_out, velocity_out, disp_out = out[:3]
    out = out[3:]
    if not last:
        payload_out, out = out[0], out[1:]
    if first:
        plate_ext, out = out[0], out[1:]
    sides, sec_pair = out[0], out[1:3]
    out = out[3:]
    if last:
        sides_again, out = out[0], out[1:]
    else:
        picked_out, out = out[0], out[1:]
    res_ext, vel_ext = out[:2]
    if last:
        stress_ext, velocity, disp = stress_out, velocity_out, disp_out
    else:
        stress_ext, velocity, disp, payload = out[2:6]
    sent = out[-1]

    _, rows, cols = velocity.shape
    devices = incoming.shape[0] // 2
    total = picked.shape[1]
    half = total // 2
    by_device, by_place = slot_marks(devices, half // devices)
    sends = []

    def send(source, target):
        if last:
            return
        copy = pltpu.make_async_copy(source, target, sent.at[len(sends)])
        copy.start()
        sends.append(copy)

    above, below = in_order("sec", sec_first[...], sec_second[...])
    left, right = in_order("girth", girth_first[...], girth_second[...])
    if first:
        for k in range(RESULTS):
            stress_ext[k, :rows, :cols] = stress_in[k]
        load_stress(stress_ext, plate_ext, thickness, above, below, left, right)
    else:
        load_velocity(vel_ext, velocity_in, incoming, above, below, left, right)
    for start in range(0, rows + PAD_ROWS, 8):
        plate = plate_ext[0, start : start + 8, :]
        source = stress_ext if first else stress_in
        chunk = [source[k, start : start + 8, :] for k in range(RESULTS)]
        if not first:
            chunk = stress_chunk(vel_ext, chunk, plate, start)
            for k, value in enumerate(chunk):
                stress_ext[k, start : start + 8, :] = value
        for k, value in enumerate(resultants(chunk, plate)):
            res_ext[k, start : start + 8, :] = value
        for part in pieces(rows + PAD_ROWS):
            if part.stop == start + 8:
                send(stress_ext.at[:, part, :], stress_out.at[:, part, :])

    for start in range(0, rows, 8):
        part = slice(start, start + 8)
        rates = [linear[part, :]] * 3 + [angular[part, :]] * 2
        force = force_chunk(res_ext, start, cols)
        force[2] = force[2] + pressure[part, :]
        for f in range(FIELDS):
            joined = force[f] + weld[f * rows + start : f * rows + start + 8, :]
            speed = velocity_in[f, part, :] + rates[f] * joined
            velocity[f, part, :] = speed
            disp[f, part, :] = disp_in[f, part, :] + time_step * speed
        if start % 32 == 24:
            done = slice(start - 24, start + 8)
            for source, target in ((velocity, velocity_out), (disp, disp_out)):
                send(source.at[:, done, :], target.at[:, done, :])

    ends = (cols - LANES, cols)
    left_lanes = [velocity[f, :, 0:LANES] for f in range(FIELDS)]
    right_lanes = [velocity[f, :, ends[0] : ends[1]] for f in range(FIELDS)]
    if last:
        sides[...] = edge_rows(left_lanes, right_lanes, 1)
        sides_again[...] = sides[...]
        send_ends(
            sec_pair,
            [velocity[f, 0:1, :] for f in range(FIELDS)],
            [velocity[f, rows - 1 : rows, :] for f in range(FIELDS)],
        )
        for copy in sends:
            copy.wait()
        return
    values = pick([disp[f] for f in range(FIELDS)], column_marks[...], row_marks[...])
    picked_out[...] = jnp.concatenate(values + [values[0]] * 3, axis=0)
    near_out = collapse([value[:, :half] for value in values], by_device, by_place)
    far_out = collapse([value[:, half:] for value in values], by_device, by_place)
    corners = []
    lane = lax.broadcasted_iota(jnp.int32, (8, LANES), 1)
    for row in (0, rows - 1):
        tile = slice(row // 8 * 8, row // 8 * 8 + 8)
        for side in (0, 1):
            value = jnp.zeros((8, LANES), F32)
            for f in range(FIELDS):
                part = velocity[f, tile, ends[0] : ends[1]] if side else velocity[f, tile, 0:LANES]
                source = LANES - 1 if side else 0
                target = CORNER_LANE + f
                value = jnp.where(lane == target, pltpu.roll(part, (target - source) % LANES, 1), value)
            corners.append(jnp.broadcast_to(value[row % 8 : row % 8 + 1], (8, LANES)))
    send_joints(payload, near_out, far_out, corners)
    send(payload, payload_out)
    sides[...] = edge_rows(left_lanes, right_lanes, 2)
    send_ends(
        sec_pair,
        [velocity[f, 0:2, :] for f in range(FIELDS)],
        [velocity[f, rows - 2 : rows, :] for f in range(FIELDS)],
    )
    for copy in sends:
        copy.wait()


def final_kernel(membrane, *refs):
    if membrane:
        stress, velocity = refs[:2]
        sec_second, sec_first, girth_second, girth_first, plate_ext, height = refs[2:8]
        made, moment, vel_ext = refs[8:11]
    else:
        stress, velocity, disp, ready = refs[:4]
        sec_second, sec_first, girth_second, girth_first, plate_ext = refs[4:9]
        stress_out, velocity_out, disp_out = refs[9:12]
        made, vel_ext, sent = refs[12:]
    _, rows, cols = velocity.shape
    fields = range(0, 2) if membrane else range(2, FIELDS)
    kinds = range(0, 3) if membrane else range(3, RESULTS)
    sends = []

    def send(source, target):
        copy = pltpu.make_async_copy(source, target, sent.at[len(sends)])
        copy.start()
        sends.append(copy)

    if not membrane:
        send(ready, stress_out.at[0:3])
        send(velocity, velocity_out)
        send(disp, disp_out)
    above, below = in_order("sec", sec_first[...], sec_second[...])
    left, right = in_order("girth", girth_first[...], girth_second[...])
    columns = edge_columns(left, right, 1, rows)
    empty = jnp.zeros((PAD_ROWS, LANES), F32)
    for k, f in enumerate(fields):
        vel_ext[k, :rows, :cols] = velocity[f]
        sides = side_block(columns, f, 1)
        fill_halo(vel_ext, k, above[f : f + 1, :], below[f : f + 1, :], sides, empty)
    parts = []
    for start in range(0, rows, 8):
        part = slice(start, start + 8)
        chunk = [stress[k, part, :cols] for k in kinds]
        plate = plate_ext[0, part, :cols]
        current, along_x, along_y = [
            [value[:, :cols] for value in values]
            for values in differences(vel_ext, range(len(fields)), start)
        ]
        if membrane:
            chunk = membrane_chunk(along_x, along_y, chunk)
            weighted = plate * chunk[0] * height[0:1, :]
            parts.append(jnp.sum(weighted, axis=1, keepdims=True))
        else:
            chunk = plate_chunk(along_x, along_y, current[1:], chunk, plate)
        for k, value in enumerate(chunk):
            made[k, part, :] = value
        if not membrane and start % 16 == 8:
            done = slice(start - 8, start + 8)
            send(made.at[:, done, :], stress_out.at[kinds.start : kinds.stop, done, :])
    if membrane:
        column = jnp.broadcast_to(jnp.concatenate(parts, axis=0), (rows, LANES))
        if rows < LANES:
            column = jnp.concatenate([column, jnp.zeros((LANES - rows, LANES), F32)], axis=0)
        moment[...] = column.T[0:1, :rows]
    for copy in sends:
        copy.wait()


def call(
    kernel, vmem_bytes, outs, scratch, *operands, far=0, kept=0, far_out=0, kept_out=0,
    copies=(1,),
):
    def placed(k, away, here):
        return pltpu.HBM if k < away else pltpu.VMEM if k < away + here else None

    operands = [
        value if placed(k, far, kept) is None
        else pltpu.with_memory_space_constraint(value, placed(k, far, kept))
        for k, value in enumerate(operands)
    ]
    results = [
        (placed(k, far_out, kept_out) or jax.ShapeDtypeStruct)(shape, dtype)
        for k, (shape, dtype) in enumerate(outs)
    ]
    whole = pl.BlockSpec(memory_space=pltpu.VMEM)
    away = pl.BlockSpec(memory_space=pltpu.HBM)
    scratch = [pltpu.VMEM(shape, dtype) for shape, dtype in scratch]
    scratch += [pltpu.SemaphoreType.DMA((count,)) for count in copies]
    return pl.pallas_call(
        kernel,
        out_shape=results,
        in_specs=[away] * far + [whole] * (len(operands) - far),
        out_specs=[away] * far_out + [whole] * (len(outs) - far_out),
        scratch_shapes=scratch,
        compiler_params=pltpu.CompilerParams(vmem_limit_bytes=vmem_bytes),
    )(*operands)


def swap(pair, axis, around):
    count = lax.axis_size(axis)
    out = []
    for start, value in reversed(list(enumerate(pair))):
        couples = [(i, (i + 1) % count) for i in range(start, count, 2)]
        couples = [(i, j) for i, j in couples if j > i or around]
        out.append(lax.ppermute(value, axis, couples + [(j, i) for i, j in couples]))
    return out


def sum_over(value, axis):
    count = lax.axis_size(axis)
    if count & (count - 1):
        return lax.psum(value, axis)
    parts = [
        lax.ppermute(value, axis, [(i, i ^ step) for i in range(count)])
        for step in range(count - 1, 0, -1)
    ]
    parts = parts + [value]
    while len(parts) > 1:
        parts = [a + b for a, b in zip(parts[0::2], parts[1::2])]
    return parts[0]


def exchange(joints):
    blocks = joints.reshape(joints.shape[0] // 2, 2, LANES)
    blocks = lax.all_to_all(blocks, ("sec", "girth"), 0, 0, tiled=True)
    return blocks.reshape(joints.shape)


def local(displacement, velocity, stress, thickness, pressure, weld_from, weld_to, weld_stiff):
    rows, cols = thickness.shape
    _, devices, slots = weld_from.shape
    total = 2 * devices * slots
    girth_total = cols * lax.axis_size("girth")
    column = (lax.axis_index("girth") * cols + lax.iota(jnp.int32, cols)).astype(F32)
    height = jnp.sin(2.0 * jnp.pi / girth_total * (column + 0.5)) / girth_total
    height = jnp.broadcast_to(height[None, :], (8, cols))

    vmem_bytes = 8 * 1024 * 1024 + total * VMEM_PER_SLOT
    message = (devices * 2, LANES)
    edge = (SIDE_ROWS, LANES)
    strip = (16, cols)
    block = (FIELDS, rows, cols)
    stress_shape = (RESULTS, rows + PAD_ROWS, cols + LANES)
    plate_shape = (1, rows + PAD_ROWS, cols + LANES)
    slot_rows = (8, total)
    scratch = [(stress_shape, F32), ((FIELDS, rows + PAD_ROWS, cols + LANES), F32)]

    (payload, sec_first, sec_second, sides,
     column_marks, row_marks, picked, spring) = call(
        start_kernel,
        vmem_bytes,
        [
            (message, F32), (strip, F32), (strip, F32), (edge, F32),
            ((cols, total), BF16), ((rows, total), BF16), (slot_rows, F32), ((8, total // 2), F32),
        ],
        [
            (block, F32), ((RESULTS, rows, LANES), F32), ((RESULTS, rows, LANES), F32),
            ((RESULTS, 8, cols), F32), ((RESULTS, 8, cols), F32), ((rows, cols), jnp.int32),
            ((1, slots, devices), jnp.int32), ((1, slots, devices), jnp.int32),
            ((1, slots, devices), F32), (message, F32),
        ],
        displacement, stress, thickness,
        *[jnp.swapaxes(array, 1, 2) for array in (weld_from, weld_to, weld_stiff)],
        far=6,
        far_out=1,
        copies=(10,),
    )
    plate = None
    for step in range(STEPS):
        first, last = step == 0, step == STEPS - 1
        incoming = exchange(payload)
        ends = swap((sec_first, sec_second), "sec", False)
        sides = swap((sides, sides), "girth", True)
        state = [stress, velocity, displacement, pressure] + [thickness] * first
        *state, weld, linear, angular = call(
            functools.partial(joint_kernel, first),
            vmem_bytes,
            [(value.shape, value.dtype) for value in state]
            + [((FIELDS * rows, cols), F32), ((rows, cols), F32), ((rows, cols), F32)]
            + [(slot_rows, F32)] * first,
            [],
            *state, incoming, column_marks, row_marks, picked, spring,
            *([] if first else [plate]),
            far=len(state),
            kept_out=len(state) + 3,
            copies=(len(state),),
        )
        if first:
            *state, weld, linear, angular, spring = *state, weld, linear, angular
        outs = [(stress_shape, F32), (block, F32), (block, F32)] + [(message, F32)] * (not last)
        own = [] if last else outs
        outs = outs + [(plate_shape, F32)] * first
        outs += [(edge, F32), (strip, F32), (strip, F32), (edge if last else slot_rows, F32)]
        results = call(
            functools.partial(step_kernel, first, last),
            vmem_bytes,
            outs,
            scratch + own,
            *state, weld, linear, angular, incoming, *ends, *sides, column_marks, row_marks, picked,
            *([] if first else [plate]),
            kept=len(state) + 3,
            far_out=0 if last else 4,
            kept_out=3 if last else 0,
            copies=(4 + 2 * (rows // 32),),
        )
        stress, velocity, displacement = results[:3]
        results = results[3:]
        if not last:
            payload, results = results[0], results[1:]
        if first:
            plate, results = results[0], results[1:]
        sides, sec_first, sec_second = results[:3]
        if last:
            sides_again = results[3]
        else:
            picked = results[3]

    ends = swap((sec_first, sec_second), "sec", False)
    sides = swap((sides, sides_again), "girth", True)
    membrane, partial_moment = call(
        functools.partial(final_kernel, True),
        vmem_bytes,
        [((3, rows, cols), F32), ((1, rows), F32)],
        [((2, rows + PAD_ROWS, cols + LANES), F32)],
        stress, velocity, *ends, *sides, plate, height,
        kept=2,
        kept_out=1,
        copies=(),
    )
    stress, velocity, displacement = call(
        functools.partial(final_kernel, False),
        vmem_bytes,
        [((RESULTS, rows, cols), F32), (block, F32), (block, F32)],
        [((5, rows, cols), F32), ((3, rows + PAD_ROWS, cols + LANES), F32)],
        stress, velocity, displacement, membrane, *ends, *sides, plate,
        kept=4,
        far_out=3,
        copies=(3 + rows // 16,),
    )
    moment = sum_over(partial_moment, "girth")[0]
    return (displacement, velocity, stress, moment)


def solution(mesh):
    in_specs = (
        P(None, "sec", "girth"),
        P(None, "sec", "girth"),
        P(None, "sec", "girth"),
        P("sec", "girth"),
        P("sec", "girth"),
        P(("sec", "girth"), None, None),
        P(("sec", "girth"), None, None),
        P(("sec", "girth"), None, None),
    )
    out_specs = (
        P(None, "sec", "girth"),
        P(None, "sec", "girth"),
        P(None, "sec", "girth"),
        P("sec"),
    )
    return jax.shard_map(local, mesh=mesh, in_specs=in_specs, out_specs=out_specs, check_vma=False)
```
